32 devices in a mesh: chan: 16 (over z, y, core), win: 2 (over x).
Axes of the slice: x: 2, y: 2, z: 4, core: 2. Of those that a mesh axis runs over, the one named last changes fastest.
Arguments:
- traces: bfloat16 [24, 1024, 4096], P('win', 'chan'), may hold values from -6 to 6
- quality: int32 [1024], P('chan'), may hold values 0 or 1
- fold_block: int32 [1024, 1], replicated, may hold values from 0 to 15; in each aligned block of 64 rows (0 to 63, 64 to 127, ...) at most 8 rows name the same one
- fold_offset: int32 [1024], replicated, may hold values from 0 to 63
Outputs:
- neighbour_lags: float32 [1024, 64, 256], P(('chan', 'win'))
- fold_lags: float32 [1024, 256], P(('chan', 'win'))
The draws below stay inside these ranges and needn't reach their ends.
Inputs may be any that keep to these rules, and one draw needn't show every extreme that they name: `fold_block`: within each aligned block of 64 channels no block number appears more than 8 times.
All inputs are finite; a program needn't handle non-finite values. No bound on the sum of `quality` on one device may be relied on, other than what follows from the above.
Results may differ from the reference program's by a relative error of at most 0.0052.
Values may be sent and summed in bfloat16 or wider, within the bound.
No kernel may reach another device: no remote copies, remote signals or barrier semaphores. Data moves between devices by JAX's collectives and lax.ppermute only.
A program may use at most 128 MiB of HBM per device.

```python
import math
import jax
import jax.numpy as jnp
import numpy as np
from jax import lax

L = 4096
F = 256
BAND_LO = 32
NLAG = 256
REACH = 64
CAP = 8
CH_DEV = 64
CHANNELS = 1024
WINDOWS = 24
N_CHAN = 16


def plant(array, rng, least, high):
    longest = array.shape.index(max(array.shape))
    spots = []
    for shift in (0, 1):
        where = [jax.random.randint(jax.random.fold_in(rng, axis), (), 0, length) for axis, length in enumerate(array.shape)]
        where[longest] = (where[longest] + shift) % array.shape[longest]
        spots.append(tuple(where))
    return array.at[spots[0]].set(least).at[spots[1]].set(high)


def block_levels(stream_key, dims, pieces, least, high):
    factor_of = 1.0
    for position, parts in pieces:
        heights = jax.random.uniform(jax.random.fold_in(jax.random.fold_in(stream_key, 6), position), (parts,), jnp.float32, least / len(pieces), high / len(pieces))
        factor_of = factor_of * jnp.repeat(jnp.exp(heights), dims[position] // parts).reshape((-1,) + (1,) * (len(dims) - 1 - position))
    return factor_of


def routed_block(rng, own, number, rows, number_of, top, reach, skew):
    ranking = jax.random.permutation(rng, number_of)
    crowded, ordinary = portions_of(number_of, rows * top, reach, skew, True), portions_of(number_of, rows * top, reach, skew, False)
    places = jnp.arange(number_of)

    def named(sizes, offset_by):
        used = int((sizes > 0).sum())
        fixed = max(1, used // 4)
        moved = fixed + (places - fixed + offset_by * (used - fixed)) % max(1, number_of - fixed)
        return jnp.zeros((number_of,), jnp.int32).at[ranking[jnp.where(places < fixed, places, moved)]].set(jnp.asarray(sizes, jnp.int32))

    sizes = jnp.where(number % 4 == 0, named(crowded, number // 4), named(ordinary, number - number // 4 - 1))
    mixed = jax.random.permutation(jax.random.fold_in(own, 3), number_of)
    donor, receiver = mixed[0:number_of // 2 * 2:2], mixed[1:number_of // 2 * 2:2]
    room = jnp.minimum(sizes[donor] - 1, reach - sizes[receiver]) // 2
    room = jnp.where((donor == ranking[0]) | (receiver == ranking[0]) | (sizes[receiver] == 0), 0, jnp.maximum(room, 0))
    moved = jax.random.randint(jax.random.fold_in(own, 4), (number_of // 2,), 0, 1 << 20) % (room + 1)
    sizes = sizes.at[donor].add(-moved).at[receiver].add(moved)
    labels = jnp.searchsorted(jnp.cumsum(sizes), jnp.arange(rows * top), side="right").astype(jnp.int32)
    listing = labels.reshape(top, rows).T
    listing = listing[jax.random.permutation(jax.random.fold_in(own, 1), rows)]
    offset_by = jax.random.randint(jax.random.fold_in(own, 2), (rows, 1), 0, top)
    return jnp.take_along_axis(listing, (jnp.arange(top)[None, :] + offset_by) % top, axis=1)


def portions_of(count, total, bound, skew, full):
    weights = [(1 << 20) // math.isqrt(grade ** skew) + 1 for grade in range(1, count + 1)]
    largest = bound if full else min(bound, max(-(-total // count), total * weights[0] // sum(weights)))
    least = 1 if total - largest >= count - 1 else 0
    holding, rest = [largest] + [least] * (count - 1), total - largest - least * (count - 1)
    while rest > 0:
        free = [i for i in range(1, count) if holding[i] < largest] or [i for i in range(1, count) if holding[i] < bound]
        pool, remaining = sum([weights[i] for i in free]), rest
        for i in free:
            extra = min(bound - holding[i], max(1, remaining * weights[i] // pool), rest)
            holding[i] = holding[i] + extra
            rest = rest - extra
    return np.array(holding)


def bell_draw(key, extent, deviation, limit, split=(), kind=jnp.bfloat16):
    gain = block_levels(key, extent, split, -0.22, 0.18) if split else 1.0
    entries = jax.random.normal(key, extent, jnp.float32) * deviation * gain
    return jnp.minimum(jnp.maximum(entries, -limit), limit).astype(kind)


def setup_inputs(seed: int = 0) -> dict:
    key_of = jax.random.split(jax.random.key(seed), 5)
    traces = bell_draw(key_of[0], (WINDOWS, CHANNELS, L), 1.0, 6.0, ((0, 2), (1, 16)))
    quality = plant((jax.random.randint(key_of[1], (CHANNELS,), 0, 8) < 7).astype(jnp.int32), jax.random.fold_in(key_of[1], 1), 0, 1)
    fold_block_keys = jax.random.split(jax.random.fold_in(key_of[2], 1), CHANNELS // CH_DEV)
    fold_block_turns = jax.random.permutation(jax.random.fold_in(key_of[2], 3), CHANNELS // CH_DEV)
    fold_block = jax.vmap(lambda own, number: routed_block(jax.random.fold_in(key_of[2], 2), own, number, CH_DEV, N_CHAN, 1, CAP, 1))(fold_block_keys, fold_block_turns).reshape((CHANNELS, 1))
    fold_offset = plant(jax.random.randint(key_of[3], (CHANNELS,), 0, CH_DEV), jax.random.fold_in(key_of[3], 1), 0, CH_DEV - 1).astype(jnp.int32)
    return dict(traces=traces, quality=quality, fold_block=fold_block, fold_offset=fold_offset)


smooth_reach = 4

def forward_table(length, bin_count, lowest):
    samples = jnp.arange(length, dtype=jnp.int32)[:, None]
    frequency = (jnp.arange(bin_count, dtype=jnp.int32) + lowest)[None, :]
    angles = (samples * frequency % length).astype(jnp.float32) * (2.0 * math.pi / length)
    return jnp.concatenate([jnp.cos(angles), -jnp.sin(angles)], axis=1).astype(jnp.bfloat16)

def inverse_table(bin_count, lowest, lag_count):
    shifts = jnp.arange(lag_count, dtype=jnp.int32)[None, :] + lag_count // 2
    frequency = (jnp.arange(bin_count, dtype=jnp.int32) + lowest)[:, None]
    angles = (frequency * shifts % lag_count).astype(jnp.float32) * (2.0 * math.pi / lag_count)
    return jnp.concatenate([jnp.cos(angles), -jnp.sin(angles)], axis=0)

def whiten(spectra, keep_mask):
    bin_count = spectra.shape[-1] // 2
    real_part = spectra[..., :bin_count]
    imag_part = spectra[..., bin_count:]
    energy = real_part * real_part + imag_part * imag_part
    padded = jnp.pad(energy, ((0, 0), (0, 0), (smooth_reach, smooth_reach)))
    smooth = sum([padded[..., offset:offset + bin_count] for offset in range(2 * smooth_reach + 1)]) / (2.0 * smooth_reach + 1.0)
    water_level = lax.optimization_barrier(jnp.mean(energy, axis=-1, keepdims=True))
    scaling = lax.rsqrt(smooth + 0.1 * water_level + 1e-06) * keep_mask[None, :, None]
    return jnp.concatenate([real_part * scaling, imag_part * scaling], axis=-1).astype(jnp.bfloat16)

def cross_spectrum(left_block, right_block):
    half_width = left_block.shape[-1] // 2
    left_real = left_block[..., :half_width].astype(jnp.float32)
    left_imag = left_block[..., half_width:].astype(jnp.float32)
    right_real = right_block[..., :half_width].astype(jnp.float32)
    right_imag = right_block[..., half_width:].astype(jnp.float32)
    real_part = lax.optimization_barrier(jnp.sum(left_real * right_real + left_imag * right_imag, axis=0))
    imag_part = lax.optimization_barrier(jnp.sum(left_imag * right_real - left_real * right_imag, axis=0))
    return jnp.concatenate([real_part, imag_part], axis=-1)

def reference(traces, quality, fold_block, fold_offset):
    forward = forward_table(L, F, BAND_LO)
    keep_mask = quality.astype(jnp.float32)

    def one_window(window_traces):
        spectra = jnp.dot(window_traces, forward, preferred_element_type=jnp.float32)
        return whiten(spectra[None], keep_mask)[0]
    whitened = lax.map(one_window, traces)
    padded = jnp.pad(whitened, ((0, 0), (0, REACH), (0, 0)))

    def one_offset(offset):
        shifted = lax.dynamic_slice_in_dim(padded, offset, CHANNELS, axis=1)
        return cross_spectrum(whitened, shifted)
    offsets = jnp.arange(1, REACH + 1, dtype=jnp.int32)
    neighbour_terms = lax.map(one_offset, offsets)
    partner_index = (fold_block[:, 0] * CH_DEV + fold_offset).astype(jnp.int32)
    partner_terms = cross_spectrum(whitened, jnp.take(whitened, partner_index, axis=1))
    stacks = jnp.concatenate([jnp.transpose(neighbour_terms, (1, 0, 2)), partner_terms[:, None, :]], axis=1)
    inverse = inverse_table(F, BAND_LO, NLAG)
    factor = 1.0 / math.sqrt(F * WINDOWS)
    lagged = jnp.einsum('cpf,fl->cpl', stacks, inverse, precision=lax.Precision.HIGHEST) * factor
    return (lagged[:, :REACH, :], lagged[:, REACH, :])
```

```python
import functools
import math

import jax
import jax.numpy as jnp
import numpy as np
from jax import lax
from jax.experimental import pallas as pl
from jax.experimental.pallas import tpu as pltpu
from jax.sharding import PartitionSpec as P

F = 256
H = F // 2
BAND_LO = 32
NLAG = 256
REACH = 64
CAP = 8
SPAN = REACH + 8
smooth_reach = 4
K_STEPS = 8
VMEM_LIMIT = 48 * 1024 * 1024


def bin_order():
    lanes = np.arange(H)
    first = (lanes - BAND_LO) % F
    second = (-lanes - BAND_LO) % F
    second[0] = (H - BAND_LO) % F
    return first, second


def forward_table(length):
    samples = np.arange(length, dtype=np.int64)[:, None]
    parts = []
    for bins in bin_order():
        angles = (samples * (bins + BAND_LO)[None, :] % length) * (2.0 * math.pi / length)
        parts += [np.cos(angles), -np.sin(angles)]
    return np.concatenate(parts, axis=1).astype(np.float32).astype(jnp.bfloat16)


def band_matrix():
    order = np.concatenate(bin_order())
    return (np.abs(order[:, None] - order[None, :]) <= smooth_reach).astype(np.float32).astype(jnp.bfloat16)


def inverse_tables(factor):
    shifts = (np.arange(NLAG) + NLAG // 2)[None, :]
    lanes = np.arange(H)[:, None]
    angles = (lanes * shifts % NLAG) * (2.0 * math.pi / NLAG)
    sign = np.where(shifts[0] % 2 == 0, 1.0, -1.0)
    real, imag = np.cos(angles), -np.sin(angles)
    real[0] = (1.0 + sign) / 2.0
    imag[0] = (1.0 - sign) / 2.0
    table = np.concatenate([real, imag], axis=0) * factor
    high = table.astype(np.float32).astype(jnp.bfloat16)
    low = (table - high.astype(np.float64)).astype(np.float32).astype(jnp.bfloat16)
    return high, low


def lag_transform(stacks, high, low):
    top = stacks.astype(jnp.bfloat16)
    rest = (stacks - top.astype(jnp.float32)).astype(jnp.bfloat16)
    dot = functools.partial(jnp.dot, preferred_element_type=jnp.float32)
    return dot(top, high) + (dot(rest, high) + dot(top, low))


def fold_columns(first, second, imag):
    lane = lax.broadcasted_iota(jnp.int32, first.shape, first.ndim - 1)
    return first + second, jnp.where(lane == 0, first - second, imag)


def spectra_kernel(traces_ref, table_ref, band_ref, keep_ref, wanted_ref, whitened_ref, outgoing_ref, spectra):
    step = pl.program_id(0)
    product = jnp.dot(traces_ref[...], table_ref[...], preferred_element_type=jnp.float32)

    @pl.when(step == 0)
    def _():
        spectra[...] = product

    @pl.when(step > 0)
    def _():
        spectra[...] += product

    @pl.when(step == pl.num_programs(0) - 1)
    def _():
        rows = keep_ref.shape[0]
        band = band_ref[...]
        keep = keep_ref[...]
        place = lax.broadcasted_iota(jnp.int32, (wanted_ref.shape[0], rows), 1)
        selector = (place == wanted_ref[...]).astype(jnp.float32).astype(jnp.bfloat16)
        count = outgoing_ref.shape[0]

        def pair(index, carry):
            values = spectra[pl.ds(pl.multiple_of(index * rows, rows), rows), :]
            parts = [values[:, q * H : (q + 1) * H] for q in range(4)]
            energy = jnp.concatenate(
                [parts[0] * parts[0] + parts[1] * parts[1], parts[2] * parts[2] + parts[3] * parts[3]], axis=1
            )
            top = energy.astype(jnp.bfloat16)
            rest = (energy - top.astype(jnp.float32)).astype(jnp.bfloat16)
            smooth = jnp.dot(top, band, preferred_element_type=jnp.float32) + jnp.dot(
                rest, band, preferred_element_type=jnp.float32
            )
            water = jnp.sum(energy, axis=1, keepdims=True) * (1.0 / F)
            scaling = lax.rsqrt(smooth / (2.0 * smooth_reach + 1.0) + 0.1 * water + 1e-06) * keep
            near, far = scaling[:, :H], scaling[:, H:]
            white = jnp.concatenate(
                [parts[0] * near, parts[1] * near, parts[2] * far, parts[3] * far], axis=1
            ).astype(jnp.bfloat16)
            whitened_ref[pl.ds(pl.multiple_of(index * rows, rows), rows), :] = white
            sent = jnp.dot(selector, white, preferred_element_type=jnp.float32).astype(jnp.bfloat16)
            outgoing_ref[:, pl.ds(pl.multiple_of(index * 2 * CAP, 2 * CAP), 2 * CAP), :] = sent.reshape(
                count, 2 * CAP, sent.shape[-1]
            )
            return carry

        lax.fori_loop(0, spectra.shape[0] // rows, pair, 0)


def spectra_call(traces, keep, wanted, chan_count):
    rows, length = traces.shape
    pair_rows = keep.shape[0]
    block = length // K_STEPS
    return pl.pallas_call(
        spectra_kernel,
        grid=(K_STEPS,),
        in_specs=[
            pl.BlockSpec((rows, block), lambda k: (0, k)),
            pl.BlockSpec((block, 2 * F), lambda k: (k, 0)),
            pl.BlockSpec((F, F), lambda k: (0, 0)),
            pl.BlockSpec(keep.shape, lambda k: (0, 0)),
            pl.BlockSpec(wanted.shape, lambda k: (0, 0)),
        ],
        out_specs=[
            pl.BlockSpec((rows, 2 * F), lambda k: (0, 0)),
            pl.BlockSpec((chan_count, rows // pair_rows * 2 * CAP, 2 * F), lambda k: (0, 0, 0)),
        ],
        out_shape=[
            jax.ShapeDtypeStruct((rows, 2 * F), jnp.bfloat16),
            jax.ShapeDtypeStruct((chan_count, rows // pair_rows * 2 * CAP, 2 * F), jnp.bfloat16),
        ],
        scratch_shapes=[pltpu.VMEM((rows, 2 * F), jnp.float32)],
        compiler_params=pltpu.CompilerParams(vmem_limit_bytes=VMEM_LIMIT),
        cost_estimate=pl.CostEstimate(
            flops=2 * rows * length * 2 * F, bytes_accessed=2 * (rows + 2 * F) * length, transcendentals=rows * F
        ),
        name="spectra",
    )(traces, jnp.asarray(forward_table(length)), jnp.asarray(band_matrix()), keep, wanted)


def cross_kernel(last, with_sum, base_ref, own_ref, next_ref, *refs):
    refs = list(refs)
    sum_ref = refs.pop(0) if with_sum else None
    if last:
        high_ref, low_ref, out_ref, wide, spread, total = refs
    else:
        out_ref, wide, spread = refs
        total = out_ref
    windows, ch_dev, _ = own_ref.shape
    own_count = spread.shape[1]
    base = pl.multiple_of(base_ref[0], 8)

    def widen(w, carry):
        wide[w, :ch_dev, :] = own_ref[w].astype(jnp.float32)
        wide[w, ch_dev:, :] = next_ref[w].astype(jnp.float32)
        for tile in range(own_count // 8):
            rows = wide[w, pl.ds(pl.multiple_of(base + 8 * tile, 8), 8), :]
            for i in range(8):
                for q in range(4):
                    spread[w, 8 * tile + i, q] = jnp.broadcast_to(rows[i : i + 1, q * H : (q + 1) * H], (8, H))
        return carry

    lax.fori_loop(0, windows, widen, 0)

    group, tiles = 4, 3
    rounds = SPAN // (8 * tiles)

    def block(index, carry):
        g = index // rounds
        j = index % rounds
        start = pl.multiple_of(base + 8 * (g // 2) + 8 * tiles * j, 8)

        def add_window(w, sums):
            sums = list(sums)
            right = [
                [wide[w, pl.ds(pl.multiple_of(start + 8 * t, 8), 8), q * H : (q + 1) * H] for q in range(4)]
                for t in range(tiles)
            ]
            for i in range(group):
                left = [spread[w, group * g + i, q] for q in range(4)]
                for t in range(tiles):
                    at = 3 * (i * tiles + t)
                    r = right[t]
                    sums[at] = sums[at] + (left[0] * r[0] + left[1] * r[1])
                    sums[at + 1] = sums[at + 1] + (left[2] * r[2] + left[3] * r[3])
                    sums[at + 2] = sums[at + 2] + ((left[1] * r[0] - left[0] * r[1]) + (left[2] * r[3] - left[3] * r[2]))
            return tuple(sums)

        zero = jnp.zeros((8, H), jnp.float32)
        sums = lax.fori_loop(0, windows, add_window, (zero,) * (3 * group * tiles), unroll=2)
        for i in range(group):
            for t in range(tiles):
                at = 3 * (i * tiles + t)
                real, imag = fold_columns(sums[at], sums[at + 1], sums[at + 2])
                where = pl.ds(pl.multiple_of(8 * tiles * j + 8 * t, 8), 8)
                if with_sum:
                    real = real + sum_ref[group * g + i, where, :H]
                    imag = imag + sum_ref[group * g + i, where, H:]
                total[group * g + i, where, :H] = real
                total[group * g + i, where, H:] = imag
        return carry

    lax.fori_loop(0, own_count // group * rounds, block, 0)

    if last:

        def finish(eight, carry):
            first = pl.multiple_of(8 * eight, 8)
            stacks = total[pl.ds(first, 8)].reshape(8 * SPAN, F)
            lagged = lag_transform(stacks, high_ref[...], low_ref[...]).reshape(8, SPAN, NLAG)
            for i in range(8):
                out_ref[first + i] = lagged[i, i + 1 : i + 1 + REACH, :]
            return carry

        lax.fori_loop(0, own_count // 8, finish, 0)


def cross_call(own, upper, base, own_count, sums, tables):
    windows, ch_dev, columns = own.shape
    last = tables is not None
    with_sum = sums is not None
    operands = [base, own, upper]
    if with_sum:
        operands.append(sums)
    scratch = [
        pltpu.VMEM((windows, 2 * ch_dev, columns), jnp.float32),
        pltpu.VMEM((windows, own_count, 4, 8, H), jnp.float32),
    ]
    if last:
        operands += list(tables)
        scratch.append(pltpu.VMEM((own_count, SPAN, F), jnp.float32))
    shape = (own_count, REACH, NLAG) if last else (own_count, SPAN, F)
    vmem = pl.BlockSpec(memory_space=pltpu.VMEM)
    return pl.pallas_call(
        functools.partial(cross_kernel, last, with_sum),
        in_specs=[pl.BlockSpec(memory_space=pltpu.SMEM)] + [vmem] * (len(operands) - 1),
        out_specs=vmem,
        out_shape=jax.ShapeDtypeStruct(shape, jnp.float32),
        scratch_shapes=scratch,
        compiler_params=pltpu.CompilerParams(vmem_limit_bytes=VMEM_LIMIT),
        cost_estimate=pl.CostEstimate(
            flops=10_000_000_000, bytes_accessed=4 * own.size + 4 * own_count * SPAN * F, transcendentals=0
        ),
        name="cross",
    )(*operands)


def fold_kernel(incoming_ref, own_ref, source_ref, high_ref, low_ref, out_ref, sums):
    step = pl.program_id(0)

    @pl.when(step == 0)
    def _():
        sums[...] = jnp.zeros_like(sums)

    count, slots, columns = incoming_ref.shape
    rows = own_ref.shape[0]
    ch_dev = rows // 2
    place = lax.broadcasted_iota(jnp.int32, (rows, count * slots), 1)
    picker = (place == source_ref[...]).astype(jnp.float32).astype(jnp.bfloat16)
    right = jnp.dot(picker, incoming_ref[...].reshape(count * slots, columns), preferred_element_type=jnp.float32)
    left = own_ref[...].astype(jnp.float32)
    l = [left[:, q * H : (q + 1) * H] for q in range(4)]
    r = [right[:, q * H : (q + 1) * H] for q in range(4)]
    first = l[0] * r[0] + l[1] * r[1]
    second = l[2] * r[2] + l[3] * r[3]
    imag = (l[1] * r[0] - l[0] * r[1]) + (l[2] * r[3] - l[3] * r[2])
    for n, term in enumerate((first, second, imag)):
        sums[n] += term[:ch_dev] + term[ch_dev:]

    @pl.when(step == pl.num_programs(0) - 1)
    def _():
        stacks = jnp.concatenate(fold_columns(sums[0], sums[1], sums[2]), axis=1)
        out_ref[...] = lag_transform(stacks, high_ref[...], low_ref[...])


def fold_call(incoming, own, source, tables):
    count, slots, columns = incoming.shape
    rows = source.shape[0]
    pairs = own.shape[0] // rows
    whole = lambda array: pl.BlockSpec(array.shape, lambda s: (0,) * array.ndim)
    return pl.pallas_call(
        fold_kernel,
        grid=(pairs,),
        in_specs=[
            pl.BlockSpec((count, slots // pairs, columns), lambda s: (0, s, 0)),
            pl.BlockSpec((rows, columns), lambda s: (s, 0)),
            whole(source),
            whole(tables[0]),
            whole(tables[1]),
        ],
        out_specs=pl.BlockSpec((rows // 2, NLAG), lambda s: (0, 0)),
        out_shape=jax.ShapeDtypeStruct((rows // 2, NLAG), jnp.float32),
        scratch_shapes=[pltpu.VMEM((3, rows // 2, H), jnp.float32)],
        compiler_params=pltpu.CompilerParams(vmem_limit_bytes=VMEM_LIMIT),
        cost_estimate=pl.CostEstimate(
            flops=2 * rows * pairs * count * 2 * CAP * columns,
            bytes_accessed=2 * (incoming.size + own.size),
            transcendentals=0,
        ),
        name="fold",
    )(incoming, own, source, *tables)


def fold_routes(fold_block, fold_offset, device, chan_count, ch_dev):
    owners = fold_block[:, 0].reshape(chan_count, ch_dev)
    places = fold_offset.reshape(chan_count, ch_dev)
    row_ids = jnp.arange(ch_dev, dtype=jnp.int32)
    earlier = row_ids[None, :] < row_ids[:, None]
    same = owners[:, :, None] == owners[:, None, :]
    ranks = jnp.sum((same & earlier[None]).astype(jnp.int32), axis=2)
    slots = jnp.arange(CAP, dtype=jnp.int32)
    chosen = (owners == device)[:, None, :] & (ranks[:, None, :] == slots[None, :, None])
    picked = jnp.sum(jnp.where(chosen, places[:, None, :] + 1, 0), axis=2) - 1
    half = jnp.arange(2, dtype=jnp.int32)
    wanted = jnp.where(picked[:, None, :] >= 0, picked[:, None, :] + ch_dev * half[None, :, None], -1)
    own_blocks = lax.dynamic_index_in_dim(owners, device, 0, keepdims=False)
    own_ranks = lax.dynamic_index_in_dim(ranks, device, 0, keepdims=False)
    source = 2 * CAP * own_blocks[None, :] + CAP * half[:, None] + own_ranks[None, :]
    return wanted.reshape(-1, 1), source.reshape(-1, 1)


def from_above(block):
    count = lax.axis_size("chan")
    return lax.ppermute(block, "chan", [(i, i - 1) for i in range(1, count)])


def round_win(block, shift):
    count = lax.axis_size("win")
    return lax.ppermute(block, "win", [(i, (i + shift) % count) for i in range(count)])


def local(traces, quality, fold_block, fold_offset):
    win_dev, ch_dev, length = traces.shape
    chan_count = lax.axis_size("chan")
    win_count = lax.axis_size("win")
    device = lax.axis_index("chan")
    window_part = lax.axis_index("win")
    own_count = ch_dev // win_count
    tables = [jnp.asarray(t) for t in inverse_tables(1.0 / math.sqrt(F * win_dev * win_count))]
    wanted, source = fold_routes(fold_block, fold_offset, device, chan_count, ch_dev)
    keep = jnp.tile(quality.astype(jnp.float32), 2)[:, None]
    flat, outgoing = spectra_call(traces.reshape(win_dev * ch_dev, length), keep, wanted, chan_count)
    whitened = flat.reshape(win_dev, ch_dev, 2 * F)
    base = (window_part * own_count).astype(jnp.int32).reshape(1)
    blocks = [whitened] + [round_win(whitened, shift) for shift in range(1, win_count)]
    incoming = lax.all_to_all(outgoing, "chan", split_axis=0, concat_axis=0, tiled=True)
    sums = None
    for n, block in enumerate(blocks):
        sums = cross_call(
            block, from_above(block), base, own_count, sums, tables if n == win_count - 1 else None
        )
    share = fold_call(incoming, flat, source, tables)
    fold = lax.dynamic_slice_in_dim(share, base[0], own_count, 0)
    for shift in range(1, win_count):
        target = (window_part + shift) % win_count * own_count
        fold = fold + round_win(lax.dynamic_slice_in_dim(share, target, own_count, 0), shift)
    return (sums, fold)


def solution(mesh):
    in_specs = (P("win", "chan", None), P("chan"), P(), P())
    out_specs = (P(("chan", "win"), None, None), P(("chan", "win"), None))
    return jax.shard_map(local, mesh=mesh, in_specs=in_specs, out_specs=out_specs, check_vma=False)
```

```python
import functools
import math

import jax
import jax.numpy as jnp
import numpy as np
from jax import lax
from jax.experimental import pallas as pl
from jax.experimental.pallas import tpu as pltpu
from jax.sharding import PartitionSpec as P

F = 256
H = F // 2
BAND_LO = 32
NLAG = 256
REACH = 64
CAP = 8
SPAN = REACH + 8
smooth_reach = 4
K_STEPS = 8
VMEM_LIMIT = 32 * 1024 * 1024
SPECTRA_VMEM_LIMIT = 56 * 1024 * 1024


def bin_order():
    lanes = np.arange(H)
    first = (lanes - BAND_LO) % F
    second = (-lanes - BAND_LO) % F
    second[0] = (H - BAND_LO) % F
    return first, second


def forward_table(length):
    samples = np.arange(length, dtype=np.int64)[:, None]
    parts = []
    for bins in bin_order():
        angles = (samples * (bins + BAND_LO)[None, :] % length) * (2.0 * math.pi / length)
        parts += [np.cos(angles), -np.sin(angles)]
    return np.concatenate(parts, axis=1).astype(np.float32).astype(jnp.bfloat16)


def inverse_tables(factor):
    shifts = (np.arange(NLAG) + NLAG // 2)[None, :]
    lanes = np.arange(H)[:, None]
    angles = (lanes * shifts % NLAG) * (2.0 * math.pi / NLAG)
    sign = np.where(shifts[0] % 2 == 0, 1.0, -1.0)
    real, imag = np.cos(angles), -np.sin(angles)
    real[0] = (1.0 + sign) / 2.0
    imag[0] = (1.0 - sign) / 2.0
    table = np.concatenate([real, imag], axis=0) * factor
    high = table.astype(np.float32).astype(jnp.bfloat16)
    low = (table - high.astype(np.float64)).astype(np.float32).astype(jnp.bfloat16)
    return high, low


def lag_transform(stacks, high, low):
    top = stacks.astype(jnp.bfloat16)
    rest = (stacks - top.astype(jnp.float32)).astype(jnp.bfloat16)
    dot = functools.partial(jnp.dot, preferred_element_type=jnp.float32)
    return dot(top, high) + (dot(rest, high) + dot(top, low))


def fold_columns(first, second, imag):
    lane = lax.broadcasted_iota(jnp.int32, first.shape, first.ndim - 1)
    return first + second, jnp.where(lane == 0, first - second, imag)


def lanes_of(shape):
    return lax.broadcasted_iota(jnp.int32, shape, len(shape) - 1)


def rows_of(shape):
    return lax.broadcasted_iota(jnp.int32, shape, len(shape) - 2)


def band_matrix():
    def bins(index):
        residue = jnp.where(index < H, index, jnp.where(index == H, H, 2 * F - (index - H)))
        return (residue - BAND_LO + F) & (F - 1)

    apart = bins(rows_of((F, F))) - bins(lanes_of((F, F)))
    return (jnp.abs(apart) <= smooth_reach).astype(jnp.float32).astype(jnp.bfloat16)


def exact_dot(left, right):
    return jnp.dot(left.astype(jnp.bfloat16), right.astype(jnp.bfloat16), preferred_element_type=jnp.float32)


def slot_selector(owners, places, device, ch_dev):
    height, width = owners.shape
    per_row = width // ch_dev
    wanted = (owners == device).astype(jnp.float32)
    before = rows_of((width, width))
    after = lanes_of((width, width))
    earlier = ((before < after) & (before // ch_dev == after // ch_dev)).astype(jnp.float32)
    ranks = exact_dot(wanted, earlier)
    slots = jnp.where(wanted > 0, ranks, float(CAP))
    count = height * per_row * 2 * CAP
    to_row = (rows_of((count, height)) // (2 * CAP * per_row) == lanes_of((count, height))).astype(jnp.float32)
    row_slots = exact_dot(to_row, slots)
    row_places = exact_dot(to_row, places.astype(jnp.float32))
    shape = (count, width)
    row = rows_of(shape)
    mine = (row_slots == (row % CAP).astype(jnp.float32)) & (lanes_of(shape) // ch_dev == row // (2 * CAP) % per_row)
    place = jnp.sum(jnp.where(mine, row_places + 1.0, 0.0), axis=1, keepdims=True).astype(jnp.int32) - 1
    shape = (count, 2 * ch_dev)
    half = rows_of(shape) // CAP % 2
    lane = lanes_of(shape)
    return ((lane == place + ch_dev * half) & (place >= 0)).astype(jnp.float32).astype(jnp.bfloat16)


def spectra_kernel(where_ref, traces_ref, table_ref, quality_ref, owners_ref, places_ref, whitened_ref, outgoing_ref,
                   traces, table, spectra, selector, sems):
    steps, _, block = traces.shape

    def copies(k):
        at = pl.ds(k * block, block)
        return (
            pltpu.make_async_copy(traces_ref.at[:, at], traces.at[k], sems.at[0, k]),
            pltpu.make_async_copy(table_ref.at[at, :], table.at[k], sems.at[1, k]),
        )

    for k in range(steps):
        for copy in copies(k):
            copy.start()

    ch_dev = quality_ref.shape[1]
    selector[...] = slot_selector(owners_ref[...], places_ref[...], where_ref[0], ch_dev)
    band = band_matrix()
    rows = 4 * ch_dev if spectra.shape[0] % (4 * ch_dev) == 0 else 2 * ch_dev
    shape = (rows, ch_dev)
    keep = jnp.sum(
        jnp.where(rows_of(shape) % ch_dev == lanes_of(shape), quality_ref[...].astype(jnp.float32), 0.0),
        axis=1, keepdims=True,
    )

    def product(k):
        for copy in copies(k):
            copy.wait()
        return jnp.dot(traces[k], table[k], preferred_element_type=jnp.float32)

    spectra[...] = product(0)

    def accumulate(k, carry):
        spectra[...] += product(k)
        return carry

    lax.fori_loop(1, steps, accumulate, 0)
    count = outgoing_ref.shape[0]

    def whiten(index, carry):
        at = pl.ds(pl.multiple_of(index * rows, rows), rows)
        values = spectra[at, :]
        parts = [values[:, q * H : (q + 1) * H] for q in range(4)]
        energy = jnp.concatenate(
            [parts[0] * parts[0] + parts[1] * parts[1], parts[2] * parts[2] + parts[3] * parts[3]], axis=1
        )
        top = energy.astype(jnp.bfloat16)
        rest = (energy - top.astype(jnp.float32)).astype(jnp.bfloat16)
        smooth = jnp.dot(top, band, preferred_element_type=jnp.float32) + jnp.dot(
            rest, band, preferred_element_type=jnp.float32
        )
        water = jnp.sum(energy, axis=1, keepdims=True) * (1.0 / F)
        scaling = lax.rsqrt(smooth * (1.0 / (2.0 * smooth_reach + 1.0)) + (0.1 * water + 1e-06)) * keep
        near, far = scaling[:, :H], scaling[:, H:]
        white = jnp.concatenate(
            [parts[0] * near, parts[1] * near, parts[2] * far, parts[3] * far], axis=1
        ).astype(jnp.bfloat16)
        whitened_ref[at, :] = white
        for n in range(rows // (2 * ch_dev)):
            sent = jnp.dot(
                selector[...], white[2 * ch_dev * n : 2 * ch_dev * (n + 1)], preferred_element_type=jnp.float32
            ).astype(jnp.bfloat16)
            first = pl.multiple_of((index * (rows // (2 * ch_dev)) + n) * 2 * CAP, 2 * CAP)
            outgoing_ref[:, pl.ds(first, 2 * CAP), :] = sent.reshape(count, 2 * CAP, sent.shape[-1])
        return carry

    lax.fori_loop(0, spectra.shape[0] // rows, whiten, 0)


def vmem_spec():
    return pl.BlockSpec(memory_space=pltpu.VMEM)


def smem_spec():
    return pl.BlockSpec(memory_space=pltpu.SMEM)


def spectra_call(where, traces, quality, owners, places, chan_count):
    rows, length = traces.shape
    ch_dev = quality.shape[1]
    block = length // K_STEPS
    slots = rows // (2 * ch_dev) * 2 * CAP
    anywhere = pl.BlockSpec(memory_space=pltpu.HBM)
    return pl.pallas_call(
        spectra_kernel,
        in_specs=[smem_spec(), anywhere, anywhere, vmem_spec(), vmem_spec(), vmem_spec()],
        out_specs=[vmem_spec(), vmem_spec()],
        out_shape=[
            jax.ShapeDtypeStruct((rows, 2 * F), jnp.bfloat16),
            jax.ShapeDtypeStruct((chan_count, slots, 2 * F), jnp.bfloat16),
        ],
        scratch_shapes=[
            pltpu.VMEM((K_STEPS, rows, block), jnp.bfloat16),
            pltpu.VMEM((K_STEPS, block, 2 * F), jnp.bfloat16),
            pltpu.VMEM((rows, 2 * F), jnp.float32),
            pltpu.VMEM((chan_count * 2 * CAP, 2 * ch_dev), jnp.bfloat16),
            pltpu.SemaphoreType.DMA((2, K_STEPS)),
        ],
        compiler_params=pltpu.CompilerParams(vmem_limit_bytes=SPECTRA_VMEM_LIMIT),
        cost_estimate=pl.CostEstimate(
            flops=2 * rows * length * 2 * F, bytes_accessed=2 * (rows + 2 * F) * length, transcendentals=rows * F
        ),
        name="spectra",
    )(where, traces, jnp.asarray(forward_table(length)), quality, owners, places)


def cross_kernel(last, with_sum, local_windows, where_ref, first_ref, second_ref, *refs):
    refs = list(refs)
    sum_ref = refs.pop(0) if with_sum else None
    if last:
        high_ref, low_ref, out_ref, wide, spread, total = refs
    else:
        out_ref, wide, spread = refs
        total = out_ref
    windows, own_count = spread.shape[:2]
    ch_dev = wide.shape[1] // 2
    base = pl.multiple_of(where_ref[1] * own_count, 8)

    def widen(w, carry):
        if local_windows:
            wide[w, :ch_dev, :] = first_ref[w].astype(jnp.float32)
            wide[w, ch_dev:, :] = second_ref[w].astype(jnp.float32)
        else:
            shared = ch_dev - own_count
            wide[w, shared:ch_dev, :] = first_ref[w].astype(jnp.float32)
            rows = second_ref[w].astype(jnp.float32)
            for tile in range(ch_dev // 8):
                at = base + 8 * tile
                at = pl.multiple_of(jnp.where(at < shared, at, at + own_count), 8)
                wide[w, pl.ds(at, 8), :] = rows[8 * tile : 8 * tile + 8]
        for tile in range(own_count // 8):
            rows = wide[w, pl.ds(pl.multiple_of(base + 8 * tile, 8), 8), :]
            for i in range(8):
                for q in range(4):
                    spread[w, 8 * tile + i, q] = jnp.broadcast_to(rows[i : i + 1, q * H : (q + 1) * H], (8, H))
        return carry

    lax.fori_loop(0, windows, widen, 0)

    group, tiles = 4, 3
    rounds = SPAN // (8 * tiles)

    def block(index, carry):
        g = index // rounds
        j = index % rounds
        start = pl.multiple_of(base + 8 * (g // 2) + 8 * tiles * j, 8)

        def add_window(w, sums):
            sums = list(sums)
            right = [
                [wide[w, pl.ds(pl.multiple_of(start + 8 * t, 8), 8), q * H : (q + 1) * H] for q in range(4)]
                for t in range(tiles)
            ]
            for i in range(group):
                left = [spread[w, group * g + i, q] for q in range(4)]
                for t in range(tiles):
                    at = 3 * (i * tiles + t)
                    r = right[t]
                    sums[at] = sums[at] + (left[0] * r[0] + left[1] * r[1])
                    sums[at + 1] = sums[at + 1] + (left[2] * r[2] + left[3] * r[3])
                    sums[at + 2] = sums[at + 2] + ((left[1] * r[0] - left[0] * r[1]) + (left[2] * r[3] - left[3] * r[2]))
            return tuple(sums)

        zero = jnp.zeros((8, H), jnp.float32)
        sums = lax.fori_loop(0, windows, add_window, (zero,) * (3 * group * tiles), unroll=2)
        for i in range(group):
            for t in range(tiles):
                at = 3 * (i * tiles + t)
                real, imag = fold_columns(sums[at], sums[at + 1], sums[at + 2])
                where = pl.ds(pl.multiple_of(8 * tiles * j + 8 * t, 8), 8)
                if with_sum:
                    real = real + sum_ref[group * g + i, where, :H]
                    imag = imag + sum_ref[group * g + i, where, H:]
                total[group * g + i, where, :H] = real
                total[group * g + i, where, H:] = imag
        return carry

    lax.fori_loop(0, own_count // group * rounds, block, 0)

    if last:

        def finish(eight, carry):
            first = pl.multiple_of(8 * eight, 8)
            stacks = total[pl.ds(first, 8)].reshape(8 * SPAN, F)
            lagged = lag_transform(stacks, high_ref[...], low_ref[...]).reshape(8, SPAN, NLAG)
            for i in range(8):
                out_ref[first + i] = lagged[i, i + 1 : i + 1 + REACH, :]
            return carry

        lax.fori_loop(0, own_count // 8, finish, 0)


def cross_call(where, first, second, ch_dev, own_count, sums, tables, local_windows):
    windows, _, columns = first.shape
    last = tables is not None
    with_sum = sums is not None
    operands = [where, first, second]
    if with_sum:
        operands.append(sums)
    scratch = [
        pltpu.VMEM((windows, 2 * ch_dev, columns), jnp.float32),
        pltpu.VMEM((windows, own_count, 4, 8, H), jnp.float32),
    ]
    if last:
        operands += list(tables)
        scratch.append(pltpu.VMEM((own_count, SPAN, F), jnp.float32))
    shape = (own_count, REACH, NLAG) if last else (own_count, SPAN, F)
    return pl.pallas_call(
        functools.partial(cross_kernel, last, with_sum, local_windows),
        in_specs=[smem_spec()] + [vmem_spec()] * (len(operands) - 1),
        out_specs=vmem_spec(),
        out_shape=jax.ShapeDtypeStruct(shape, jnp.float32),
        scratch_shapes=scratch,
        compiler_params=pltpu.CompilerParams(vmem_limit_bytes=VMEM_LIMIT),
        cost_estimate=pl.CostEstimate(
            flops=10_000_000_000, bytes_accessed=4 * windows * ch_dev * columns + 4 * own_count * SPAN * F, transcendentals=0
        ),
        name="cross",
    )(*operands)


def fold_kernel(where_ref, incoming_ref, own_ref, owners_ref, high_ref, low_ref, out_ref, sums, picker):
    step = pl.program_id(0)
    rows = own_ref.shape[0]
    ch_dev = rows // 2

    @pl.when(step == 0)
    def _():
        sums[...] = jnp.zeros_like(sums)
        owners = owners_ref[...].astype(jnp.float32)
        per_row = owners.shape[1] // ch_dev
        device = where_ref[0]
        line = jnp.sum(jnp.where(rows_of(owners.shape) == device // per_row, owners, 0.0), axis=0, keepdims=True)
        shape = (rows, owners.shape[1])
        line = jnp.broadcast_to(line, shape)
        first = device % per_row * ch_dev
        place = first + rows_of(shape) % ch_dev
        lane = lanes_of(shape)
        owner = jnp.sum(jnp.where(lane == place, line, 0.0), axis=1, keepdims=True)
        earlier = (lane >= first) & (lane < place) & (line == owner)
        rank = jnp.sum(earlier.astype(jnp.float32), axis=1, keepdims=True)
        source = (2 * CAP * owner + rank).astype(jnp.int32)
        shape = picker.shape
        target = source + CAP * (rows_of(shape) // ch_dev)
        picker[...] = (lanes_of(shape) == target).astype(jnp.float32).astype(jnp.bfloat16)

    count, slots, columns = incoming_ref.shape
    right = jnp.dot(
        picker[...], incoming_ref[...].reshape(count * slots, columns), preferred_element_type=jnp.float32
    )
    left = own_ref[...].astype(jnp.float32)
    l = [left[:, q * H : (q + 1) * H] for q in range(4)]
    r = [right[:, q * H : (q + 1) * H] for q in range(4)]
    first = l[0] * r[0] + l[1] * r[1]
    second = l[2] * r[2] + l[3] * r[3]
    imag = (l[1] * r[0] - l[0] * r[1]) + (l[2] * r[3] - l[3] * r[2])
    for n, term in enumerate((first, second, imag)):
        sums[n] += term[:ch_dev] + term[ch_dev:]

    @pl.when(step == pl.num_programs(0) - 1)
    def _():
        stacks = jnp.concatenate(fold_columns(sums[0], sums[1], sums[2]), axis=1)
        out_ref[...] = lag_transform(stacks, high_ref[...], low_ref[...])


def fold_call(where, incoming, own, owners, ch_dev, tables):
    count, slots, columns = incoming.shape
    rows = 2 * ch_dev
    pairs = own.shape[0] // rows
    whole = lambda array: pl.BlockSpec(array.shape, lambda s: (0,) * array.ndim)
    return pl.pallas_call(
        fold_kernel,
        grid=(pairs,),
        in_specs=[
            smem_spec(),
            pl.BlockSpec((count, slots // pairs, columns), lambda s: (0, s, 0)),
            pl.BlockSpec((rows, columns), lambda s: (s, 0)),
            whole(owners),
            whole(tables[0]),
            whole(tables[1]),
        ],
        out_specs=pl.BlockSpec((ch_dev, NLAG), lambda s: (0, 0)),
        out_shape=jax.ShapeDtypeStruct((ch_dev, NLAG), jnp.float32),
        scratch_shapes=[
            pltpu.VMEM((3, ch_dev, H), jnp.float32),
            pltpu.VMEM((rows, count * slots // pairs), jnp.bfloat16),
        ],
        compiler_params=pltpu.CompilerParams(vmem_limit_bytes=VMEM_LIMIT),
        cost_estimate=pl.CostEstimate(
            flops=2 * rows * pairs * count * 2 * CAP * columns,
            bytes_accessed=2 * (incoming.size + own.size),
            transcendentals=0,
        ),
        name="fold",
    )(where, incoming, own, owners, *tables)


def from_above(block):
    count = lax.axis_size("chan")
    return lax.ppermute(block, "chan", [(i, i - 1) for i in range(1, count)])


def round_win(block, shift):
    count = lax.axis_size("win")
    return lax.ppermute(block, "win", [(i, (i + shift) % count) for i in range(count)])


def local(traces, quality, fold_block, fold_offset):
    win_dev, ch_dev, length = traces.shape
    chan_count = lax.axis_size("chan")
    win_count = lax.axis_size("win")
    window_part = lax.axis_index("win")
    own_count = ch_dev // win_count
    shared = ch_dev - own_count
    where = jnp.stack([lax.axis_index("chan"), window_part]).astype(jnp.int32)
    tables = [jnp.asarray(t) for t in inverse_tables(1.0 / math.sqrt(F * win_dev * win_count))]
    owners = fold_block.reshape(-1, 2 * ch_dev)
    places = fold_offset.reshape(-1, 2 * ch_dev)
    flat, outgoing = spectra_call(
        where, traces.reshape(win_dev * ch_dev, length), quality.reshape(1, ch_dev), owners, places, chan_count
    )
    whitened = flat.reshape(win_dev, ch_dev, 2 * F)
    upper = from_above(whitened)
    common = [round_win(whitened[:, shared:], shift) for shift in range(1, win_count)]
    incoming = lax.all_to_all(outgoing, "chan", split_axis=0, concat_axis=0, tiled=True)
    offered = jnp.concatenate([whitened[:, :shared], upper], axis=1)
    special = [
        round_win(
            lax.dynamic_slice_in_dim(offered, (window_part + shift) % win_count * own_count, ch_dev, 1), shift
        )
        for shift in range(1, win_count)
    ]
    arrived = [(whitened, upper)] + list(zip(common, special))
    sums = None
    for n, (first, second) in enumerate(arrived):
        ends = tables if n == win_count - 1 else None
        sums = cross_call(where, first, second, ch_dev, own_count, sums, ends, n == 0)
    share = fold_call(where, incoming, flat, owners, ch_dev, tables)
    fold = lax.dynamic_slice_in_dim(share, window_part * own_count, own_count, 0)
    for shift in range(1, win_count):
        target = (window_part + shift) % win_count * own_count
        fold = fold + round_win(lax.dynamic_slice_in_dim(share, target, own_count, 0), shift)
    return (sums, fold)


def solution(mesh):
    in_specs = (P("win", "chan", None), P("chan"), P(), P())
    out_specs = (P(("chan", "win"), None, None), P(("chan", "win"), None))
    return jax.shard_map(local, mesh=mesh, in_specs=in_specs, out_specs=out_specs, check_vma=False)
```

```python
import functools
import math

import jax
import jax.numpy as jnp
import numpy as np
from jax import lax
from jax.experimental import pallas as pl
from jax.experimental.pallas import tpu as pltpu
from jax.sharding import PartitionSpec as P

F = 256
H = F // 2
BAND_LO = 32
NLAG = 256
REACH = 64
CAP = 8
SPAN = REACH + 8
smooth_reach = 4
ROW_STEPS = 3
VMEM_LIMIT = 32 * 1024 * 1024
SPECTRA_VMEM_LIMIT = 56 * 1024 * 1024


def lane_residues():
    return np.concatenate([np.arange(0, H, 2), np.arange(1, H, 2)])


def bin_order():
    residues = lane_residues()
    first = (residues - BAND_LO) % F
    second = (-residues - BAND_LO) % F
    second[0] = (H - BAND_LO) % F
    return first, second


def forward_table(length):
    samples = np.arange(length // 2, dtype=np.int64)[:, None]
    parts = []
    for parity in range(2):
        for bins in bin_order():
            bins = bins[parity * H // 2 : (parity + 1) * H // 2]
            angles = (samples * (bins + BAND_LO)[None, :] % length) * (2.0 * math.pi / length)
            parts += [np.cos(angles), -np.sin(angles)]
    return np.concatenate(parts, axis=1).astype(np.float32).astype(jnp.bfloat16)


def inverse_tables(factor):
    shifts = (np.arange(NLAG) + NLAG // 2)[None, :]
    residues = lane_residues()[:, None]
    angles = (residues * shifts % NLAG) * (2.0 * math.pi / NLAG)
    sign = np.where(shifts[0] % 2 == 0, 1.0, -1.0)
    real, imag = np.cos(angles), -np.sin(angles)
    real[0] = (1.0 + sign) / 2.0
    imag[0] = (1.0 - sign) / 2.0
    table = np.concatenate([real, imag], axis=0) * factor
    high = table.astype(np.float32).astype(jnp.bfloat16)
    low = (table - high.astype(np.float64)).astype(np.float32).astype(jnp.bfloat16)
    return high, low


def lag_transform(stacks, high, low):
    top = stacks.astype(jnp.bfloat16)
    rest = (stacks - top.astype(jnp.float32)).astype(jnp.bfloat16)
    dot = functools.partial(jnp.dot, preferred_element_type=jnp.float32)
    return dot(top, high) + (dot(rest, high) + dot(top, low))


def fold_columns(first, second, imag):
    lane = lax.broadcasted_iota(jnp.int32, first.shape, first.ndim - 1)
    return first + second, jnp.where(lane == 0, first - second, imag)


def lanes_of(shape):
    return lax.broadcasted_iota(jnp.int32, shape, len(shape) - 1)


def rows_of(shape):
    return lax.broadcasted_iota(jnp.int32, shape, len(shape) - 2)


def band_matrix():
    def bins(index):
        lane = index & (H - 1)
        residue = jnp.where(lane < H // 2, 2 * lane, 2 * lane - H + 1)
        residue = jnp.where(index < H, residue, jnp.where(lane == 0, H, F - residue))
        return (residue - BAND_LO + F) & (F - 1)

    apart = bins(rows_of((F, F))) - bins(lanes_of((F, F)))
    return (jnp.abs(apart) <= smooth_reach).astype(jnp.float32).astype(jnp.bfloat16)


def exact_dot(left, right):
    return jnp.dot(left.astype(jnp.bfloat16), right.astype(jnp.bfloat16), preferred_element_type=jnp.float32)


def slot_selector(owners, places, device, ch_dev):
    height, width = owners.shape
    per_row = width // ch_dev
    wanted = (owners == device).astype(jnp.float32)
    before = rows_of((width, width))
    after = lanes_of((width, width))
    earlier = ((before < after) & (before // ch_dev == after // ch_dev)).astype(jnp.float32)
    ranks = exact_dot(wanted, earlier)
    slots = jnp.where(wanted > 0, ranks, float(CAP))
    count = height * per_row * 2 * CAP
    to_row = (rows_of((count, height)) // (2 * CAP * per_row) == lanes_of((count, height))).astype(jnp.float32)
    row_slots = exact_dot(to_row, slots)
    row_places = exact_dot(to_row, places.astype(jnp.float32))
    shape = (count, width)
    row = rows_of(shape)
    mine = (row_slots == (row % CAP).astype(jnp.float32)) & (lanes_of(shape) // ch_dev == row // (2 * CAP) % per_row)
    place = jnp.sum(jnp.where(mine, row_places + 1.0, 0.0), axis=1, keepdims=True).astype(jnp.int32) - 1
    shape = (count, 2 * ch_dev)
    half = rows_of(shape) // CAP % 2
    lane = lanes_of(shape)
    return ((lane == place + ch_dev * half) & (place >= 0)).astype(jnp.float32).astype(jnp.bfloat16)


def spectra_kernel(traces_ref, table_ref, quality_ref, whitened_ref, band_ref, keep_ref):
    rows, length = traces_ref.shape
    ch_dev = quality_ref.shape[1]

    @pl.when(pl.program_id(0) == 0)
    def _():
        band_ref[...] = band_matrix()
        shape = (rows, ch_dev)
        keep = jnp.sum(
            jnp.where(rows_of(shape) % ch_dev == lanes_of(shape), quality_ref[...].astype(jnp.float32), 0.0),
            axis=1, keepdims=True,
        )
        keep_ref[...] = jnp.broadcast_to(keep, keep_ref.shape)

    early, late = traces_ref[:, : length // 2], traces_ref[:, length // 2 :]
    even = jnp.dot(early + late, table_ref[:, :F], preferred_element_type=jnp.float32)
    odd = jnp.dot(early - late, table_ref[:, F:], preferred_element_type=jnp.float32)
    part = H // 2
    parts = [
        jnp.concatenate([even[:, q * part : (q + 1) * part], odd[:, q * part : (q + 1) * part]], axis=1)
        for q in range(4)
    ]
    energy = jnp.concatenate(
        [parts[0] * parts[0] + parts[1] * parts[1], parts[2] * parts[2] + parts[3] * parts[3]], axis=1
    )
    top = energy.astype(jnp.bfloat16)
    rest = (energy - top.astype(jnp.float32)).astype(jnp.bfloat16)
    band = band_ref[...]
    smooth = jnp.dot(top, band, preferred_element_type=jnp.float32) + jnp.dot(
        rest, band, preferred_element_type=jnp.float32
    )
    water = jnp.sum(energy, axis=1, keepdims=True) * (1.0 / F)
    scaling = lax.rsqrt(smooth * (1.0 / (2.0 * smooth_reach + 1.0)) + (0.1 * water + 1e-06))
    keep = keep_ref[...]
    near, far = scaling[:, :H] * keep, scaling[:, H:] * keep
    white = [parts[0] * near, parts[1] * near, parts[2] * far, parts[3] * far]
    for q in range(4):
        whitened_ref[:, q * H : (q + 1) * H] = white[q].astype(jnp.bfloat16)


def select_kernel(where_ref, whitened_ref, owners_ref, places_ref, outgoing_ref, selector):
    rows = selector.shape[1]

    @pl.when(pl.program_id(0) == 0)
    def _():
        selector[...] = slot_selector(owners_ref[...], places_ref[...], where_ref[0], rows // 2)

    count, slots, columns = outgoing_ref.shape
    for n in range(slots // (2 * CAP)):
        sent = jnp.dot(
            selector[...], whitened_ref[rows * n : rows * (n + 1), :], preferred_element_type=jnp.float32
        ).astype(jnp.bfloat16)
        outgoing_ref[:, 2 * CAP * n : 2 * CAP * (n + 1), :] = sent.reshape(count, 2 * CAP, columns)


def vmem_spec():
    return pl.BlockSpec(memory_space=pltpu.VMEM)


def smem_spec():
    return pl.BlockSpec(memory_space=pltpu.SMEM)


def whole(array):
    return pl.BlockSpec(array.shape, lambda s: (0,) * array.ndim)


def spectra_call(traces, quality):
    rows, length = traces.shape
    block = rows // ROW_STEPS
    table = jnp.asarray(forward_table(length))
    return pl.pallas_call(
        spectra_kernel,
        grid=(ROW_STEPS,),
        in_specs=[pl.BlockSpec((block, length), lambda s: (s, 0)), whole(table), whole(quality)],
        out_specs=pl.BlockSpec((block, 2 * F), lambda s: (s, 0)),
        out_shape=jax.ShapeDtypeStruct((rows, 2 * F), jnp.bfloat16),
        scratch_shapes=[pltpu.VMEM((F, F), jnp.bfloat16), pltpu.VMEM((block, H), jnp.float32)],
        compiler_params=pltpu.CompilerParams(vmem_limit_bytes=SPECTRA_VMEM_LIMIT),
        cost_estimate=pl.CostEstimate(
            flops=rows * length * 2 * F, bytes_accessed=2 * (rows + F) * length, transcendentals=rows * F
        ),
        name="spectra",
    )(traces, table, quality)


def select_call(where, whitened, owners, places, chan_count, ch_dev):
    rows, columns = whitened.shape
    block = rows // ROW_STEPS
    slots = block // (2 * ch_dev) * 2 * CAP
    return pl.pallas_call(
        select_kernel,
        grid=(ROW_STEPS,),
        in_specs=[smem_spec(), pl.BlockSpec((block, columns), lambda s: (s, 0)), whole(owners), whole(places)],
        out_specs=pl.BlockSpec((chan_count, slots, columns), lambda s: (0, s, 0)),
        out_shape=jax.ShapeDtypeStruct((chan_count, ROW_STEPS * slots, columns), jnp.bfloat16),
        scratch_shapes=[pltpu.VMEM((chan_count * 2 * CAP, 2 * ch_dev), jnp.bfloat16)],
        compiler_params=pltpu.CompilerParams(vmem_limit_bytes=VMEM_LIMIT),
        cost_estimate=pl.CostEstimate(
            flops=4 * rows * chan_count * 2 * CAP * columns, bytes_accessed=2 * rows * columns * 3, transcendentals=0
        ),
        name="select",
    )(where, whitened, owners, places)


def cross_kernel(last, with_sum, local_windows, where_ref, first_ref, second_ref, *refs):
    refs = list(refs)
    sum_ref = refs.pop(0) if with_sum else None
    if last:
        high_ref, low_ref, out_ref, wide, spread, total = refs
    else:
        out_ref, wide, spread = refs
        total = out_ref
    windows, own_count = spread.shape[:2]
    ch_dev = wide.shape[1] // 2
    base = pl.multiple_of(where_ref[1] * own_count, 8)

    def widen(w, carry):
        if local_windows:
            wide[w, :ch_dev, :] = first_ref[w].astype(jnp.float32)
            wide[w, ch_dev:, :] = second_ref[w].astype(jnp.float32)
        else:
            shared = ch_dev - own_count
            wide[w, shared:ch_dev, :] = first_ref[w].astype(jnp.float32)
            rows = second_ref[w].astype(jnp.float32)
            for tile in range(ch_dev // 8):
                at = base + 8 * tile
                at = pl.multiple_of(jnp.where(at < shared, at, at + own_count), 8)
                wide[w, pl.ds(at, 8), :] = rows[8 * tile : 8 * tile + 8]
        for tile in range(own_count // 8):
            rows = wide[w, pl.ds(pl.multiple_of(base + 8 * tile, 8), 8), :]
            for i in range(8):
                for q in range(4):
                    spread[w, 8 * tile + i, q] = jnp.broadcast_to(rows[i : i + 1, q * H : (q + 1) * H], (8, H))
        return carry

    lax.fori_loop(0, windows, widen, 0)

    group, tiles = 4, 3
    rounds = SPAN // (8 * tiles)

    def block(index, carry):
        g = index // rounds
        j = index % rounds
        start = pl.multiple_of(base + 8 * (g // 2) + 8 * tiles * j, 8)

        def add_window(w, sums):
            sums = list(sums)
            right = [
                [wide[w, pl.ds(pl.multiple_of(start + 8 * t, 8), 8), q * H : (q + 1) * H] for q in range(4)]
                for t in range(tiles)
            ]
            for i in range(group):
                left = [spread[w, group * g + i, q] for q in range(4)]
                for t in range(tiles):
                    at = 3 * (i * tiles + t)
                    r = right[t]
                    sums[at] = sums[at] + (left[0] * r[0] + left[1] * r[1])
                    sums[at + 1] = sums[at + 1] + (left[2] * r[2] + left[3] * r[3])
                    sums[at + 2] = sums[at + 2] + ((left[1] * r[0] - left[0] * r[1]) + (left[2] * r[3] - left[3] * r[2]))
            return tuple(sums)

        zero = jnp.zeros((8, H), jnp.float32)
        sums = lax.fori_loop(0, windows, add_window, (zero,) * (3 * group * tiles), unroll=2)
        for i in range(group):
            for t in range(tiles):
                at = 3 * (i * tiles + t)
                real, imag = fold_columns(sums[at], sums[at + 1], sums[at + 2])
                where = pl.ds(pl.multiple_of(8 * tiles * j + 8 * t, 8), 8)
                if with_sum:
                    real = real + sum_ref[group * g + i, where, :H]
                    imag = imag + sum_ref[group * g + i, where, H:]
                total[group * g + i, where, :H] = real
                total[group * g + i, where, H:] = imag
        return carry

    lax.fori_loop(0, own_count // group * rounds, block, 0)

    if last:

        def finish(eight, carry):
            first = pl.multiple_of(8 * eight, 8)
            stacks = total[pl.ds(first, 8)].reshape(8 * SPAN, F)
            lagged = lag_transform(stacks, high_ref[...], low_ref[...]).reshape(8, SPAN, NLAG)
            for i in range(8):
                out_ref[first + i] = lagged[i, i + 1 : i + 1 + REACH, :]
            return carry

        lax.fori_loop(0, own_count // 8, finish, 0)


def cross_call(where, first, second, ch_dev, own_count, sums, tables, local_windows):
    windows, _, columns = first.shape
    last = tables is not None
    with_sum = sums is not None
    operands = [where, first, second]
    if with_sum:
        operands.append(sums)
    scratch = [
        pltpu.VMEM((windows, 2 * ch_dev, columns), jnp.float32),
        pltpu.VMEM((windows, own_count, 4, 8, H), jnp.float32),
    ]
    if last:
        operands += list(tables)
        scratch.append(pltpu.VMEM((own_count, SPAN, F), jnp.float32))
    shape = (own_count, REACH, NLAG) if last else (own_count, SPAN, F)
    return pl.pallas_call(
        functools.partial(cross_kernel, last, with_sum, local_windows),
        in_specs=[smem_spec()] + [vmem_spec()] * (len(operands) - 1),
        out_specs=vmem_spec(),
        out_shape=jax.ShapeDtypeStruct(shape, jnp.float32),
        scratch_shapes=scratch,
        compiler_params=pltpu.CompilerParams(vmem_limit_bytes=VMEM_LIMIT),
        cost_estimate=pl.CostEstimate(
            flops=10_000_000_000, bytes_accessed=4 * windows * ch_dev * columns + 4 * own_count * SPAN * F, transcendentals=0
        ),
        name="cross",
    )(*operands)


def fold_kernel(where_ref, incoming_ref, own_ref, owners_ref, high_ref, low_ref, out_ref, sums, picker):
    step = pl.program_id(0)
    rows = own_ref.shape[0]
    ch_dev = rows // 2

    @pl.when(step == 0)
    def _():
        sums[...] = jnp.zeros_like(sums)
        owners = owners_ref[...].astype(jnp.float32)
        per_row = owners.shape[1] // ch_dev
        device = where_ref[0]
        line = jnp.sum(jnp.where(rows_of(owners.shape) == device // per_row, owners, 0.0), axis=0, keepdims=True)
        shape = (rows, owners.shape[1])
        line = jnp.broadcast_to(line, shape)
        first = device % per_row * ch_dev
        place = first + rows_of(shape) % ch_dev
        lane = lanes_of(shape)
        owner = jnp.sum(jnp.where(lane == place, line, 0.0), axis=1, keepdims=True)
        earlier = (lane >= first) & (lane < place) & (line == owner)
        rank = jnp.sum(earlier.astype(jnp.float32), axis=1, keepdims=True)
        source = (2 * CAP * owner + rank).astype(jnp.int32)
        shape = picker.shape
        target = source + CAP * (rows_of(shape) // ch_dev)
        picker[...] = (lanes_of(shape) == target).astype(jnp.float32).astype(jnp.bfloat16)

    count, slots, columns = incoming_ref.shape
    right = jnp.dot(
        picker[...], incoming_ref[...].reshape(count * slots, columns), preferred_element_type=jnp.float32
    )
    left = own_ref[...].astype(jnp.float32)
    l = [left[:, q * H : (q + 1) * H] for q in range(4)]
    r = [right[:, q * H : (q + 1) * H] for q in range(4)]
    first = l[0] * r[0] + l[1] * r[1]
    second = l[2] * r[2] + l[3] * r[3]
    imag = (l[1] * r[0] - l[0] * r[1]) + (l[2] * r[3] - l[3] * r[2])
    for n, term in enumerate((first, second, imag)):
        sums[n] += term[:ch_dev] + term[ch_dev:]

    @pl.when(step == pl.num_programs(0) - 1)
    def _():
        stacks = jnp.concatenate(fold_columns(sums[0], sums[1], sums[2]), axis=1)
        out_ref[...] = lag_transform(stacks, high_ref[...], low_ref[...])


def fold_call(where, incoming, own, owners, ch_dev, tables):
    count, slots, columns = incoming.shape
    rows = 2 * ch_dev
    pairs = own.shape[0] // rows
    return pl.pallas_call(
        fold_kernel,
        grid=(pairs,),
        in_specs=[
            smem_spec(),
            pl.BlockSpec((count, slots // pairs, columns), lambda s: (0, s, 0)),
            pl.BlockSpec((rows, columns), lambda s: (s, 0)),
            whole(owners),
            whole(tables[0]),
            whole(tables[1]),
        ],
        out_specs=pl.BlockSpec((ch_dev, NLAG), lambda s: (0, 0)),
        out_shape=jax.ShapeDtypeStruct((ch_dev, NLAG), jnp.float32),
        scratch_shapes=[
            pltpu.VMEM((3, ch_dev, H), jnp.float32),
            pltpu.VMEM((rows, count * slots // pairs), jnp.bfloat16),
        ],
        compiler_params=pltpu.CompilerParams(vmem_limit_bytes=VMEM_LIMIT),
        cost_estimate=pl.CostEstimate(
            flops=2 * rows * pairs * count * 2 * CAP * columns,
            bytes_accessed=2 * (incoming.size + own.size),
            transcendentals=0,
        ),
        name="fold",
    )(where, incoming, own, owners, *tables)


def from_above(block):
    count = lax.axis_size("chan")
    return lax.ppermute(block, "chan", [(i, i - 1) for i in range(1, count)])


def round_win(block, shift):
    count = lax.axis_size("win")
    return lax.ppermute(block, "win", [(i, (i + shift) % count) for i in range(count)])


def local(traces, quality, fold_block, fold_offset):
    win_dev, ch_dev, length = traces.shape
    chan_count = lax.axis_size("chan")
    win_count = lax.axis_size("win")
    window_part = lax.axis_index("win")
    own_count = ch_dev // win_count
    shared = ch_dev - own_count
    where = jnp.stack([lax.axis_index("chan"), window_part]).astype(jnp.int32)
    tables = [jnp.asarray(t) for t in inverse_tables(1.0 / math.sqrt(F * win_dev * win_count))]
    owners = fold_block.reshape(-1, 2 * ch_dev)
    places = fold_offset.reshape(-1, 2 * ch_dev)
    flat = spectra_call(traces.reshape(win_dev * ch_dev, length), quality.reshape(1, ch_dev))
    whitened = flat.reshape(win_dev, ch_dev, 2 * F)
    upper = from_above(whitened)
    common = [round_win(whitened[:, shared:], shift) for shift in range(1, win_count)]
    outgoing = select_call(where, flat, owners, places, chan_count, ch_dev)
    incoming = lax.all_to_all(outgoing, "chan", split_axis=0, concat_axis=0, tiled=True)
    offered = jnp.concatenate([whitened[:, :shared], upper], axis=1)
    special = [
        round_win(
            lax.dynamic_slice_in_dim(offered, (window_part + shift) % win_count * own_count, ch_dev, 1), shift
        )
        for shift in range(1, win_count)
    ]
    arrived = [(whitened, upper)] + list(zip(common, special))
    sums = None
    for n, (first, second) in enumerate(arrived):
        ends = tables if n == win_count - 1 else None
        sums = cross_call(where, first, second, ch_dev, own_count, sums, ends, n == 0)
    share = fold_call(where, incoming, flat, owners, ch_dev, tables)
    fold = lax.dynamic_slice_in_dim(share, window_part * own_count, own_count, 0)
    for shift in range(1, win_count):
        target = (window_part + shift) % win_count * own_count
        fold = fold + round_win(lax.dynamic_slice_in_dim(share, target, own_count, 0), shift)
    return (sums, fold)


def solution(mesh):
    in_specs = (P("win", "chan", None), P("chan"), P(), P())
    out_specs = (P(("chan", "win"), None, None), P(("chan", "win"), None))
    return jax.shard_map(local, mesh=mesh, in_specs=in_specs, out_specs=out_specs, check_vma=False)
```

```python
import functools
import math

import jax
import jax.numpy as jnp
import numpy as np
from jax import lax
from jax.experimental import pallas as pl
from jax.experimental.pallas import tpu as pltpu
from jax.sharding import PartitionSpec as P

F = 256
H = F // 2
BAND_LO = 32
NLAG = 256
REACH = 64
CAP = 8
SPAN = REACH + 8
smooth_reach = 4
ROW_STEPS = 3
K_STEPS = 4
VMEM_LIMIT = 24 * 1024 * 1024
FOLD_VMEM_LIMIT = 16 * 1024 * 1024
SPECTRA_VMEM_LIMIT = 48 * 1024 * 1024


def bin_order():
    residues = np.arange(H)
    first = (residues - BAND_LO) % F
    second = (-residues - BAND_LO) % F
    second[0] = (H - BAND_LO) % F
    return first, second


def forward_table(length):
    samples = np.arange(length, dtype=np.int64)[:, None]
    parts = []
    for bins in bin_order():
        angles = (samples * (bins + BAND_LO)[None, :] % length) * (2.0 * math.pi / length)
        parts += [np.cos(angles), -np.sin(angles)]
    return np.concatenate(parts, axis=1).astype(np.float32).astype(jnp.bfloat16)


def inverse_tables(factor):
    shifts = (np.arange(NLAG) + NLAG // 2)[None, :]
    residues = np.arange(H)[:, None]
    angles = (residues * shifts % NLAG) * (2.0 * math.pi / NLAG)
    sign = np.where(shifts[0] % 2 == 0, 1.0, -1.0)
    real, imag = np.cos(angles), -np.sin(angles)
    real[0] = (1.0 + sign) / 2.0
    imag[0] = (1.0 - sign) / 2.0
    table = np.concatenate([real, imag], axis=0) * factor
    high = table.astype(np.float32).astype(jnp.bfloat16)
    low = (table - high.astype(np.float64)).astype(np.float32).astype(jnp.bfloat16)
    return high, low


def lag_transform(stacks, high, low):
    top = stacks.astype(jnp.bfloat16)
    rest = (stacks - top.astype(jnp.float32)).astype(jnp.bfloat16)
    dot = functools.partial(jnp.dot, preferred_element_type=jnp.float32)
    return dot(top, high) + (dot(rest, high) + dot(top, low))


def fold_columns(first, second, imag):
    lane = lax.broadcasted_iota(jnp.int32, first.shape, first.ndim - 1)
    return first + second, jnp.where(lane == 0, first - second, imag)


def lanes_of(shape):
    return lax.broadcasted_iota(jnp.int32, shape, len(shape) - 1)


def rows_of(shape):
    return lax.broadcasted_iota(jnp.int32, shape, len(shape) - 2)


def band_matrix():
    def bins(index):
        lane = index & (H - 1)
        residue = jnp.where(index < H, lane, jnp.where(lane == 0, H, F - lane))
        return (residue - BAND_LO + F) & (F - 1)

    apart = bins(rows_of((F, F))) - bins(lanes_of((F, F)))
    return (jnp.abs(apart) <= smooth_reach).astype(jnp.float32).astype(jnp.bfloat16)


def exact_dot(left, right):
    return jnp.dot(left.astype(jnp.bfloat16), right.astype(jnp.bfloat16), preferred_element_type=jnp.float32)


def slot_selector(owners, places, device, ch_dev):
    height, width = owners.shape
    per_row = width // ch_dev
    wanted = (owners == device).astype(jnp.float32)
    before = rows_of((width, width))
    after = lanes_of((width, width))
    earlier = ((before < after) & (before // ch_dev == after // ch_dev)).astype(jnp.float32)
    ranks = exact_dot(wanted, earlier)
    slots = jnp.where(wanted > 0, ranks, float(CAP))
    count = height * per_row * 2 * CAP
    to_row = (rows_of((count, height)) // (2 * CAP * per_row) == lanes_of((count, height))).astype(jnp.float32)
    row_slots = exact_dot(to_row, slots)
    row_places = exact_dot(to_row, places.astype(jnp.float32))
    shape = (count, width)
    row = rows_of(shape)
    mine = (row_slots == (row % CAP).astype(jnp.float32)) & (lanes_of(shape) // ch_dev == row // (2 * CAP) % per_row)
    place = jnp.sum(jnp.where(mine, row_places + 1.0, 0.0), axis=1, keepdims=True).astype(jnp.int32) - 1
    shape = (count, 2 * ch_dev)
    half = rows_of(shape) // CAP % 2
    lane = lanes_of(shape)
    return ((lane == place + ch_dev * half) & (place >= 0)).astype(jnp.float32).astype(jnp.bfloat16)


def spectra_kernel(traces_ref, table_ref, quality_ref, whitened_ref, traces, table, sems):
    row_parts, chunks, rows, depth = traces.shape
    ch_dev = quality_ref.shape[1]

    def traces_copy(part, k):
        source = traces_ref.at[pl.ds(part * rows, rows), pl.ds(k * depth, depth)]
        return pltpu.make_async_copy(source, traces.at[part, k], sems.at[part, k])

    def table_copy(k):
        return pltpu.make_async_copy(table_ref.at[pl.ds(k * depth, depth), :], table.at[k], sems.at[row_parts, k])

    for part in range(row_parts):
        for k in range(chunks):
            traces_copy(part, k).start()
            if part == 0:
                table_copy(k).start()

    band = band_matrix()
    shape = (rows, ch_dev)
    keep = jnp.sum(
        jnp.where(rows_of(shape) % ch_dev == lanes_of(shape), quality_ref[...].astype(jnp.float32), 0.0),
        axis=1, keepdims=True,
    )

    def whiten(part, carry):
        spectra = None
        for k in range(chunks):
            traces_copy(part, k).wait()

            @pl.when(part == 0)
            def _():
                table_copy(k).wait()

            product = jnp.dot(traces[part, k], table[k], preferred_element_type=jnp.float32)
            spectra = product if spectra is None else spectra + product
        parts = [spectra[:, q * H : (q + 1) * H] for q in range(4)]
        energy = jnp.concatenate(
            [parts[0] * parts[0] + parts[1] * parts[1], parts[2] * parts[2] + parts[3] * parts[3]], axis=1
        )
        top = energy.astype(jnp.bfloat16)
        rest = (energy - top.astype(jnp.float32)).astype(jnp.bfloat16)
        smooth = jnp.dot(top, band, preferred_element_type=jnp.float32) + jnp.dot(
            rest, band, preferred_element_type=jnp.float32
        )
        water = jnp.sum(energy, axis=1, keepdims=True) * (1.0 / F)
        scaling = lax.rsqrt(smooth * (1.0 / (2.0 * smooth_reach + 1.0)) + (0.1 * water + 1e-06)) * keep
        near, far = scaling[:, :H], scaling[:, H:]
        white = [parts[0] * near, parts[1] * near, parts[2] * far, parts[3] * far]
        at = pl.ds(pl.multiple_of(part * rows, rows), rows)
        for q in range(4):
            whitened_ref[at, q * H : (q + 1) * H] = white[q].astype(jnp.bfloat16)
        return carry

    lax.fori_loop(0, row_parts, whiten, 0)


def select_kernel(where_ref, whitened_ref, owners_ref, places_ref, outgoing_ref, selector):
    rows = selector.shape[1]

    @pl.when(pl.program_id(0) == 0)
    def _():
        selector[...] = slot_selector(owners_ref[...], places_ref[...], where_ref[0], rows // 2)

    count, slots, columns = outgoing_ref.shape
    for n in range(slots // (2 * CAP)):
        sent = jnp.dot(
            selector[...], whitened_ref[rows * n : rows * (n + 1), :], preferred_element_type=jnp.float32
        ).astype(jnp.bfloat16)
        outgoing_ref[:, 2 * CAP * n : 2 * CAP * (n + 1), :] = sent.reshape(count, 2 * CAP, columns)


def vmem_spec():
    return pl.BlockSpec(memory_space=pltpu.VMEM)


def smem_spec():
    return pl.BlockSpec(memory_space=pltpu.SMEM)


def whole(array):
    return pl.BlockSpec(array.shape, lambda s: (0,) * array.ndim)


def spectra_call(traces, quality):
    rows, length = traces.shape
    part, depth = rows // ROW_STEPS, length // K_STEPS
    anywhere = pl.BlockSpec(memory_space=pl.ANY)
    return pl.pallas_call(
        spectra_kernel,
        in_specs=[anywhere, anywhere, vmem_spec()],
        out_specs=vmem_spec(),
        out_shape=jax.ShapeDtypeStruct((rows, 2 * F), jnp.bfloat16),
        scratch_shapes=[
            pltpu.VMEM((ROW_STEPS, K_STEPS, part, depth), jnp.bfloat16),
            pltpu.VMEM((K_STEPS, depth, 2 * F), jnp.bfloat16),
            pltpu.SemaphoreType.DMA((ROW_STEPS + 1, K_STEPS)),
        ],
        compiler_params=pltpu.CompilerParams(vmem_limit_bytes=SPECTRA_VMEM_LIMIT),
        cost_estimate=pl.CostEstimate(
            flops=2 * rows * length * 2 * F, bytes_accessed=2 * (rows + 2 * F) * length, transcendentals=rows * F
        ),
        name="spectra",
    )(traces, jnp.asarray(forward_table(length)), quality)


def after(first, second):
    anywhere = pl.BlockSpec(memory_space=pl.ANY)
    return pl.pallas_call(
        lambda first_ref, second_ref, out_ref: None,
        in_specs=[anywhere, anywhere],
        out_specs=anywhere,
        out_shape=jax.ShapeDtypeStruct(first.shape, first.dtype),
        input_output_aliases={0: 0},
        name="after",
    )(first, second)


def select_call(where, whitened, owners, places, chan_count, ch_dev):
    rows, columns = whitened.shape
    block = rows // ROW_STEPS
    slots = block // (2 * ch_dev) * 2 * CAP
    return pl.pallas_call(
        select_kernel,
        grid=(ROW_STEPS,),
        in_specs=[smem_spec(), pl.BlockSpec((block, columns), lambda s: (s, 0)), whole(owners), whole(places)],
        out_specs=pl.BlockSpec((chan_count, slots, columns), lambda s: (0, s, 0)),
        out_shape=jax.ShapeDtypeStruct((chan_count, ROW_STEPS * slots, columns), jnp.bfloat16),
        scratch_shapes=[pltpu.VMEM((chan_count * 2 * CAP, 2 * ch_dev), jnp.bfloat16)],
        compiler_params=pltpu.CompilerParams(vmem_limit_bytes=SPECTRA_VMEM_LIMIT),
        cost_estimate=pl.CostEstimate(
            flops=4 * rows * chan_count * 2 * CAP * columns, bytes_accessed=2 * rows * columns * 3, transcendentals=0
        ),
        name="select",
    )(where, whitened, owners, places)


def cross_kernel(last, with_sum, local_windows, where_ref, first_ref, second_ref, *refs):
    refs = list(refs)
    sum_ref = refs.pop(0) if with_sum else None
    if last:
        high_ref, low_ref, out_ref, wide, spread, total = refs
    else:
        out_ref, wide, spread = refs
        total = out_ref
    windows, own_count = spread.shape[:2]
    ch_dev = wide.shape[1] // 2
    base = pl.multiple_of(where_ref[1] * own_count, 8)

    def widen(w, carry):
        if local_windows:
            wide[w, :ch_dev, :] = first_ref[w].astype(jnp.float32)
            wide[w, ch_dev:, :] = second_ref[w].astype(jnp.float32)
        else:
            shared = ch_dev - own_count
            wide[w, shared:ch_dev, :] = first_ref[w].astype(jnp.float32)
            rows = second_ref[w].astype(jnp.float32)
            for tile in range(ch_dev // 8):
                at = base + 8 * tile
                at = pl.multiple_of(jnp.where(at < shared, at, at + own_count), 8)
                wide[w, pl.ds(at, 8), :] = rows[8 * tile : 8 * tile + 8]
        for tile in range(own_count // 8):
            rows = wide[w, pl.ds(pl.multiple_of(base + 8 * tile, 8), 8), :]
            for i in range(8):
                for q in range(4):
                    spread[w, 8 * tile + i, q] = jnp.broadcast_to(rows[i : i + 1, q * H : (q + 1) * H], (8, H))
        return carry

    lax.fori_loop(0, windows, widen, 0)

    group, tiles = 4, 3
    rounds = SPAN // (8 * tiles)

    def block(index, carry):
        g = index // rounds
        j = index % rounds
        start = pl.multiple_of(base + 8 * (g // 2) + 8 * tiles * j, 8)

        def add_window(w, sums):
            sums = list(sums)
            right = [
                [wide[w, pl.ds(pl.multiple_of(start + 8 * t, 8), 8), q * H : (q + 1) * H] for q in range(4)]
                for t in range(tiles)
            ]
            for i in range(group):
                left = [spread[w, group * g + i, q] for q in range(4)]
                for t in range(tiles):
                    at = 3 * (i * tiles + t)
                    r = right[t]
                    sums[at] = sums[at] + (left[0] * r[0] + left[1] * r[1])
                    sums[at + 1] = sums[at + 1] + (left[2] * r[2] + left[3] * r[3])
                    sums[at + 2] = sums[at + 2] + ((left[1] * r[0] - left[0] * r[1]) + (left[2] * r[3] - left[3] * r[2]))
            return tuple(sums)

        zero = jnp.zeros((8, H), jnp.float32)
        sums = lax.fori_loop(0, windows, add_window, (zero,) * (3 * group * tiles), unroll=2)
        for i in range(group):
            for t in range(tiles):
                at = 3 * (i * tiles + t)
                real, imag = fold_columns(sums[at], sums[at + 1], sums[at + 2])
                where = pl.ds(pl.multiple_of(8 * tiles * j + 8 * t, 8), 8)
                if with_sum:
                    real = real + sum_ref[group * g + i, where, :H]
                    imag = imag + sum_ref[group * g + i, where, H:]
                total[group * g + i, where, :H] = real
                total[group * g + i, where, H:] = imag
        return carry

    lax.fori_loop(0, own_count // group * rounds, block, 0)

    if last:

        def finish(eight, carry):
            first = pl.multiple_of(8 * eight, 8)
            stacks = total[pl.ds(first, 8)].reshape(8 * SPAN, F)
            lagged = lag_transform(stacks, high_ref[...], low_ref[...]).reshape(8, SPAN, NLAG)
            for i in range(8):
                out_ref[first + i] = lagged[i, i + 1 : i + 1 + REACH, :]
            return carry

        lax.fori_loop(0, own_count // 8, finish, 0)


def cross_call(where, first, second, ch_dev, own_count, sums, tables, local_windows):
    windows, _, columns = first.shape
    last = tables is not None
    with_sum = sums is not None
    operands = [where, first, second]
    if with_sum:
        operands.append(sums)
    scratch = [
        pltpu.VMEM((windows, 2 * ch_dev, columns), jnp.float32),
        pltpu.VMEM((windows, own_count, 4, 8, H), jnp.float32),
    ]
    if last:
        operands += list(tables)
        scratch.append(pltpu.VMEM((own_count, SPAN, F), jnp.float32))
    shape = (own_count, REACH, NLAG) if last else (own_count, SPAN, F)
    return pl.pallas_call(
        functools.partial(cross_kernel, last, with_sum, local_windows),
        in_specs=[smem_spec()] + [vmem_spec()] * (len(operands) - 1),
        out_specs=vmem_spec(),
        out_shape=jax.ShapeDtypeStruct(shape, jnp.float32),
        scratch_shapes=scratch,
        compiler_params=pltpu.CompilerParams(vmem_limit_bytes=VMEM_LIMIT),
        cost_estimate=pl.CostEstimate(
            flops=10_000_000_000, bytes_accessed=4 * windows * ch_dev * columns + 4 * own_count * SPAN * F, transcendentals=0
        ),
        name="cross",
    )(*operands)


def fold_kernel(where_ref, incoming_ref, own_ref, owners_ref, high_ref, low_ref, out_ref, sums, picker):
    step = pl.program_id(0)
    rows = own_ref.shape[0]
    ch_dev = rows // 2

    @pl.when(step == 0)
    def _():
        sums[...] = jnp.zeros_like(sums)
        owners = owners_ref[...].astype(jnp.float32)
        per_row = owners.shape[1] // ch_dev
        device = where_ref[0]
        line = jnp.sum(jnp.where(rows_of(owners.shape) == device // per_row, owners, 0.0), axis=0, keepdims=True)
        shape = (rows, owners.shape[1])
        line = jnp.broadcast_to(line, shape)
        first = device % per_row * ch_dev
        place = first + rows_of(shape) % ch_dev
        lane = lanes_of(shape)
        owner = jnp.sum(jnp.where(lane == place, line, 0.0), axis=1, keepdims=True)
        earlier = (lane >= first) & (lane < place) & (line == owner)
        rank = jnp.sum(earlier.astype(jnp.float32), axis=1, keepdims=True)
        source = (2 * CAP * owner + rank).astype(jnp.int32)
        shape = picker.shape
        target = source + CAP * (rows_of(shape) // ch_dev)
        picker[...] = (lanes_of(shape) == target).astype(jnp.float32).astype(jnp.bfloat16)

    count, slots, columns = incoming_ref.shape
    right = jnp.dot(
        picker[...], incoming_ref[...].reshape(count * slots, columns), preferred_element_type=jnp.float32
    )
    left = own_ref[...].astype(jnp.float32)
    l = [left[:, q * H : (q + 1) * H] for q in range(4)]
    r = [right[:, q * H : (q + 1) * H] for q in range(4)]
    first = l[0] * r[0] + l[1] * r[1]
    second = l[2] * r[2] + l[3] * r[3]
    imag = (l[1] * r[0] - l[0] * r[1]) + (l[2] * r[3] - l[3] * r[2])
    for n, term in enumerate((first, second, imag)):
        sums[n] += term[:ch_dev] + term[ch_dev:]

    @pl.when(step == pl.num_programs(0) - 1)
    def _():
        stacks = jnp.concatenate(fold_columns(sums[0], sums[1], sums[2]), axis=1)
        out_ref[...] = lag_transform(stacks, high_ref[...], low_ref[...])


def fold_call(where, incoming, own, owners, ch_dev, tables):
    count, slots, columns = incoming.shape
    rows = 2 * ch_dev
    pairs = own.shape[0] // rows
    return pl.pallas_call(
        fold_kernel,
        grid=(pairs,),
        in_specs=[
            smem_spec(),
            pl.BlockSpec((count, slots // pairs, columns), lambda s: (0, s, 0)),
            pl.BlockSpec((rows, columns), lambda s: (s, 0)),
            whole(owners),
            whole(tables[0]),
            whole(tables[1]),
        ],
        out_specs=pl.BlockSpec((ch_dev, NLAG), lambda s: (0, 0)),
        out_shape=jax.ShapeDtypeStruct((ch_dev, NLAG), jnp.float32),
        scratch_shapes=[
            pltpu.VMEM((3, ch_dev, H), jnp.float32),
            pltpu.VMEM((rows, count * slots // pairs), jnp.bfloat16),
        ],
        compiler_params=pltpu.CompilerParams(vmem_limit_bytes=FOLD_VMEM_LIMIT),
        cost_estimate=pl.CostEstimate(
            flops=2 * rows * pairs * count * 2 * CAP * columns,
            bytes_accessed=2 * (incoming.size + own.size),
            transcendentals=0,
        ),
        name="fold",
    )(where, incoming, own, owners, *tables)


def from_above(block):
    count = lax.axis_size("chan")
    return lax.ppermute(block, "chan", [(i, i - 1) for i in range(1, count)])


def round_win(block, shift):
    count = lax.axis_size("win")
    return lax.ppermute(block, "win", [(i, (i + shift) % count) for i in range(count)])


def local(traces, quality, fold_block, fold_offset):
    win_dev, ch_dev, length = traces.shape
    chan_count = lax.axis_size("chan")
    win_count = lax.axis_size("win")
    window_part = lax.axis_index("win")
    own_count = ch_dev // win_count
    shared = ch_dev - own_count
    where = jnp.stack([lax.axis_index("chan"), window_part]).astype(jnp.int32)
    tables = [jnp.asarray(t) for t in inverse_tables(1.0 / math.sqrt(F * win_dev * win_count))]
    owners = fold_block.reshape(-1, 2 * ch_dev)
    places = fold_offset.reshape(-1, 2 * ch_dev)
    flat = spectra_call(traces.reshape(win_dev * ch_dev, length), quality.reshape(1, ch_dev))
    whitened = flat.reshape(win_dev, ch_dev, 2 * F)
    upper = from_above(whitened)
    common = [round_win(whitened[:, shared:], shift) for shift in range(1, win_count)]
    outgoing = select_call(where, flat, owners, places, chan_count, ch_dev)
    incoming = lax.all_to_all(after(outgoing, upper), "chan", split_axis=0, concat_axis=0, tiled=True)
    offered = jnp.concatenate([whitened[:, :shared], upper], axis=1)
    special = [
        round_win(
            lax.dynamic_slice_in_dim(offered, (window_part + shift) % win_count * own_count, ch_dev, 1), shift
        )
        for shift in range(1, win_count)
    ]
    arrived = [(whitened, upper)] + list(zip(common, special))
    sums = None
    for n, (first, second) in enumerate(arrived):
        ends = tables if n == win_count - 1 else None
        sums = cross_call(where, first, second, ch_dev, own_count, sums, ends, n == 0)
    share = fold_call(where, incoming, flat, owners, ch_dev, tables)
    fold = lax.dynamic_slice_in_dim(share, window_part * own_count, own_count, 0)
    for shift in range(1, win_count):
        target = (window_part + shift) % win_count * own_count
        fold = fold + round_win(lax.dynamic_slice_in_dim(share, target, own_count, 0), shift)
    return (sums, fold)


def solution(mesh):
    in_specs = (P("win", "chan", None), P("chan"), P(), P())
    out_specs = (P(("chan", "win"), None, None), P(("chan", "win"), None))
    return jax.shard_map(local, mesh=mesh, in_specs=in_specs, out_specs=out_specs, check_vma=False)
```

```python
import functools
import math

import jax
import jax.numpy as jnp
import numpy as np
from jax import lax
from jax.experimental import pallas as pl
from jax.experimental.pallas import tpu as pltpu
from jax.sharding import PartitionSpec as P

F = 256
H = F // 2
BAND_LO = 32
NLAG = 256
REACH = 64
CAP = 8
SPAN = REACH + 8
smooth_reach = 4
ROW_STEPS = 3
K_STEPS = 4
VMEM_LIMIT = 24 * 1024 * 1024
FOLD_VMEM_LIMIT = 16 * 1024 * 1024
SPECTRA_VMEM_LIMIT = 59 * 1024 * 1024


def bin_order():
    residues = np.arange(H)
    first = (residues - BAND_LO) % F
    second = (-residues - BAND_LO) % F
    second[0] = (H - BAND_LO) % F
    return first, second


def forward_table(length):
    samples = np.arange(length, dtype=np.int64)[:, None]
    parts = []
    for bins in bin_order():
        angles = (samples * (bins + BAND_LO)[None, :] % length) * (2.0 * math.pi / length)
        parts += [np.cos(angles), -np.sin(angles)]
    return np.concatenate(parts, axis=1).astype(np.float32).astype(jnp.bfloat16)


def inverse_tables(factor):
    shifts = (np.arange(NLAG) + NLAG // 2)[None, :]
    residues = np.arange(H)[:, None]
    angles = (residues * shifts % NLAG) * (2.0 * math.pi / NLAG)
    sign = np.where(shifts[0] % 2 == 0, 1.0, -1.0)
    real, imag = np.cos(angles), -np.sin(angles)
    real[0] = (1.0 + sign) / 2.0
    imag[0] = (1.0 - sign) / 2.0
    table = np.concatenate([real, imag], axis=0) * factor
    high = table.astype(np.float32).astype(jnp.bfloat16)
    low = (table - high.astype(np.float64)).astype(np.float32).astype(jnp.bfloat16)
    return high, low


def lag_transform(stacks, high, low):
    top = stacks.astype(jnp.bfloat16)
    rest = (stacks - top.astype(jnp.float32)).astype(jnp.bfloat16)
    dot = functools.partial(jnp.dot, preferred_element_type=jnp.float32)
    return dot(top, high) + (dot(rest, high) + dot(top, low))


def fold_columns(first, second, imag):
    lane = lax.broadcasted_iota(jnp.int32, first.shape, first.ndim - 1)
    return first + second, jnp.where(lane == 0, first - second, imag)


def lanes_of(shape):
    return lax.broadcasted_iota(jnp.int32, shape, len(shape) - 1)


def rows_of(shape):
    return lax.broadcasted_iota(jnp.int32, shape, len(shape) - 2)


def band_matrix():
    def bins(index):
        lane = index & (H - 1)
        residue = jnp.where(index < H, lane, jnp.where(lane == 0, H, F - lane))
        return (residue - BAND_LO + F) & (F - 1)

    apart = bins(rows_of((F, F))) - bins(lanes_of((F, F)))
    return (jnp.abs(apart) <= smooth_reach).astype(jnp.float32).astype(jnp.bfloat16)


def exact_dot(left, right):
    return jnp.dot(left.astype(jnp.bfloat16), right.astype(jnp.bfloat16), preferred_element_type=jnp.float32)


def slot_selector(owners, places, device, ch_dev):
    height, width = owners.shape
    per_row = width // ch_dev
    wanted = (owners == device).astype(jnp.float32)
    before = rows_of((width, width))
    after = lanes_of((width, width))
    earlier = ((before < after) & (before // ch_dev == after // ch_dev)).astype(jnp.float32)
    ranks = exact_dot(wanted, earlier)
    slots = jnp.where(wanted > 0, ranks, float(CAP))
    count = height * per_row * 2 * CAP
    to_row = (rows_of((count, height)) // (2 * CAP * per_row) == lanes_of((count, height))).astype(jnp.float32)
    row_slots = exact_dot(to_row, slots)
    row_places = exact_dot(to_row, places.astype(jnp.float32))
    shape = (count, width)
    row = rows_of(shape)
    mine = (row_slots == (row % CAP).astype(jnp.float32)) & (lanes_of(shape) // ch_dev == row // (2 * CAP) % per_row)
    place = jnp.sum(jnp.where(mine, row_places + 1.0, 0.0), axis=1, keepdims=True).astype(jnp.int32) - 1
    shape = (count, 2 * ch_dev)
    half = rows_of(shape) // CAP % 2
    lane = lanes_of(shape)
    return ((lane == place + ch_dev * half) & (place >= 0)).astype(jnp.float32).astype(jnp.bfloat16)


def spectra_kernel(traces_ref, table_ref, quality_ref, whitened_ref, traces, table, sems):
    row_parts, chunks, rows, depth = traces.shape
    ch_dev = quality_ref.shape[1]

    def traces_copy(part, k):
        source = traces_ref.at[pl.ds(part * rows, rows), pl.ds(k * depth, depth)]
        return pltpu.make_async_copy(source, traces.at[part, k], sems.at[part, k])

    def table_copy(k):
        return pltpu.make_async_copy(table_ref.at[pl.ds(k * depth, depth), :], table.at[k], sems.at[row_parts, k])

    for part in range(row_parts):
        for k in range(chunks):
            traces_copy(part, k).start()
            if part == 0:
                table_copy(k).start()

    band = band_matrix()
    shape = (rows, ch_dev)
    keep = jnp.sum(
        jnp.where(rows_of(shape) % ch_dev == lanes_of(shape), quality_ref[...].astype(jnp.float32), 0.0),
        axis=1, keepdims=True,
    )

    def whiten(part, carry):
        spectra = None
        for k in range(chunks):
            traces_copy(part, k).wait()

            @pl.when(part == 0)
            def _():
                table_copy(k).wait()

            product = jnp.dot(traces[part, k], table[k], preferred_element_type=jnp.float32)
            spectra = product if spectra is None else spectra + product
        parts = [spectra[:, q * H : (q + 1) * H] for q in range(4)]
        energy = jnp.concatenate(
            [parts[0] * parts[0] + parts[1] * parts[1], parts[2] * parts[2] + parts[3] * parts[3]], axis=1
        )
        top = energy.astype(jnp.bfloat16)
        rest = (energy - top.astype(jnp.float32)).astype(jnp.bfloat16)
        smooth = jnp.dot(top, band, preferred_element_type=jnp.float32) + jnp.dot(
            rest, band, preferred_element_type=jnp.float32
        )
        water = jnp.sum(energy, axis=1, keepdims=True) * (1.0 / F)
        scaling = lax.rsqrt(smooth * (1.0 / (2.0 * smooth_reach + 1.0)) + (0.1 * water + 1e-06)) * keep
        near, far = scaling[:, :H], scaling[:, H:]
        white = [parts[0] * near, parts[1] * near, parts[2] * far, parts[3] * far]
        at = pl.ds(pl.multiple_of(part * rows, rows), rows)
        for q in range(4):
            whitened_ref[at, q * H : (q + 1) * H] = white[q].astype(jnp.bfloat16)
        return carry

    lax.fori_loop(0, row_parts, whiten, 0)


def select_kernel(where_ref, whitened_ref, owners_ref, places_ref, outgoing_ref, selector):
    rows = selector.shape[1]

    @pl.when(pl.program_id(0) == 0)
    def _():
        selector[...] = slot_selector(owners_ref[...], places_ref[...], where_ref[0], rows // 2)

    count, slots, columns = outgoing_ref.shape
    for n in range(slots // (2 * CAP)):
        sent = jnp.dot(
            selector[...], whitened_ref[rows * n : rows * (n + 1), :], preferred_element_type=jnp.float32
        ).astype(jnp.bfloat16)
        outgoing_ref[:, 2 * CAP * n : 2 * CAP * (n + 1), :] = sent.reshape(count, 2 * CAP, columns)


def vmem_spec():
    return pl.BlockSpec(memory_space=pltpu.VMEM)


def smem_spec():
    return pl.BlockSpec(memory_space=pltpu.SMEM)


def whole(array):
    return pl.BlockSpec(array.shape, lambda s: (0,) * array.ndim)


def spectra_call(traces, quality):
    rows, length = traces.shape
    part, depth = rows // ROW_STEPS, length // K_STEPS
    anywhere = pl.BlockSpec(memory_space=pl.ANY)
    return pl.pallas_call(
        spectra_kernel,
        in_specs=[anywhere, anywhere, vmem_spec()],
        out_specs=vmem_spec(),
        out_shape=jax.ShapeDtypeStruct((rows, 2 * F), jnp.bfloat16),
        scratch_shapes=[
            pltpu.VMEM((ROW_STEPS, K_STEPS, part, depth), jnp.bfloat16),
            pltpu.VMEM((K_STEPS, depth, 2 * F), jnp.bfloat16),
            pltpu.SemaphoreType.DMA((ROW_STEPS + 1, K_STEPS)),
        ],
        compiler_params=pltpu.CompilerParams(vmem_limit_bytes=SPECTRA_VMEM_LIMIT),
        cost_estimate=pl.CostEstimate(
            flops=2 * rows * length * 2 * F, bytes_accessed=2 * (rows + 2 * F) * length, transcendentals=rows * F
        ),
        name="spectra",
    )(traces, jnp.asarray(forward_table(length)), quality)


def select_call(where, whitened, owners, places, chan_count, ch_dev):
    rows, columns = whitened.shape
    block = rows // ROW_STEPS
    slots = block // (2 * ch_dev) * 2 * CAP
    return pl.pallas_call(
        select_kernel,
        grid=(ROW_STEPS,),
        in_specs=[smem_spec(), pl.BlockSpec((block, columns), lambda s: (s, 0)), whole(owners), whole(places)],
        out_specs=pl.BlockSpec((chan_count, slots, columns), lambda s: (0, s, 0)),
        out_shape=jax.ShapeDtypeStruct((chan_count, ROW_STEPS * slots, columns), jnp.bfloat16),
        scratch_shapes=[pltpu.VMEM((chan_count * 2 * CAP, 2 * ch_dev), jnp.bfloat16)],
        compiler_params=pltpu.CompilerParams(vmem_limit_bytes=SPECTRA_VMEM_LIMIT),
        cost_estimate=pl.CostEstimate(
            flops=4 * rows * chan_count * 2 * CAP * columns, bytes_accessed=2 * rows * columns * 3, transcendentals=0
        ),
        name="select",
    )(where, whitened, owners, places)


def cross_kernel(last, with_sum, local_windows, where_ref, first_ref, second_ref, *refs):
    refs = list(refs)
    sum_ref = refs.pop(0) if with_sum else None
    if last:
        high_ref, low_ref, out_ref, wide, spread, total = refs
    else:
        out_ref, wide, spread = refs
        total = out_ref
    windows, own_count = spread.shape[:2]
    ch_dev = wide.shape[1] // 2
    base = pl.multiple_of(where_ref[1] * own_count, 8)

    def widen(w, carry):
        if local_windows:
            wide[w, :ch_dev, :] = first_ref[w].astype(jnp.float32)
            wide[w, ch_dev:, :] = second_ref[w].astype(jnp.float32)
        else:
            shared = ch_dev - own_count
            wide[w, shared:ch_dev, :] = first_ref[w].astype(jnp.float32)
            rows = second_ref[w].astype(jnp.float32)
            for tile in range(ch_dev // 8):
                at = base + 8 * tile
                at = pl.multiple_of(jnp.where(at < shared, at, at + own_count), 8)
                wide[w, pl.ds(at, 8), :] = rows[8 * tile : 8 * tile + 8]
        for tile in range(own_count // 8):
            rows = wide[w, pl.ds(pl.multiple_of(base + 8 * tile, 8), 8), :]
            for i in range(8):
                for q in range(4):
                    spread[w, 8 * tile + i, q] = jnp.broadcast_to(rows[i : i + 1, q * H : (q + 1) * H], (8, H))
        return carry

    lax.fori_loop(0, windows, widen, 0)

    group, tiles = 4, 3
    rounds = SPAN // (8 * tiles)

    def block(index, carry):
        g = index // rounds
        j = index % rounds
        start = pl.multiple_of(base + 8 * (g // 2) + 8 * tiles * j, 8)

        def add_window(w, sums):
            sums = list(sums)
            right = [
                [wide[w, pl.ds(pl.multiple_of(start + 8 * t, 8), 8), q * H : (q + 1) * H] for q in range(4)]
                for t in range(tiles)
            ]
            for i in range(group):
                left = [spread[w, group * g + i, q] for q in range(4)]
                for t in range(tiles):
                    at = 3 * (i * tiles + t)
                    r = right[t]
                    sums[at] = sums[at] + (left[0] * r[0] + left[1] * r[1])
                    sums[at + 1] = sums[at + 1] + (left[2] * r[2] + left[3] * r[3])
                    sums[at + 2] = sums[at + 2] + ((left[1] * r[0] - left[0] * r[1]) + (left[2] * r[3] - left[3] * r[2]))
            return tuple(sums)

        zero = jnp.zeros((8, H), jnp.float32)
        sums = lax.fori_loop(0, windows, add_window, (zero,) * (3 * group * tiles), unroll=2)
        for i in range(group):
            for t in range(tiles):
                at = 3 * (i * tiles + t)
                real, imag = fold_columns(sums[at], sums[at + 1], sums[at + 2])
                where = pl.ds(pl.multiple_of(8 * tiles * j + 8 * t, 8), 8)
                if with_sum:
                    real = real + sum_ref[group * g + i, where, :H]
                    imag = imag + sum_ref[group * g + i, where, H:]
                total[group * g + i, where, :H] = real
                total[group * g + i, where, H:] = imag
        return carry

    lax.fori_loop(0, own_count // group * rounds, block, 0)

    if last:

        def finish(eight, carry):
            first = pl.multiple_of(8 * eight, 8)
            stacks = total[pl.ds(first, 8)].reshape(8 * SPAN, F)
            lagged = lag_transform(stacks, high_ref[...], low_ref[...]).reshape(8, SPAN, NLAG)
            for i in range(8):
                out_ref[first + i] = lagged[i, i + 1 : i + 1 + REACH, :]
            return carry

        lax.fori_loop(0, own_count // 8, finish, 0)


def cross_call(where, first, second, ch_dev, own_count, sums, tables, local_windows):
    windows, _, columns = first.shape
    last = tables is not None
    with_sum = sums is not None
    operands = [where, first, second]
    if with_sum:
        operands.append(sums)
    scratch = [
        pltpu.VMEM((windows, 2 * ch_dev, columns), jnp.float32),
        pltpu.VMEM((windows, own_count, 4, 8, H), jnp.float32),
    ]
    if last:
        operands += list(tables)
        scratch.append(pltpu.VMEM((own_count, SPAN, F), jnp.float32))
    shape = (own_count, REACH, NLAG) if last else (own_count, SPAN, F)
    return pl.pallas_call(
        functools.partial(cross_kernel, last, with_sum, local_windows),
        in_specs=[smem_spec()] + [vmem_spec()] * (len(operands) - 1),
        out_specs=vmem_spec(),
        out_shape=jax.ShapeDtypeStruct(shape, jnp.float32),
        scratch_shapes=scratch,
        compiler_params=pltpu.CompilerParams(vmem_limit_bytes=VMEM_LIMIT),
        cost_estimate=pl.CostEstimate(
            flops=10_000_000_000, bytes_accessed=4 * windows * ch_dev * columns + 4 * own_count * SPAN * F, transcendentals=0
        ),
        name="cross",
    )(*operands)


def fold_kernel(where_ref, incoming_ref, own_ref, owners_ref, high_ref, low_ref, earlier_ref, out_ref, sums, picker):
    step = pl.program_id(0)
    rows = own_ref.shape[0]
    ch_dev = rows // 2

    @pl.when(step == 0)
    def _():
        sums[...] = jnp.zeros_like(sums)
        owners = owners_ref[...].astype(jnp.float32)
        per_row = owners.shape[1] // ch_dev
        device = where_ref[0]
        line = jnp.sum(jnp.where(rows_of(owners.shape) == device // per_row, owners, 0.0), axis=0, keepdims=True)
        shape = (rows, owners.shape[1])
        line = jnp.broadcast_to(line, shape)
        first = device % per_row * ch_dev
        place = first + rows_of(shape) % ch_dev
        lane = lanes_of(shape)
        owner = jnp.sum(jnp.where(lane == place, line, 0.0), axis=1, keepdims=True)
        earlier = (lane >= first) & (lane < place) & (line == owner)
        rank = jnp.sum(earlier.astype(jnp.float32), axis=1, keepdims=True)
        source = (2 * CAP * owner + rank).astype(jnp.int32)
        shape = picker.shape
        target = source + CAP * (rows_of(shape) // ch_dev)
        picker[...] = (lanes_of(shape) == target).astype(jnp.float32).astype(jnp.bfloat16)

    count, slots, columns = incoming_ref.shape
    right = jnp.dot(
        picker[...], incoming_ref[...].reshape(count * slots, columns), preferred_element_type=jnp.float32
    )
    left = own_ref[...].astype(jnp.float32)
    l = [left[:, q * H : (q + 1) * H] for q in range(4)]
    r = [right[:, q * H : (q + 1) * H] for q in range(4)]
    first = l[0] * r[0] + l[1] * r[1]
    second = l[2] * r[2] + l[3] * r[3]
    imag = (l[1] * r[0] - l[0] * r[1]) + (l[2] * r[3] - l[3] * r[2])
    for n, term in enumerate((first, second, imag)):
        sums[n] += term[:ch_dev] + term[ch_dev:]

    @pl.when(step == pl.num_programs(0) - 1)
    def _():
        stacks = jnp.concatenate(fold_columns(sums[0], sums[1], sums[2]), axis=1)
        out_ref[...] = lag_transform(stacks, high_ref[...], low_ref[...])


def fold_call(where, incoming, own, owners, ch_dev, tables, earlier):
    count, slots, columns = incoming.shape
    rows = 2 * ch_dev
    pairs = own.shape[0] // rows
    return pl.pallas_call(
        fold_kernel,
        grid=(pairs,),
        in_specs=[
            smem_spec(),
            pl.BlockSpec((count, slots // pairs, columns), lambda s: (0, s, 0)),
            pl.BlockSpec((rows, columns), lambda s: (s, 0)),
            whole(owners),
            whole(tables[0]),
            whole(tables[1]),
            pl.BlockSpec(memory_space=pl.ANY),
        ],
        out_specs=pl.BlockSpec((ch_dev, NLAG), lambda s: (0, 0)),
        out_shape=jax.ShapeDtypeStruct((ch_dev, NLAG), jnp.float32),
        scratch_shapes=[
            pltpu.VMEM((3, ch_dev, H), jnp.float32),
            pltpu.VMEM((rows, count * slots // pairs), jnp.bfloat16),
        ],
        compiler_params=pltpu.CompilerParams(vmem_limit_bytes=FOLD_VMEM_LIMIT),
        cost_estimate=pl.CostEstimate(
            flops=2 * rows * pairs * count * 2 * CAP * columns,
            bytes_accessed=2 * (incoming.size + own.size),
            transcendentals=0,
        ),
        name="fold",
    )(where, incoming, own, owners, *tables, earlier)


def from_above(block):
    count = lax.axis_size("chan")
    return lax.ppermute(block, "chan", [(i, i - 1) for i in range(1, count)])


def round_win(block, shift):
    count = lax.axis_size("win")
    return lax.ppermute(block, "win", [(i, (i + shift) % count) for i in range(count)])


def local(traces, quality, fold_block, fold_offset):
    win_dev, ch_dev, length = traces.shape
    chan_count = lax.axis_size("chan")
    win_count = lax.axis_size("win")
    window_part = lax.axis_index("win")
    own_count = ch_dev // win_count
    shared = ch_dev - own_count
    where = jnp.stack([lax.axis_index("chan"), window_part]).astype(jnp.int32)
    tables = [jnp.asarray(t) for t in inverse_tables(1.0 / math.sqrt(F * win_dev * win_count))]
    owners = fold_block.reshape(-1, 2 * ch_dev)
    places = fold_offset.reshape(-1, 2 * ch_dev)
    flat = spectra_call(traces.reshape(win_dev * ch_dev, length), quality.reshape(1, ch_dev))
    whitened = flat.reshape(win_dev, ch_dev, 2 * F)
    upper = from_above(whitened)
    common = [round_win(whitened[:, shared:], shift) for shift in range(1, win_count)]
    outgoing = select_call(where, flat, owners, places, chan_count, ch_dev)
    incoming = lax.all_to_all(outgoing, "chan", split_axis=0, concat_axis=0, tiled=True)
    offered = jnp.concatenate([whitened[:, :shared], upper], axis=1)
    special = [
        round_win(
            lax.dynamic_slice_in_dim(offered, (window_part + shift) % win_count * own_count, ch_dev, 1), shift
        )
        for shift in range(1, win_count)
    ]
    arrived = [(whitened, upper)] + list(zip(common, special))
    sums = None
    for n, (first, second) in enumerate(arrived):
        ends = tables if n == win_count - 1 else None
        sums = cross_call(where, first, second, ch_dev, own_count, sums, ends, n == 0)
    share = fold_call(where, incoming, flat, owners, ch_dev, tables, sums)
    fold = lax.dynamic_slice_in_dim(share, window_part * own_count, own_count, 0)
    for shift in range(1, win_count):
        target = (window_part + shift) % win_count * own_count
        fold = fold + round_win(lax.dynamic_slice_in_dim(share, target, own_count, 0), shift)
    return (sums, fold)


def solution(mesh):
    in_specs = (P("win", "chan", None), P("chan"), P(), P())
    out_specs = (P(("chan", "win"), None, None), P(("chan", "win"), None))
    return jax.shard_map(local, mesh=mesh, in_specs=in_specs, out_specs=out_specs, check_vma=False)
```

```python
import functools
import math

import jax
import jax.numpy as jnp
import numpy as np
from jax import lax
from jax.experimental import pallas as pl
from jax.experimental.pallas import tpu as pltpu
from jax.sharding import PartitionSpec as P

F = 256
H = F // 2
BAND_LO = 32
NLAG = 256
REACH = 64
CAP = 8
SPAN = REACH + 8
smooth_reach = 4
ROW_STEPS = 3
QUARTERS = 4
VMEM_LIMIT = 24 * 1024 * 1024
FOLD_VMEM_LIMIT = 16 * 1024 * 1024
SPECTRA_VMEM_LIMIT = 50 * 1024 * 1024


def bin_order():
    residues = np.arange(H)
    first = (residues - BAND_LO) % F
    second = (-residues - BAND_LO) % F
    second[0] = (H - BAND_LO) % F
    return first, second


def forward_table(length):
    samples = np.arange(length // 4, dtype=np.int64)[:, None]
    parts = []
    for bins in bin_order():
        angles = (samples * (bins + BAND_LO)[None, :] % length) * (2.0 * math.pi / length)
        parts += [np.cos(angles), -np.sin(angles)]
    return np.concatenate(parts, axis=1).astype(np.float32).astype(jnp.bfloat16)


def inverse_tables(factor):
    shifts = (np.arange(NLAG) + NLAG // 2)[None, :]
    residues = np.arange(H)[:, None]
    angles = (residues * shifts % NLAG) * (2.0 * math.pi / NLAG)
    sign = np.where(shifts[0] % 2 == 0, 1.0, -1.0)
    real, imag = np.cos(angles), -np.sin(angles)
    real[0] = (1.0 + sign) / 2.0
    imag[0] = (1.0 - sign) / 2.0
    table = np.concatenate([real, imag], axis=0) * factor
    high = table.astype(np.float32).astype(jnp.bfloat16)
    low = (table - high.astype(np.float64)).astype(np.float32).astype(jnp.bfloat16)
    return high, low


def lag_transform(stacks, high, low):
    top = stacks.astype(jnp.bfloat16)
    rest = (stacks - top.astype(jnp.float32)).astype(jnp.bfloat16)
    dot = functools.partial(jnp.dot, preferred_element_type=jnp.float32)
    return dot(top, high) + (dot(rest, high) + dot(top, low))


def fold_columns(first, second, imag):
    lane = lax.broadcasted_iota(jnp.int32, first.shape, first.ndim - 1)
    return first + second, jnp.where(lane == 0, first - second, imag)


def lanes_of(shape):
    return lax.broadcasted_iota(jnp.int32, shape, len(shape) - 1)


def rows_of(shape):
    return lax.broadcasted_iota(jnp.int32, shape, len(shape) - 2)


def band_matrix():
    def bins(index):
        lane = index & (H - 1)
        residue = jnp.where(index < H, lane, jnp.where(lane == 0, H, F - lane))
        return (residue - BAND_LO + F) & (F - 1)

    apart = bins(rows_of((F, F))) - bins(lanes_of((F, F)))
    return (jnp.abs(apart) <= smooth_reach).astype(jnp.float32).astype(jnp.bfloat16)


def exact_dot(left, right):
    return jnp.dot(left.astype(jnp.bfloat16), right.astype(jnp.bfloat16), preferred_element_type=jnp.float32)


def slot_selector(owners, places, device, ch_dev):
    height, width = owners.shape
    per_row = width // ch_dev
    wanted = (owners == device).astype(jnp.float32)
    before = rows_of((width, width))
    after = lanes_of((width, width))
    earlier = ((before < after) & (before // ch_dev == after // ch_dev)).astype(jnp.float32)
    ranks = exact_dot(wanted, earlier)
    slots = jnp.where(wanted > 0, ranks, float(CAP))
    count = height * per_row * 2 * CAP
    to_row = (rows_of((count, height)) // (2 * CAP * per_row) == lanes_of((count, height))).astype(jnp.float32)
    row_slots = exact_dot(to_row, slots)
    row_places = exact_dot(to_row, places.astype(jnp.float32))
    shape = (count, width)
    row = rows_of(shape)
    mine = (row_slots == (row % CAP).astype(jnp.float32)) & (lanes_of(shape) // ch_dev == row // (2 * CAP) % per_row)
    place = jnp.sum(jnp.where(mine, row_places + 1.0, 0.0), axis=1, keepdims=True).astype(jnp.int32) - 1
    shape = (count, 2 * ch_dev)
    half = rows_of(shape) // CAP % 2
    lane = lanes_of(shape)
    return ((lane == place + ch_dev * half) & (place >= 0)).astype(jnp.float32).astype(jnp.bfloat16)


def turned_sum(quarters, real, imag, negative):
    rows = quarters[0].shape[0]
    lane = lanes_of((rows, H))
    residue = ((F - lane) if negative else lane) & 3
    sign = jnp.where((residue & 1) == 0, 1.0, -1.0)
    straight = jnp.where(residue == 0, 1.0, jnp.where(residue == 2, -1.0, 0.0))
    turned = jnp.where(residue == 1, 1.0, jnp.where(residue == 3, -1.0, 0.0))
    re = [quarter[:, real * H : (real + 1) * H] for quarter in quarters]
    im = [quarter[:, imag * H : (imag + 1) * H] for quarter in quarters]
    odd_re, odd_im = re[1] + sign * re[3], im[1] + sign * im[3]
    return (
        re[0] + sign * re[2] + (straight * odd_re + turned * odd_im),
        im[0] + sign * im[2] + (straight * odd_im - turned * odd_re),
    )


def spectra_kernel(traces_ref, table_ref, quality_ref, whitened_ref, traces, table, sems):
    row_parts, chunks, rows, depth = traces.shape
    ch_dev = quality_ref.shape[1]

    def traces_copy(part, k):
        source = traces_ref.at[pl.ds(part * rows, rows), pl.ds(k * depth, depth)]
        return pltpu.make_async_copy(source, traces.at[part, k], sems.at[part, k])

    table_copy = pltpu.make_async_copy(table_ref, table, sems.at[row_parts, 0])
    table_copy.start()
    for part in range(row_parts):
        for k in range(chunks):
            traces_copy(part, k).start()

    band = band_matrix()
    shape = (rows, ch_dev)
    keep = jnp.sum(
        jnp.where(rows_of(shape) % ch_dev == lanes_of(shape), quality_ref[...].astype(jnp.float32), 0.0),
        axis=1, keepdims=True,
    )

    def whiten(part, carry):
        @pl.when(part == 0)
        def _():
            table_copy.wait()

        quarters = []
        for k in range(chunks):
            traces_copy(part, k).wait()
            quarters.append(jnp.dot(traces[part, k], table[...], preferred_element_type=jnp.float32))
        parts = turned_sum(quarters, 0, 1, False) + turned_sum(quarters, 2, 3, True)
        energy = jnp.concatenate(
            [parts[0] * parts[0] + parts[1] * parts[1], parts[2] * parts[2] + parts[3] * parts[3]], axis=1
        )
        top = energy.astype(jnp.bfloat16)
        rest = (energy - top.astype(jnp.float32)).astype(jnp.bfloat16)
        smooth = jnp.dot(top, band, preferred_element_type=jnp.float32) + jnp.dot(
            rest, band, preferred_element_type=jnp.float32
        )
        water = jnp.sum(energy, axis=1, keepdims=True) * (1.0 / F)
        scaling = lax.rsqrt(smooth * (1.0 / (2.0 * smooth_reach + 1.0)) + (0.1 * water + 1e-06)) * keep
        near, far = scaling[:, :H], scaling[:, H:]
        white = [parts[0] * near, parts[1] * near, parts[2] * far, parts[3] * far]
        at = pl.ds(pl.multiple_of(part * rows, rows), rows)
        for q in range(4):
            whitened_ref[at, q * H : (q + 1) * H] = white[q].astype(jnp.bfloat16)
        return carry

    lax.fori_loop(0, row_parts, whiten, 0)


def select_kernel(where_ref, whitened_ref, owners_ref, places_ref, outgoing_ref, selector):
    rows = selector.shape[1]

    @pl.when(pl.program_id(0) == 0)
    def _():
        selector[...] = slot_selector(owners_ref[...], places_ref[...], where_ref[0], rows // 2)

    count, slots, columns = outgoing_ref.shape
    for n in range(slots // (2 * CAP)):
        sent = jnp.dot(
            selector[...], whitened_ref[rows * n : rows * (n + 1), :], preferred_element_type=jnp.float32
        ).astype(jnp.bfloat16)
        outgoing_ref[:, 2 * CAP * n : 2 * CAP * (n + 1), :] = sent.reshape(count, 2 * CAP, columns)


def vmem_spec():
    return pl.BlockSpec(memory_space=pltpu.VMEM)


def smem_spec():
    return pl.BlockSpec(memory_space=pltpu.SMEM)


def whole(array):
    return pl.BlockSpec(array.shape, lambda s: (0,) * array.ndim)


def spectra_call(traces, quality):
    rows, length = traces.shape
    part, depth = rows // ROW_STEPS, length // QUARTERS
    anywhere = pl.BlockSpec(memory_space=pl.ANY)
    return pl.pallas_call(
        spectra_kernel,
        in_specs=[anywhere, anywhere, vmem_spec()],
        out_specs=vmem_spec(),
        out_shape=jax.ShapeDtypeStruct((rows, 2 * F), jnp.bfloat16),
        scratch_shapes=[
            pltpu.VMEM((ROW_STEPS, QUARTERS, part, depth), jnp.bfloat16),
            pltpu.VMEM((depth, 2 * F), jnp.bfloat16),
            pltpu.SemaphoreType.DMA((ROW_STEPS + 1, QUARTERS)),
        ],
        compiler_params=pltpu.CompilerParams(vmem_limit_bytes=SPECTRA_VMEM_LIMIT),
        cost_estimate=pl.CostEstimate(
            flops=2 * rows * length * 2 * F, bytes_accessed=2 * rows * length, transcendentals=rows * F
        ),
        name="spectra",
    )(traces, jnp.asarray(forward_table(length)), quality)


def select_call(where, whitened, owners, places, chan_count, ch_dev):
    rows, columns = whitened.shape
    block = rows // ROW_STEPS
    slots = block // (2 * ch_dev) * 2 * CAP
    return pl.pallas_call(
        select_kernel,
        grid=(ROW_STEPS,),
        in_specs=[smem_spec(), pl.BlockSpec((block, columns), lambda s: (s, 0)), whole(owners), whole(places)],
        out_specs=pl.BlockSpec((chan_count, slots, columns), lambda s: (0, s, 0)),
        out_shape=jax.ShapeDtypeStruct((chan_count, ROW_STEPS * slots, columns), jnp.bfloat16),
        scratch_shapes=[pltpu.VMEM((chan_count * 2 * CAP, 2 * ch_dev), jnp.bfloat16)],
        compiler_params=pltpu.CompilerParams(vmem_limit_bytes=SPECTRA_VMEM_LIMIT),
        cost_estimate=pl.CostEstimate(
            flops=4 * rows * chan_count * 2 * CAP * columns, bytes_accessed=2 * rows * columns * 3, transcendentals=0
        ),
        name="select",
    )(where, whitened, owners, places)


def cross_kernel(last, with_sum, local_windows, where_ref, first_ref, second_ref, *refs):
    refs = list(refs)
    sum_ref = refs.pop(0) if with_sum else None
    if last:
        high_ref, low_ref, out_ref, done_ref, wide, spread, total = refs
        done_ref[...] = jnp.zeros_like(done_ref)
    else:
        out_ref, wide, spread = refs
        total = out_ref
    windows, own_count = spread.shape[:2]
    ch_dev = wide.shape[1] // 2
    base = pl.multiple_of(where_ref[1] * own_count, 8)

    def widen(w, carry):
        if local_windows:
            wide[w, :ch_dev, :] = first_ref[w].astype(jnp.float32)
            wide[w, ch_dev:, :] = second_ref[w].astype(jnp.float32)
        else:
            shared = ch_dev - own_count
            wide[w, shared:ch_dev, :] = first_ref[w].astype(jnp.float32)
            rows = second_ref[w].astype(jnp.float32)
            for tile in range(ch_dev // 8):
                at = base + 8 * tile
                at = pl.multiple_of(jnp.where(at < shared, at, at + own_count), 8)
                wide[w, pl.ds(at, 8), :] = rows[8 * tile : 8 * tile + 8]
        for tile in range(own_count // 8):
            rows = wide[w, pl.ds(pl.multiple_of(base + 8 * tile, 8), 8), :]
            for i in range(8):
                for q in range(4):
                    spread[w, 8 * tile + i, q] = jnp.broadcast_to(rows[i : i + 1, q * H : (q + 1) * H], (8, H))
        return carry

    lax.fori_loop(0, windows, widen, 0)

    group, tiles = 4, 3
    rounds = SPAN // (8 * tiles)

    def block(index, carry):
        g = index // rounds
        j = index % rounds
        start = pl.multiple_of(base + 8 * (g // 2) + 8 * tiles * j, 8)

        def add_window(w, sums):
            sums = list(sums)
            right = [
                [wide[w, pl.ds(pl.multiple_of(start + 8 * t, 8), 8), q * H : (q + 1) * H] for q in range(4)]
                for t in range(tiles)
            ]
            for i in range(group):
                left = [spread[w, group * g + i, q] for q in range(4)]
                for t in range(tiles):
                    at = 3 * (i * tiles + t)
                    r = right[t]
                    sums[at] = sums[at] + (left[0] * r[0] + left[1] * r[1])
                    sums[at + 1] = sums[at + 1] + (left[2] * r[2] + left[3] * r[3])
                    sums[at + 2] = sums[at + 2] + ((left[1] * r[0] - left[0] * r[1]) + (left[2] * r[3] - left[3] * r[2]))
            return tuple(sums)

        zero = jnp.zeros((8, H), jnp.float32)
        sums = lax.fori_loop(0, windows, add_window, (zero,) * (3 * group * tiles), unroll=2)
        for i in range(group):
            for t in range(tiles):
                at = 3 * (i * tiles + t)
                real, imag = fold_columns(sums[at], sums[at + 1], sums[at + 2])
                where = pl.ds(pl.multiple_of(8 * tiles * j + 8 * t, 8), 8)
                if with_sum:
                    real = real + sum_ref[group * g + i, where, :H]
                    imag = imag + sum_ref[group * g + i, where, H:]
                total[group * g + i, where, :H] = real
                total[group * g + i, where, H:] = imag
        return carry

    lax.fori_loop(0, own_count // group * rounds, block, 0)

    if last:

        def finish(eight, carry):
            first = pl.multiple_of(8 * eight, 8)
            stacks = total[pl.ds(first, 8)].reshape(8 * SPAN, F)
            lagged = lag_transform(stacks, high_ref[...], low_ref[...]).reshape(8, SPAN, NLAG)
            for i in range(8):
                out_ref[first + i] = lagged[i, i + 1 : i + 1 + REACH, :]
            return carry

        lax.fori_loop(0, own_count // 8, finish, 0)


def cross_call(where, first, second, ch_dev, own_count, sums, tables, local_windows):
    windows, _, columns = first.shape
    last = tables is not None
    with_sum = sums is not None
    operands = [where, first, second]
    if with_sum:
        operands.append(sums)
    scratch = [
        pltpu.VMEM((windows, 2 * ch_dev, columns), jnp.float32),
        pltpu.VMEM((windows, own_count, 4, 8, H), jnp.float32),
    ]
    if last:
        operands += list(tables)
        scratch.append(pltpu.VMEM((own_count, SPAN, F), jnp.float32))
    shape = (own_count, REACH, NLAG) if last else (own_count, SPAN, F)
    out_shape = [jax.ShapeDtypeStruct(shape, jnp.float32)]
    if last:
        out_shape.append(jax.ShapeDtypeStruct((8, H), jnp.float32))
    return pl.pallas_call(
        functools.partial(cross_kernel, last, with_sum, local_windows),
        in_specs=[smem_spec()] + [vmem_spec()] * (len(operands) - 1),
        out_specs=[vmem_spec()] * len(out_shape),
        out_shape=out_shape,
        scratch_shapes=scratch,
        compiler_params=pltpu.CompilerParams(vmem_limit_bytes=VMEM_LIMIT),
        cost_estimate=pl.CostEstimate(
            flops=30_000_000_000, bytes_accessed=4 * windows * ch_dev * columns + 4 * own_count * SPAN * F, transcendentals=0
        ),
        name="cross",
    )(*operands)


def fold_kernel(where_ref, incoming_ref, own_ref, owners_ref, high_ref, low_ref, earlier_ref, out_ref, sums, picker):
    step = pl.program_id(0)
    rows = own_ref.shape[0]
    ch_dev = rows // 2

    @pl.when(step == 0)
    def _():
        sums[...] = jnp.zeros_like(sums)
        owners = owners_ref[...].astype(jnp.float32)
        per_row = owners.shape[1] // ch_dev
        device = where_ref[0]
        line = jnp.sum(jnp.where(rows_of(owners.shape) == device // per_row, owners, 0.0), axis=0, keepdims=True)
        shape = (rows, owners.shape[1])
        line = jnp.broadcast_to(line, shape)
        first = device % per_row * ch_dev
        place = first + rows_of(shape) % ch_dev
        lane = lanes_of(shape)
        owner = jnp.sum(jnp.where(lane == place, line, 0.0), axis=1, keepdims=True)
        earlier = (lane >= first) & (lane < place) & (line == owner)
        rank = jnp.sum(earlier.astype(jnp.float32), axis=1, keepdims=True)
        source = (2 * CAP * owner + rank).astype(jnp.int32)
        shape = picker.shape
        target = source + CAP * (rows_of(shape) // ch_dev)
        picker[...] = (lanes_of(shape) == target).astype(jnp.float32).astype(jnp.bfloat16)

    count, slots, columns = incoming_ref.shape
    right = jnp.dot(
        picker[...], incoming_ref[...].reshape(count * slots, columns), preferred_element_type=jnp.float32
    )
    left = own_ref[...].astype(jnp.float32)
    l = [left[:, q * H : (q + 1) * H] for q in range(4)]
    r = [right[:, q * H : (q + 1) * H] for q in range(4)]
    first = l[0] * r[0] + l[1] * r[1]
    second = l[2] * r[2] + l[3] * r[3]
    imag = (l[1] * r[0] - l[0] * r[1]) + (l[2] * r[3] - l[3] * r[2])
    for n, term in enumerate((first, second, imag)):
        sums[n] += term[:ch_dev] + term[ch_dev:]

    @pl.when(step == pl.num_programs(0) - 1)
    def _():
        stacks = jnp.concatenate(fold_columns(sums[0], sums[1], sums[2]), axis=1)
        out_ref[...] = lag_transform(stacks, high_ref[...], low_ref[...])


def fold_call(where, incoming, own, owners, ch_dev, tables, earlier):
    count, slots, columns = incoming.shape
    rows = 2 * ch_dev
    pairs = own.shape[0] // rows
    return pl.pallas_call(
        fold_kernel,
        grid=(pairs,),
        in_specs=[
            smem_spec(),
            pl.BlockSpec((count, slots // pairs, columns), lambda s: (0, s, 0)),
            pl.BlockSpec((rows, columns), lambda s: (s, 0)),
            whole(owners),
            whole(tables[0]),
            whole(tables[1]),
            pl.BlockSpec(memory_space=pl.ANY),
        ],
        out_specs=pl.BlockSpec((ch_dev, NLAG), lambda s: (0, 0)),
        out_shape=jax.ShapeDtypeStruct((ch_dev, NLAG), jnp.float32),
        scratch_shapes=[
            pltpu.VMEM((3, ch_dev, H), jnp.float32),
            pltpu.VMEM((rows, count * slots // pairs), jnp.bfloat16),
        ],
        compiler_params=pltpu.CompilerParams(vmem_limit_bytes=FOLD_VMEM_LIMIT),
        cost_estimate=pl.CostEstimate(
            flops=2 * rows * pairs * count * 2 * CAP * columns,
            bytes_accessed=2 * (incoming.size + own.size),
            transcendentals=0,
        ),
        name="fold",
    )(where, incoming, own, owners, *tables, earlier)


def from_above(block):
    count = lax.axis_size("chan")
    return lax.ppermute(block, "chan", [(i, i - 1) for i in range(1, count)])


def round_win(block, shift):
    count = lax.axis_size("win")
    return lax.ppermute(block, "win", [(i, (i + shift) % count) for i in range(count)])


def local(traces, quality, fold_block, fold_offset):
    win_dev, ch_dev, length = traces.shape
    chan_count = lax.axis_size("chan")
    win_count = lax.axis_size("win")
    window_part = lax.axis_index("win")
    own_count = ch_dev // win_count
    shared = ch_dev - own_count
    where = jnp.stack([lax.axis_index("chan"), window_part]).astype(jnp.int32)
    tables = [jnp.asarray(t) for t in inverse_tables(1.0 / math.sqrt(F * win_dev * win_count))]
    owners = fold_block.reshape(-1, 2 * ch_dev)
    places = fold_offset.reshape(-1, 2 * ch_dev)
    flat = spectra_call(traces.reshape(win_dev * ch_dev, length), quality.reshape(1, ch_dev))
    whitened = flat.reshape(win_dev, ch_dev, 2 * F)
    upper = from_above(whitened)
    common = [round_win(whitened[:, shared:], shift) for shift in range(1, win_count)]
    outgoing = select_call(where, flat, owners, places, chan_count, ch_dev)
    incoming = lax.all_to_all(outgoing, "chan", split_axis=0, concat_axis=0, tiled=True)
    offered = jnp.concatenate([whitened[:, :shared], upper], axis=1)
    special = [
        round_win(
            lax.dynamic_slice_in_dim(offered, (window_part + shift) % win_count * own_count, ch_dev, 1), shift
        )
        for shift in range(1, win_count)
    ]
    arrived = [(whitened, upper)] + list(zip(common, special))
    sums = None
    for n, (first, second) in enumerate(arrived):
        ends = tables if n == win_count - 1 else None
        sums, *done = cross_call(where, first, second, ch_dev, own_count, sums, ends, n == 0)
    share = fold_call(where, incoming, flat, owners, ch_dev, tables, done[0])
    fold = lax.dynamic_slice_in_dim(share, window_part * own_count, own_count, 0)
    for shift in range(1, win_count):
        target = (window_part + shift) % win_count * own_count
        fold = fold + round_win(lax.dynamic_slice_in_dim(share, target, own_count, 0), shift)
    return (sums, fold)


def solution(mesh):
    in_specs = (P("win", "chan", None), P("chan"), P(), P())
    out_specs = (P(("chan", "win"), None, None), P(("chan", "win"), None))
    return jax.shard_map(local, mesh=mesh, in_specs=in_specs, out_specs=out_specs, check_vma=False)
```

```python
import functools
import math

import jax
import jax.numpy as jnp
import numpy as np
from jax import lax
from jax.experimental import pallas as pl
from jax.experimental.pallas import tpu as pltpu
from jax.sharding import PartitionSpec as P

F = 256
H = F // 2
BAND_LO = 32
NLAG = 256
REACH = 64
CAP = 8
SPAN = REACH + 16
FLUSH = 4
smooth_reach = 4
ROW_STEPS = 3
QUARTERS = 4
VMEM_LIMIT = 24 * 1024 * 1024
FOLD_VMEM_LIMIT = 16 * 1024 * 1024
SPECTRA_VMEM_LIMIT = 50 * 1024 * 1024


def bin_order():
    residues = np.arange(H)
    first = (residues - BAND_LO) % F
    second = (-residues - BAND_LO) % F
    second[0] = (H - BAND_LO) % F
    return first, second


def forward_table(length):
    samples = np.arange(length // 4, dtype=np.int64)[:, None]
    parts = []
    for bins in bin_order():
        angles = (samples * (bins + BAND_LO)[None, :] % length) * (2.0 * math.pi / length)
        parts += [np.cos(angles), -np.sin(angles)]
    return np.concatenate(parts, axis=1).astype(np.float32).astype(jnp.bfloat16)


def inverse_tables(factor):
    shifts = (np.arange(NLAG) + NLAG // 2)[None, :]
    residues = np.arange(H)[:, None]
    angles = (residues * shifts % NLAG) * (2.0 * math.pi / NLAG)
    sign = np.where(shifts[0] % 2 == 0, 1.0, -1.0)
    real, imag = np.cos(angles), -np.sin(angles)
    real[0] = (1.0 + sign) / 2.0
    imag[0] = (1.0 - sign) / 2.0
    table = np.concatenate([real, imag], axis=0) * factor
    high = table.astype(np.float32).astype(jnp.bfloat16)
    low = (table - high.astype(np.float64)).astype(np.float32).astype(jnp.bfloat16)
    return high, low


def lag_transform(stacks, high, low):
    top = stacks.astype(jnp.bfloat16)
    rest = (stacks - top.astype(jnp.float32)).astype(jnp.bfloat16)
    dot = functools.partial(jnp.dot, preferred_element_type=jnp.float32)
    return dot(top, high) + (dot(rest, high) + dot(top, low))


def fold_columns(first, second, imag):
    lane = lax.broadcasted_iota(jnp.int32, first.shape, first.ndim - 1)
    return first + second, jnp.where(lane == 0, first - second, imag)


def lanes_of(shape):
    return lax.broadcasted_iota(jnp.int32, shape, len(shape) - 1)


def rows_of(shape):
    return lax.broadcasted_iota(jnp.int32, shape, len(shape) - 2)


def band_matrix():
    def bins(index):
        lane = index & (H - 1)
        residue = jnp.where(index < H, lane, jnp.where(lane == 0, H, F - lane))
        return (residue - BAND_LO + F) & (F - 1)

    apart = bins(rows_of((F, F))) - bins(lanes_of((F, F)))
    return (jnp.abs(apart) <= smooth_reach).astype(jnp.float32).astype(jnp.bfloat16)


def exact_dot(left, right):
    return jnp.dot(left.astype(jnp.bfloat16), right.astype(jnp.bfloat16), preferred_element_type=jnp.float32)


def slot_selector(owners, places, device, ch_dev):
    height, width = owners.shape
    per_row = width // ch_dev
    wanted = (owners == device).astype(jnp.float32)
    before = rows_of((width, width))
    after = lanes_of((width, width))
    earlier = ((before < after) & (before // ch_dev == after // ch_dev)).astype(jnp.float32)
    ranks = exact_dot(wanted, earlier)
    slots = jnp.where(wanted > 0, ranks, float(CAP))
    count = height * per_row * 2 * CAP
    to_row = (rows_of((count, height)) // (2 * CAP * per_row) == lanes_of((count, height))).astype(jnp.float32)
    row_slots = exact_dot(to_row, slots)
    row_places = exact_dot(to_row, places.astype(jnp.float32))
    shape = (count, width)
    row = rows_of(shape)
    mine = (row_slots == (row % CAP).astype(jnp.float32)) & (lanes_of(shape) // ch_dev == row // (2 * CAP) % per_row)
    place = jnp.sum(jnp.where(mine, row_places + 1.0, 0.0), axis=1, keepdims=True).astype(jnp.int32) - 1
    shape = (count, 2 * ch_dev)
    half = rows_of(shape) // CAP % 2
    lane = lanes_of(shape)
    return ((lane == place + ch_dev * half) & (place >= 0)).astype(jnp.float32).astype(jnp.bfloat16)


def turned_sum(quarters, real, imag, negative):
    rows = quarters[0].shape[0]
    lane = lanes_of((rows, H))
    residue = ((F - lane) if negative else lane) & 3
    sign = jnp.where((residue & 1) == 0, 1.0, -1.0)
    straight = jnp.where(residue == 0, 1.0, jnp.where(residue == 2, -1.0, 0.0))
    turned = jnp.where(residue == 1, 1.0, jnp.where(residue == 3, -1.0, 0.0))
    re = [quarter[:, real * H : (real + 1) * H] for quarter in quarters]
    im = [quarter[:, imag * H : (imag + 1) * H] for quarter in quarters]
    odd_re, odd_im = re[1] + sign * re[3], im[1] + sign * im[3]
    return (
        re[0] + sign * re[2] + (straight * odd_re + turned * odd_im),
        im[0] + sign * im[2] + (straight * odd_im - turned * odd_re),
    )


def spectra_kernel(traces_ref, table_ref, quality_ref, whitened_ref, traces, table, quality, sems):
    row_parts, chunks, rows, depth = traces.shape
    ch_dev = quality.shape[1]

    def traces_copy(part, k):
        source = traces_ref.at[pl.ds(part * rows, rows), pl.ds(k * depth, depth)]
        return pltpu.make_async_copy(source, traces.at[part, k], sems.at[part, k])

    table_copy = pltpu.make_async_copy(table_ref, table, sems.at[row_parts, 0])
    table_copy.start()
    quality_copy = pltpu.make_async_copy(quality_ref, quality, sems.at[row_parts, 1])
    quality_copy.start()
    for part in range(row_parts):
        for k in range(chunks):
            traces_copy(part, k).start()

    band = band_matrix()
    quality_copy.wait()
    shape = (rows, ch_dev)
    keep = jnp.sum(
        jnp.where(rows_of(shape) % ch_dev == lanes_of(shape), quality[...].astype(jnp.float32), 0.0),
        axis=1, keepdims=True,
    )

    def whiten(part, carry):
        @pl.when(part == 0)
        def _():
            table_copy.wait()

        quarters = []
        for k in range(chunks):
            traces_copy(part, k).wait()
            quarters.append(jnp.dot(traces[part, k], table[...], preferred_element_type=jnp.float32))
        parts = turned_sum(quarters, 0, 1, False) + turned_sum(quarters, 2, 3, True)
        energy = jnp.concatenate(
            [parts[0] * parts[0] + parts[1] * parts[1], parts[2] * parts[2] + parts[3] * parts[3]], axis=1
        )
        top = energy.astype(jnp.bfloat16)
        rest = (energy - top.astype(jnp.float32)).astype(jnp.bfloat16)
        smooth = jnp.dot(top, band, preferred_element_type=jnp.float32) + jnp.dot(
            rest, band, preferred_element_type=jnp.float32
        )
        water = jnp.sum(energy, axis=1, keepdims=True) * (1.0 / F)
        scaling = lax.rsqrt(smooth * (1.0 / (2.0 * smooth_reach + 1.0)) + (0.1 * water + 1e-06)) * keep
        near, far = scaling[:, :H], scaling[:, H:]
        white = [parts[0] * near, parts[1] * near, parts[2] * far, parts[3] * far]
        at = pl.ds(pl.multiple_of(part * rows, rows), rows)
        for q in range(4):
            whitened_ref[at, q * H : (q + 1) * H] = white[q].astype(jnp.bfloat16)
        return carry

    lax.fori_loop(0, row_parts, whiten, 0)


def select_kernel(where_ref, whitened_ref, owners_ref, places_ref, outgoing_ref, common_ref, selector):
    rows = selector.shape[1]
    ch_dev, shared = rows // 2, rows // 2 - common_ref.shape[1]
    for w in range(common_ref.shape[0]):
        common_ref[w] = whitened_ref[ch_dev * w + shared : ch_dev * (w + 1), :]

    @pl.when(pl.program_id(0) == 0)
    def _():
        selector[...] = slot_selector(owners_ref[...], places_ref[...], where_ref[0], rows // 2)

    count, slots, columns = outgoing_ref.shape
    for n in range(slots // (2 * CAP)):
        sent = jnp.dot(
            selector[...], whitened_ref[rows * n : rows * (n + 1), :], preferred_element_type=jnp.float32
        ).astype(jnp.bfloat16)
        outgoing_ref[:, 2 * CAP * n : 2 * CAP * (n + 1), :] = sent.reshape(count, 2 * CAP, columns)


def vmem_spec():
    return pl.BlockSpec(memory_space=pltpu.VMEM)


def smem_spec():
    return pl.BlockSpec(memory_space=pltpu.SMEM)


def whole(array):
    return pl.BlockSpec(array.shape, lambda s: (0,) * array.ndim)


def spectra_call(traces, quality):
    rows, length = traces.shape
    part, depth = rows // ROW_STEPS, length // QUARTERS
    anywhere = pl.BlockSpec(memory_space=pl.ANY)
    return pl.pallas_call(
        spectra_kernel,
        in_specs=[anywhere, anywhere, anywhere],
        out_specs=vmem_spec(),
        out_shape=jax.ShapeDtypeStruct((rows, 2 * F), jnp.bfloat16),
        scratch_shapes=[
            pltpu.VMEM((ROW_STEPS, QUARTERS, part, depth), jnp.bfloat16),
            pltpu.VMEM((depth, 2 * F), jnp.bfloat16),
            pltpu.VMEM(quality.shape, jnp.int32),
            pltpu.SemaphoreType.DMA((ROW_STEPS + 1, QUARTERS)),
        ],
        compiler_params=pltpu.CompilerParams(vmem_limit_bytes=SPECTRA_VMEM_LIMIT),
        cost_estimate=pl.CostEstimate(
            flops=2 * rows * length * 2 * F, bytes_accessed=2 * rows * length, transcendentals=rows * F
        ),
        name="spectra",
    )(traces, jnp.asarray(forward_table(length)), quality)


def select_call(where, whitened, owners, places, chan_count, ch_dev, own_count):
    rows, columns = whitened.shape
    block = rows // ROW_STEPS
    slots = block // (2 * ch_dev) * 2 * CAP
    return pl.pallas_call(
        select_kernel,
        grid=(ROW_STEPS,),
        in_specs=[smem_spec(), pl.BlockSpec((block, columns), lambda s: (s, 0)), whole(owners), whole(places)],
        out_specs=[
            pl.BlockSpec((chan_count, slots, columns), lambda s: (0, s, 0)),
            pl.BlockSpec((block // ch_dev, own_count, columns), lambda s: (s, 0, 0)),
        ],
        out_shape=[
            jax.ShapeDtypeStruct((chan_count, ROW_STEPS * slots, columns), jnp.bfloat16),
            jax.ShapeDtypeStruct((rows // ch_dev, own_count, columns), jnp.bfloat16),
        ],
        scratch_shapes=[pltpu.VMEM((chan_count * 2 * CAP, 2 * ch_dev), jnp.bfloat16)],
        compiler_params=pltpu.CompilerParams(vmem_limit_bytes=SPECTRA_VMEM_LIMIT),
        cost_estimate=pl.CostEstimate(
            flops=4 * rows * chan_count * 2 * CAP * columns, bytes_accessed=2 * rows * columns * 3, transcendentals=0
        ),
        name="select",
    )(where, whitened, owners, places)


def cross_kernel(last, with_sum, local_windows, where_ref, first_ref, second_ref, *refs):
    refs = list(refs)
    sum_ref = refs.pop(0) if with_sum else None
    if last:
        table_ref, out_ref, done_ref, wide, spread, staged, lags, total, sems = refs
        done_ref[...] = jnp.zeros_like(done_ref)
    else:
        total, wide, spread, staged = refs
    windows, own_count = spread.shape[:2]
    ch_dev = wide.shape[1] // 2
    base = pl.multiple_of(where_ref[1] * own_count, 8)

    def widen(w, carry):
        if local_windows:
            wide[w, :ch_dev, :] = first_ref[w]
            wide[w, ch_dev:, :] = second_ref[w]
        else:
            shared = ch_dev - own_count
            if own_count % 16 == 0:
                height, rows, place = 16, wide.at[w], second_ref.at[w]
                wide[w, shared:ch_dev, :] = first_ref[w]
            else:
                height, rows, place = 8, staged, second_ref[w].astype(jnp.float32)
                staged[shared:ch_dev, :] = first_ref[w].astype(jnp.float32)
            for tile in range(ch_dev // height):
                at = base + height * tile
                at = pl.multiple_of(jnp.where(at < shared, at, at + own_count), height)
                rows[pl.ds(at, height), :] = place[height * tile : height * (tile + 1), :]
            if own_count % 16:
                wide[w] = staged[...].astype(jnp.bfloat16)
        for eight in range(own_count // 8):
            at = base + 8 * eight
            rows = wide[w, pl.ds(pl.multiple_of(at // 16 * 16, 16), 16), :].astype(jnp.float32)
            rows = jnp.where(at % 16 == 0, rows[:8], rows[8:])
            for i in range(8):
                for q in range(4):
                    row = jnp.broadcast_to(rows[i : i + 1, q * H : (q + 1) * H], (16, H))
                    spread[w, 8 * eight + i, q] = row.astype(jnp.bfloat16)
        return carry

    lax.fori_loop(0, windows, widen, 0)

    group = 4
    rounds = SPAN // 16

    def block(index, carry):
        g = index // rounds
        j = index % rounds
        start = pl.multiple_of((base + group * g) // 16 * 16 + 16 * j, 16)

        def add_windows(part, sums):
            short = [None] * (3 * group)
            for n in range(FLUSH):
                w = part * FLUSH + n
                r = [wide[w, pl.ds(start, 16), q * H : (q + 1) * H] for q in range(4)]
                for i in range(group):
                    l = [spread[w, group * g + i, q] for q in range(4)]
                    terms = (
                        l[0] * r[0] + l[1] * r[1],
                        l[2] * r[2] + l[3] * r[3],
                        (l[1] * r[0] - l[0] * r[1]) + (l[2] * r[3] - l[3] * r[2]),
                    )
                    for k in range(3):
                        at = 3 * i + k
                        short[at] = terms[k] if n == 0 else short[at] + terms[k]
            return tuple(total + term.astype(jnp.float32) for total, term in zip(sums, short))

        zero = jnp.zeros((16, H), jnp.float32)
        sums = lax.fori_loop(0, windows // FLUSH, add_windows, (zero,) * (3 * group))
        for i in range(group):
            real, imag = fold_columns(*sums[3 * i : 3 * i + 3])
            where = pl.ds(pl.multiple_of(16 * j, 16), 16)
            if with_sum:
                real = real + sum_ref[group * g + i, where, :H]
                imag = imag + sum_ref[group * g + i, where, H:]
            total[group * g + i, where, :H] = real
            total[group * g + i, where, H:] = imag
        return carry

    lax.fori_loop(0, own_count // group * rounds, block, 0)

    if last:
        copies = []
        height = REACH + 8
        for eight in range(own_count // 8):
            first = 8 * eight
            skip = pl.multiple_of((base + first) % 16, 8)
            stacks = total[first : first + 8, pl.ds(skip, height), :].reshape(8 * height, F)
            lagged = jnp.dot(stacks.astype(jnp.bfloat16), table_ref[...], preferred_element_type=jnp.float32)
            lagged = lagged.reshape(8, height, NLAG)
            for i in range(8):
                lags[first + i] = lagged[i, i + 1 : i + 1 + REACH, :]
            some = pl.ds(first, 8)
            copies.append(pltpu.make_async_copy(lags.at[some], out_ref.at[some], sems.at[eight]))
            copies[-1].start()
        for copy in copies:
            copy.wait()


def cross_call(where, first, second, ch_dev, own_count, sums, table, local_windows):
    windows, _, columns = first.shape
    last = table is not None
    with_sum = sums is not None
    operands = [where, first, second]
    if with_sum:
        operands.append(sums)
    scratch = [
        pltpu.VMEM((windows, 2 * ch_dev, columns), jnp.bfloat16),
        pltpu.VMEM((windows, own_count, 4, 16, H), jnp.bfloat16),
        pltpu.VMEM((2 * ch_dev, columns), jnp.float32),
    ]
    sums_shape = (own_count, SPAN, F)
    if last:
        operands.append(table)
        lags_shape = (own_count, REACH, NLAG)
        scratch += [
            pltpu.VMEM(lags_shape, jnp.float32),
            pltpu.VMEM(sums_shape, jnp.float32),
            pltpu.SemaphoreType.DMA((own_count // 8,)),
        ]
        out_shape = [jax.ShapeDtypeStruct(lags_shape, jnp.float32), jax.ShapeDtypeStruct((8, H), jnp.float32)]
        out_specs = [pl.BlockSpec(memory_space=pl.ANY), vmem_spec()]
    else:
        out_shape = [jax.ShapeDtypeStruct(sums_shape, jnp.float32)]
        out_specs = [vmem_spec()]
    return pl.pallas_call(
        functools.partial(cross_kernel, last, with_sum, local_windows),
        in_specs=[smem_spec()] + [vmem_spec()] * (len(operands) - 1),
        out_specs=out_specs,
        out_shape=out_shape,
        scratch_shapes=scratch,
        compiler_params=pltpu.CompilerParams(vmem_limit_bytes=VMEM_LIMIT),
        cost_estimate=pl.CostEstimate(
            flops=30_000_000_000, bytes_accessed=4 * windows * ch_dev * columns + 4 * own_count * SPAN * F, transcendentals=0
        ),
        name="cross",
    )(*operands)


def fold_kernel(where_ref, incoming_ref, own_ref, owners_ref, high_ref, low_ref, earlier_ref, out_ref, sums, picker):
    step = pl.program_id(0)
    rows = own_ref.shape[0]
    ch_dev = rows // 2

    @pl.when(step == 0)
    def _():
        sums[...] = jnp.zeros_like(sums)
        owners = owners_ref[...].astype(jnp.float32)
        per_row = owners.shape[1] // ch_dev
        device = where_ref[0]
        line = jnp.sum(jnp.where(rows_of(owners.shape) == device // per_row, owners, 0.0), axis=0, keepdims=True)
        shape = (rows, owners.shape[1])
        line = jnp.broadcast_to(line, shape)
        first = device % per_row * ch_dev
        place = first + rows_of(shape) % ch_dev
        lane = lanes_of(shape)
        owner = jnp.sum(jnp.where(lane == place, line, 0.0), axis=1, keepdims=True)
        earlier = (lane >= first) & (lane < place) & (line == owner)
        rank = jnp.sum(earlier.astype(jnp.float32), axis=1, keepdims=True)
        source = (2 * CAP * owner + rank).astype(jnp.int32)
        shape = picker.shape
        target = source + CAP * (rows_of(shape) // ch_dev)
        picker[...] = (lanes_of(shape) == target).astype(jnp.float32).astype(jnp.bfloat16)

    count, slots, columns = incoming_ref.shape
    right = jnp.dot(
        picker[...], incoming_ref[...].reshape(count * slots, columns), preferred_element_type=jnp.float32
    )
    left = own_ref[...].astype(jnp.float32)
    l = [left[:, q * H : (q + 1) * H] for q in range(4)]
    r = [right[:, q * H : (q + 1) * H] for q in range(4)]
    first = l[0] * r[0] + l[1] * r[1]
    second = l[2] * r[2] + l[3] * r[3]
    imag = (l[1] * r[0] - l[0] * r[1]) + (l[2] * r[3] - l[3] * r[2])
    for n, term in enumerate((first, second, imag)):
        sums[n] += term[:ch_dev] + term[ch_dev:]

    @pl.when(step == pl.num_programs(0) - 1)
    def _():
        stacks = jnp.concatenate(fold_columns(sums[0], sums[1], sums[2]), axis=1)
        out_ref[...] = lag_transform(stacks, high_ref[...], low_ref[...])


def fold_call(where, incoming, own, owners, ch_dev, tables, earlier):
    count, slots, columns = incoming.shape
    rows = 2 * ch_dev
    pairs = own.shape[0] // rows
    return pl.pallas_call(
        fold_kernel,
        grid=(pairs,),
        in_specs=[
            smem_spec(),
            pl.BlockSpec((count, slots // pairs, columns), lambda s: (0, s, 0)),
            pl.BlockSpec((rows, columns), lambda s: (s, 0)),
            whole(owners),
            whole(tables[0]),
            whole(tables[1]),
            pl.BlockSpec(memory_space=pl.ANY),
        ],
        out_specs=pl.BlockSpec((ch_dev, NLAG), lambda s: (0, 0)),
        out_shape=jax.ShapeDtypeStruct((ch_dev, NLAG), jnp.float32),
        scratch_shapes=[
            pltpu.VMEM((3, ch_dev, H), jnp.float32),
            pltpu.VMEM((rows, count * slots // pairs), jnp.bfloat16),
        ],
        compiler_params=pltpu.CompilerParams(vmem_limit_bytes=FOLD_VMEM_LIMIT),
        cost_estimate=pl.CostEstimate(
            flops=2 * rows * pairs * count * 2 * CAP * columns,
            bytes_accessed=2 * (incoming.size + own.size),
            transcendentals=0,
        ),
        name="fold",
    )(where, incoming, own, owners, *tables, earlier)


def from_above(block):
    count = lax.axis_size("chan")
    return lax.ppermute(block, "chan", [(i, i - 1) for i in range(1, count)])


def round_win(block, shift):
    count = lax.axis_size("win")
    return lax.ppermute(block, "win", [(i, (i + shift) % count) for i in range(count)])


def local(traces, quality, fold_block, fold_offset):
    win_dev, ch_dev, length = traces.shape
    chan_count = lax.axis_size("chan")
    win_count = lax.axis_size("win")
    window_part = lax.axis_index("win")
    own_count = ch_dev // win_count
    shared = ch_dev - own_count
    where = jnp.stack([lax.axis_index("chan"), window_part]).astype(jnp.int32)
    tables = [jnp.asarray(t) for t in inverse_tables(1.0 / math.sqrt(F * win_dev * win_count))]
    owners = fold_block.reshape(-1, 2 * ch_dev)
    places = fold_offset.reshape(-1, 2 * ch_dev)
    flat = spectra_call(traces.reshape(win_dev * ch_dev, length), quality.reshape(1, ch_dev))
    whitened = flat.reshape(win_dev, ch_dev, 2 * F)
    upper = from_above(whitened)
    outgoing, shared_rows = select_call(where, flat, owners, places, chan_count, ch_dev, own_count)
    common = [round_win(shared_rows, shift) for shift in range(1, win_count)]
    incoming = lax.all_to_all(outgoing, "chan", split_axis=0, concat_axis=0, tiled=True)
    offered = jnp.concatenate([whitened[:, :shared], upper], axis=1)
    special = [
        round_win(
            lax.dynamic_slice_in_dim(offered, (window_part + shift) % win_count * own_count, ch_dev, 1), shift
        )
        for shift in range(1, win_count)
    ]
    arrived = [(whitened, upper)] + list(zip(common, special))
    sums = None
    for n, (first, second) in enumerate(arrived):
        ends = tables[0] if n == win_count - 1 else None
        sums, *done = cross_call(where, first, second, ch_dev, own_count, sums, ends, n == 0)
    share = fold_call(where, incoming, flat, owners, ch_dev, tables, done[0])
    fold = lax.dynamic_slice_in_dim(share, window_part * own_count, own_count, 0)
    for shift in range(1, win_count):
        target = (window_part + shift) % win_count * own_count
        fold = fold + round_win(lax.dynamic_slice_in_dim(share, target, own_count, 0), shift)
    return (sums, fold)


def solution(mesh):
    in_specs = (P("win", "chan", None), P("chan"), P(), P())
    out_specs = (P(("chan", "win"), None, None), P(("chan", "win"), None))
    return jax.shard_map(local, mesh=mesh, in_specs=in_specs, out_specs=out_specs, check_vma=False)
```

```python
import functools
import math

import jax
import jax.numpy as jnp
import numpy as np
from jax import lax
from jax.experimental import pallas as pl
from jax.experimental.pallas import tpu as pltpu
from jax.sharding import PartitionSpec as P

F = 256
H = F // 2
BAND_LO = 32
NLAG = 256
REACH = 64
CAP = 8
SPAN = REACH + 8
smooth_reach = 4
ROW_STEPS = 3
QUARTERS = 4
VMEM_LIMIT = 24 * 1024 * 1024
FOLD_VMEM_LIMIT = 16 * 1024 * 1024
SPECTRA_VMEM_LIMIT = 59 * 1024 * 1024


def bin_order():
    residues = np.arange(H)
    first = (residues - BAND_LO) % F
    second = (-residues - BAND_LO) % F
    second[0] = (H - BAND_LO) % F
    return first, second


def forward_table(length):
    samples = np.arange(length // 4, dtype=np.int64)[:, None]
    parts = []
    for bins in bin_order():
        angles = (samples * (bins + BAND_LO)[None, :] % length) * (2.0 * math.pi / length)
        parts += [np.cos(angles), -np.sin(angles)]
    return np.concatenate(parts, axis=1).astype(np.float32).astype(jnp.bfloat16)


def inverse_tables(factor):
    shifts = (np.arange(NLAG) + NLAG // 2)[None, :]
    residues = np.arange(H)[:, None]
    angles = (residues * shifts % NLAG) * (2.0 * math.pi / NLAG)
    sign = np.where(shifts[0] % 2 == 0, 1.0, -1.0)
    real, imag = np.cos(angles), -np.sin(angles)
    real[0] = (1.0 + sign) / 2.0
    imag[0] = (1.0 - sign) / 2.0
    table = np.concatenate([real, imag], axis=0) * factor
    high = table.astype(np.float32).astype(jnp.bfloat16)
    low = (table - high.astype(np.float64)).astype(np.float32).astype(jnp.bfloat16)
    return high, low


def lag_transform(stacks, high, low):
    top = stacks.astype(jnp.bfloat16)
    rest = (stacks - top.astype(jnp.float32)).astype(jnp.bfloat16)
    dot = functools.partial(jnp.dot, preferred_element_type=jnp.float32)
    return dot(top, high) + (dot(rest, high) + dot(top, low))


def fold_columns(first, second, imag):
    lane = lax.broadcasted_iota(jnp.int32, first.shape, first.ndim - 1)
    return first + second, jnp.where(lane == 0, first - second, imag)


def lanes_of(shape):
    return lax.broadcasted_iota(jnp.int32, shape, len(shape) - 1)


def rows_of(shape):
    return lax.broadcasted_iota(jnp.int32, shape, len(shape) - 2)


def band_matrix():
    def bins(index):
        lane = index & (H - 1)
        residue = jnp.where(index < H, lane, jnp.where(lane == 0, H, F - lane))
        return (residue - BAND_LO + F) & (F - 1)

    apart = bins(rows_of((F, F))) - bins(lanes_of((F, F)))
    return (jnp.abs(apart) <= smooth_reach).astype(jnp.float32).astype(jnp.bfloat16)


def exact_dot(left, right):
    return jnp.dot(left.astype(jnp.bfloat16), right.astype(jnp.bfloat16), preferred_element_type=jnp.float32)


def slot_selector(owners, places, device, ch_dev):
    height, width = owners.shape
    per_row = width // ch_dev
    wanted = (owners == device).astype(jnp.float32)
    before = rows_of((width, width))
    after = lanes_of((width, width))
    earlier = ((before < after) & (before // ch_dev == after // ch_dev)).astype(jnp.float32)
    ranks = exact_dot(wanted, earlier)
    slots = jnp.where(wanted > 0, ranks, float(CAP))
    count = height * per_row * 2 * CAP
    to_row = (rows_of((count, height)) // (2 * CAP * per_row) == lanes_of((count, height))).astype(jnp.float32)
    row_slots = exact_dot(to_row, slots)
    row_places = exact_dot(to_row, places.astype(jnp.float32))
    shape = (count, width)
    row = rows_of(shape)
    mine = (row_slots == (row % CAP).astype(jnp.float32)) & (lanes_of(shape) // ch_dev == row // (2 * CAP) % per_row)
    place = jnp.sum(jnp.where(mine, row_places + 1.0, 0.0), axis=1, keepdims=True).astype(jnp.int32) - 1
    shape = (count, 2 * ch_dev)
    half = rows_of(shape) // CAP % 2
    lane = lanes_of(shape)
    return ((lane == place + ch_dev * half) & (place >= 0)).astype(jnp.float32).astype(jnp.bfloat16)


def turned_sum(quarters, real, imag, negative):
    rows = quarters[0].shape[0]
    lane = lanes_of((rows, H))
    residue = ((F - lane) if negative else lane) & 3
    sign = jnp.where((residue & 1) == 0, 1.0, -1.0)
    straight = jnp.where(residue == 0, 1.0, jnp.where(residue == 2, -1.0, 0.0))
    turned = jnp.where(residue == 1, 1.0, jnp.where(residue == 3, -1.0, 0.0))
    re = [quarter[:, real * H : (real + 1) * H] for quarter in quarters]
    im = [quarter[:, imag * H : (imag + 1) * H] for quarter in quarters]
    odd_re, odd_im = re[1] + sign * re[3], im[1] + sign * im[3]
    return (
        re[0] + sign * re[2] + (straight * odd_re + turned * odd_im),
        im[0] + sign * im[2] + (straight * odd_im - turned * odd_re),
    )


def spectra_kernel(chan_ref, traces_ref, table_ref, quality_ref, owners_ref, places_ref, *refs):
    whitened_ref, outgoing_ref, *shared_ref = refs[:-10]
    traces, table, quality, owners, places, white, sent, selector, sems, out_sems = refs[-10:]
    row_parts, chunks, rows, depth = traces.shape
    ch_dev = quality.shape[1]
    pair = 2 * ch_dev
    count = outgoing_ref.shape[0]
    slots = sent.shape[2]

    def traces_copy(part, k):
        source = traces_ref.at[pl.ds(part * rows, rows), pl.ds(k * depth, depth)]
        return pltpu.make_async_copy(source, traces.at[part, k], sems.at[part, k])

    small = [
        pltpu.make_async_copy(source, target, sems.at[row_parts, k])
        for k, (source, target) in enumerate(
            ((table_ref, table), (quality_ref, quality), (owners_ref, owners), (places_ref, places))
        )
    ]
    for copy in small:
        copy.start()
    for part in range(row_parts):
        for k in range(chunks):
            traces_copy(part, k).start()

    band = band_matrix()
    for copy in small[1:]:
        copy.wait()
    shape = (rows, ch_dev)
    keep = jnp.sum(
        jnp.where(rows_of(shape) % ch_dev == lanes_of(shape), quality[...].astype(jnp.float32), 0.0),
        axis=1, keepdims=True,
    )
    selector[...] = slot_selector(owners[...], places[...], chan_ref[0], ch_dev)
    small[0].wait()

    leaving = []
    for part in range(row_parts):
        quarters = []
        for k in range(chunks):
            traces_copy(part, k).wait()
            quarters.append(jnp.dot(traces[part, k], table[...], preferred_element_type=jnp.float32))
        parts = turned_sum(quarters, 0, 1, False) + turned_sum(quarters, 2, 3, True)
        energy = jnp.concatenate(
            [parts[0] * parts[0] + parts[1] * parts[1], parts[2] * parts[2] + parts[3] * parts[3]], axis=1
        )
        top = energy.astype(jnp.bfloat16)
        rest = (energy - top.astype(jnp.float32)).astype(jnp.bfloat16)
        smooth = jnp.dot(top, band, preferred_element_type=jnp.float32) + jnp.dot(
            rest, band, preferred_element_type=jnp.float32
        )
        water = jnp.sum(energy, axis=1, keepdims=True) * (1.0 / F)
        scaling = lax.rsqrt(smooth * (1.0 / (2.0 * smooth_reach + 1.0)) + (0.1 * water + 1e-06)) * keep
        near, far = scaling[:, :H], scaling[:, H:]
        for q, values in enumerate((parts[0] * near, parts[1] * near, parts[2] * far, parts[3] * far)):
            white[part, :, q * H : (q + 1) * H] = values.astype(jnp.bfloat16)
        leaving.append(
            pltpu.make_async_copy(
                white.at[part], whitened_ref.at[pl.ds(part * rows, rows), :], out_sems.at[part, 0]
            )
        )
        leaving[-1].start()
        if shared_ref:
            height = shared_ref[0].shape[1]
            for w in range(rows // ch_dev):
                leaving.append(
                    pltpu.make_async_copy(
                        white.at[part, pl.ds((w + 1) * ch_dev - height, height), :],
                        shared_ref[0].at[part * (rows // ch_dev) + w],
                        out_sems.at[part, 2 + w],
                    )
                )
                leaving[-1].start()
        for n in range(rows // pair):
            chosen = jnp.dot(
                selector[...], white[part, pair * n : pair * (n + 1), :], preferred_element_type=jnp.float32
            ).astype(jnp.bfloat16)
            sent[part, :, 2 * CAP * n : 2 * CAP * (n + 1), :] = chosen.reshape(count, 2 * CAP, chosen.shape[-1])
        leaving.append(
            pltpu.make_async_copy(
                sent.at[part], outgoing_ref.at[:, pl.ds(part * slots, slots), :], out_sems.at[part, 1]
            )
        )
        leaving[-1].start()
    for copy in leaving:
        copy.wait()


def vmem_spec():
    return pl.BlockSpec(memory_space=pltpu.VMEM)


def smem_spec():
    return pl.BlockSpec(memory_space=pltpu.SMEM)


def whole(array):
    return pl.BlockSpec(array.shape, lambda s: (0,) * array.ndim)


def spectra_call(chan, traces, quality, owners, places, chan_count, own_count):
    rows, length = traces.shape
    ch_dev = quality.shape[1]
    part, depth = rows // ROW_STEPS, length // QUARTERS
    slots = part // (2 * ch_dev) * 2 * CAP
    anywhere = pl.BlockSpec(memory_space=pl.ANY)
    out_shape = [
        jax.ShapeDtypeStruct((rows, 2 * F), jnp.bfloat16),
        jax.ShapeDtypeStruct((chan_count, ROW_STEPS * slots, 2 * F), jnp.bfloat16),
    ]
    if own_count % 16 == 0:
        out_shape.append(jax.ShapeDtypeStruct((rows // ch_dev, own_count, 2 * F), jnp.bfloat16))
    return pl.pallas_call(
        spectra_kernel,
        in_specs=[smem_spec()] + [anywhere] * 5,
        out_specs=[anywhere] * len(out_shape),
        out_shape=out_shape,
        scratch_shapes=[
            pltpu.VMEM((ROW_STEPS, QUARTERS, part, depth), jnp.bfloat16),
            pltpu.VMEM((depth, 2 * F), jnp.bfloat16),
            pltpu.VMEM(quality.shape, jnp.int32),
            pltpu.VMEM(owners.shape, jnp.int32),
            pltpu.VMEM(places.shape, jnp.int32),
            pltpu.VMEM((ROW_STEPS, part, 2 * F), jnp.bfloat16),
            pltpu.VMEM((ROW_STEPS, chan_count, slots, 2 * F), jnp.bfloat16),
            pltpu.VMEM((chan_count * 2 * CAP, 2 * ch_dev), jnp.bfloat16),
            pltpu.SemaphoreType.DMA((ROW_STEPS + 1, QUARTERS)),
            pltpu.SemaphoreType.DMA((ROW_STEPS, 2 + part // ch_dev)),
        ],
        compiler_params=pltpu.CompilerParams(vmem_limit_bytes=SPECTRA_VMEM_LIMIT),
        cost_estimate=pl.CostEstimate(
            flops=2 * rows * length * 2 * F, bytes_accessed=2 * rows * length, transcendentals=rows * F
        ),
        name="spectra",
    )(chan, traces, jnp.asarray(forward_table(length)), quality, owners, places)


def cross_kernel(last, with_sum, local_windows, win_ref, first_ref, second_ref, *refs):
    refs = list(refs)
    sum_ref = refs.pop(0) if with_sum else None
    if last:
        table_ref, out_ref, done_ref, wide, spread, total, lags, sems = refs
        done_ref[...] = jnp.zeros_like(done_ref)
    else:
        out_ref, wide, spread = refs
        total = out_ref
    windows, own_count = spread.shape[:2]
    ch_dev = wide.shape[1] // 2
    base = pl.multiple_of(win_ref[0] * own_count, 8)

    def widen(w, carry):
        if local_windows:
            wide[w, :ch_dev, :] = first_ref[w].astype(jnp.float32)
            wide[w, ch_dev:, :] = second_ref[w].astype(jnp.float32)
        else:
            shared = ch_dev - own_count
            wide[w, shared:ch_dev, :] = first_ref[w].astype(jnp.float32)
            rows = second_ref[w].astype(jnp.float32)
            for tile in range(ch_dev // 8):
                at = base + 8 * tile
                at = pl.multiple_of(jnp.where(at < shared, at, at + own_count), 8)
                wide[w, pl.ds(at, 8), :] = rows[8 * tile : 8 * tile + 8]
        for tile in range(own_count // 8):
            rows = wide[w, pl.ds(pl.multiple_of(base + 8 * tile, 8), 8), :]
            for i in range(8):
                for q in range(4):
                    spread[w, 8 * tile + i, q] = jnp.broadcast_to(rows[i : i + 1, q * H : (q + 1) * H], (8, H))
        return carry

    lax.fori_loop(0, windows, widen, 0)

    group, tiles = 4, 3
    rounds = SPAN // (8 * tiles)

    def block(index, carry):
        g = index // rounds
        j = index % rounds
        start = pl.multiple_of(base + 8 * (g // 2) + 8 * tiles * j, 8)

        def add_window(w, sums):
            sums = list(sums)
            right = [
                [wide[w, pl.ds(pl.multiple_of(start + 8 * t, 8), 8), q * H : (q + 1) * H] for q in range(4)]
                for t in range(tiles)
            ]
            for i in range(group):
                left = [spread[w, group * g + i, q] for q in range(4)]
                for t in range(tiles):
                    at = 3 * (i * tiles + t)
                    r = right[t]
                    sums[at] = sums[at] + (left[0] * r[0] + left[1] * r[1])
                    sums[at + 1] = sums[at + 1] + (left[2] * r[2] + left[3] * r[3])
                    sums[at + 2] = sums[at + 2] + ((left[1] * r[0] - left[0] * r[1]) + (left[2] * r[3] - left[3] * r[2]))
            return tuple(sums)

        zero = jnp.zeros((8, H), jnp.float32)
        sums = lax.fori_loop(0, windows, add_window, (zero,) * (3 * group * tiles), unroll=2)
        for i in range(group):
            for t in range(tiles):
                at = 3 * (i * tiles + t)
                real, imag = fold_columns(sums[at], sums[at + 1], sums[at + 2])
                where = pl.ds(pl.multiple_of(8 * tiles * j + 8 * t, 8), 8)
                if with_sum:
                    real = real + sum_ref[group * g + i, where, :H]
                    imag = imag + sum_ref[group * g + i, where, H:]
                total[group * g + i, where, :H] = real
                total[group * g + i, where, H:] = imag
        return carry

    lax.fori_loop(0, own_count // group * rounds, block, 0)

    if last:
        copies = []
        for eight in range(own_count // 8):
            first = 8 * eight
            stacks = total[first : first + 8].reshape(8 * SPAN, F).astype(jnp.bfloat16)
            lagged = jnp.dot(stacks, table_ref[...], preferred_element_type=jnp.float32).reshape(8, SPAN, NLAG)
            for i in range(8):
                lags[first + i] = lagged[i, i + 1 : i + 1 + REACH, :]
            some = pl.ds(first, 8)
            copies.append(pltpu.make_async_copy(lags.at[some], out_ref.at[some], sems.at[eight]))
            copies[-1].start()
        for copy in copies:
            copy.wait()


def cross_call(win, first, second, ch_dev, own_count, sums, table, local_windows):
    windows, _, columns = first.shape
    last = table is not None
    with_sum = sums is not None
    operands = [win, first, second]
    if with_sum:
        operands.append(sums)
    scratch = [
        pltpu.VMEM((windows, 2 * ch_dev, columns), jnp.float32),
        pltpu.VMEM((windows, own_count, 4, 8, H), jnp.float32),
    ]
    if last:
        operands.append(table)
        scratch += [
            pltpu.VMEM((own_count, SPAN, F), jnp.float32),
            pltpu.VMEM((own_count, REACH, NLAG), jnp.float32),
            pltpu.SemaphoreType.DMA((own_count // 8,)),
        ]
    shape = (own_count, REACH, NLAG) if last else (own_count, SPAN, F)
    out_shape, out_specs = [jax.ShapeDtypeStruct(shape, jnp.float32)], [vmem_spec()]
    if last:
        out_shape.append(jax.ShapeDtypeStruct((8, H), jnp.float32))
        out_specs = [pl.BlockSpec(memory_space=pl.ANY), vmem_spec()]
    return pl.pallas_call(
        functools.partial(cross_kernel, last, with_sum, local_windows),
        in_specs=[smem_spec()] + [vmem_spec()] * (len(operands) - 1),
        out_specs=out_specs,
        out_shape=out_shape,
        scratch_shapes=scratch,
        compiler_params=pltpu.CompilerParams(vmem_limit_bytes=VMEM_LIMIT),
        cost_estimate=pl.CostEstimate(
            flops=30_000_000_000, bytes_accessed=4 * windows * ch_dev * columns + 4 * own_count * SPAN * F, transcendentals=0
        ),
        name="cross",
    )(*operands)


def fold_kernel(chan_ref, incoming_ref, own_ref, owners_ref, high_ref, low_ref, earlier_ref, out_ref):
    ch_dev = out_ref.shape[0]
    rows = 2 * ch_dev
    pairs = own_ref.shape[0] // rows
    count, slots, columns = incoming_ref.shape
    owners = owners_ref[...].astype(jnp.float32)
    per_row = owners.shape[1] // ch_dev
    device = chan_ref[0]
    line = jnp.sum(jnp.where(rows_of(owners.shape) == device // per_row, owners, 0.0), axis=0, keepdims=True)
    shape = (rows, owners.shape[1])
    line = jnp.broadcast_to(line, shape)
    first = device % per_row * ch_dev
    place = first + rows_of(shape) % ch_dev
    lane = lanes_of(shape)
    owner = jnp.sum(jnp.where(lane == place, line, 0.0), axis=1, keepdims=True)
    earlier = (lane >= first) & (lane < place) & (line == owner)
    rank = jnp.sum(earlier.astype(jnp.float32), axis=1, keepdims=True)
    source = (2 * CAP * owner + rank).astype(jnp.int32)
    shape = (rows, count * 2 * CAP)
    target = source + CAP * (rows_of(shape) // ch_dev)
    picker = (lanes_of(shape) == target).astype(jnp.float32).astype(jnp.bfloat16)
    sums = None
    for n in range(pairs):
        arrived = incoming_ref[:, 2 * CAP * n : 2 * CAP * (n + 1), :].reshape(count * 2 * CAP, columns)
        right = jnp.dot(picker, arrived, preferred_element_type=jnp.float32)
        left = own_ref[rows * n : rows * (n + 1), :].astype(jnp.float32)
        l = [left[:, q * H : (q + 1) * H] for q in range(4)]
        r = [right[:, q * H : (q + 1) * H] for q in range(4)]
        terms = [
            l[0] * r[0] + l[1] * r[1],
            l[2] * r[2] + l[3] * r[3],
            (l[1] * r[0] - l[0] * r[1]) + (l[2] * r[3] - l[3] * r[2]),
        ]
        sums = terms if sums is None else [total + term for total, term in zip(sums, terms)]
    stacks = jnp.concatenate(fold_columns(*[total[:ch_dev] + total[ch_dev:] for total in sums]), axis=1)
    out_ref[...] = lag_transform(stacks, high_ref[...], low_ref[...])


def fold_call(chan, incoming, own, owners, ch_dev, tables, earlier):
    return pl.pallas_call(
        fold_kernel,
        in_specs=[smem_spec()] + [vmem_spec()] * 5 + [pl.BlockSpec(memory_space=pl.ANY)],
        out_specs=vmem_spec(),
        out_shape=jax.ShapeDtypeStruct((ch_dev, NLAG), jnp.float32),
        compiler_params=pltpu.CompilerParams(vmem_limit_bytes=FOLD_VMEM_LIMIT),
        cost_estimate=pl.CostEstimate(
            flops=4 * ch_dev * incoming.size, bytes_accessed=2 * (incoming.size + own.size), transcendentals=0
        ),
        name="fold",
    )(chan, incoming, own, owners, *tables, earlier)


def from_above(block):
    count = lax.axis_size("chan")
    return lax.ppermute(block, "chan", [(i, i - 1) for i in range(1, count)])


def round_win(block, shift):
    count = lax.axis_size("win")
    return lax.ppermute(block, "win", [(i, (i + shift) % count) for i in range(count)])


def local(traces, quality, fold_block, fold_offset):
    win_dev, ch_dev, length = traces.shape
    chan_count = lax.axis_size("chan")
    win_count = lax.axis_size("win")
    window_part = lax.axis_index("win")
    own_count = ch_dev // win_count
    shared = ch_dev - own_count
    chan = lax.axis_index("chan").astype(jnp.int32).reshape(1)
    win = window_part.astype(jnp.int32).reshape(1)
    tables = [jnp.asarray(t) for t in inverse_tables(1.0 / math.sqrt(F * win_dev * win_count))]
    owners = fold_block.reshape(-1, 2 * ch_dev)
    places = fold_offset.reshape(-1, 2 * ch_dev)
    flat, outgoing, *ready = spectra_call(
        chan, traces.reshape(win_dev * ch_dev, length), quality.reshape(1, ch_dev), owners, places, chan_count, own_count
    )
    whitened = flat.reshape(win_dev, ch_dev, 2 * F)
    upper = from_above(whitened)
    ready = ready[0] if ready else whitened[:, shared:]
    common = [round_win(ready, shift) for shift in range(1, win_count)]
    incoming = lax.all_to_all(outgoing, "chan", split_axis=0, concat_axis=0, tiled=True)
    offered = jnp.concatenate([whitened[:, :shared], upper], axis=1)
    special = [
        round_win(
            lax.dynamic_slice_in_dim(offered, (window_part + shift) % win_count * own_count, ch_dev, 1), shift
        )
        for shift in range(1, win_count)
    ]
    arrived = [(whitened, upper)] + list(zip(common, special))
    sums = None
    for n, (first, second) in enumerate(arrived):
        ends = tables[0] if n == win_count - 1 else None
        sums, *done = cross_call(win, first, second, ch_dev, own_count, sums, ends, n == 0)
    share = fold_call(chan, incoming, flat, owners, ch_dev, tables, done[0])
    fold = lax.dynamic_slice_in_dim(share, window_part * own_count, own_count, 0)
    for shift in range(1, win_count):
        target = (window_part + shift) % win_count * own_count
        fold = fold + round_win(lax.dynamic_slice_in_dim(share, target, own_count, 0), shift)
    return (sums, fold)


def solution(mesh):
    in_specs = (P("win", "chan", None), P("chan"), P(), P())
    out_specs = (P(("chan", "win"), None, None), P(("chan", "win"), None))
    return jax.shard_map(local, mesh=mesh, in_specs=in_specs, out_specs=out_specs, check_vma=False)
```

```python
import functools
import math

import jax
import jax.numpy as jnp
import numpy as np
from jax import lax
from jax.experimental import pallas as pl
from jax.experimental.pallas import tpu as pltpu
from jax.sharding import PartitionSpec as P

F = 256
H = F // 2
BAND_LO = 32
NLAG = 256
REACH = 64
CAP = 8
SPAN = REACH + 8
smooth_reach = 4
ROW_STEPS = 3
QUARTERS = 4
VMEM_LIMIT = 24 * 1024 * 1024
FOLD_VMEM_LIMIT = 16 * 1024 * 1024
SPECTRA_VMEM_LIMIT = 59 * 1024 * 1024


def bin_order():
    residues = np.arange(H)
    first = (residues - BAND_LO) % F
    second = (-residues - BAND_LO) % F
    second[0] = (H - BAND_LO) % F
    return first, second


def forward_table(length):
    samples = np.arange(length // 4, dtype=np.int64)[:, None]
    parts = []
    for bins in bin_order():
        angles = (samples * (bins + BAND_LO)[None, :] % length) * (2.0 * math.pi / length)
        parts += [np.cos(angles), -np.sin(angles)]
    return np.concatenate(parts, axis=1).astype(np.float32).astype(jnp.bfloat16)


def inverse_tables(factor):
    shifts = (np.arange(NLAG) + NLAG // 2)[None, :]
    residues = np.arange(H)[:, None]
    angles = (residues * shifts % NLAG) * (2.0 * math.pi / NLAG)
    sign = np.where(shifts[0] % 2 == 0, 1.0, -1.0)
    real, imag = np.cos(angles), -np.sin(angles)
    real[0] = (1.0 + sign) / 2.0
    imag[0] = (1.0 - sign) / 2.0
    table = np.concatenate([real, imag], axis=0) * factor
    high = table.astype(np.float32).astype(jnp.bfloat16)
    low = (table - high.astype(np.float64)).astype(np.float32).astype(jnp.bfloat16)
    return high, low


def lag_transform(stacks, high, low):
    top = stacks.astype(jnp.bfloat16)
    rest = (stacks - top.astype(jnp.float32)).astype(jnp.bfloat16)
    dot = functools.partial(jnp.dot, preferred_element_type=jnp.float32)
    return dot(top, high) + (dot(rest, high) + dot(top, low))


def fold_columns(first, second, imag):
    lane = lax.broadcasted_iota(jnp.int32, first.shape, first.ndim - 1)
    return first + second, jnp.where(lane == 0, first - second, imag)


def lanes_of(shape):
    return lax.broadcasted_iota(jnp.int32, shape, len(shape) - 1)


def rows_of(shape):
    return lax.broadcasted_iota(jnp.int32, shape, len(shape) - 2)


def band_matrix():
    def bins(index):
        lane = index & (H - 1)
        residue = jnp.where(index < H, lane, jnp.where(lane == 0, H, F - lane))
        return (residue - BAND_LO + F) & (F - 1)

    apart = bins(rows_of((F, F))) - bins(lanes_of((F, F)))
    return (jnp.abs(apart) <= smooth_reach).astype(jnp.float32).astype(jnp.bfloat16)


def exact_dot(left, right):
    return jnp.dot(left.astype(jnp.bfloat16), right.astype(jnp.bfloat16), preferred_element_type=jnp.float32)


def slot_selector(owners, places, device, ch_dev):
    height, width = owners.shape
    per_row = width // ch_dev
    wanted = (owners == device).astype(jnp.float32)
    before = rows_of((width, width))
    after = lanes_of((width, width))
    earlier = ((before < after) & (before // ch_dev == after // ch_dev)).astype(jnp.float32)
    ranks = exact_dot(wanted, earlier)
    slots = jnp.where(wanted > 0, ranks, float(CAP))
    count = height * per_row * 2 * CAP
    to_row = (rows_of((count, height)) // (2 * CAP * per_row) == lanes_of((count, height))).astype(jnp.float32)
    row_slots = exact_dot(to_row, slots)
    row_places = exact_dot(to_row, places.astype(jnp.float32))
    shape = (count, width)
    row = rows_of(shape)
    mine = (row_slots == (row % CAP).astype(jnp.float32)) & (lanes_of(shape) // ch_dev == row // (2 * CAP) % per_row)
    place = jnp.sum(jnp.where(mine, row_places + 1.0, 0.0), axis=1, keepdims=True).astype(jnp.int32) - 1
    shape = (count, 2 * ch_dev)
    half = rows_of(shape) // CAP % 2
    lane = lanes_of(shape)
    return ((lane == place + ch_dev * half) & (place >= 0)).astype(jnp.float32).astype(jnp.bfloat16)


def turned_sum(quarters, real, imag, negative):
    rows = quarters[0].shape[0]
    lane = lanes_of((rows, H))
    residue = ((F - lane) if negative else lane) & 3
    sign = jnp.where((residue & 1) == 0, 1.0, -1.0)
    straight = jnp.where(residue == 0, 1.0, jnp.where(residue == 2, -1.0, 0.0))
    turned = jnp.where(residue == 1, 1.0, jnp.where(residue == 3, -1.0, 0.0))
    re = [quarter[:, real * H : (real + 1) * H] for quarter in quarters]
    im = [quarter[:, imag * H : (imag + 1) * H] for quarter in quarters]
    odd_re, odd_im = re[1] + sign * re[3], im[1] + sign * im[3]
    return (
        re[0] + sign * re[2] + (straight * odd_re + turned * odd_im),
        im[0] + sign * im[2] + (straight * odd_im - turned * odd_re),
    )


def spectra_kernel(chan_ref, traces_ref, table_ref, quality_ref, owners_ref, places_ref, *refs):
    whitened_ref, outgoing_ref, near_ref, far_ref, *shared_ref = refs[:-10]
    traces, table, quality, owners, places, white, sent, selector, sems, out_sems = refs[-10:]
    row_parts, chunks, rows, depth = traces.shape
    ch_dev = quality.shape[1]
    pair = 2 * ch_dev
    count = outgoing_ref.shape[0]
    slots = sent.shape[2]

    def traces_copy(part, k):
        source = traces_ref.at[pl.ds(part * rows, rows), pl.ds(k * depth, depth)]
        return pltpu.make_async_copy(source, traces.at[part, k], sems.at[part, k])

    small = [
        pltpu.make_async_copy(source, target, sems.at[row_parts, k])
        for k, (source, target) in enumerate(
            ((table_ref, table), (quality_ref, quality), (owners_ref, owners), (places_ref, places))
        )
    ]
    for copy in small:
        copy.start()
    for part in range(row_parts):
        for k in range(chunks):
            traces_copy(part, k).start()

    band = band_matrix()
    for copy in small[1:]:
        copy.wait()
    shape = (rows, ch_dev)
    keep = jnp.sum(
        jnp.where(rows_of(shape) % ch_dev == lanes_of(shape), quality[...].astype(jnp.float32), 0.0),
        axis=1, keepdims=True,
    )
    selector[...] = slot_selector(owners[...], places[...], chan_ref[0], ch_dev)
    small[0].wait()

    leaving = []
    for part in range(row_parts):
        quarters = []
        for k in range(chunks):
            traces_copy(part, k).wait()
            quarters.append(jnp.dot(traces[part, k], table[...], preferred_element_type=jnp.float32))
        parts = turned_sum(quarters, 0, 1, False) + turned_sum(quarters, 2, 3, True)
        energy = jnp.concatenate(
            [parts[0] * parts[0] + parts[1] * parts[1], parts[2] * parts[2] + parts[3] * parts[3]], axis=1
        )
        top = energy.astype(jnp.bfloat16)
        rest = (energy - top.astype(jnp.float32)).astype(jnp.bfloat16)
        smooth = jnp.dot(top, band, preferred_element_type=jnp.float32) + jnp.dot(
            rest, band, preferred_element_type=jnp.float32
        )
        water = jnp.sum(energy, axis=1, keepdims=True) * (1.0 / F)
        scaling = lax.rsqrt(smooth * (1.0 / (2.0 * smooth_reach + 1.0)) + (0.1 * water + 1e-06)) * keep
        near, far = scaling[:, :H], scaling[:, H:]
        for q, values in enumerate((parts[0] * near, parts[1] * near, parts[2] * far, parts[3] * far)):
            white[part, :, q * H : (q + 1) * H] = values.astype(jnp.bfloat16)
        leaving.append(
            pltpu.make_async_copy(
                white.at[part], whitened_ref.at[pl.ds(part * rows, rows), :], out_sems.at[part, 0]
            )
        )
        leaving[-1].start()
        for half, target in enumerate((near_ref, far_ref)):
            leaving.append(
                pltpu.make_async_copy(
                    white.at[part, :, pl.ds(half * F, F)],
                    target.at[pl.ds(part * rows, rows), :],
                    out_sems.at[part, 2 + half],
                )
            )
            leaving[-1].start()
        if shared_ref:
            height = shared_ref[0].shape[1]
            for w in range(rows // ch_dev):
                leaving.append(
                    pltpu.make_async_copy(
                        white.at[part, pl.ds((w + 1) * ch_dev - height, height), :],
                        shared_ref[0].at[part * (rows // ch_dev) + w],
                        out_sems.at[part, 4 + w],
                    )
                )
                leaving[-1].start()
        for n in range(rows // pair):
            chosen = jnp.dot(
                selector[...], white[part, pair * n : pair * (n + 1), :], preferred_element_type=jnp.float32
            ).astype(jnp.bfloat16)
            sent[part, :, 2 * CAP * n : 2 * CAP * (n + 1), :] = chosen.reshape(count, 2 * CAP, chosen.shape[-1])
        leaving.append(
            pltpu.make_async_copy(
                sent.at[part], outgoing_ref.at[:, pl.ds(part * slots, slots), :], out_sems.at[part, 1]
            )
        )
        leaving[-1].start()
    for copy in leaving:
        copy.wait()


def vmem_spec():
    return pl.BlockSpec(memory_space=pltpu.VMEM)


def smem_spec():
    return pl.BlockSpec(memory_space=pltpu.SMEM)


def whole(array):
    return pl.BlockSpec(array.shape, lambda s: (0,) * array.ndim)


def spectra_call(chan, traces, quality, owners, places, chan_count, own_count):
    rows, length = traces.shape
    ch_dev = quality.shape[1]
    part, depth = rows // ROW_STEPS, length // QUARTERS
    slots = part // (2 * ch_dev) * 2 * CAP
    anywhere = pl.BlockSpec(memory_space=pl.ANY)
    out_shape = [
        jax.ShapeDtypeStruct((rows, 2 * F), jnp.bfloat16),
        jax.ShapeDtypeStruct((chan_count, ROW_STEPS * slots, 2 * F), jnp.bfloat16),
        jax.ShapeDtypeStruct((rows, F), jnp.bfloat16),
        jax.ShapeDtypeStruct((rows, F), jnp.bfloat16),
    ]
    if own_count % 16 == 0:
        out_shape.append(jax.ShapeDtypeStruct((rows // ch_dev, own_count, 2 * F), jnp.bfloat16))
    return pl.pallas_call(
        spectra_kernel,
        in_specs=[smem_spec()] + [anywhere] * 5,
        out_specs=[anywhere] * len(out_shape),
        out_shape=out_shape,
        scratch_shapes=[
            pltpu.VMEM((ROW_STEPS, QUARTERS, part, depth), jnp.bfloat16),
            pltpu.VMEM((depth, 2 * F), jnp.bfloat16),
            pltpu.VMEM(quality.shape, jnp.int32),
            pltpu.VMEM(owners.shape, jnp.int32),
            pltpu.VMEM(places.shape, jnp.int32),
            pltpu.VMEM((ROW_STEPS, part, 2 * F), jnp.bfloat16),
            pltpu.VMEM((ROW_STEPS, chan_count, slots, 2 * F), jnp.bfloat16),
            pltpu.VMEM((chan_count * 2 * CAP, 2 * ch_dev), jnp.bfloat16),
            pltpu.SemaphoreType.DMA((ROW_STEPS + 1, QUARTERS)),
            pltpu.SemaphoreType.DMA((ROW_STEPS, 4 + part // ch_dev)),
        ],
        compiler_params=pltpu.CompilerParams(vmem_limit_bytes=SPECTRA_VMEM_LIMIT),
        cost_estimate=pl.CostEstimate(
            flops=2 * rows * length * 2 * F, bytes_accessed=2 * rows * length, transcendentals=rows * F
        ),
        name="spectra",
    )(chan, traces, jnp.asarray(forward_table(length)), quality, owners, places)


def cross_kernel(last, with_sum, local_windows, awaited, win_ref, first_ref, second_ref, *refs):
    refs = list(refs)
    far_ref = refs.pop(0) if local_windows else None
    refs = refs[awaited:]
    sum_ref = refs.pop(0) if with_sum else None
    if last:
        table_ref, out_ref, done_ref, wide, spread, total, lags, sems = refs
        done_ref[...] = jnp.zeros_like(done_ref)
    else:
        out_ref, wide, spread = refs
        total = out_ref
    windows, own_count = spread.shape[:2]
    ch_dev = wide.shape[1] // 2
    base = pl.multiple_of(win_ref[0] * own_count, 8)

    def widen(w, carry):
        if local_windows:
            wide[w, :ch_dev, :] = first_ref[w].astype(jnp.float32)
            wide[w, ch_dev:, :F] = second_ref[w].astype(jnp.float32)
            wide[w, ch_dev:, F:] = far_ref[w].astype(jnp.float32)
        else:
            shared = ch_dev - own_count
            wide[w, shared:ch_dev, :] = first_ref[w].astype(jnp.float32)
            rows = second_ref[w].astype(jnp.float32)
            for tile in range(ch_dev // 8):
                at = base + 8 * tile
                at = pl.multiple_of(jnp.where(at < shared, at, at + own_count), 8)
                wide[w, pl.ds(at, 8), :] = rows[8 * tile : 8 * tile + 8]
        for tile in range(own_count // 8):
            rows = wide[w, pl.ds(pl.multiple_of(base + 8 * tile, 8), 8), :]
            for i in range(8):
                for q in range(4):
                    spread[w, 8 * tile + i, q] = jnp.broadcast_to(rows[i : i + 1, q * H : (q + 1) * H], (8, H))
        return carry

    lax.fori_loop(0, windows, widen, 0)

    group, tiles = 4, 3
    rounds = SPAN // (8 * tiles)

    def block(index, carry):
        g = index // rounds
        j = index % rounds
        start = pl.multiple_of(base + 8 * (g // 2) + 8 * tiles * j, 8)

        def add_window(w, sums):
            sums = list(sums)
            right = [
                [wide[w, pl.ds(pl.multiple_of(start + 8 * t, 8), 8), q * H : (q + 1) * H] for q in range(4)]
                for t in range(tiles)
            ]
            for i in range(group):
                left = [spread[w, group * g + i, q] for q in range(4)]
                for t in range(tiles):
                    at = 3 * (i * tiles + t)
                    r = right[t]
                    sums[at] = sums[at] + (left[0] * r[0] + left[1] * r[1])
                    sums[at + 1] = sums[at + 1] + (left[2] * r[2] + left[3] * r[3])
                    sums[at + 2] = sums[at + 2] + ((left[1] * r[0] - left[0] * r[1]) + (left[2] * r[3] - left[3] * r[2]))
            return tuple(sums)

        zero = jnp.zeros((8, H), jnp.float32)
        sums = lax.fori_loop(0, windows, add_window, (zero,) * (3 * group * tiles), unroll=2)
        for i in range(group):
            for t in range(tiles):
                at = 3 * (i * tiles + t)
                real, imag = fold_columns(sums[at], sums[at + 1], sums[at + 2])
                where = pl.ds(pl.multiple_of(8 * tiles * j + 8 * t, 8), 8)
                if with_sum:
                    real = real + sum_ref[group * g + i, where, :H]
                    imag = imag + sum_ref[group * g + i, where, H:]
                total[group * g + i, where, :H] = real
                total[group * g + i, where, H:] = imag
        return carry

    lax.fori_loop(0, own_count // group * rounds, block, 0)

    if last:
        copies = []
        for eight in range(own_count // 8):
            first = 8 * eight
            stacks = total[first : first + 8].reshape(8 * SPAN, F).astype(jnp.bfloat16)
            lagged = jnp.dot(stacks, table_ref[...], preferred_element_type=jnp.float32).reshape(8, SPAN, NLAG)
            for i in range(8):
                lags[first + i] = lagged[i, i + 1 : i + 1 + REACH, :]
            some = pl.ds(first, 8)
            copies.append(pltpu.make_async_copy(lags.at[some], out_ref.at[some], sems.at[eight]))
            copies[-1].start()
        for copy in copies:
            copy.wait()


def cross_call(win, first, second, ch_dev, own_count, sums, table, awaited=()):
    local_windows = len(second) == 2
    windows, _, columns = first.shape
    last = table is not None
    with_sum = sums is not None
    operands = [win, first, *second, *awaited]
    in_specs = [smem_spec()] + [vmem_spec()] * (1 + len(second)) + [pl.BlockSpec(memory_space=pl.ANY)] * len(awaited)
    if with_sum:
        operands.append(sums)
    scratch = [
        pltpu.VMEM((windows, 2 * ch_dev, columns), jnp.float32),
        pltpu.VMEM((windows, own_count, 4, 8, H), jnp.float32),
    ]
    if last:
        operands.append(table)
        scratch += [
            pltpu.VMEM((own_count, SPAN, F), jnp.float32),
            pltpu.VMEM((own_count, REACH, NLAG), jnp.float32),
            pltpu.SemaphoreType.DMA((own_count // 8,)),
        ]
    shape = (own_count, REACH, NLAG) if last else (own_count, SPAN, F)
    out_shape, out_specs = [jax.ShapeDtypeStruct(shape, jnp.float32)], [vmem_spec()]
    if last:
        out_shape.append(jax.ShapeDtypeStruct((8, H), jnp.float32))
        out_specs = [pl.BlockSpec(memory_space=pl.ANY), vmem_spec()]
    return pl.pallas_call(
        functools.partial(cross_kernel, last, with_sum, local_windows, len(awaited)),
        in_specs=in_specs + [vmem_spec()] * (len(operands) - len(in_specs)),
        out_specs=out_specs,
        out_shape=out_shape,
        scratch_shapes=scratch,
        compiler_params=pltpu.CompilerParams(vmem_limit_bytes=VMEM_LIMIT),
        cost_estimate=pl.CostEstimate(
            flops=30_000_000_000, bytes_accessed=4 * windows * ch_dev * columns + 4 * own_count * SPAN * F, transcendentals=0
        ),
        name="cross",
    )(*operands)


def fold_kernel(chan_ref, incoming_ref, own_ref, owners_ref, high_ref, low_ref, earlier_ref, out_ref):
    ch_dev = out_ref.shape[0]
    rows = 2 * ch_dev
    pairs = own_ref.shape[0] // rows
    count, slots, columns = incoming_ref.shape
    owners = owners_ref[...].astype(jnp.float32)
    per_row = owners.shape[1] // ch_dev
    device = chan_ref[0]
    line = jnp.sum(jnp.where(rows_of(owners.shape) == device // per_row, owners, 0.0), axis=0, keepdims=True)
    shape = (rows, owners.shape[1])
    line = jnp.broadcast_to(line, shape)
    first = device % per_row * ch_dev
    place = first + rows_of(shape) % ch_dev
    lane = lanes_of(shape)
    owner = jnp.sum(jnp.where(lane == place, line, 0.0), axis=1, keepdims=True)
    earlier = (lane >= first) & (lane < place) & (line == owner)
    rank = jnp.sum(earlier.astype(jnp.float32), axis=1, keepdims=True)
    source = (2 * CAP * owner + rank).astype(jnp.int32)
    shape = (rows, count * 2 * CAP)
    target = source + CAP * (rows_of(shape) // ch_dev)
    picker = (lanes_of(shape) == target).astype(jnp.float32).astype(jnp.bfloat16)
    sums = None
    for n in range(pairs):
        arrived = incoming_ref[:, 2 * CAP * n : 2 * CAP * (n + 1), :].reshape(count * 2 * CAP, columns)
        right = jnp.dot(picker, arrived, preferred_element_type=jnp.float32)
        left = own_ref[rows * n : rows * (n + 1), :].astype(jnp.float32)
        l = [left[:, q * H : (q + 1) * H] for q in range(4)]
        r = [right[:, q * H : (q + 1) * H] for q in range(4)]
        terms = [
            l[0] * r[0] + l[1] * r[1],
            l[2] * r[2] + l[3] * r[3],
            (l[1] * r[0] - l[0] * r[1]) + (l[2] * r[3] - l[3] * r[2]),
        ]
        sums = terms if sums is None else [total + term for total, term in zip(sums, terms)]
    stacks = jnp.concatenate(fold_columns(*[total[:ch_dev] + total[ch_dev:] for total in sums]), axis=1)
    out_ref[...] = lag_transform(stacks, high_ref[...], low_ref[...])


def fold_call(chan, incoming, own, owners, ch_dev, tables, earlier):
    return pl.pallas_call(
        fold_kernel,
        in_specs=[smem_spec()] + [vmem_spec()] * 5 + [pl.BlockSpec(memory_space=pl.ANY)],
        out_specs=vmem_spec(),
        out_shape=jax.ShapeDtypeStruct((ch_dev, NLAG), jnp.float32),
        compiler_params=pltpu.CompilerParams(vmem_limit_bytes=FOLD_VMEM_LIMIT),
        cost_estimate=pl.CostEstimate(
            flops=4 * ch_dev * incoming.size, bytes_accessed=2 * (incoming.size + own.size), transcendentals=0
        ),
        name="fold",
    )(chan, incoming, own, owners, *tables, earlier)


def from_above(block):
    count = lax.axis_size("chan")
    return lax.ppermute(block, "chan", [(i, i - 1) for i in range(1, count)])


def round_win(block, shift):
    count = lax.axis_size("win")
    return lax.ppermute(block, "win", [(i, (i + shift) % count) for i in range(count)])


def local(traces, quality, fold_block, fold_offset):
    win_dev, ch_dev, length = traces.shape
    chan_count = lax.axis_size("chan")
    win_count = lax.axis_size("win")
    window_part = lax.axis_index("win")
    own_count = ch_dev // win_count
    shared = ch_dev - own_count
    chan = lax.axis_index("chan").astype(jnp.int32).reshape(1)
    win = window_part.astype(jnp.int32).reshape(1)
    tables = [jnp.asarray(t) for t in inverse_tables(1.0 / math.sqrt(F * win_dev * win_count))]
    owners = fold_block.reshape(-1, 2 * ch_dev)
    places = fold_offset.reshape(-1, 2 * ch_dev)
    flat, outgoing, near, far, *ready = spectra_call(
        chan, traces.reshape(win_dev * ch_dev, length), quality.reshape(1, ch_dev), owners, places, chan_count, own_count
    )
    whitened = flat.reshape(win_dev, ch_dev, 2 * F)
    upper = [from_above(half.reshape(win_dev, ch_dev, F)) for half in (near, far)]
    ready = ready[0] if ready else whitened[:, shared:]
    common = [round_win(ready, shift) for shift in range(1, win_count)]
    incoming = lax.all_to_all(outgoing, "chan", split_axis=0, concat_axis=0, tiled=True)
    offered = jnp.concatenate([whitened[:, :shared], jnp.concatenate(upper, axis=2)], axis=1)
    special = [
        round_win(
            lax.dynamic_slice_in_dim(offered, (window_part + shift) % win_count * own_count, ch_dev, 1), shift
        )
        for shift in range(1, win_count)
    ]
    arrived = [(whitened, upper, common)] + [(rows, [others], []) for rows, others in zip(common, special)]
    sums = None
    for n, (first, second, awaited) in enumerate(arrived):
        ends = tables[0] if n == win_count - 1 else None
        sums, *done = cross_call(win, first, second, ch_dev, own_count, sums, ends, awaited)
    share = fold_call(chan, incoming, flat, owners, ch_dev, tables, done[0])
    fold = lax.dynamic_slice_in_dim(share, window_part * own_count, own_count, 0)
    for shift in range(1, win_count):
        target = (window_part + shift) % win_count * own_count
        fold = fold + round_win(lax.dynamic_slice_in_dim(share, target, own_count, 0), shift)
    return (sums, fold)


def solution(mesh):
    in_specs = (P("win", "chan", None), P("chan"), P(), P())
    out_specs = (P(("chan", "win"), None, None), P(("chan", "win"), None))
    return jax.shard_map(local, mesh=mesh, in_specs=in_specs, out_specs=out_specs, check_vma=False)
```

```python
import functools
import math

import jax
import jax.numpy as jnp
import numpy as np
from jax import lax
from jax.experimental import pallas as pl
from jax.experimental.pallas import tpu as pltpu
from jax.sharding import PartitionSpec as P

F = 256
H = F // 2
BAND_LO = 32
NLAG = 256
REACH = 64
CAP = 8
SPAN = REACH + 8
smooth_reach = 4
ROW_STEPS = 3
QUARTERS = 4
VMEM_LIMIT = 24 * 1024 * 1024
FOLD_VMEM_LIMIT = 16 * 1024 * 1024
SPECTRA_VMEM_LIMIT = 59 * 1024 * 1024


def bin_order():
    residues = np.arange(H)
    first = (residues - BAND_LO) % F
    second = (-residues - BAND_LO) % F
    second[0] = (H - BAND_LO) % F
    return first, second


def forward_table(length):
    samples = np.arange(length // 4, dtype=np.int64)[:, None]
    parts = []
    for bins in bin_order():
        angles = (samples * (bins + BAND_LO)[None, :] % length) * (2.0 * math.pi / length)
        parts += [np.cos(angles), -np.sin(angles)]
    return np.concatenate(parts, axis=1).astype(np.float32).astype(jnp.bfloat16)


def inverse_tables(factor):
    shifts = (np.arange(NLAG) + NLAG // 2)[None, :]
    residues = np.arange(H)[:, None]
    angles = (residues * shifts % NLAG) * (2.0 * math.pi / NLAG)
    sign = np.where(shifts[0] % 2 == 0, 1.0, -1.0)
    real, imag = np.cos(angles), -np.sin(angles)
    real[0] = (1.0 + sign) / 2.0
    imag[0] = (1.0 - sign) / 2.0
    table = np.concatenate([real, imag], axis=0) * factor
    high = table.astype(np.float32).astype(jnp.bfloat16)
    low = (table - high.astype(np.float64)).astype(np.float32).astype(jnp.bfloat16)
    return high, low


def lag_transform(stacks, high, low):
    top = stacks.astype(jnp.bfloat16)
    rest = (stacks - top.astype(jnp.float32)).astype(jnp.bfloat16)
    dot = functools.partial(jnp.dot, preferred_element_type=jnp.float32)
    return dot(top, high) + (dot(rest, high) + dot(top, low))


def fold_columns(first, second, imag):
    lane = lax.broadcasted_iota(jnp.int32, first.shape, first.ndim - 1)
    return first + second, jnp.where(lane == 0, first - second, imag)


def lanes_of(shape):
    return lax.broadcasted_iota(jnp.int32, shape, len(shape) - 1)


def rows_of(shape):
    return lax.broadcasted_iota(jnp.int32, shape, len(shape) - 2)


def band_matrix():
    def bins(index):
        lane = index & (H - 1)
        residue = jnp.where(index < H, lane, jnp.where(lane == 0, H, F - lane))
        return (residue - BAND_LO + F) & (F - 1)

    apart = bins(rows_of((F, F))) - bins(lanes_of((F, F)))
    return (jnp.abs(apart) <= smooth_reach).astype(jnp.float32).astype(jnp.bfloat16)


def exact_dot(left, right):
    return jnp.dot(left.astype(jnp.bfloat16), right.astype(jnp.bfloat16), preferred_element_type=jnp.float32)


def slot_selector(owners, places, device, ch_dev):
    height, width = owners.shape
    per_row = width // ch_dev
    wanted = (owners == device).astype(jnp.float32)
    before = rows_of((width, width))
    after = lanes_of((width, width))
    earlier = ((before < after) & (before // ch_dev == after // ch_dev)).astype(jnp.float32)
    ranks = exact_dot(wanted, earlier)
    slots = jnp.where(wanted > 0, ranks, float(CAP))
    count = height * per_row * 2 * CAP
    to_row = (rows_of((count, height)) // (2 * CAP * per_row) == lanes_of((count, height))).astype(jnp.float32)
    row_slots = exact_dot(to_row, slots)
    row_places = exact_dot(to_row, places.astype(jnp.float32))
    shape = (count, width)
    row = rows_of(shape)
    mine = (row_slots == (row % CAP).astype(jnp.float32)) & (lanes_of(shape) // ch_dev == row // (2 * CAP) % per_row)
    place = jnp.sum(jnp.where(mine, row_places + 1.0, 0.0), axis=1, keepdims=True).astype(jnp.int32) - 1
    shape = (count, 2 * ch_dev)
    half = rows_of(shape) // CAP % 2
    lane = lanes_of(shape)
    return ((lane == place + ch_dev * half) & (place >= 0)).astype(jnp.float32).astype(jnp.bfloat16)


def turned_sum(quarters, real, imag, negative):
    rows = quarters[0].shape[0]
    lane = lanes_of((rows, H))
    residue = ((F - lane) if negative else lane) & 3
    sign = jnp.where((residue & 1) == 0, 1.0, -1.0)
    straight = jnp.where(residue == 0, 1.0, jnp.where(residue == 2, -1.0, 0.0))
    turned = jnp.where(residue == 1, 1.0, jnp.where(residue == 3, -1.0, 0.0))
    re = [quarter[:, real * H : (real + 1) * H] for quarter in quarters]
    im = [quarter[:, imag * H : (imag + 1) * H] for quarter in quarters]
    odd_re, odd_im = re[1] + sign * re[3], im[1] + sign * im[3]
    return (
        re[0] + sign * re[2] + (straight * odd_re + turned * odd_im),
        im[0] + sign * im[2] + (straight * odd_im - turned * odd_re),
    )


def spectra_kernel(chan_ref, traces_ref, table_ref, quality_ref, owners_ref, places_ref, *refs):
    whitened_ref, outgoing_ref, *shared_ref = refs[:-10]
    traces, table, quality, owners, places, white, sent, selector, sems, out_sems = refs[-10:]
    row_parts, chunks, rows, depth = traces.shape
    ch_dev = quality.shape[1]
    pair = 2 * ch_dev
    count = outgoing_ref.shape[0]
    slots = sent.shape[2]

    def traces_copy(part, k):
        source = traces_ref.at[pl.ds(part * rows, rows), pl.ds(k * depth, depth)]
        return pltpu.make_async_copy(source, traces.at[part, k], sems.at[part, k])

    small = [
        pltpu.make_async_copy(source, target, sems.at[row_parts, k])
        for k, (source, target) in enumerate(
            ((table_ref, table), (quality_ref, quality), (owners_ref, owners), (places_ref, places))
        )
    ]
    for copy in small:
        copy.start()
    for k in range(chunks):
        traces_copy(0, k).start()

    band = band_matrix()
    for copy in small[1:]:
        copy.wait()
    shape = (rows, ch_dev)
    keep = jnp.sum(
        jnp.where(rows_of(shape) % ch_dev == lanes_of(shape), quality[...].astype(jnp.float32), 0.0),
        axis=1, keepdims=True,
    )
    selector[...] = slot_selector(owners[...], places[...], chan_ref[0], ch_dev)
    small[0].wait()

    leaving = []
    for part in range(row_parts):
        quarters = []
        for k in range(chunks):
            traces_copy(part, k).wait()
            if part + 1 < row_parts:
                traces_copy(part + 1, k).start()
            quarters.append(jnp.dot(traces[part, k], table[...], preferred_element_type=jnp.float32))
        parts = turned_sum(quarters, 0, 1, False) + turned_sum(quarters, 2, 3, True)
        energy = jnp.concatenate(
            [parts[0] * parts[0] + parts[1] * parts[1], parts[2] * parts[2] + parts[3] * parts[3]], axis=1
        )
        top = energy.astype(jnp.bfloat16)
        rest = (energy - top.astype(jnp.float32)).astype(jnp.bfloat16)
        smooth = jnp.dot(top, band, preferred_element_type=jnp.float32) + jnp.dot(
            rest, band, preferred_element_type=jnp.float32
        )
        water = jnp.sum(energy, axis=1, keepdims=True) * (1.0 / F)
        scaling = lax.rsqrt(smooth * (1.0 / (2.0 * smooth_reach + 1.0)) + (0.1 * water + 1e-06)) * keep
        near, far = scaling[:, :H], scaling[:, H:]
        for q, values in enumerate((parts[0] * near, parts[1] * near, parts[2] * far, parts[3] * far)):
            white[part, :, q * H : (q + 1) * H] = values.astype(jnp.bfloat16)
        leaving.append(
            pltpu.make_async_copy(
                white.at[part], whitened_ref.at[pl.ds(part * rows, rows), :], out_sems.at[part, 0]
            )
        )
        leaving[-1].start()
        if shared_ref:
            height = shared_ref[0].shape[1]
            for w in range(rows // ch_dev):
                leaving.append(
                    pltpu.make_async_copy(
                        white.at[part, pl.ds((w + 1) * ch_dev - height, height), :],
                        shared_ref[0].at[part * (rows // ch_dev) + w],
                        out_sems.at[part, 2 + w],
                    )
                )
                leaving[-1].start()
        for n in range(rows // pair):
            chosen = jnp.dot(
                selector[...], white[part, pair * n : pair * (n + 1), :], preferred_element_type=jnp.float32
            ).astype(jnp.bfloat16)
            sent[part, :, 2 * CAP * n : 2 * CAP * (n + 1), :] = chosen.reshape(count, 2 * CAP, chosen.shape[-1])
        leaving.append(
            pltpu.make_async_copy(
                sent.at[part], outgoing_ref.at[:, pl.ds(part * slots, slots), :], out_sems.at[part, 1]
            )
        )
        leaving[-1].start()
    for copy in leaving:
        copy.wait()


def vmem_spec():
    return pl.BlockSpec(memory_space=pltpu.VMEM)


def smem_spec():
    return pl.BlockSpec(memory_space=pltpu.SMEM)


def whole(array):
    return pl.BlockSpec(array.shape, lambda s: (0,) * array.ndim)


def spectra_call(chan, traces, quality, owners, places, chan_count, own_count):
    rows, length = traces.shape
    ch_dev = quality.shape[1]
    part, depth = rows // ROW_STEPS, length // QUARTERS
    slots = part // (2 * ch_dev) * 2 * CAP
    anywhere = pl.BlockSpec(memory_space=pl.ANY)
    out_shape = [
        jax.ShapeDtypeStruct((rows, 2 * F), jnp.bfloat16),
        jax.ShapeDtypeStruct((chan_count, ROW_STEPS * slots, 2 * F), jnp.bfloat16),
    ]
    if own_count % 16 == 0:
        out_shape.append(jax.ShapeDtypeStruct((rows // ch_dev, own_count, 2 * F), jnp.bfloat16))
    return pl.pallas_call(
        spectra_kernel,
        in_specs=[smem_spec()] + [anywhere] * 5,
        out_specs=[anywhere] * len(out_shape),
        out_shape=out_shape,
        scratch_shapes=[
            pltpu.VMEM((ROW_STEPS, QUARTERS, part, depth), jnp.bfloat16),
            pltpu.VMEM((depth, 2 * F), jnp.bfloat16),
            pltpu.VMEM(quality.shape, jnp.int32),
            pltpu.VMEM(owners.shape, jnp.int32),
            pltpu.VMEM(places.shape, jnp.int32),
            pltpu.VMEM((ROW_STEPS, part, 2 * F), jnp.bfloat16),
            pltpu.VMEM((ROW_STEPS, chan_count, slots, 2 * F), jnp.bfloat16),
            pltpu.VMEM((chan_count * 2 * CAP, 2 * ch_dev), jnp.bfloat16),
            pltpu.SemaphoreType.DMA((ROW_STEPS + 1, QUARTERS)),
            pltpu.SemaphoreType.DMA((ROW_STEPS, 2 + part // ch_dev)),
        ],
        compiler_params=pltpu.CompilerParams(vmem_limit_bytes=SPECTRA_VMEM_LIMIT),
        cost_estimate=pl.CostEstimate(
            flops=2 * rows * length * 2 * F, bytes_accessed=2 * rows * length, transcendentals=rows * F
        ),
        name="spectra",
    )(chan, traces, jnp.asarray(forward_table(length)), quality, owners, places)


def cross_kernel(last, with_sum, local_windows, awaited, win_ref, first_ref, second_ref, *refs):
    refs = list(refs)
    refs = refs[awaited:]
    sum_ref = refs.pop(0) if with_sum else None
    if last:
        table_ref, out_ref, done_ref, wide, spread, total, lags, sems = refs
        done_ref[...] = jnp.zeros_like(done_ref)
    else:
        out_ref, wide, spread = refs
        total = out_ref
    windows, own_count = spread.shape[:2]
    ch_dev = wide.shape[1] // 2
    base = pl.multiple_of(win_ref[0] * own_count, 8)

    def widen(w, carry):
        if local_windows:
            wide[w, :ch_dev, :] = first_ref[w].astype(jnp.float32)
            wide[w, ch_dev:, :] = second_ref[w].astype(jnp.float32)
        else:
            shared = ch_dev - own_count
            wide[w, shared:ch_dev, :] = first_ref[w].astype(jnp.float32)
            rows = second_ref[w].astype(jnp.float32)
            for tile in range(ch_dev // 8):
                at = base + 8 * tile
                at = pl.multiple_of(jnp.where(at < shared, at, at + own_count), 8)
                wide[w, pl.ds(at, 8), :] = rows[8 * tile : 8 * tile + 8]
        for tile in range(own_count // 8):
            rows = wide[w, pl.ds(pl.multiple_of(base + 8 * tile, 8), 8), :]
            for i in range(8):
                for q in range(4):
                    spread[w, 8 * tile + i, q] = jnp.broadcast_to(rows[i : i + 1, q * H : (q + 1) * H], (8, H))
        return carry

    lax.fori_loop(0, windows, widen, 0)

    group, tiles = 4, 3
    rounds = SPAN // (8 * tiles)

    def block(index, carry):
        g = index // rounds
        j = index % rounds
        start = pl.multiple_of(base + 8 * (g // 2) + 8 * tiles * j, 8)

        def add_window(w, sums):
            sums = list(sums)
            right = [
                [wide[w, pl.ds(pl.multiple_of(start + 8 * t, 8), 8), q * H : (q + 1) * H] for q in range(4)]
                for t in range(tiles)
            ]
            for i in range(group):
                left = [spread[w, group * g + i, q] for q in range(4)]
                for t in range(tiles):
                    at = 3 * (i * tiles + t)
                    r = right[t]
                    sums[at] = sums[at] + (left[0] * r[0] + left[1] * r[1])
                    sums[at + 1] = sums[at + 1] + (left[2] * r[2] + left[3] * r[3])
                    sums[at + 2] = sums[at + 2] + ((left[1] * r[0] - left[0] * r[1]) + (left[2] * r[3] - left[3] * r[2]))
            return tuple(sums)

        zero = jnp.zeros((8, H), jnp.float32)
        sums = lax.fori_loop(0, windows, add_window, (zero,) * (3 * group * tiles), unroll=2)
        for i in range(group):
            for t in range(tiles):
                at = 3 * (i * tiles + t)
                real, imag = fold_columns(sums[at], sums[at + 1], sums[at + 2])
                where = pl.ds(pl.multiple_of(8 * tiles * j + 8 * t, 8), 8)
                if with_sum:
                    real = real + sum_ref[group * g + i, where, :H]
                    imag = imag + sum_ref[group * g + i, where, H:]
                total[group * g + i, where, :H] = real
                total[group * g + i, where, H:] = imag
        return carry

    lax.fori_loop(0, own_count // group * rounds, block, 0)

    if last:
        copies = []
        for eight in range(own_count // 8):
            first = 8 * eight
            stacks = total[first : first + 8].reshape(8 * SPAN, F).astype(jnp.bfloat16)
            lagged = jnp.dot(stacks, table_ref[...], preferred_element_type=jnp.float32).reshape(8, SPAN, NLAG)
            for i in range(8):
                lags[first + i] = lagged[i, i + 1 : i + 1 + REACH, :]
            some = pl.ds(first, 8)
            copies.append(pltpu.make_async_copy(lags.at[some], out_ref.at[some], sems.at[eight]))
            copies[-1].start()
        for copy in copies:
            copy.wait()


def cross_call(win, first, second, ch_dev, own_count, sums, table, awaited):
    local_windows = sums is None
    windows, _, columns = first.shape
    last = table is not None
    with_sum = sums is not None
    operands = [win, first, second, *awaited]
    in_specs = [smem_spec(), vmem_spec(), vmem_spec()] + [pl.BlockSpec(memory_space=pl.ANY)] * len(awaited)
    if with_sum:
        operands.append(sums)
    scratch = [
        pltpu.VMEM((windows, 2 * ch_dev, columns), jnp.float32),
        pltpu.VMEM((windows, own_count, 4, 8, H), jnp.float32),
    ]
    if last:
        operands.append(table)
        scratch += [
            pltpu.VMEM((own_count, SPAN, F), jnp.float32),
            pltpu.VMEM((own_count, REACH, NLAG), jnp.float32),
            pltpu.SemaphoreType.DMA((own_count // 8,)),
        ]
    shape = (own_count, REACH, NLAG) if last else (own_count, SPAN, F)
    out_shape, out_specs = [jax.ShapeDtypeStruct(shape, jnp.float32)], [vmem_spec()]
    if last:
        out_shape.append(jax.ShapeDtypeStruct((8, H), jnp.float32))
        out_specs = [pl.BlockSpec(memory_space=pl.ANY), vmem_spec()]
    return pl.pallas_call(
        functools.partial(cross_kernel, last, with_sum, local_windows, len(awaited)),
        in_specs=in_specs + [vmem_spec()] * (len(operands) - len(in_specs)),
        out_specs=out_specs,
        out_shape=out_shape,
        scratch_shapes=scratch,
        compiler_params=pltpu.CompilerParams(vmem_limit_bytes=VMEM_LIMIT),
        cost_estimate=pl.CostEstimate(
            flops=30_000_000_000, bytes_accessed=4 * windows * ch_dev * columns + 4 * own_count * SPAN * F, transcendentals=0
        ),
        name="cross",
    )(*operands)


def fold_kernel(chan_ref, incoming_ref, own_ref, owners_ref, high_ref, low_ref, earlier_ref, out_ref):
    ch_dev = out_ref.shape[0]
    rows = 2 * ch_dev
    pairs = own_ref.shape[0] // rows
    count, slots, columns = incoming_ref.shape
    owners = owners_ref[...].astype(jnp.float32)
    per_row = owners.shape[1] // ch_dev
    device = chan_ref[0]
    line = jnp.sum(jnp.where(rows_of(owners.shape) == device // per_row, owners, 0.0), axis=0, keepdims=True)
    shape = (rows, owners.shape[1])
    line = jnp.broadcast_to(line, shape)
    first = device % per_row * ch_dev
    place = first + rows_of(shape) % ch_dev
    lane = lanes_of(shape)
    owner = jnp.sum(jnp.where(lane == place, line, 0.0), axis=1, keepdims=True)
    earlier = (lane >= first) & (lane < place) & (line == owner)
    rank = jnp.sum(earlier.astype(jnp.float32), axis=1, keepdims=True)
    source = (2 * CAP * owner + rank).astype(jnp.int32)
    shape = (rows, count * 2 * CAP)
    target = source + CAP * (rows_of(shape) // ch_dev)
    picker = (lanes_of(shape) == target).astype(jnp.float32).astype(jnp.bfloat16)
    sums = None
    for n in range(pairs):
        arrived = incoming_ref[:, 2 * CAP * n : 2 * CAP * (n + 1), :].reshape(count * 2 * CAP, columns)
        right = jnp.dot(picker, arrived, preferred_element_type=jnp.float32)
        left = own_ref[rows * n : rows * (n + 1), :].astype(jnp.float32)
        l = [left[:, q * H : (q + 1) * H] for q in range(4)]
        r = [right[:, q * H : (q + 1) * H] for q in range(4)]
        terms = [
            l[0] * r[0] + l[1] * r[1],
            l[2] * r[2] + l[3] * r[3],
            (l[1] * r[0] - l[0] * r[1]) + (l[2] * r[3] - l[3] * r[2]),
        ]
        sums = terms if sums is None else [total + term for total, term in zip(sums, terms)]
    stacks = jnp.concatenate(fold_columns(*[total[:ch_dev] + total[ch_dev:] for total in sums]), axis=1)
    out_ref[...] = lag_transform(stacks, high_ref[...], low_ref[...])


def fold_call(chan, incoming, own, owners, ch_dev, tables, earlier):
    return pl.pallas_call(
        fold_kernel,
        in_specs=[smem_spec()] + [vmem_spec()] * 5 + [pl.BlockSpec(memory_space=pl.ANY)],
        out_specs=vmem_spec(),
        out_shape=jax.ShapeDtypeStruct((ch_dev, NLAG), jnp.float32),
        compiler_params=pltpu.CompilerParams(vmem_limit_bytes=FOLD_VMEM_LIMIT),
        cost_estimate=pl.CostEstimate(
            flops=4 * ch_dev * incoming.size, bytes_accessed=2 * (incoming.size + own.size), transcendentals=0
        ),
        name="fold",
    )(chan, incoming, own, owners, *tables, earlier)


def from_above(block):
    count = lax.axis_size("chan")
    return lax.ppermute(block, "chan", [(i, i - 1) for i in range(1, count)])


def round_win(block, shift):
    count = lax.axis_size("win")
    return lax.ppermute(block, "win", [(i, (i + shift) % count) for i in range(count)])


def local(traces, quality, fold_block, fold_offset):
    win_dev, ch_dev, length = traces.shape
    chan_count = lax.axis_size("chan")
    win_count = lax.axis_size("win")
    window_part = lax.axis_index("win")
    own_count = ch_dev // win_count
    shared = ch_dev - own_count
    chan = lax.axis_index("chan").astype(jnp.int32).reshape(1)
    win = window_part.astype(jnp.int32).reshape(1)
    tables = [jnp.asarray(t) for t in inverse_tables(1.0 / math.sqrt(F * win_dev * win_count))]
    owners = fold_block.reshape(-1, 2 * ch_dev)
    places = fold_offset.reshape(-1, 2 * ch_dev)
    flat, outgoing, *ready = spectra_call(
        chan, traces.reshape(win_dev * ch_dev, length), quality.reshape(1, ch_dev), owners, places, chan_count, own_count
    )
    whitened = flat.reshape(win_dev, ch_dev, 2 * F)
    upper = from_above(whitened)
    ready = ready[0] if ready else whitened[:, shared:]
    common = [round_win(ready, shift) for shift in range(1, win_count)]
    incoming = lax.all_to_all(outgoing, "chan", split_axis=0, concat_axis=0, tiled=True)
    offered = jnp.concatenate([whitened[:, :shared], upper], axis=1)
    special = [
        round_win(
            lax.dynamic_slice_in_dim(offered, (window_part + shift) % win_count * own_count, ch_dev, 1), shift
        )
        for shift in range(1, win_count)
    ]
    arrived = [(whitened, upper, common)] + [(rows, others, []) for rows, others in zip(common, special)]
    sums = None
    for n, (first, second, awaited) in enumerate(arrived):
        ends = tables[0] if n == win_count - 1 else None
        sums, *done = cross_call(win, first, second, ch_dev, own_count, sums, ends, awaited)
    share = fold_call(chan, incoming, flat, owners, ch_dev, tables, done[0])
    fold = lax.dynamic_slice_in_dim(share, window_part * own_count, own_count, 0)
    for shift in range(1, win_count):
        target = (window_part + shift) % win_count * own_count
        fold = fold + round_win(lax.dynamic_slice_in_dim(share, target, own_count, 0), shift)
    return (sums, fold)


def solution(mesh):
    in_specs = (P("win", "chan", None), P("chan"), P(), P())
    out_specs = (P(("chan", "win"), None, None), P(("chan", "win"), None))
    return jax.shard_map(local, mesh=mesh, in_specs=in_specs, out_specs=out_specs, check_vma=False)
```

```python
import functools
import math

import jax
import jax.numpy as jnp
import numpy as np
from jax import lax
from jax.experimental import pallas as pl
from jax.experimental.pallas import tpu as pltpu
from jax.sharding import PartitionSpec as P

F = 256
H = F // 2
BAND_LO = 32
NLAG = 256
REACH = 64
CAP = 8
SPAN = REACH + 8
smooth_reach = 4
QUARTERS = 4
VMEM_LIMIT = 24 * 1024 * 1024
FOLD_VMEM_LIMIT = 16 * 1024 * 1024
SPECTRA_VMEM_LIMIT = 59 * 1024 * 1024


def bin_order():
    residues = np.arange(H)
    first = (residues - BAND_LO) % F
    second = (-residues - BAND_LO) % F
    second[0] = (H - BAND_LO) % F
    return first, second


def forward_table(length):
    samples = np.arange(length // 4, dtype=np.int64)[:, None]
    parts = []
    for bins in bin_order():
        angles = (samples * (bins + BAND_LO)[None, :] % length) * (2.0 * math.pi / length)
        parts += [np.cos(angles), -np.sin(angles)]
    return np.concatenate(parts, axis=1).astype(np.float32).astype(jnp.bfloat16)


def inverse_tables(factor):
    shifts = (np.arange(NLAG) + NLAG // 2)[None, :]
    residues = np.arange(H)[:, None]
    angles = (residues * shifts % NLAG) * (2.0 * math.pi / NLAG)
    sign = np.where(shifts[0] % 2 == 0, 1.0, -1.0)
    real, imag = np.cos(angles), -np.sin(angles)
    real[0] = (1.0 + sign) / 2.0
    imag[0] = (1.0 - sign) / 2.0
    table = np.concatenate([real, imag], axis=0) * factor
    high = table.astype(np.float32).astype(jnp.bfloat16)
    low = (table - high.astype(np.float64)).astype(np.float32).astype(jnp.bfloat16)
    return high, low


def lag_transform(stacks, high, low):
    top = stacks.astype(jnp.bfloat16)
    rest = (stacks - top.astype(jnp.float32)).astype(jnp.bfloat16)
    dot = functools.partial(jnp.dot, preferred_element_type=jnp.float32)
    return dot(top, high) + (dot(rest, high) + dot(top, low))


def fold_columns(first, second, imag):
    lane = lax.broadcasted_iota(jnp.int32, first.shape, first.ndim - 1)
    return first + second, jnp.where(lane == 0, first - second, imag)


def lanes_of(shape):
    return lax.broadcasted_iota(jnp.int32, shape, len(shape) - 1)


def rows_of(shape):
    return lax.broadcasted_iota(jnp.int32, shape, len(shape) - 2)


def band_matrix():
    def bins(index):
        lane = index & (H - 1)
        residue = jnp.where(index < H, lane, jnp.where(lane == 0, H, F - lane))
        return (residue - BAND_LO + F) & (F - 1)

    apart = bins(rows_of((F, F))) - bins(lanes_of((F, F)))
    return (jnp.abs(apart) <= smooth_reach).astype(jnp.float32).astype(jnp.bfloat16)


def exact_dot(left, right):
    return jnp.dot(left.astype(jnp.bfloat16), right.astype(jnp.bfloat16), preferred_element_type=jnp.float32)


def slot_selector(owners, places, device, ch_dev):
    height, width = owners.shape
    per_row = width // ch_dev
    wanted = (owners == device).astype(jnp.float32)
    before = rows_of((width, width))
    after = lanes_of((width, width))
    earlier = ((before < after) & (before // ch_dev == after // ch_dev)).astype(jnp.float32)
    ranks = exact_dot(wanted, earlier)
    slots = jnp.where(wanted > 0, ranks, float(CAP))
    count = height * per_row * 2 * CAP
    to_row = (rows_of((count, height)) // (2 * CAP * per_row) == lanes_of((count, height))).astype(jnp.float32)
    row_slots = exact_dot(to_row, slots)
    row_places = exact_dot(to_row, places.astype(jnp.float32))
    shape = (count, width)
    row = rows_of(shape)
    mine = (row_slots == (row % CAP).astype(jnp.float32)) & (lanes_of(shape) // ch_dev == row // (2 * CAP) % per_row)
    place = jnp.sum(jnp.where(mine, row_places + 1.0, 0.0), axis=1, keepdims=True).astype(jnp.int32) - 1
    shape = (count, 2 * ch_dev)
    half = rows_of(shape) // CAP % 2
    lane = lanes_of(shape)
    return ((lane == place + ch_dev * half) & (place >= 0)).astype(jnp.float32).astype(jnp.bfloat16)


def turned_sum(quarters, real, imag, negative):
    rows = quarters[0].shape[0]
    lane = lanes_of((rows, H))
    residue = ((F - lane) if negative else lane) & 3
    sign = jnp.where((residue & 1) == 0, 1.0, -1.0)
    straight = jnp.where(residue == 0, 1.0, jnp.where(residue == 2, -1.0, 0.0))
    turned = jnp.where(residue == 1, 1.0, jnp.where(residue == 3, -1.0, 0.0))
    re = [quarter[:, real * H : (real + 1) * H] for quarter in quarters]
    im = [quarter[:, imag * H : (imag + 1) * H] for quarter in quarters]
    odd_re, odd_im = re[1] + sign * re[3], im[1] + sign * im[3]
    return (
        re[0] + sign * re[2] + (straight * odd_re + turned * odd_im),
        im[0] + sign * im[2] + (straight * odd_im - turned * odd_re),
    )


def spectra_kernel(chan_ref, traces_ref, table_ref, quality_ref, owners_ref, places_ref, *refs):
    whitened_ref, outgoing_ref, near_ref, far_ref, *shared_ref = refs[:-11]
    traces, table, quality, owners, places, products, white, sent, selector, sems, out_sems = refs[-11:]
    row_parts, chunks, rows, depth = traces.shape
    ch_dev = quality.shape[1]
    pair = 2 * ch_dev
    count = outgoing_ref.shape[0]
    slots = sent.shape[2]

    def traces_copy(part, k):
        source = traces_ref.at[pl.ds(part * rows, rows), pl.ds(k * depth, depth)]
        return pltpu.make_async_copy(source, traces.at[part, k], sems.at[part, k])

    small = [
        pltpu.make_async_copy(source, target, sems.at[row_parts, k])
        for k, (source, target) in enumerate(
            ((table_ref, table), (quality_ref, quality), (owners_ref, owners), (places_ref, places))
        )
    ]
    for copy in small:
        copy.start()
    for part in range(row_parts):
        for k in range(chunks):
            traces_copy(part, k).start()

    band = band_matrix()
    for copy in small[1:]:
        copy.wait()
    shape = (rows, ch_dev)
    keep = jnp.sum(
        jnp.where(rows_of(shape) % ch_dev == lanes_of(shape), quality[...].astype(jnp.float32), 0.0),
        axis=1, keepdims=True,
    )
    selector[...] = slot_selector(owners[...], places[...], chan_ref[0], ch_dev)
    small[0].wait()
    leaving = []

    def transform(part):
        for k in range(chunks):
            traces_copy(part, k).wait()
        stacked = traces[part].reshape(chunks * rows, depth)
        products[part % 2] = jnp.dot(stacked, table[...], preferred_element_type=jnp.float32)

    def whiten(part):
        quarters = [products[part % 2, k * rows : (k + 1) * rows, :] for k in range(chunks)]
        parts = turned_sum(quarters, 0, 1, False) + turned_sum(quarters, 2, 3, True)
        energy = jnp.concatenate(
            [parts[0] * parts[0] + parts[1] * parts[1], parts[2] * parts[2] + parts[3] * parts[3]], axis=1
        )
        top = energy.astype(jnp.bfloat16)
        rest = (energy - top.astype(jnp.float32)).astype(jnp.bfloat16)
        smooth = jnp.dot(top, band, preferred_element_type=jnp.float32) + jnp.dot(
            rest, band, preferred_element_type=jnp.float32
        )
        water = jnp.sum(energy, axis=1, keepdims=True) * (1.0 / F)
        scaling = lax.rsqrt(smooth * (1.0 / (2.0 * smooth_reach + 1.0)) + (0.1 * water + 1e-06)) * keep
        near, far = scaling[:, :H], scaling[:, H:]
        values = jnp.concatenate(
            [parts[0] * near, parts[1] * near, parts[2] * far, parts[3] * far], axis=1
        ).astype(jnp.bfloat16)
        white[part] = values
        for n in range(rows // pair):
            chosen = jnp.dot(
                selector[...], values[pair * n : pair * (n + 1), :], preferred_element_type=jnp.float32
            ).astype(jnp.bfloat16)
            sent[part, :, 2 * CAP * n : 2 * CAP * (n + 1), :] = chosen.reshape(count, 2 * CAP, chosen.shape[-1])

    def leave(part):
        at = pl.ds(part * rows, rows)
        copies = [
            (white.at[part, :, pl.ds(0, F)], near_ref.at[at, :]),
            (white.at[part, :, pl.ds(F, F)], far_ref.at[at, :]),
            (sent.at[part], outgoing_ref.at[:, pl.ds(part * slots, slots), :]),
            (white.at[part], whitened_ref.at[at, :]),
        ]
        if shared_ref:
            height = shared_ref[0].shape[1]
            for w in range(rows // ch_dev):
                copies.append(
                    (
                        white.at[part, pl.ds((w + 1) * ch_dev - height, height), :],
                        shared_ref[0].at[part * (rows // ch_dev) + w],
                    )
                )
        for n, (source, target) in enumerate(copies):
            leaving.append(pltpu.make_async_copy(source, target, out_sems.at[part, n]))
            leaving[-1].start()

    for part in range(row_parts + 1):
        if part < row_parts:
            transform(part)
        if part > 0:
            whiten(part - 1)
            leave(part - 1)
    for copy in leaving:
        copy.wait()


def vmem_spec():
    return pl.BlockSpec(memory_space=pltpu.VMEM)


def smem_spec():
    return pl.BlockSpec(memory_space=pltpu.SMEM)


def whole(array):
    return pl.BlockSpec(array.shape, lambda s: (0,) * array.ndim)


def spectra_call(chan, traces, quality, owners, places, chan_count, own_count):
    rows, length = traces.shape
    ch_dev = quality.shape[1]
    row_steps = rows // (2 * ch_dev)
    part, depth = rows // row_steps, length // QUARTERS
    slots = part // (2 * ch_dev) * 2 * CAP
    anywhere = pl.BlockSpec(memory_space=pl.ANY)
    out_shape = [
        jax.ShapeDtypeStruct((rows, 2 * F), jnp.bfloat16),
        jax.ShapeDtypeStruct((chan_count, row_steps * slots, 2 * F), jnp.bfloat16),
        jax.ShapeDtypeStruct((rows, F), jnp.bfloat16),
        jax.ShapeDtypeStruct((rows, F), jnp.bfloat16),
    ]
    if own_count % 16 == 0:
        out_shape.append(jax.ShapeDtypeStruct((rows // ch_dev, own_count, 2 * F), jnp.bfloat16))
    return pl.pallas_call(
        spectra_kernel,
        in_specs=[smem_spec()] + [anywhere] * 5,
        out_specs=[anywhere] * len(out_shape),
        out_shape=out_shape,
        scratch_shapes=[
            pltpu.VMEM((row_steps, QUARTERS, part, depth), jnp.bfloat16),
            pltpu.VMEM((depth, 2 * F), jnp.bfloat16),
            pltpu.VMEM(quality.shape, jnp.int32),
            pltpu.VMEM(owners.shape, jnp.int32),
            pltpu.VMEM(places.shape, jnp.int32),
            pltpu.VMEM((2, QUARTERS * part, 2 * F), jnp.float32),
            pltpu.VMEM((row_steps, part, 2 * F), jnp.bfloat16),
            pltpu.VMEM((row_steps, chan_count, slots, 2 * F), jnp.bfloat16),
            pltpu.VMEM((chan_count * 2 * CAP, 2 * ch_dev), jnp.bfloat16),
            pltpu.SemaphoreType.DMA((row_steps + 1, QUARTERS)),
            pltpu.SemaphoreType.DMA((row_steps, 4 + part // ch_dev)),
        ],
        compiler_params=pltpu.CompilerParams(vmem_limit_bytes=SPECTRA_VMEM_LIMIT),
        cost_estimate=pl.CostEstimate(
            flops=2 * rows * length * 2 * F, bytes_accessed=2 * rows * length, transcendentals=rows * F
        ),
        name="spectra",
    )(chan, traces, jnp.asarray(forward_table(length)), quality, owners, places)


def cross_kernel(last, with_sum, local_windows, awaited, win_ref, first_ref, second_ref, *refs):
    refs = list(refs)
    far_ref = refs.pop(0) if local_windows else None
    refs = refs[awaited:]
    sum_ref = refs.pop(0) if with_sum else None
    if last:
        table_ref, out_ref, done_ref, wide, spread, total, lags, sems = refs
        done_ref[...] = jnp.zeros_like(done_ref)
    else:
        out_ref, wide, spread = refs
        total = out_ref
    windows, own_count = spread.shape[:2]
    ch_dev = wide.shape[1] // 2
    base = pl.multiple_of(win_ref[0] * own_count, 8)

    def widen(w, carry):
        if local_windows:
            wide[w, :ch_dev, :] = first_ref[w].astype(jnp.float32)
            wide[w, ch_dev:, :F] = second_ref[w].astype(jnp.float32)
            wide[w, ch_dev:, F:] = far_ref[w].astype(jnp.float32)
        else:
            shared = ch_dev - own_count
            wide[w, shared:ch_dev, :] = first_ref[w].astype(jnp.float32)
            rows = second_ref[w].astype(jnp.float32)
            for tile in range(ch_dev // 8):
                at = base + 8 * tile
                at = pl.multiple_of(jnp.where(at < shared, at, at + own_count), 8)
                wide[w, pl.ds(at, 8), :] = rows[8 * tile : 8 * tile + 8]
        for tile in range(own_count // 8):
            rows = wide[w, pl.ds(pl.multiple_of(base + 8 * tile, 8), 8), :]
            for i in range(8):
                for q in range(4):
                    spread[w, 8 * tile + i, q] = jnp.broadcast_to(rows[i : i + 1, q * H : (q + 1) * H], (8, H))
        return carry

    lax.fori_loop(0, windows, widen, 0)

    group, tiles = 4, 3
    rounds = SPAN // (8 * tiles)

    def block(index, carry):
        g = index // rounds
        j = index % rounds
        start = pl.multiple_of(base + 8 * (g // 2) + 8 * tiles * j, 8)

        def add_window(w, sums):
            sums = list(sums)
            right = [
                [wide[w, pl.ds(pl.multiple_of(start + 8 * t, 8), 8), q * H : (q + 1) * H] for q in range(4)]
                for t in range(tiles)
            ]
            for i in range(group):
                left = [spread[w, group * g + i, q] for q in range(4)]
                for t in range(tiles):
                    at = 3 * (i * tiles + t)
                    r = right[t]
                    sums[at] = sums[at] + (left[0] * r[0] + left[1] * r[1])
                    sums[at + 1] = sums[at + 1] + (left[2] * r[2] + left[3] * r[3])
                    sums[at + 2] = sums[at + 2] + ((left[1] * r[0] - left[0] * r[1]) + (left[2] * r[3] - left[3] * r[2]))
            return tuple(sums)

        zero = jnp.zeros((8, H), jnp.float32)
        sums = lax.fori_loop(0, windows, add_window, (zero,) * (3 * group * tiles), unroll=2)
        for i in range(group):
            for t in range(tiles):
                at = 3 * (i * tiles + t)
                real, imag = fold_columns(sums[at], sums[at + 1], sums[at + 2])
                where = pl.ds(pl.multiple_of(8 * tiles * j + 8 * t, 8), 8)
                if with_sum:
                    real = real + sum_ref[group * g + i, where, :H]
                    imag = imag + sum_ref[group * g + i, where, H:]
                total[group * g + i, where, :H] = real
                total[group * g + i, where, H:] = imag
        return carry

    lax.fori_loop(0, own_count // group * rounds, block, 0)

    if last:
        copies = []
        for eight in range(own_count // 8):
            first = 8 * eight
            stacks = total[first : first + 8].reshape(8 * SPAN, F).astype(jnp.bfloat16)
            lagged = jnp.dot(stacks, table_ref[...], preferred_element_type=jnp.float32).reshape(8, SPAN, NLAG)
            for i in range(8):
                lags[first + i] = lagged[i, i + 1 : i + 1 + REACH, :]
            some = pl.ds(first, 8)
            copies.append(pltpu.make_async_copy(lags.at[some], out_ref.at[some], sems.at[eight]))
            copies[-1].start()
        for copy in copies:
            copy.wait()


def cross_call(win, first, second, ch_dev, own_count, sums, table, awaited=()):
    local_windows = len(second) == 2
    windows, _, columns = first.shape
    last = table is not None
    with_sum = sums is not None
    operands = [win, first, *second, *awaited]
    in_specs = [smem_spec()] + [vmem_spec()] * (1 + len(second)) + [pl.BlockSpec(memory_space=pl.ANY)] * len(awaited)
    if with_sum:
        operands.append(sums)
    scratch = [
        pltpu.VMEM((windows, 2 * ch_dev, columns), jnp.float32),
        pltpu.VMEM((windows, own_count, 4, 8, H), jnp.float32),
    ]
    if last:
        operands.append(table)
        scratch += [
            pltpu.VMEM((own_count, SPAN, F), jnp.float32),
            pltpu.VMEM((own_count, REACH, NLAG), jnp.float32),
            pltpu.SemaphoreType.DMA((own_count // 8,)),
        ]
    shape = (own_count, REACH, NLAG) if last else (own_count, SPAN, F)
    out_shape, out_specs = [jax.ShapeDtypeStruct(shape, jnp.float32)], [vmem_spec()]
    if last:
        out_shape.append(jax.ShapeDtypeStruct((8, H), jnp.float32))
        out_specs = [pl.BlockSpec(memory_space=pl.ANY), vmem_spec()]
    return pl.pallas_call(
        functools.partial(cross_kernel, last, with_sum, local_windows, len(awaited)),
        in_specs=in_specs + [vmem_spec()] * (len(operands) - len(in_specs)),
        out_specs=out_specs,
        out_shape=out_shape,
        scratch_shapes=scratch,
        compiler_params=pltpu.CompilerParams(vmem_limit_bytes=VMEM_LIMIT),
        cost_estimate=pl.CostEstimate(
            flops=30_000_000_000, bytes_accessed=4 * windows * ch_dev * columns + 4 * own_count * SPAN * F, transcendentals=0
        ),
        name="cross",
    )(*operands)


def fold_kernel(chan_ref, incoming_ref, own_ref, owners_ref, high_ref, low_ref, earlier_ref, out_ref):
    ch_dev = out_ref.shape[0]
    rows = 2 * ch_dev
    pairs = own_ref.shape[0] // rows
    count, slots, columns = incoming_ref.shape
    owners = owners_ref[...].astype(jnp.float32)
    per_row = owners.shape[1] // ch_dev
    device = chan_ref[0]
    line = jnp.sum(jnp.where(rows_of(owners.shape) == device // per_row, owners, 0.0), axis=0, keepdims=True)
    shape = (rows, owners.shape[1])
    line = jnp.broadcast_to(line, shape)
    first = device % per_row * ch_dev
    place = first + rows_of(shape) % ch_dev
    lane = lanes_of(shape)
    owner = jnp.sum(jnp.where(lane == place, line, 0.0), axis=1, keepdims=True)
    earlier = (lane >= first) & (lane < place) & (line == owner)
    rank = jnp.sum(earlier.astype(jnp.float32), axis=1, keepdims=True)
    source = (2 * CAP * owner + rank).astype(jnp.int32)
    shape = (rows, count * 2 * CAP)
    target = source + CAP * (rows_of(shape) // ch_dev)
    picker = (lanes_of(shape) == target).astype(jnp.float32).astype(jnp.bfloat16)
    sums = None
    for n in range(pairs):
        arrived = incoming_ref[:, 2 * CAP * n : 2 * CAP * (n + 1), :].reshape(count * 2 * CAP, columns)
        right = jnp.dot(picker, arrived, preferred_element_type=jnp.float32)
        left = own_ref[rows * n : rows * (n + 1), :].astype(jnp.float32)
        l = [left[:, q * H : (q + 1) * H] for q in range(4)]
        r = [right[:, q * H : (q + 1) * H] for q in range(4)]
        terms = [
            l[0] * r[0] + l[1] * r[1],
            l[2] * r[2] + l[3] * r[3],
            (l[1] * r[0] - l[0] * r[1]) + (l[2] * r[3] - l[3] * r[2]),
        ]
        sums = terms if sums is None else [total + term for total, term in zip(sums, terms)]
    stacks = jnp.concatenate(fold_columns(*[total[:ch_dev] + total[ch_dev:] for total in sums]), axis=1)
    out_ref[...] = lag_transform(stacks, high_ref[...], low_ref[...])


def fold_call(chan, incoming, own, owners, ch_dev, tables, earlier):
    return pl.pallas_call(
        fold_kernel,
        in_specs=[smem_spec()] + [vmem_spec()] * 5 + [pl.BlockSpec(memory_space=pl.ANY)],
        out_specs=vmem_spec(),
        out_shape=jax.ShapeDtypeStruct((ch_dev, NLAG), jnp.float32),
        compiler_params=pltpu.CompilerParams(vmem_limit_bytes=FOLD_VMEM_LIMIT),
        cost_estimate=pl.CostEstimate(
            flops=4 * ch_dev * incoming.size, bytes_accessed=2 * (incoming.size + own.size), transcendentals=0
        ),
        name="fold",
    )(chan, incoming, own, owners, *tables, earlier)


def from_above(block):
    count = lax.axis_size("chan")
    return lax.ppermute(block, "chan", [(i, i - 1) for i in range(1, count)])


def round_win(block, shift):
    count = lax.axis_size("win")
    return lax.ppermute(block, "win", [(i, (i + shift) % count) for i in range(count)])


def local(traces, quality, fold_block, fold_offset):
    win_dev, ch_dev, length = traces.shape
    chan_count = lax.axis_size("chan")
    win_count = lax.axis_size("win")
    window_part = lax.axis_index("win")
    own_count = ch_dev // win_count
    shared = ch_dev - own_count
    chan = lax.axis_index("chan").astype(jnp.int32).reshape(1)
    win = window_part.astype(jnp.int32).reshape(1)
    tables = [jnp.asarray(t) for t in inverse_tables(1.0 / math.sqrt(F * win_dev * win_count))]
    owners = fold_block.reshape(-1, 2 * ch_dev)
    places = fold_offset.reshape(-1, 2 * ch_dev)
    flat, outgoing, near, far, *ready = spectra_call(
        chan, traces.reshape(win_dev * ch_dev, length), quality.reshape(1, ch_dev), owners, places, chan_count, own_count
    )
    whitened = flat.reshape(win_dev, ch_dev, 2 * F)
    upper = [from_above(half.reshape(win_dev, ch_dev, F)) for half in (near, far)]
    ready = ready[0] if ready else whitened[:, shared:]
    common = [round_win(ready, shift) for shift in range(1, win_count)]
    incoming = lax.all_to_all(outgoing, "chan", split_axis=0, concat_axis=0, tiled=True)
    offered = jnp.concatenate([whitened[:, :shared], jnp.concatenate(upper, axis=2)], axis=1)
    special = [
        round_win(
            lax.dynamic_slice_in_dim(offered, (window_part + shift) % win_count * own_count, ch_dev, 1), shift
        )
        for shift in range(1, win_count)
    ]
    arrived = [(whitened, upper, [])] + [(rows, [others], []) for rows, others in zip(common, special)]
    sums = None
    for n, (first, second, awaited) in enumerate(arrived):
        ends = tables[0] if n == win_count - 1 else None
        sums, *done = cross_call(win, first, second, ch_dev, own_count, sums, ends, awaited)
    share = fold_call(chan, incoming, flat, owners, ch_dev, tables, done[0])
    fold = lax.dynamic_slice_in_dim(share, window_part * own_count, own_count, 0)
    for shift in range(1, win_count):
        target = (window_part + shift) % win_count * own_count
        fold = fold + round_win(lax.dynamic_slice_in_dim(share, target, own_count, 0), shift)
    return (sums, fold)


def solution(mesh):
    in_specs = (P("win", "chan", None), P("chan"), P(), P())
    out_specs = (P(("chan", "win"), None, None), P(("chan", "win"), None))
    return jax.shard_map(local, mesh=mesh, in_specs=in_specs, out_specs=out_specs, check_vma=False)
```

```python
import functools
import math

import jax
import jax.numpy as jnp
import numpy as np
from jax import lax
from jax.experimental import pallas as pl
from jax.experimental.pallas import tpu as pltpu
from jax.sharding import PartitionSpec as P

F = 256
H = F // 2
BAND_LO = 32
NLAG = 256
REACH = 64
CAP = 8
SPAN = REACH + 8
smooth_reach = 4
QUARTERS = 4
VMEM_LIMIT = 24 * 1024 * 1024
FOLD_VMEM_LIMIT = 16 * 1024 * 1024
SPECTRA_VMEM_LIMIT = 59 * 1024 * 1024


def bin_order():
    residues = np.arange(H)
    first = (residues - BAND_LO) % F
    second = (-residues - BAND_LO) % F
    second[0] = (H - BAND_LO) % F
    return first, second


def forward_table(length):
    samples = np.arange(length // 4, dtype=np.int64)[:, None]
    parts = []
    for bins in bin_order():
        angles = (samples * (bins + BAND_LO)[None, :] % length) * (2.0 * math.pi / length)
        parts += [np.cos(angles), -np.sin(angles)]
    return np.concatenate(parts, axis=1).astype(np.float32).astype(jnp.bfloat16)


def inverse_tables(factor):
    shifts = (np.arange(NLAG) + NLAG // 2)[None, :]
    residues = np.arange(H)[:, None]
    angles = (residues * shifts % NLAG) * (2.0 * math.pi / NLAG)
    sign = np.where(shifts[0] % 2 == 0, 1.0, -1.0)
    real, imag = np.cos(angles), -np.sin(angles)
    real[0] = (1.0 + sign) / 2.0
    imag[0] = (1.0 - sign) / 2.0
    table = np.concatenate([real, imag], axis=0) * factor
    high = table.astype(np.float32).astype(jnp.bfloat16)
    low = (table - high.astype(np.float64)).astype(np.float32).astype(jnp.bfloat16)
    return high, low


def lag_transform(stacks, high, low):
    top = stacks.astype(jnp.bfloat16)
    rest = (stacks - top.astype(jnp.float32)).astype(jnp.bfloat16)
    dot = functools.partial(jnp.dot, preferred_element_type=jnp.float32)
    return dot(top, high) + (dot(rest, high) + dot(top, low))


def fold_columns(first, second, imag):
    lane = lax.broadcasted_iota(jnp.int32, first.shape, first.ndim - 1)
    return first + second, jnp.where(lane == 0, first - second, imag)


def lanes_of(shape):
    return lax.broadcasted_iota(jnp.int32, shape, len(shape) - 1)


def rows_of(shape):
    return lax.broadcasted_iota(jnp.int32, shape, len(shape) - 2)


def band_matrix():
    def bins(index):
        lane = index & (H - 1)
        residue = jnp.where(index < H, lane, jnp.where(lane == 0, H, F - lane))
        return (residue - BAND_LO + F) & (F - 1)

    apart = bins(rows_of((F, F))) - bins(lanes_of((F, F)))
    return (jnp.abs(apart) <= smooth_reach).astype(jnp.float32).astype(jnp.bfloat16)


def exact_dot(left, right):
    return jnp.dot(left.astype(jnp.bfloat16), right.astype(jnp.bfloat16), preferred_element_type=jnp.float32)


def over(value, power):
    return value >> (power.bit_length() - 1)


def within(value, power):
    return value & (power - 1)


def slot_selector(owners, places, device, ch_dev):
    height, width = owners.shape
    per_row = width // ch_dev
    wanted = (owners == device).astype(jnp.float32)
    before = rows_of((width, width))
    after = lanes_of((width, width))
    earlier = ((before < after) & (over(before, ch_dev) == over(after, ch_dev))).astype(jnp.float32)
    ranks = exact_dot(wanted, earlier)
    slots = jnp.where(wanted > 0, ranks, float(CAP))
    count = height * per_row * 2 * CAP
    to_row = (over(rows_of((count, height)), 2 * CAP * per_row) == lanes_of((count, height))).astype(jnp.float32)
    row_slots = exact_dot(to_row, slots)
    row_places = exact_dot(to_row, places.astype(jnp.float32))
    shape = (count, width)
    row = rows_of(shape)
    mine = (row_slots == within(row, CAP).astype(jnp.float32)) & (
        over(lanes_of(shape), ch_dev) == within(over(row, 2 * CAP), per_row)
    )
    place = jnp.sum(jnp.where(mine, row_places + 1.0, 0.0), axis=1, keepdims=True).astype(jnp.int32) - 1
    shape = (count, 2 * ch_dev)
    half = within(over(rows_of(shape), CAP), 2)
    lane = lanes_of(shape)
    return ((lane == place + ch_dev * half) & (place >= 0)).astype(jnp.float32).astype(jnp.bfloat16)


def turned_sum(quarters, real, imag, negative):
    rows = quarters[0].shape[0]
    lane = lanes_of((rows, H))
    residue = ((F - lane) if negative else lane) & 3
    sign = jnp.where((residue & 1) == 0, 1.0, -1.0)
    straight = jnp.where(residue == 0, 1.0, jnp.where(residue == 2, -1.0, 0.0))
    turned = jnp.where(residue == 1, 1.0, jnp.where(residue == 3, -1.0, 0.0))
    re = [quarter[:, real * H : (real + 1) * H] for quarter in quarters]
    im = [quarter[:, imag * H : (imag + 1) * H] for quarter in quarters]
    odd_re, odd_im = re[1] + sign * re[3], im[1] + sign * im[3]
    return (
        re[0] + sign * re[2] + (straight * odd_re + turned * odd_im),
        im[0] + sign * im[2] + (straight * odd_im - turned * odd_re),
    )


def spectra_kernel(chan_ref, traces_ref, table_ref, quality_ref, owners_ref, places_ref, *refs):
    whitened_ref, outgoing_ref, near_ref, far_ref, *shared_ref = refs[:-13]
    traces, table, quality, owners, places, band, keep_rows, products, white, sent, selector, sems, out_sems = refs[-13:]
    row_parts, chunks, rows, depth = traces.shape
    ch_dev = quality.shape[1]
    pair = 2 * ch_dev
    count = outgoing_ref.shape[0]
    slots = sent.shape[2]

    def traces_copy(part, k):
        source = traces_ref.at[pl.ds(part * rows, rows), pl.ds(k * depth, depth)]
        return pltpu.make_async_copy(source, traces.at[part, k], sems.at[part, k])

    small = [
        pltpu.make_async_copy(source, target, sems.at[row_parts, k])
        for k, (source, target) in enumerate(
            ((table_ref, table), (quality_ref, quality), (owners_ref, owners), (places_ref, places))
        )
    ]
    for copy in small:
        copy.start()
    for part in range(row_parts):
        for k in range(chunks):
            traces_copy(part, k).start()

    small[0].wait()
    leaving = []

    def prepare():
        band[...] = band_matrix()
        for copy in small[1:]:
            copy.wait()
        shape = (rows, ch_dev)
        keep = jnp.sum(
            jnp.where(within(rows_of(shape), ch_dev) == lanes_of(shape), quality[...].astype(jnp.float32), 0.0),
            axis=1, keepdims=True,
        )
        selector[...] = slot_selector(owners[...], places[...], chan_ref[0], ch_dev)
        keep_rows[...] = jnp.broadcast_to(keep, keep_rows.shape)

    def transform(part):
        for k in range(chunks):
            traces_copy(part, k).wait()
        stacked = traces[part].reshape(chunks * rows, depth)
        products[part % 2] = jnp.dot(stacked, table[...], preferred_element_type=jnp.float32)

    def whiten(part):
        quarters = [products[part % 2, k * rows : (k + 1) * rows, :] for k in range(chunks)]
        parts = turned_sum(quarters, 0, 1, False) + turned_sum(quarters, 2, 3, True)
        energy = jnp.concatenate(
            [parts[0] * parts[0] + parts[1] * parts[1], parts[2] * parts[2] + parts[3] * parts[3]], axis=1
        )
        top = energy.astype(jnp.bfloat16)
        rest = (energy - top.astype(jnp.float32)).astype(jnp.bfloat16)
        smooth = jnp.dot(top, band[...], preferred_element_type=jnp.float32) + jnp.dot(
            rest, band[...], preferred_element_type=jnp.float32
        )
        water = jnp.sum(energy, axis=1, keepdims=True) * (1.0 / F)
        scaling = lax.rsqrt(smooth * (1.0 / (2.0 * smooth_reach + 1.0)) + (0.1 * water + 1e-06))
        near, far = scaling[:, :H] * keep_rows[...], scaling[:, H:] * keep_rows[...]
        values = jnp.concatenate(
            [parts[0] * near, parts[1] * near, parts[2] * far, parts[3] * far], axis=1
        ).astype(jnp.bfloat16)
        white[part] = values
        for n in range(rows // pair):
            chosen = jnp.dot(
                selector[...], values[pair * n : pair * (n + 1), :], preferred_element_type=jnp.float32
            ).astype(jnp.bfloat16)
            sent[part, :, 2 * CAP * n : 2 * CAP * (n + 1), :] = chosen.reshape(count, 2 * CAP, chosen.shape[-1])

    def leave(part):
        at = pl.ds(part * rows, rows)
        copies = [
            (white.at[part, :, pl.ds(0, F)], near_ref.at[at, :]),
            (white.at[part, :, pl.ds(F, F)], far_ref.at[at, :]),
            (sent.at[part], outgoing_ref.at[:, pl.ds(part * slots, slots), :]),
            (white.at[part], whitened_ref.at[at, :]),
        ]
        if shared_ref:
            height = shared_ref[0].shape[1]
            for w in range(rows // ch_dev):
                copies.append(
                    (
                        white.at[part, pl.ds((w + 1) * ch_dev - height, height), :],
                        shared_ref[0].at[part * (rows // ch_dev) + w],
                    )
                )
        for n, (source, target) in enumerate(copies):
            leaving.append(pltpu.make_async_copy(source, target, out_sems.at[part, n]))
            leaving[-1].start()

    for part in range(row_parts + 1):
        if part < row_parts:
            transform(part)
        if part == 0:
            prepare()
        else:
            whiten(part - 1)
            leave(part - 1)
    for copy in leaving:
        copy.wait()


def vmem_spec():
    return pl.BlockSpec(memory_space=pltpu.VMEM)


def smem_spec():
    return pl.BlockSpec(memory_space=pltpu.SMEM)


def whole(array):
    return pl.BlockSpec(array.shape, lambda s: (0,) * array.ndim)


def spectra_call(chan, traces, quality, owners, places, chan_count, own_count):
    rows, length = traces.shape
    ch_dev = quality.shape[1]
    row_steps = rows // (2 * ch_dev)
    part, depth = rows // row_steps, length // QUARTERS
    slots = part // (2 * ch_dev) * 2 * CAP
    anywhere = pl.BlockSpec(memory_space=pl.ANY)
    out_shape = [
        jax.ShapeDtypeStruct((rows, 2 * F), jnp.bfloat16),
        jax.ShapeDtypeStruct((chan_count, row_steps * slots, 2 * F), jnp.bfloat16),
        jax.ShapeDtypeStruct((rows, F), jnp.bfloat16),
        jax.ShapeDtypeStruct((rows, F), jnp.bfloat16),
    ]
    if own_count % 16 == 0:
        out_shape.append(jax.ShapeDtypeStruct((rows // ch_dev, own_count, 2 * F), jnp.bfloat16))
    return pl.pallas_call(
        spectra_kernel,
        in_specs=[smem_spec()] + [anywhere] * 5,
        out_specs=[anywhere] * len(out_shape),
        out_shape=out_shape,
        scratch_shapes=[
            pltpu.VMEM((row_steps, QUARTERS, part, depth), jnp.bfloat16),
            pltpu.VMEM((depth, 2 * F), jnp.bfloat16),
            pltpu.VMEM(quality.shape, jnp.int32),
            pltpu.VMEM(owners.shape, jnp.int32),
            pltpu.VMEM(places.shape, jnp.int32),
            pltpu.VMEM((F, F), jnp.bfloat16),
            pltpu.VMEM((part, H), jnp.float32),
            pltpu.VMEM((2, QUARTERS * part, 2 * F), jnp.float32),
            pltpu.VMEM((row_steps, part, 2 * F), jnp.bfloat16),
            pltpu.VMEM((row_steps, chan_count, slots, 2 * F), jnp.bfloat16),
            pltpu.VMEM((chan_count * 2 * CAP, 2 * ch_dev), jnp.bfloat16),
            pltpu.SemaphoreType.DMA((row_steps + 1, QUARTERS)),
            pltpu.SemaphoreType.DMA((row_steps, 4 + part // ch_dev)),
        ],
        compiler_params=pltpu.CompilerParams(vmem_limit_bytes=SPECTRA_VMEM_LIMIT),
        cost_estimate=pl.CostEstimate(
            flops=2 * rows * length * 2 * F, bytes_accessed=2 * rows * length, transcendentals=rows * F
        ),
        name="spectra",
    )(chan, traces, jnp.asarray(forward_table(length)), quality, owners, places)


def cross_kernel(last, with_sum, local_windows, skipped, win_ref, first_ref, second_ref, *refs):
    refs = list(refs)
    far_ref = refs.pop(0) if local_windows else None
    sum_ref = refs.pop(0) if with_sum else None
    if last:
        table_ref, out_ref, done_ref, wide, spread, total, lags, sems = refs
        done_ref[...] = jnp.zeros_like(done_ref)
    else:
        out_ref, wide, spread = refs
        total = out_ref
    windows, own_count = spread.shape[:2]
    ch_dev = wide.shape[1] // 2
    base = pl.multiple_of(win_ref[0] * own_count, 8)

    def widen(w, carry):
        if local_windows:
            wide[w, :ch_dev, :] = first_ref[w].astype(jnp.float32)
            wide[w, ch_dev:, :F] = second_ref[w].astype(jnp.float32)
            wide[w, ch_dev:, F:] = far_ref[w].astype(jnp.float32)
        else:
            shared = ch_dev - own_count
            wide[w, shared:ch_dev, :] = first_ref[skipped + w].astype(jnp.float32)
            rows = second_ref[w].astype(jnp.float32)
            for tile in range(ch_dev // 8):
                at = base + 8 * tile
                at = pl.multiple_of(jnp.where(at < shared, at, at + own_count), 8)
                wide[w, pl.ds(at, 8), :] = rows[8 * tile : 8 * tile + 8]
        for tile in range(own_count // 8):
            rows = wide[w, pl.ds(pl.multiple_of(base + 8 * tile, 8), 8), :]
            for i in range(8):
                for q in range(4):
                    spread[w, 8 * tile + i, q] = jnp.broadcast_to(rows[i : i + 1, q * H : (q + 1) * H], (8, H))
        return carry

    lax.fori_loop(0, windows, widen, 0)

    group, tiles = 4, 3
    rounds = SPAN // (8 * tiles)

    def block(index, carry):
        g = index // rounds
        j = index % rounds
        start = pl.multiple_of(base + 8 * (g // 2) + 8 * tiles * j, 8)

        def add_window(w, sums):
            sums = list(sums)
            right = [
                [wide[w, pl.ds(pl.multiple_of(start + 8 * t, 8), 8), q * H : (q + 1) * H] for q in range(4)]
                for t in range(tiles)
            ]
            for i in range(group):
                left = [spread[w, group * g + i, q] for q in range(4)]
                for t in range(tiles):
                    at = 3 * (i * tiles + t)
                    r = right[t]
                    sums[at] = sums[at] + (left[0] * r[0] + left[1] * r[1])
                    sums[at + 1] = sums[at + 1] + (left[2] * r[2] + left[3] * r[3])
                    sums[at + 2] = sums[at + 2] + ((left[1] * r[0] - left[0] * r[1]) + (left[2] * r[3] - left[3] * r[2]))
            return tuple(sums)

        zero = jnp.zeros((8, H), jnp.float32)
        sums = lax.fori_loop(0, windows, add_window, (zero,) * (3 * group * tiles), unroll=2)
        for i in range(group):
            for t in range(tiles):
                at = 3 * (i * tiles + t)
                real, imag = fold_columns(sums[at], sums[at + 1], sums[at + 2])
                where = pl.ds(pl.multiple_of(8 * tiles * j + 8 * t, 8), 8)
                if with_sum:
                    real = real + sum_ref[group * g + i, where, :H]
                    imag = imag + sum_ref[group * g + i, where, H:]
                total[group * g + i, where, :H] = real
                total[group * g + i, where, H:] = imag
        return carry

    lax.fori_loop(0, own_count // group * rounds, block, 0)

    if last:
        copies = []
        for eight in range(own_count // 8):
            first = 8 * eight
            stacks = total[first : first + 8].reshape(8 * SPAN, F).astype(jnp.bfloat16)
            lagged = jnp.dot(stacks, table_ref[...], preferred_element_type=jnp.float32).reshape(8, SPAN, NLAG)
            for i in range(8):
                lags[first + i] = lagged[i, i + 1 : i + 1 + REACH, :]
            some = pl.ds(first, 8)
            copies.append(pltpu.make_async_copy(lags.at[some], out_ref.at[some], sems.at[eight]))
            copies[-1].start()
        for copy in copies:
            copy.wait()


def cross_call(win, first, second, ch_dev, own_count, sums, table, skipped, share):
    local_windows = len(second) == 2
    windows, _, columns = second[0].shape
    columns = first.shape[2]
    last = table is not None
    with_sum = sums is not None
    operands = [win, first, *second]
    if with_sum:
        operands.append(sums)
    scratch = [
        pltpu.VMEM((windows, 2 * ch_dev, columns), jnp.float32),
        pltpu.VMEM((windows, own_count, 4, 8, H), jnp.float32),
    ]
    if last:
        operands.append(table)
        scratch += [
            pltpu.VMEM((own_count, SPAN, F), jnp.float32),
            pltpu.VMEM((own_count, REACH, NLAG), jnp.float32),
            pltpu.SemaphoreType.DMA((own_count // 8,)),
        ]
    shape = (own_count, REACH, NLAG) if last else (own_count, SPAN, F)
    out_shape, out_specs = [jax.ShapeDtypeStruct(shape, jnp.float32)], [vmem_spec()]
    if last:
        out_shape.append(jax.ShapeDtypeStruct((8, H), jnp.float32))
        out_specs = [pl.BlockSpec(memory_space=pl.ANY), vmem_spec()]
    return pl.pallas_call(
        functools.partial(cross_kernel, last, with_sum, local_windows, skipped),
        in_specs=[smem_spec()] + [vmem_spec()] * (len(operands) - 1),
        out_specs=out_specs,
        out_shape=out_shape,
        scratch_shapes=scratch,
        compiler_params=pltpu.CompilerParams(vmem_limit_bytes=VMEM_LIMIT),
        cost_estimate=pl.CostEstimate(
            flops=int(30_000_000_000 * share), bytes_accessed=4 * windows * ch_dev * columns + 4 * own_count * SPAN * F, transcendentals=0
        ),
        name="cross",
    )(*operands)


def fold_kernel(chan_ref, incoming_ref, own_ref, owners_ref, high_ref, low_ref, earlier_ref, out_ref):
    ch_dev = out_ref.shape[0]
    rows = 2 * ch_dev
    pairs = own_ref.shape[0] // rows
    count, slots, columns = incoming_ref.shape
    owners = owners_ref[...].astype(jnp.float32)
    per_row = owners.shape[1] // ch_dev
    device = chan_ref[0]
    line = jnp.sum(jnp.where(rows_of(owners.shape) == device // per_row, owners, 0.0), axis=0, keepdims=True)
    shape = (rows, owners.shape[1])
    line = jnp.broadcast_to(line, shape)
    first = device % per_row * ch_dev
    place = first + rows_of(shape) % ch_dev
    lane = lanes_of(shape)
    owner = jnp.sum(jnp.where(lane == place, line, 0.0), axis=1, keepdims=True)
    earlier = (lane >= first) & (lane < place) & (line == owner)
    rank = jnp.sum(earlier.astype(jnp.float32), axis=1, keepdims=True)
    source = (2 * CAP * owner + rank).astype(jnp.int32)
    shape = (rows, count * 2 * CAP)
    target = source + CAP * (rows_of(shape) // ch_dev)
    picker = (lanes_of(shape) == target).astype(jnp.float32).astype(jnp.bfloat16)
    sums = None
    for n in range(pairs):
        arrived = incoming_ref[:, 2 * CAP * n : 2 * CAP * (n + 1), :].reshape(count * 2 * CAP, columns)
        right = jnp.dot(picker, arrived, preferred_element_type=jnp.float32)
        left = own_ref[rows * n : rows * (n + 1), :].astype(jnp.float32)
        l = [left[:, q * H : (q + 1) * H] for q in range(4)]
        r = [right[:, q * H : (q + 1) * H] for q in range(4)]
        terms = [
            l[0] * r[0] + l[1] * r[1],
            l[2] * r[2] + l[3] * r[3],
            (l[1] * r[0] - l[0] * r[1]) + (l[2] * r[3] - l[3] * r[2]),
        ]
        sums = terms if sums is None else [total + term for total, term in zip(sums, terms)]
    stacks = jnp.concatenate(fold_columns(*[total[:ch_dev] + total[ch_dev:] for total in sums]), axis=1)
    out_ref[...] = lag_transform(stacks, high_ref[...], low_ref[...])


def fold_call(chan, incoming, own, owners, ch_dev, tables, earlier):
    return pl.pallas_call(
        fold_kernel,
        in_specs=[smem_spec()] + [vmem_spec()] * 5 + [pl.BlockSpec(memory_space=pl.ANY)],
        out_specs=vmem_spec(),
        out_shape=jax.ShapeDtypeStruct((ch_dev, NLAG), jnp.float32),
        compiler_params=pltpu.CompilerParams(vmem_limit_bytes=FOLD_VMEM_LIMIT),
        cost_estimate=pl.CostEstimate(
            flops=4 * ch_dev * incoming.size, bytes_accessed=2 * (incoming.size + own.size), transcendentals=0
        ),
        name="fold",
    )(chan, incoming, own, owners, *tables, earlier)


def from_above(block):
    count = lax.axis_size("chan")
    return lax.ppermute(block, "chan", [(i, i - 1) for i in range(1, count)])


def round_win(block, shift):
    count = lax.axis_size("win")
    return lax.ppermute(block, "win", [(i, (i + shift) % count) for i in range(count)])


def local(traces, quality, fold_block, fold_offset):
    win_dev, ch_dev, length = traces.shape
    chan_count = lax.axis_size("chan")
    win_count = lax.axis_size("win")
    window_part = lax.axis_index("win")
    own_count = ch_dev // win_count
    shared = ch_dev - own_count
    chan = lax.axis_index("chan").astype(jnp.int32).reshape(1)
    win = window_part.astype(jnp.int32).reshape(1)
    tables = [jnp.asarray(t) for t in inverse_tables(1.0 / math.sqrt(F * win_dev * win_count))]
    owners = fold_block.reshape(-1, 2 * ch_dev)
    places = fold_offset.reshape(-1, 2 * ch_dev)
    flat, outgoing, near, far, *ready = spectra_call(
        chan, traces.reshape(win_dev * ch_dev, length), quality.reshape(1, ch_dev), owners, places, chan_count, own_count
    )
    whitened = flat.reshape(win_dev, ch_dev, 2 * F)
    upper = [from_above(half.reshape(win_dev, ch_dev, F)) for half in (near, far)]
    ready = ready[0] if ready else whitened[:, shared:]
    common = [round_win(ready, shift) for shift in range(1, win_count)]
    incoming = lax.all_to_all(outgoing, "chan", split_axis=0, concat_axis=0, tiled=True)
    offered = jnp.concatenate([whitened[:, :shared], jnp.concatenate(upper, axis=2)], axis=1)
    half = win_dev // 2
    special = []
    for shift, rows in enumerate(common, 1):
        target = (window_part + shift) % win_count * own_count
        mark = rows[0, 0, 0]
        starts = (target, target + (mark != mark).astype(jnp.int32))
        special.append([
            round_win(lax.dynamic_slice_in_dim(offered[n * half : (n + 1) * half], start, ch_dev, 1), shift)
            for n, start in enumerate(starts)
        ])
    arrived = [(whitened, upper, 0, 1.0)]
    for rows, others in zip(common, special):
        arrived += [(rows, [part], n * half, 0.5) for n, part in enumerate(others)]
    sums = None
    for n, (first, second, skipped, part) in enumerate(arrived):
        ends = tables[0] if n == len(arrived) - 1 else None
        sums, *done = cross_call(win, first, second, ch_dev, own_count, sums, ends, skipped, part)
    share = fold_call(chan, incoming, flat, owners, ch_dev, tables, done[0])
    fold = lax.dynamic_slice_in_dim(share, window_part * own_count, own_count, 0)
    for shift in range(1, win_count):
        target = (window_part + shift) % win_count * own_count
        fold = fold + round_win(lax.dynamic_slice_in_dim(share, target, own_count, 0), shift)
    return (sums, fold)


def solution(mesh):
    in_specs = (P("win", "chan", None), P("chan"), P(), P())
    out_specs = (P(("chan", "win"), None, None), P(("chan", "win"), None))
    return jax.shard_map(local, mesh=mesh, in_specs=in_specs, out_specs=out_specs, check_vma=False)
```

```python
import functools
import math

import jax
import jax.numpy as jnp
import numpy as np
from jax import lax
from jax.experimental import pallas as pl
from jax.experimental.pallas import tpu as pltpu
from jax.sharding import PartitionSpec as P

F = 256
H = F // 2
BAND_LO = 32
NLAG = 256
REACH = 64
CAP = 8
SPAN = REACH + 8
smooth_reach = 4
QUARTERS = 4
VMEM_LIMIT = 24 * 1024 * 1024
FOLD_VMEM_LIMIT = 16 * 1024 * 1024
SPECTRA_VMEM_LIMIT = 59 * 1024 * 1024


def bin_order():
    residues = np.arange(H)
    first = (residues - BAND_LO) % F
    second = (-residues - BAND_LO) % F
    second[0] = (H - BAND_LO) % F
    return first, second


def forward_table(length):
    samples = np.arange(length // 4, dtype=np.int64)[:, None]
    parts = []
    for bins in bin_order():
        angles = (samples * (bins + BAND_LO)[None, :] % length) * (2.0 * math.pi / length)
        parts += [np.cos(angles), -np.sin(angles)]
    return np.concatenate(parts, axis=1).astype(np.float32).astype(jnp.bfloat16)


def inverse_tables(factor):
    shifts = (np.arange(NLAG) + NLAG // 2)[None, :]
    residues = np.arange(H)[:, None]
    angles = (residues * shifts % NLAG) * (2.0 * math.pi / NLAG)
    sign = np.where(shifts[0] % 2 == 0, 1.0, -1.0)
    real, imag = np.cos(angles), -np.sin(angles)
    real[0] = (1.0 + sign) / 2.0
    imag[0] = (1.0 - sign) / 2.0
    table = np.concatenate([real, imag], axis=0) * factor
    high = table.astype(np.float32).astype(jnp.bfloat16)
    low = (table - high.astype(np.float64)).astype(np.float32).astype(jnp.bfloat16)
    return high, low


def lag_transform(stacks, high, low):
    top = stacks.astype(jnp.bfloat16)
    rest = (stacks - top.astype(jnp.float32)).astype(jnp.bfloat16)
    dot = functools.partial(jnp.dot, preferred_element_type=jnp.float32)
    return dot(top, high) + (dot(rest, high) + dot(top, low))


def fold_columns(first, second, imag):
    lane = lax.broadcasted_iota(jnp.int32, first.shape, first.ndim - 1)
    return first + second, jnp.where(lane == 0, first - second, imag)


def lanes_of(shape):
    return lax.broadcasted_iota(jnp.int32, shape, len(shape) - 1)


def rows_of(shape):
    return lax.broadcasted_iota(jnp.int32, shape, len(shape) - 2)


def band_matrix():
    def bins(index):
        lane = index & (H - 1)
        residue = jnp.where(index < H, lane, jnp.where(lane == 0, H, F - lane))
        return (residue - BAND_LO + F) & (F - 1)

    apart = bins(rows_of((F, F))) - bins(lanes_of((F, F)))
    return (jnp.abs(apart) <= smooth_reach).astype(jnp.float32).astype(jnp.bfloat16)


def exact_dot(left, right):
    return jnp.dot(left.astype(jnp.bfloat16), right.astype(jnp.bfloat16), preferred_element_type=jnp.float32)


def over(value, power):
    return value >> (power.bit_length() - 1)


def within(value, power):
    return value & (power - 1)


def slot_selector(owners, places, device, ch_dev):
    height, width = owners.shape
    per_row = width // ch_dev
    wanted = (owners == device).astype(jnp.float32)
    before = rows_of((width, width))
    after = lanes_of((width, width))
    earlier = ((before < after) & (over(before, ch_dev) == over(after, ch_dev))).astype(jnp.float32)
    ranks = exact_dot(wanted, earlier)
    slots = jnp.where(wanted > 0, ranks, float(CAP))
    count = height * per_row * 2 * CAP
    to_row = (over(rows_of((count, height)), 2 * CAP * per_row) == lanes_of((count, height))).astype(jnp.float32)
    row_slots = exact_dot(to_row, slots)
    row_places = exact_dot(to_row, places.astype(jnp.float32))
    shape = (count, width)
    row = rows_of(shape)
    mine = (row_slots == within(row, CAP).astype(jnp.float32)) & (
        over(lanes_of(shape), ch_dev) == within(over(row, 2 * CAP), per_row)
    )
    place = jnp.sum(jnp.where(mine, row_places + 1.0, 0.0), axis=1, keepdims=True).astype(jnp.int32) - 1
    shape = (count, 2 * ch_dev)
    half = within(over(rows_of(shape), CAP), 2)
    lane = lanes_of(shape)
    return ((lane == place + ch_dev * half) & (place >= 0)).astype(jnp.float32).astype(jnp.bfloat16)


def turned_sum(quarters, real, imag, negative):
    rows = quarters[0].shape[0]
    lane = lanes_of((rows, H))
    residue = ((F - lane) if negative else lane) & 3
    sign = jnp.where((residue & 1) == 0, 1.0, -1.0)
    straight = jnp.where(residue == 0, 1.0, jnp.where(residue == 2, -1.0, 0.0))
    turned = jnp.where(residue == 1, 1.0, jnp.where(residue == 3, -1.0, 0.0))
    re = [quarter[:, real * H : (real + 1) * H] for quarter in quarters]
    im = [quarter[:, imag * H : (imag + 1) * H] for quarter in quarters]
    odd_re, odd_im = re[1] + sign * re[3], im[1] + sign * im[3]
    return (
        re[0] + sign * re[2] + (straight * odd_re + turned * odd_im),
        im[0] + sign * im[2] + (straight * odd_im - turned * odd_re),
    )


def spectra_kernel(chan_ref, traces_ref, table_ref, quality_ref, owners_ref, places_ref, *refs):
    early_ref, late_ref, outgoing_ref, *shared_ref = refs[:-13]
    traces, table, quality, owners, places, band, keep_rows, products, white, sent, selector, sems, out_sems = refs[-13:]
    row_parts, chunks, rows, depth = traces.shape
    ch_dev = quality.shape[1]
    pair = 2 * ch_dev
    count = outgoing_ref.shape[0]
    slots = sent.shape[2]

    def traces_copy(part, k):
        source = traces_ref.at[pl.ds(part * rows, rows), pl.ds(k * depth, depth)]
        return pltpu.make_async_copy(source, traces.at[part, k], sems.at[part, k])

    small = [
        pltpu.make_async_copy(source, target, sems.at[row_parts, k])
        for k, (source, target) in enumerate(
            ((table_ref, table), (quality_ref, quality), (owners_ref, owners), (places_ref, places))
        )
    ]
    for copy in small:
        copy.start()
    for part in range(row_parts):
        for k in range(chunks):
            traces_copy(part, k).start()

    small[0].wait()
    leaving = []

    def prepare():
        band[...] = band_matrix()
        for copy in small[1:]:
            copy.wait()
        shape = (rows, ch_dev)
        keep = jnp.sum(
            jnp.where(within(rows_of(shape), ch_dev) == lanes_of(shape), quality[...].astype(jnp.float32), 0.0),
            axis=1, keepdims=True,
        )
        selector[...] = slot_selector(owners[...], places[...], chan_ref[0], ch_dev)
        keep_rows[...] = jnp.broadcast_to(keep, keep_rows.shape)

    def transform(part):
        for k in range(chunks):
            traces_copy(part, k).wait()
        stacked = traces[part].reshape(chunks * rows, depth)
        products[part % 2] = jnp.dot(stacked, table[...], preferred_element_type=jnp.float32)

    def whiten(part):
        quarters = [products[part % 2, k * rows : (k + 1) * rows, :] for k in range(chunks)]
        parts = turned_sum(quarters, 0, 1, False) + turned_sum(quarters, 2, 3, True)
        energy = jnp.concatenate(
            [parts[0] * parts[0] + parts[1] * parts[1], parts[2] * parts[2] + parts[3] * parts[3]], axis=1
        )
        top = energy.astype(jnp.bfloat16)
        rest = (energy - top.astype(jnp.float32)).astype(jnp.bfloat16)
        smooth = jnp.dot(top, band[...], preferred_element_type=jnp.float32) + jnp.dot(
            rest, band[...], preferred_element_type=jnp.float32
        )
        water = jnp.sum(energy, axis=1, keepdims=True) * (1.0 / F)
        scaling = lax.rsqrt(smooth * (1.0 / (2.0 * smooth_reach + 1.0)) + (0.1 * water + 1e-06))
        near, far = scaling[:, :H] * keep_rows[...], scaling[:, H:] * keep_rows[...]
        values = jnp.concatenate(
            [parts[0] * near, parts[1] * near, parts[2] * far, parts[3] * far], axis=1
        ).astype(jnp.bfloat16)
        white[part] = values
        for n in range(rows // pair):
            chosen = jnp.dot(
                selector[...], values[pair * n : pair * (n + 1), :], preferred_element_type=jnp.float32
            ).astype(jnp.bfloat16)
            sent[part, :, 2 * CAP * n : 2 * CAP * (n + 1), :] = chosen.reshape(count, 2 * CAP, chosen.shape[-1])

    def leave(part):
        late, place = divmod(part, row_parts // 2)
        copies = [
            (white.at[part], (early_ref, late_ref)[late].at[pl.ds(place * rows, rows), :]),
            (sent.at[part], outgoing_ref.at[:, pl.ds(part * slots, slots), :]),
        ]
        if shared_ref:
            height = shared_ref[0].shape[1]
            for w in range(rows // ch_dev):
                copies.append(
                    (
                        white.at[part, pl.ds((w + 1) * ch_dev - height, height), :],
                        shared_ref[0].at[part * (rows // ch_dev) + w],
                    )
                )
        for n, (source, target) in enumerate(copies):
            leaving.append(pltpu.make_async_copy(source, target, out_sems.at[part, n]))
            leaving[-1].start()

    for part in range(row_parts + 1):
        if part < row_parts:
            transform(part)
        if part == 0:
            prepare()
        else:
            whiten(part - 1)
            leave(part - 1)
    for copy in leaving:
        copy.wait()


def vmem_spec():
    return pl.BlockSpec(memory_space=pltpu.VMEM)


def smem_spec():
    return pl.BlockSpec(memory_space=pltpu.SMEM)


def whole(array):
    return pl.BlockSpec(array.shape, lambda s: (0,) * array.ndim)


def spectra_call(chan, traces, quality, owners, places, chan_count, own_count):
    rows, length = traces.shape
    ch_dev = quality.shape[1]
    row_steps = rows // (2 * ch_dev)
    part, depth = rows // row_steps, length // QUARTERS
    slots = part // (2 * ch_dev) * 2 * CAP
    anywhere = pl.BlockSpec(memory_space=pl.ANY)
    out_shape = [
        jax.ShapeDtypeStruct((rows // 2, 2 * F), jnp.bfloat16),
        jax.ShapeDtypeStruct((rows // 2, 2 * F), jnp.bfloat16),
        jax.ShapeDtypeStruct((chan_count, row_steps * slots, 2 * F), jnp.bfloat16),
    ]
    if own_count % 16 == 0:
        out_shape.append(jax.ShapeDtypeStruct((rows // ch_dev, own_count, 2 * F), jnp.bfloat16))
    return pl.pallas_call(
        spectra_kernel,
        in_specs=[smem_spec()] + [anywhere] * 5,
        out_specs=[anywhere] * len(out_shape),
        out_shape=out_shape,
        scratch_shapes=[
            pltpu.VMEM((row_steps, QUARTERS, part, depth), jnp.bfloat16),
            pltpu.VMEM((depth, 2 * F), jnp.bfloat16),
            pltpu.VMEM(quality.shape, jnp.int32),
            pltpu.VMEM(owners.shape, jnp.int32),
            pltpu.VMEM(places.shape, jnp.int32),
            pltpu.VMEM((F, F), jnp.bfloat16),
            pltpu.VMEM((part, H), jnp.float32),
            pltpu.VMEM((2, QUARTERS * part, 2 * F), jnp.float32),
            pltpu.VMEM((row_steps, part, 2 * F), jnp.bfloat16),
            pltpu.VMEM((row_steps, chan_count, slots, 2 * F), jnp.bfloat16),
            pltpu.VMEM((chan_count * 2 * CAP, 2 * ch_dev), jnp.bfloat16),
            pltpu.SemaphoreType.DMA((row_steps + 1, QUARTERS)),
            pltpu.SemaphoreType.DMA((row_steps, 2 + part // ch_dev)),
        ],
        compiler_params=pltpu.CompilerParams(vmem_limit_bytes=SPECTRA_VMEM_LIMIT),
        cost_estimate=pl.CostEstimate(
            flops=2 * rows * length * 2 * F, bytes_accessed=2 * rows * length, transcendentals=rows * F
        ),
        name="spectra",
    )(chan, traces, jnp.asarray(forward_table(length)), quality, owners, places)


def cross_kernel(last, with_sum, skipped, win_ref, *refs):
    refs = list(refs)
    blocks = [refs.pop(0) for _ in range(2 if with_sum else 4)]
    sum_ref = refs.pop(0) if with_sum else None
    if last:
        table_ref, out_ref, zero_ref, wide, spread, total, lags, sems = refs
    else:
        total, zero_ref, wide, spread = refs
    zero_ref[0] = 0
    windows, own_count = spread.shape[:2]
    ch_dev = wide.shape[1] // 2
    base = pl.multiple_of(win_ref[0] * own_count, 8)

    def widen(w, carry):
        if with_sum:
            shared = ch_dev - own_count
            wide[w, shared:ch_dev, :] = blocks[0][skipped + w].astype(jnp.float32)
            rows = blocks[1][w].astype(jnp.float32)
            for tile in range(ch_dev // 8):
                at = base + 8 * tile
                at = pl.multiple_of(jnp.where(at < shared, at, at + own_count), 8)
                wide[w, pl.ds(at, 8), :] = rows[8 * tile : 8 * tile + 8]
        else:
            for half in range(2):
                place = half * (windows // 2) + w
                wide[place, :ch_dev, :] = blocks[half][w].astype(jnp.float32)
                wide[place, ch_dev:, :] = blocks[2 + half][w].astype(jnp.float32)
        return carry

    lax.fori_loop(0, windows if with_sum else windows // 2, widen, 0)

    def repeat(w, carry):
        for tile in range(own_count // 8):
            rows = wide[w, pl.ds(pl.multiple_of(base + 8 * tile, 8), 8), :]
            for i in range(8):
                for q in range(4):
                    spread[w, 8 * tile + i, q] = jnp.broadcast_to(rows[i : i + 1, q * H : (q + 1) * H], (8, H))
        return carry

    lax.fori_loop(0, windows, repeat, 0)

    group, tiles = 4, 3
    rounds = SPAN // (8 * tiles)

    def block(index, carry):
        g = index // rounds
        j = index % rounds
        start = pl.multiple_of(base + 8 * (g // 2) + 8 * tiles * j, 8)

        def add_window(w, sums):
            sums = list(sums)
            right = [
                [wide[w, pl.ds(pl.multiple_of(start + 8 * t, 8), 8), q * H : (q + 1) * H] for q in range(4)]
                for t in range(tiles)
            ]
            for i in range(group):
                left = [spread[w, group * g + i, q] for q in range(4)]
                for t in range(tiles):
                    at = 3 * (i * tiles + t)
                    r = right[t]
                    sums[at] = sums[at] + (left[0] * r[0] + left[1] * r[1])
                    sums[at + 1] = sums[at + 1] + (left[2] * r[2] + left[3] * r[3])
                    sums[at + 2] = sums[at + 2] + ((left[1] * r[0] - left[0] * r[1]) + (left[2] * r[3] - left[3] * r[2]))
            return tuple(sums)

        zero = jnp.zeros((8, H), jnp.float32)
        sums = lax.fori_loop(0, windows, add_window, (zero,) * (3 * group * tiles), unroll=2)
        for i in range(group):
            for t in range(tiles):
                at = 3 * (i * tiles + t)
                real, imag = fold_columns(sums[at], sums[at + 1], sums[at + 2])
                where = pl.ds(pl.multiple_of(8 * tiles * j + 8 * t, 8), 8)
                if with_sum:
                    real = real + sum_ref[group * g + i, where, :H]
                    imag = imag + sum_ref[group * g + i, where, H:]
                total[group * g + i, where, :H] = real
                total[group * g + i, where, H:] = imag
        return carry

    lax.fori_loop(0, own_count // group * rounds, block, 0)

    if last:
        copies = []
        for eight in range(own_count // 8):
            first = 8 * eight
            stacks = total[first : first + 8].reshape(8 * SPAN, F).astype(jnp.bfloat16)
            lagged = jnp.dot(stacks, table_ref[...], preferred_element_type=jnp.float32).reshape(8, SPAN, NLAG)
            for i in range(8):
                lags[first + i] = lagged[i, i + 1 : i + 1 + REACH, :]
            some = pl.ds(first, 8)
            copies.append(pltpu.make_async_copy(lags.at[some], out_ref.at[some], sems.at[eight]))
            copies[-1].start()
        for copy in copies:
            copy.wait()


def cross_call(win, blocks, windows, ch_dev, own_count, sums, table, skipped, share):
    columns = 2 * F
    last = table is not None
    with_sum = sums is not None
    operands = [win, *blocks]
    if with_sum:
        operands.append(sums)
    scratch = [
        pltpu.VMEM((windows, 2 * ch_dev, columns), jnp.float32),
        pltpu.VMEM((windows, own_count, 4, 8, H), jnp.float32),
    ]
    if last:
        operands.append(table)
        scratch += [
            pltpu.VMEM((own_count, SPAN, F), jnp.float32),
            pltpu.VMEM((own_count, REACH, NLAG), jnp.float32),
            pltpu.SemaphoreType.DMA((own_count // 8,)),
        ]
    shape = (own_count, REACH, NLAG) if last else (own_count, SPAN, F)
    out_shape = [jax.ShapeDtypeStruct(shape, jnp.float32), jax.ShapeDtypeStruct((1,), jnp.int32)]
    out_specs = [pl.BlockSpec(memory_space=pl.ANY) if last else vmem_spec(), smem_spec()]
    return pl.pallas_call(
        functools.partial(cross_kernel, last, with_sum, skipped),
        in_specs=[smem_spec()] + [vmem_spec()] * (len(operands) - 1),
        out_specs=out_specs,
        out_shape=out_shape,
        scratch_shapes=scratch,
        compiler_params=pltpu.CompilerParams(vmem_limit_bytes=VMEM_LIMIT),
        cost_estimate=pl.CostEstimate(
            flops=int(30_000_000_000 * share), bytes_accessed=4 * windows * ch_dev * columns + 4 * own_count * SPAN * F, transcendentals=0
        ),
        name="cross",
    )(*operands)


def fold_kernel(chan_ref, incoming_ref, early_ref, late_ref, owners_ref, high_ref, low_ref, earlier_ref, out_ref):
    ch_dev = out_ref.shape[0]
    rows = 2 * ch_dev
    pairs = 2 * early_ref.shape[0] // rows
    count, slots, columns = incoming_ref.shape
    owners = owners_ref[...].astype(jnp.float32)
    per_row = owners.shape[1] // ch_dev
    device = chan_ref[0]
    line = jnp.sum(jnp.where(rows_of(owners.shape) == device // per_row, owners, 0.0), axis=0, keepdims=True)
    shape = (rows, owners.shape[1])
    line = jnp.broadcast_to(line, shape)
    first = device % per_row * ch_dev
    place = first + rows_of(shape) % ch_dev
    lane = lanes_of(shape)
    owner = jnp.sum(jnp.where(lane == place, line, 0.0), axis=1, keepdims=True)
    earlier = (lane >= first) & (lane < place) & (line == owner)
    rank = jnp.sum(earlier.astype(jnp.float32), axis=1, keepdims=True)
    source = (2 * CAP * owner + rank).astype(jnp.int32)
    shape = (rows, count * 2 * CAP)
    target = source + CAP * (rows_of(shape) // ch_dev)
    picker = (lanes_of(shape) == target).astype(jnp.float32).astype(jnp.bfloat16)
    sums = None
    for n in range(pairs):
        arrived = incoming_ref[:, 2 * CAP * n : 2 * CAP * (n + 1), :].reshape(count * 2 * CAP, columns)
        right = jnp.dot(picker, arrived, preferred_element_type=jnp.float32)
        late, place = divmod(n, pairs // 2)
        left = (early_ref, late_ref)[late][rows * place : rows * (place + 1), :].astype(jnp.float32)
        l = [left[:, q * H : (q + 1) * H] for q in range(4)]
        r = [right[:, q * H : (q + 1) * H] for q in range(4)]
        terms = [
            l[0] * r[0] + l[1] * r[1],
            l[2] * r[2] + l[3] * r[3],
            (l[1] * r[0] - l[0] * r[1]) + (l[2] * r[3] - l[3] * r[2]),
        ]
        sums = terms if sums is None else [total + term for total, term in zip(sums, terms)]
    stacks = jnp.concatenate(fold_columns(*[total[:ch_dev] + total[ch_dev:] for total in sums]), axis=1)
    out_ref[...] = lag_transform(stacks, high_ref[...], low_ref[...])


def fold_call(chan, incoming, early, late, owners, ch_dev, tables, earlier):
    return pl.pallas_call(
        fold_kernel,
        in_specs=[smem_spec()] + [vmem_spec()] * 6 + [smem_spec()],
        out_specs=vmem_spec(),
        out_shape=jax.ShapeDtypeStruct((ch_dev, NLAG), jnp.float32),
        compiler_params=pltpu.CompilerParams(vmem_limit_bytes=FOLD_VMEM_LIMIT),
        cost_estimate=pl.CostEstimate(
            flops=4 * ch_dev * incoming.size, bytes_accessed=2 * (incoming.size + 2 * early.size), transcendentals=0
        ),
        name="fold",
    )(chan, incoming, early, late, owners, *tables, earlier)


def from_above(block):
    count = lax.axis_size("chan")
    return lax.ppermute(block, "chan", [(i, i - 1) for i in range(1, count)])


def round_win(block, shift):
    count = lax.axis_size("win")
    return lax.ppermute(block, "win", [(i, (i + shift) % count) for i in range(count)])


def local(traces, quality, fold_block, fold_offset):
    win_dev, ch_dev, length = traces.shape
    chan_count = lax.axis_size("chan")
    win_count = lax.axis_size("win")
    window_part = lax.axis_index("win")
    own_count = ch_dev // win_count
    shared = ch_dev - own_count
    chan = lax.axis_index("chan").astype(jnp.int32).reshape(1)
    win = window_part.astype(jnp.int32).reshape(1)
    tables = [jnp.asarray(t) for t in inverse_tables(1.0 / math.sqrt(F * win_dev * win_count))]
    owners = fold_block.reshape(-1, 2 * ch_dev)
    places = fold_offset.reshape(-1, 2 * ch_dev)
    early, late, outgoing, *ready = spectra_call(
        chan, traces.reshape(win_dev * ch_dev, length), quality.reshape(1, ch_dev), owners, places, chan_count, own_count
    )
    half = win_dev // 2
    halves = [rows.reshape(half, ch_dev, 2 * F) for rows in (early, late)]
    ready = ready[0] if ready else jnp.concatenate([block[:, shared:] for block in halves], axis=0)
    upper = [from_above(block) for block in halves]
    common = [round_win(ready, shift) for shift in range(1, win_count)]
    incoming = lax.all_to_all(outgoing, "chan", split_axis=0, concat_axis=0, tiled=True)
    targets = [(window_part + shift) % win_count * own_count for shift in range(1, win_count)]

    def offer(part, start):
        rows = jnp.concatenate([halves[part][:, :shared], upper[part]], axis=1)
        return [
            round_win(lax.dynamic_slice_in_dim(rows, target + start, ch_dev, 1), shift)
            for shift, target in enumerate(targets, 1)
        ]

    sooner = offer(0, 0)
    sums, zero = cross_call(win, halves + upper, win_dev, ch_dev, own_count, None, None, 0, 1.0)
    later = offer(1, zero[0])
    arrived = []
    for rows, *others in zip(common, sooner, later):
        arrived += [([rows, block], n * half) for n, block in enumerate(others)]
    for n, (blocks, skipped) in enumerate(arrived):
        ends = tables[0] if n == len(arrived) - 1 else None
        sums, done = cross_call(win, blocks, half, ch_dev, own_count, sums, ends, skipped, 0.5)
    share = fold_call(chan, incoming, early, late, owners, ch_dev, tables, done)
    fold = lax.dynamic_slice_in_dim(share, window_part * own_count, own_count, 0)
    for shift in range(1, win_count):
        target = (window_part + shift) % win_count * own_count
        fold = fold + round_win(lax.dynamic_slice_in_dim(share, target, own_count, 0), shift)
    return (sums, fold)


def solution(mesh):
    in_specs = (P("win", "chan", None), P("chan"), P(), P())
    out_specs = (P(("chan", "win"), None, None), P(("chan", "win"), None))
    return jax.shard_map(local, mesh=mesh, in_specs=in_specs, out_specs=out_specs, check_vma=False)
```

```python
import functools
import math

import jax
import jax.numpy as jnp
import numpy as np
from jax import lax
from jax.experimental import pallas as pl
from jax.experimental.pallas import tpu as pltpu
from jax.sharding import PartitionSpec as P

F = 256
H = F // 2
BAND_LO = 32
NLAG = 256
REACH = 64
CAP = 8
SPAN = REACH + 8
smooth_reach = 4
QUARTERS = 4
VMEM_LIMIT = 24 * 1024 * 1024
FOLD_VMEM_LIMIT = 16 * 1024 * 1024
SPECTRA_VMEM_LIMIT = 59 * 1024 * 1024


def bin_order():
    residues = np.arange(H)
    first = (residues - BAND_LO) % F
    second = (-residues - BAND_LO) % F
    second[0] = (H - BAND_LO) % F
    return first, second


def forward_table(length):
    samples = np.arange(length // 4, dtype=np.int64)[:, None]
    parts = []
    for bins in bin_order():
        angles = (samples * (bins + BAND_LO)[None, :] % length) * (2.0 * math.pi / length)
        parts += [np.cos(angles), -np.sin(angles)]
    return np.concatenate(parts, axis=1).astype(np.float32).astype(jnp.bfloat16)


def inverse_tables(factor):
    shifts = (np.arange(NLAG) + NLAG // 2)[None, :]
    residues = np.arange(H)[:, None]
    angles = (residues * shifts % NLAG) * (2.0 * math.pi / NLAG)
    sign = np.where(shifts[0] % 2 == 0, 1.0, -1.0)
    real, imag = np.cos(angles), -np.sin(angles)
    real[0] = (1.0 + sign) / 2.0
    imag[0] = (1.0 - sign) / 2.0
    table = np.concatenate([real, imag], axis=0) * factor
    high = table.astype(np.float32).astype(jnp.bfloat16)
    low = (table - high.astype(np.float64)).astype(np.float32).astype(jnp.bfloat16)
    return high, low


def lag_transform(stacks, high, low):
    top = stacks.astype(jnp.bfloat16)
    rest = (stacks - top.astype(jnp.float32)).astype(jnp.bfloat16)
    dot = functools.partial(jnp.dot, preferred_element_type=jnp.float32)
    return dot(top, high) + (dot(rest, high) + dot(top, low))


def fold_columns(first, second, imag):
    lane = lax.broadcasted_iota(jnp.int32, first.shape, first.ndim - 1)
    return first + second, jnp.where(lane == 0, first - second, imag)


def lanes_of(shape):
    return lax.broadcasted_iota(jnp.int32, shape, len(shape) - 1)


def rows_of(shape):
    return lax.broadcasted_iota(jnp.int32, shape, len(shape) - 2)


def band_matrix():
    def bins(index):
        lane = index & (H - 1)
        residue = jnp.where(index < H, lane, jnp.where(lane == 0, H, F - lane))
        return (residue - BAND_LO + F) & (F - 1)

    apart = bins(rows_of((F, F))) - bins(lanes_of((F, F)))
    return (jnp.abs(apart) <= smooth_reach).astype(jnp.float32).astype(jnp.bfloat16)


def exact_dot(left, right):
    return jnp.dot(left.astype(jnp.bfloat16), right.astype(jnp.bfloat16), preferred_element_type=jnp.float32)


def over(value, power):
    return value >> (power.bit_length() - 1)


def within(value, power):
    return value & (power - 1)


def slot_selector(owners, places, device, ch_dev):
    height, width = owners.shape
    per_row = width // ch_dev
    wanted = (owners == device).astype(jnp.float32)
    before = rows_of((width, width))
    after = lanes_of((width, width))
    earlier = ((before < after) & (over(before, ch_dev) == over(after, ch_dev))).astype(jnp.float32)
    ranks = exact_dot(wanted, earlier)
    slots = jnp.where(wanted > 0, ranks, float(CAP))
    count = height * per_row * 2 * CAP
    to_row = (over(rows_of((count, height)), 2 * CAP * per_row) == lanes_of((count, height))).astype(jnp.float32)
    row_slots = exact_dot(to_row, slots)
    row_places = exact_dot(to_row, places.astype(jnp.float32))
    shape = (count, width)
    row = rows_of(shape)
    mine = (row_slots == within(row, CAP).astype(jnp.float32)) & (
        over(lanes_of(shape), ch_dev) == within(over(row, 2 * CAP), per_row)
    )
    place = jnp.sum(jnp.where(mine, row_places + 1.0, 0.0), axis=1, keepdims=True).astype(jnp.int32) - 1
    shape = (count, 2 * ch_dev)
    half = within(over(rows_of(shape), CAP), 2)
    lane = lanes_of(shape)
    return ((lane == place + ch_dev * half) & (place >= 0)).astype(jnp.float32).astype(jnp.bfloat16)


def turned_sum(quarters, real, imag, negative):
    rows = quarters[0].shape[0]
    lane = lanes_of((rows, H))
    residue = ((F - lane) if negative else lane) & 3
    sign = jnp.where((residue & 1) == 0, 1.0, -1.0)
    straight = jnp.where(residue == 0, 1.0, jnp.where(residue == 2, -1.0, 0.0))
    turned = jnp.where(residue == 1, 1.0, jnp.where(residue == 3, -1.0, 0.0))
    re = [quarter[:, real * H : (real + 1) * H] for quarter in quarters]
    im = [quarter[:, imag * H : (imag + 1) * H] for quarter in quarters]
    odd_re, odd_im = re[1] + sign * re[3], im[1] + sign * im[3]
    return (
        re[0] + sign * re[2] + (straight * odd_re + turned * odd_im),
        im[0] + sign * im[2] + (straight * odd_im - turned * odd_re),
    )


def spectra_kernel(chan_ref, traces_ref, table_ref, quality_ref, owners_ref, places_ref, *refs):
    early_ref, late_ref, outgoing_ref, *row_refs = refs[:-13]
    traces, table, quality, owners, places, band, keep_rows, products, white, sent, selector, sems, out_sems = refs[-13:]
    row_parts, chunks, rows, depth = traces.shape
    ch_dev = quality.shape[1]
    pair = 2 * ch_dev
    count = outgoing_ref.shape[0]
    slots = sent.shape[2]

    def traces_copy(part, k):
        source = traces_ref.at[pl.ds(part * rows, rows), pl.ds(k * depth, depth)]
        return pltpu.make_async_copy(source, traces.at[part, k], sems.at[part, k])

    small = [
        pltpu.make_async_copy(source, target, sems.at[row_parts, k])
        for k, (source, target) in enumerate(
            ((table_ref, table), (quality_ref, quality), (owners_ref, owners), (places_ref, places))
        )
    ]
    for copy in small:
        copy.start()
    for part in range(row_parts):
        for k in range(chunks):
            traces_copy(part, k).start()

    small[0].wait()
    leaving = []

    def prepare():
        band[...] = band_matrix()
        for copy in small[1:]:
            copy.wait()
        shape = (rows, ch_dev)
        keep = jnp.sum(
            jnp.where(within(rows_of(shape), ch_dev) == lanes_of(shape), quality[...].astype(jnp.float32), 0.0),
            axis=1, keepdims=True,
        )
        selector[...] = slot_selector(owners[...], places[...], chan_ref[0], ch_dev)
        keep_rows[...] = jnp.broadcast_to(keep, keep_rows.shape)

    def transform(part):
        for k in range(chunks):
            traces_copy(part, k).wait()
        stacked = traces[part].reshape(chunks * rows, depth)
        products[part % 2] = jnp.dot(stacked, table[...], preferred_element_type=jnp.float32)

    def whiten(part):
        quarters = [products[part % 2, k * rows : (k + 1) * rows, :] for k in range(chunks)]
        parts = turned_sum(quarters, 0, 1, False) + turned_sum(quarters, 2, 3, True)
        energy = jnp.concatenate(
            [parts[0] * parts[0] + parts[1] * parts[1], parts[2] * parts[2] + parts[3] * parts[3]], axis=1
        )
        top = energy.astype(jnp.bfloat16)
        rest = (energy - top.astype(jnp.float32)).astype(jnp.bfloat16)
        smooth = jnp.dot(top, band[...], preferred_element_type=jnp.float32) + jnp.dot(
            rest, band[...], preferred_element_type=jnp.float32
        )
        water = jnp.sum(energy, axis=1, keepdims=True) * (1.0 / F)
        scaling = lax.rsqrt(smooth * (1.0 / (2.0 * smooth_reach + 1.0)) + (0.1 * water + 1e-06))
        near, far = scaling[:, :H] * keep_rows[...], scaling[:, H:] * keep_rows[...]
        values = jnp.concatenate(
            [parts[0] * near, parts[1] * near, parts[2] * far, parts[3] * far], axis=1
        ).astype(jnp.bfloat16)
        white[part] = values
        for n in range(rows // pair):
            chosen = jnp.dot(
                selector[...], values[pair * n : pair * (n + 1), :], preferred_element_type=jnp.float32
            ).astype(jnp.bfloat16)
            sent[part, :, 2 * CAP * n : 2 * CAP * (n + 1), :] = chosen.reshape(count, 2 * CAP, chosen.shape[-1])

    def leave(part):
        late, place = divmod(part, row_parts // 2)
        copies = [
            (white.at[part], (early_ref, late_ref)[late].at[pl.ds(place * rows, rows), :]),
            (sent.at[part], outgoing_ref.at[:, pl.ds(part * slots, slots), :]),
        ]
        if row_refs:
            shared_ref, *lower_refs = row_refs
            height = shared_ref.shape[1]
            split = ch_dev - height
            for w in range(rows // ch_dev):
                first = w * ch_dev
                copies += [
                    (
                        white.at[part, pl.ds(first + split, height), :],
                        shared_ref.at[part * (rows // ch_dev) + w],
                    ),
                    (
                        white.at[part, pl.ds(first, split), :],
                        lower_refs[late].at[place * (rows // ch_dev) + w],
                    ),
                ]
        for n, (source, target) in enumerate(copies):
            leaving.append(pltpu.make_async_copy(source, target, out_sems.at[part, n]))
            leaving[-1].start()

    for part in range(row_parts + 1):
        if part < row_parts:
            transform(part)
        if part == 0:
            prepare()
        else:
            whiten(part - 1)
            leave(part - 1)
    for copy in leaving:
        copy.wait()


def vmem_spec():
    return pl.BlockSpec(memory_space=pltpu.VMEM)


def smem_spec():
    return pl.BlockSpec(memory_space=pltpu.SMEM)


def whole(array):
    return pl.BlockSpec(array.shape, lambda s: (0,) * array.ndim)


def spectra_call(chan, traces, quality, owners, places, chan_count, own_count):
    rows, length = traces.shape
    ch_dev = quality.shape[1]
    row_steps = rows // (2 * ch_dev)
    part, depth = rows // row_steps, length // QUARTERS
    slots = part // (2 * ch_dev) * 2 * CAP
    anywhere = pl.BlockSpec(memory_space=pl.ANY)
    out_shape = [
        jax.ShapeDtypeStruct((rows // 2, 2 * F), jnp.bfloat16),
        jax.ShapeDtypeStruct((rows // 2, 2 * F), jnp.bfloat16),
        jax.ShapeDtypeStruct((chan_count, row_steps * slots, 2 * F), jnp.bfloat16),
    ]
    if own_count % 16 == 0:
        windows, lower = rows // ch_dev, ch_dev - own_count
        out_shape += [
            jax.ShapeDtypeStruct((windows, own_count, 2 * F), jnp.bfloat16),
            jax.ShapeDtypeStruct((windows // 2, lower, 2 * F), jnp.bfloat16),
            jax.ShapeDtypeStruct((windows // 2, lower, 2 * F), jnp.bfloat16),
        ]
    return pl.pallas_call(
        spectra_kernel,
        in_specs=[smem_spec()] + [anywhere] * 5,
        out_specs=[anywhere] * len(out_shape),
        out_shape=out_shape,
        scratch_shapes=[
            pltpu.VMEM((row_steps, QUARTERS, part, depth), jnp.bfloat16),
            pltpu.VMEM((depth, 2 * F), jnp.bfloat16),
            pltpu.VMEM(quality.shape, jnp.int32),
            pltpu.VMEM(owners.shape, jnp.int32),
            pltpu.VMEM(places.shape, jnp.int32),
            pltpu.VMEM((F, F), jnp.bfloat16),
            pltpu.VMEM((part, H), jnp.float32),
            pltpu.VMEM((2, QUARTERS * part, 2 * F), jnp.float32),
            pltpu.VMEM((row_steps, part, 2 * F), jnp.bfloat16),
            pltpu.VMEM((row_steps, chan_count, slots, 2 * F), jnp.bfloat16),
            pltpu.VMEM((chan_count * 2 * CAP, 2 * ch_dev), jnp.bfloat16),
            pltpu.SemaphoreType.DMA((row_steps + 1, QUARTERS)),
            pltpu.SemaphoreType.DMA((row_steps, 2 + 2 * (part // ch_dev))),
        ],
        compiler_params=pltpu.CompilerParams(vmem_limit_bytes=SPECTRA_VMEM_LIMIT),
        cost_estimate=pl.CostEstimate(
            flops=2 * rows * length * 2 * F, bytes_accessed=2 * rows * length, transcendentals=rows * F
        ),
        name="spectra",
    )(chan, traces, jnp.asarray(forward_table(length)), quality, owners, places)


def cross_kernel(last, with_sum, skipped, through, win_ref, *refs):
    refs = list(refs)
    blocks = [refs.pop(0) for _ in range(2 if with_sum else 4)]
    refs = refs[through:]
    sum_ref = refs.pop(0) if with_sum else None
    if last:
        table_ref, out_ref, zero_ref, wide, spread, total, lags, sems = refs
    else:
        total, zero_ref, *refs = refs
        wide, spread = refs[through:]
    zero_ref[0] = 0
    windows, own_count = spread.shape[:2]
    ch_dev = wide.shape[1] // 2
    base = pl.multiple_of(win_ref[0] * own_count, 8)

    def widen(w, carry):
        if with_sum:
            shared = ch_dev - own_count
            wide[w, shared:ch_dev, :] = blocks[0][skipped + w].astype(jnp.float32)
            rows = blocks[1][w].astype(jnp.float32)
            for tile in range(ch_dev // 8):
                at = base + 8 * tile
                at = pl.multiple_of(jnp.where(at < shared, at, at + own_count), 8)
                wide[w, pl.ds(at, 8), :] = rows[8 * tile : 8 * tile + 8]
        else:
            for half in range(2):
                place = half * (windows // 2) + w
                wide[place, :ch_dev, :] = blocks[half][w].astype(jnp.float32)
                wide[place, ch_dev:, :] = blocks[2 + half][w].astype(jnp.float32)
        return carry

    lax.fori_loop(0, windows if with_sum else windows // 2, widen, 0)

    def repeat(w, carry):
        for tile in range(own_count // 8):
            rows = wide[w, pl.ds(pl.multiple_of(base + 8 * tile, 8), 8), :]
            for i in range(8):
                for q in range(4):
                    spread[w, 8 * tile + i, q] = jnp.broadcast_to(rows[i : i + 1, q * H : (q + 1) * H], (8, H))
        return carry

    lax.fori_loop(0, windows, repeat, 0)

    group, tiles = 4, 3
    rounds = SPAN // (8 * tiles)

    def block(index, carry):
        g = index // rounds
        j = index % rounds
        start = pl.multiple_of(base + 8 * (g // 2) + 8 * tiles * j, 8)

        def add_window(w, sums):
            sums = list(sums)
            right = [
                [wide[w, pl.ds(pl.multiple_of(start + 8 * t, 8), 8), q * H : (q + 1) * H] for q in range(4)]
                for t in range(tiles)
            ]
            for i in range(group):
                left = [spread[w, group * g + i, q] for q in range(4)]
                for t in range(tiles):
                    at = 3 * (i * tiles + t)
                    r = right[t]
                    sums[at] = sums[at] + (left[0] * r[0] + left[1] * r[1])
                    sums[at + 1] = sums[at + 1] + (left[2] * r[2] + left[3] * r[3])
                    sums[at + 2] = sums[at + 2] + ((left[1] * r[0] - left[0] * r[1]) + (left[2] * r[3] - left[3] * r[2]))
            return tuple(sums)

        zero = jnp.zeros((8, H), jnp.float32)
        sums = lax.fori_loop(0, windows, add_window, (zero,) * (3 * group * tiles), unroll=2)
        for i in range(group):
            for t in range(tiles):
                at = 3 * (i * tiles + t)
                real, imag = fold_columns(sums[at], sums[at + 1], sums[at + 2])
                where = pl.ds(pl.multiple_of(8 * tiles * j + 8 * t, 8), 8)
                if with_sum:
                    real = real + sum_ref[group * g + i, where, :H]
                    imag = imag + sum_ref[group * g + i, where, H:]
                total[group * g + i, where, :H] = real
                total[group * g + i, where, H:] = imag
        return carry

    lax.fori_loop(0, own_count // group * rounds, block, 0)

    if last:
        copies = []
        for eight in range(own_count // 8):
            first = 8 * eight
            stacks = total[first : first + 8].reshape(8 * SPAN, F).astype(jnp.bfloat16)
            lagged = jnp.dot(stacks, table_ref[...], preferred_element_type=jnp.float32).reshape(8, SPAN, NLAG)
            for i in range(8):
                lags[first + i] = lagged[i, i + 1 : i + 1 + REACH, :]
            some = pl.ds(first, 8)
            copies.append(pltpu.make_async_copy(lags.at[some], out_ref.at[some], sems.at[eight]))
            copies[-1].start()
        for copy in copies:
            copy.wait()


def cross_call(win, blocks, windows, ch_dev, own_count, sums, table, skipped, share, through=()):
    columns = 2 * F
    last = table is not None
    with_sum = sums is not None
    operands = [win, *blocks, *through]
    anywhere = [pl.BlockSpec(memory_space=pl.ANY)] * len(through)
    in_specs = [smem_spec()] + [vmem_spec()] * len(blocks) + anywhere
    if with_sum:
        operands.append(sums)
    scratch = [
        pltpu.VMEM((windows, 2 * ch_dev, columns), jnp.float32),
        pltpu.VMEM((windows, own_count, 4, 8, H), jnp.float32),
    ]
    if last:
        operands.append(table)
        scratch += [
            pltpu.VMEM((own_count, SPAN, F), jnp.float32),
            pltpu.VMEM((own_count, REACH, NLAG), jnp.float32),
            pltpu.SemaphoreType.DMA((own_count // 8,)),
        ]
    shape = (own_count, REACH, NLAG) if last else (own_count, SPAN, F)
    out_shape = [jax.ShapeDtypeStruct(shape, jnp.float32), jax.ShapeDtypeStruct((1,), jnp.int32)]
    out_specs = [pl.BlockSpec(memory_space=pl.ANY) if last else vmem_spec(), smem_spec()] + anywhere
    out_shape += [jax.ShapeDtypeStruct(array.shape, array.dtype) for array in through]
    return pl.pallas_call(
        functools.partial(cross_kernel, last, with_sum, skipped, len(through)),
        in_specs=in_specs + [vmem_spec()] * (len(operands) - len(in_specs)),
        input_output_aliases={1 + len(blocks) + n: 2 + n for n in range(len(through))},
        out_specs=out_specs,
        out_shape=out_shape,
        scratch_shapes=scratch,
        compiler_params=pltpu.CompilerParams(vmem_limit_bytes=VMEM_LIMIT),
        cost_estimate=pl.CostEstimate(
            flops=int(30_000_000_000 * share), bytes_accessed=4 * windows * ch_dev * columns + 4 * own_count * SPAN * F, transcendentals=0
        ),
        name="cross",
    )(*operands)


def fold_kernel(chan_ref, incoming_ref, early_ref, late_ref, owners_ref, high_ref, low_ref, earlier_ref, out_ref):
    ch_dev = out_ref.shape[0]
    rows = 2 * ch_dev
    pairs = 2 * early_ref.shape[0] // rows
    count, slots, columns = incoming_ref.shape
    owners = owners_ref[...].astype(jnp.float32)
    per_row = owners.shape[1] // ch_dev
    device = chan_ref[0]
    line = jnp.sum(jnp.where(rows_of(owners.shape) == device // per_row, owners, 0.0), axis=0, keepdims=True)
    shape = (rows, owners.shape[1])
    line = jnp.broadcast_to(line, shape)
    first = device % per_row * ch_dev
    place = first + rows_of(shape) % ch_dev
    lane = lanes_of(shape)
    owner = jnp.sum(jnp.where(lane == place, line, 0.0), axis=1, keepdims=True)
    earlier = (lane >= first) & (lane < place) & (line == owner)
    rank = jnp.sum(earlier.astype(jnp.float32), axis=1, keepdims=True)
    source = (2 * CAP * owner + rank).astype(jnp.int32)
    shape = (rows, count * 2 * CAP)
    target = source + CAP * (rows_of(shape) // ch_dev)
    picker = (lanes_of(shape) == target).astype(jnp.float32).astype(jnp.bfloat16)
    sums = None
    for n in range(pairs):
        arrived = incoming_ref[:, 2 * CAP * n : 2 * CAP * (n + 1), :].reshape(count * 2 * CAP, columns)
        right = jnp.dot(picker, arrived, preferred_element_type=jnp.float32)
        late, place = divmod(n, pairs // 2)
        left = (early_ref, late_ref)[late][rows * place : rows * (place + 1), :].astype(jnp.float32)
        l = [left[:, q * H : (q + 1) * H] for q in range(4)]
        r = [right[:, q * H : (q + 1) * H] for q in range(4)]
        terms = [
            l[0] * r[0] + l[1] * r[1],
            l[2] * r[2] + l[3] * r[3],
            (l[1] * r[0] - l[0] * r[1]) + (l[2] * r[3] - l[3] * r[2]),
        ]
        sums = terms if sums is None else [total + term for total, term in zip(sums, terms)]
    stacks = jnp.concatenate(fold_columns(*[total[:ch_dev] + total[ch_dev:] for total in sums]), axis=1)
    out_ref[...] = lag_transform(stacks, high_ref[...], low_ref[...])


def fold_call(chan, incoming, early, late, owners, ch_dev, tables, earlier):
    return pl.pallas_call(
        fold_kernel,
        in_specs=[smem_spec()] + [vmem_spec()] * 6 + [smem_spec()],
        out_specs=vmem_spec(),
        out_shape=jax.ShapeDtypeStruct((ch_dev, NLAG), jnp.float32),
        compiler_params=pltpu.CompilerParams(vmem_limit_bytes=FOLD_VMEM_LIMIT),
        cost_estimate=pl.CostEstimate(
            flops=4 * ch_dev * incoming.size, bytes_accessed=2 * (incoming.size + 2 * early.size), transcendentals=0
        ),
        name="fold",
    )(chan, incoming, early, late, owners, *tables, earlier)


def from_above(block):
    count = lax.axis_size("chan")
    return lax.ppermute(block, "chan", [(i, i - 1) for i in range(1, count)])


def round_win(block, shift):
    count = lax.axis_size("win")
    return lax.ppermute(block, "win", [(i, (i + shift) % count) for i in range(count)])


def local(traces, quality, fold_block, fold_offset):
    win_dev, ch_dev, length = traces.shape
    chan_count = lax.axis_size("chan")
    win_count = lax.axis_size("win")
    window_part = lax.axis_index("win")
    own_count = ch_dev // win_count
    shared = ch_dev - own_count
    chan = lax.axis_index("chan").astype(jnp.int32).reshape(1)
    win = window_part.astype(jnp.int32).reshape(1)
    tables = [jnp.asarray(t) for t in inverse_tables(1.0 / math.sqrt(F * win_dev * win_count))]
    owners = fold_block.reshape(-1, 2 * ch_dev)
    places = fold_offset.reshape(-1, 2 * ch_dev)
    early, late, outgoing, *row_parts = spectra_call(
        chan, traces.reshape(win_dev * ch_dev, length), quality.reshape(1, ch_dev), owners, places, chan_count, own_count
    )
    half = win_dev // 2
    halves = [rows.reshape(half, ch_dev, 2 * F) for rows in (early, late)]
    if not row_parts:
        row_parts = [jnp.concatenate([block[:, shared:] for block in halves], axis=0)]
        row_parts += [block[:, :shared] for block in halves]
    ready, *lower = row_parts
    upper = [from_above(block) for block in halves]
    common = [round_win(ready, shift) for shift in range(1, win_count)]
    incoming = lax.all_to_all(outgoing, "chan", split_axis=0, concat_axis=0, tiled=True)

    def offers(part):
        rows = jnp.concatenate([lower[part], upper[part]], axis=1)
        return [
            lax.dynamic_slice_in_dim(rows, (window_part + shift) % win_count * own_count, ch_dev, 1)
            for shift in range(1, win_count)
        ]

    sooner = [round_win(block, shift) for shift, block in enumerate(offers(0), 1)]
    sums, _, *waiting = cross_call(
        win, halves + upper, win_dev, ch_dev, own_count, None, None, 0, 1.0, through=offers(1)
    )
    later = [round_win(block, shift) for shift, block in enumerate(waiting, 1)]
    arrived = []
    for rows, *others in zip(common, sooner, later):
        arrived += [([rows, block], n * half) for n, block in enumerate(others)]
    for n, (blocks, skipped) in enumerate(arrived):
        ends = tables[0] if n == len(arrived) - 1 else None
        sums, done = cross_call(win, blocks, half, ch_dev, own_count, sums, ends, skipped, 0.5)
    share = fold_call(chan, incoming, early, late, owners, ch_dev, tables, done)
    fold = lax.dynamic_slice_in_dim(share, window_part * own_count, own_count, 0)
    for shift in range(1, win_count):
        target = (window_part + shift) % win_count * own_count
        fold = fold + round_win(lax.dynamic_slice_in_dim(share, target, own_count, 0), shift)
    return (sums, fold)


def solution(mesh):
    in_specs = (P("win", "chan", None), P("chan"), P(), P())
    out_specs = (P(("chan", "win"), None, None), P(("chan", "win"), None))
    return jax.shard_map(local, mesh=mesh, in_specs=in_specs, out_specs=out_specs, check_vma=False)
```

```python
import functools
import math

import jax
import jax.numpy as jnp
import numpy as np
from jax import lax
from jax.experimental import pallas as pl
from jax.experimental.pallas import tpu as pltpu
from jax.sharding import PartitionSpec as P

F = 256
H = F // 2
BAND_LO = 32
NLAG = 256
REACH = 64
CAP = 8
SPAN = REACH + 8
smooth_reach = 4
QUARTERS = 4
VMEM_LIMIT = 24 * 1024 * 1024
FOLD_VMEM_LIMIT = 16 * 1024 * 1024
SPECTRA_VMEM_LIMIT = 59 * 1024 * 1024


def bin_order():
    residues = np.arange(H)
    first = (residues - BAND_LO) % F
    second = (-residues - BAND_LO) % F
    second[0] = (H - BAND_LO) % F
    return first, second


def forward_table(length):
    samples = np.arange(length // 4, dtype=np.int64)[:, None]
    parts = []
    for bins in bin_order():
        angles = (samples * (bins + BAND_LO)[None, :] % length) * (2.0 * math.pi / length)
        parts += [np.cos(angles), -np.sin(angles)]
    return np.concatenate(parts, axis=1).astype(np.float32).astype(jnp.bfloat16)


def inverse_tables(factor):
    shifts = (np.arange(NLAG) + NLAG // 2)[None, :]
    residues = np.arange(H)[:, None]
    angles = (residues * shifts % NLAG) * (2.0 * math.pi / NLAG)
    sign = np.where(shifts[0] % 2 == 0, 1.0, -1.0)
    real, imag = np.cos(angles), -np.sin(angles)
    real[0] = (1.0 + sign) / 2.0
    imag[0] = (1.0 - sign) / 2.0
    table = np.concatenate([real, imag], axis=0) * factor
    high = table.astype(np.float32).astype(jnp.bfloat16)
    low = (table - high.astype(np.float64)).astype(np.float32).astype(jnp.bfloat16)
    return high, low


def lag_transform(stacks, high, low):
    top = stacks.astype(jnp.bfloat16)
    rest = (stacks - top.astype(jnp.float32)).astype(jnp.bfloat16)
    dot = functools.partial(jnp.dot, preferred_element_type=jnp.float32)
    return dot(top, high) + (dot(rest, high) + dot(top, low))


def fold_columns(first, second, imag):
    lane = lax.broadcasted_iota(jnp.int32, first.shape, first.ndim - 1)
    return first + second, jnp.where(lane == 0, first - second, imag)


def lanes_of(shape):
    return lax.broadcasted_iota(jnp.int32, shape, len(shape) - 1)


def rows_of(shape):
    return lax.broadcasted_iota(jnp.int32, shape, len(shape) - 2)


def band_matrix():
    def bins(index):
        lane = index & (H - 1)
        residue = jnp.where(index < H, lane, jnp.where(lane == 0, H, F - lane))
        return (residue - BAND_LO + F) & (F - 1)

    apart = bins(rows_of((F, F))) - bins(lanes_of((F, F)))
    return (jnp.abs(apart) <= smooth_reach).astype(jnp.float32).astype(jnp.bfloat16)


def exact_dot(left, right):
    return jnp.dot(left.astype(jnp.bfloat16), right.astype(jnp.bfloat16), preferred_element_type=jnp.float32)


def over(value, power):
    return value >> (power.bit_length() - 1)


def within(value, power):
    return value & (power - 1)


def slot_selector(owners, places, device, ch_dev):
    height, width = owners.shape
    per_row = width // ch_dev
    wanted = (owners == device).astype(jnp.float32)
    before = rows_of((width, width))
    after = lanes_of((width, width))
    earlier = ((before < after) & (over(before, ch_dev) == over(after, ch_dev))).astype(jnp.float32)
    ranks = exact_dot(wanted, earlier)
    slots = jnp.where(wanted > 0, ranks, float(CAP))
    count = height * per_row * 2 * CAP
    to_row = (over(rows_of((count, height)), 2 * CAP * per_row) == lanes_of((count, height))).astype(jnp.float32)
    row_slots = exact_dot(to_row, slots)
    row_places = exact_dot(to_row, places.astype(jnp.float32))
    shape = (count, width)
    row = rows_of(shape)
    mine = (row_slots == within(row, CAP).astype(jnp.float32)) & (
        over(lanes_of(shape), ch_dev) == within(over(row, 2 * CAP), per_row)
    )
    place = jnp.sum(jnp.where(mine, row_places + 1.0, 0.0), axis=1, keepdims=True).astype(jnp.int32) - 1
    shape = (count, 2 * ch_dev)
    half = within(over(rows_of(shape), CAP), 2)
    lane = lanes_of(shape)
    return ((lane == place + ch_dev * half) & (place >= 0)).astype(jnp.float32).astype(jnp.bfloat16)


def turned_sum(quarters, real, imag, negative):
    rows = quarters[0].shape[0]
    lane = lanes_of((rows, H))
    residue = ((F - lane) if negative else lane) & 3
    sign = jnp.where((residue & 1) == 0, 1.0, -1.0)
    straight = jnp.where(residue == 0, 1.0, jnp.where(residue == 2, -1.0, 0.0))
    turned = jnp.where(residue == 1, 1.0, jnp.where(residue == 3, -1.0, 0.0))
    re = [quarter[:, real * H : (real + 1) * H] for quarter in quarters]
    im = [quarter[:, imag * H : (imag + 1) * H] for quarter in quarters]
    odd_re, odd_im = re[1] + sign * re[3], im[1] + sign * im[3]
    return (
        re[0] + sign * re[2] + (straight * odd_re + turned * odd_im),
        im[0] + sign * im[2] + (straight * odd_im - turned * odd_re),
    )


def spectra_kernel(chan_ref, traces_ref, table_ref, quality_ref, owners_ref, places_ref, *refs):
    early_ref, late_ref, outgoing_ref, *row_refs = refs[:-13]
    traces, table, quality, owners, places, band, keep_rows, products, white, sent, selector, sems, out_sems = refs[-13:]
    row_parts, chunks, rows, depth = traces.shape
    ch_dev = quality.shape[1]
    pair = 2 * ch_dev
    count = outgoing_ref.shape[0]
    slots = sent.shape[2]

    def traces_copy(part, k):
        source = traces_ref.at[pl.ds(part * rows, rows), pl.ds(k * depth, depth)]
        return pltpu.make_async_copy(source, traces.at[part, k], sems.at[part, k])

    small = [
        pltpu.make_async_copy(source, target, sems.at[row_parts, k])
        for k, (source, target) in enumerate(
            ((table_ref, table), (quality_ref, quality), (owners_ref, owners), (places_ref, places))
        )
    ]
    for copy in small:
        copy.start()
    for part in range(row_parts):
        for k in range(chunks):
            traces_copy(part, k).start()

    small[0].wait()
    leaving = []

    def prepare():
        band[...] = band_matrix()
        for copy in small[1:]:
            copy.wait()
        shape = (rows, ch_dev)
        keep = jnp.sum(
            jnp.where(within(rows_of(shape), ch_dev) == lanes_of(shape), quality[...].astype(jnp.float32), 0.0),
            axis=1, keepdims=True,
        )
        selector[...] = slot_selector(owners[...], places[...], chan_ref[0], ch_dev)
        keep_rows[...] = jnp.broadcast_to(keep, keep_rows.shape)

    def transform(part):
        for k in range(chunks):
            traces_copy(part, k).wait()
        stacked = traces[part].reshape(chunks * rows, depth)
        products[part % 2] = jnp.dot(stacked, table[...], preferred_element_type=jnp.float32)

    def whiten(part):
        quarters = [products[part % 2, k * rows : (k + 1) * rows, :] for k in range(chunks)]
        parts = turned_sum(quarters, 0, 1, False) + turned_sum(quarters, 2, 3, True)
        energy = jnp.concatenate(
            [parts[0] * parts[0] + parts[1] * parts[1], parts[2] * parts[2] + parts[3] * parts[3]], axis=1
        )
        top = energy.astype(jnp.bfloat16)
        rest = (energy - top.astype(jnp.float32)).astype(jnp.bfloat16)
        smooth = jnp.dot(top, band[...], preferred_element_type=jnp.float32) + jnp.dot(
            rest, band[...], preferred_element_type=jnp.float32
        )
        water = jnp.sum(energy, axis=1, keepdims=True) * (1.0 / F)
        scaling = lax.rsqrt(smooth * (1.0 / (2.0 * smooth_reach + 1.0)) + (0.1 * water + 1e-06))
        near, far = scaling[:, :H] * keep_rows[...], scaling[:, H:] * keep_rows[...]
        values = jnp.concatenate(
            [parts[0] * near, parts[1] * near, parts[2] * far, parts[3] * far], axis=1
        ).astype(jnp.bfloat16)
        white[part] = values
        for n in range(rows // pair):
            chosen = jnp.dot(
                selector[...], values[pair * n : pair * (n + 1), :], preferred_element_type=jnp.float32
            ).astype(jnp.bfloat16)
            sent[part, :, 2 * CAP * n : 2 * CAP * (n + 1), :] = chosen.reshape(count, 2 * CAP, chosen.shape[-1])

    def leave(part):
        late, place = divmod(part, row_parts // 2)
        copies = [
            (white.at[part], (early_ref, late_ref)[late].at[pl.ds(place * rows, rows), :]),
            (sent.at[part], outgoing_ref.at[:, pl.ds(part * slots, slots), :]),
        ]
        if row_refs:
            shared_ref, *lower_refs = row_refs
            height = shared_ref.shape[1]
            split = ch_dev - height
            for w in range(rows // ch_dev):
                first = w * ch_dev
                copies += [
                    (
                        white.at[part, pl.ds(first + split, height), :],
                        shared_ref.at[part * (rows // ch_dev) + w],
                    ),
                    (
                        white.at[part, pl.ds(first, split), :],
                        lower_refs[late].at[place * (rows // ch_dev) + w],
                    ),
                ]
        for n, (source, target) in enumerate(copies):
            leaving.append(pltpu.make_async_copy(source, target, out_sems.at[part, n]))
            leaving[-1].start()

    for part in range(row_parts + 1):
        if part < row_parts:
            transform(part)
        if part == 0:
            prepare()
        else:
            whiten(part - 1)
            leave(part - 1)
    for copy in leaving:
        copy.wait()


def vmem_spec():
    return pl.BlockSpec(memory_space=pltpu.VMEM)


def smem_spec():
    return pl.BlockSpec(memory_space=pltpu.SMEM)


def whole(array):
    return pl.BlockSpec(array.shape, lambda s: (0,) * array.ndim)


def spectra_call(chan, traces, quality, owners, places, chan_count, own_count):
    rows, length = traces.shape
    ch_dev = quality.shape[1]
    row_steps = rows // (2 * ch_dev)
    part, depth = rows // row_steps, length // QUARTERS
    slots = part // (2 * ch_dev) * 2 * CAP
    anywhere = pl.BlockSpec(memory_space=pl.ANY)
    out_shape = [
        jax.ShapeDtypeStruct((rows // 2, 2 * F), jnp.bfloat16),
        jax.ShapeDtypeStruct((rows // 2, 2 * F), jnp.bfloat16),
        jax.ShapeDtypeStruct((chan_count, row_steps * slots, 2 * F), jnp.bfloat16),
    ]
    if own_count % 16 == 0:
        windows, lower = rows // ch_dev, ch_dev - own_count
        out_shape += [
            jax.ShapeDtypeStruct((windows, own_count, 2 * F), jnp.bfloat16),
            jax.ShapeDtypeStruct((windows // 2, lower, 2 * F), jnp.bfloat16),
            jax.ShapeDtypeStruct((windows // 2, lower, 2 * F), jnp.bfloat16),
        ]
    return pl.pallas_call(
        spectra_kernel,
        in_specs=[smem_spec()] + [anywhere] * 5,
        out_specs=[anywhere] * len(out_shape),
        out_shape=out_shape,
        scratch_shapes=[
            pltpu.VMEM((row_steps, QUARTERS, part, depth), jnp.bfloat16),
            pltpu.VMEM((depth, 2 * F), jnp.bfloat16),
            pltpu.VMEM(quality.shape, jnp.int32),
            pltpu.VMEM(owners.shape, jnp.int32),
            pltpu.VMEM(places.shape, jnp.int32),
            pltpu.VMEM((F, F), jnp.bfloat16),
            pltpu.VMEM((part, H), jnp.float32),
            pltpu.VMEM((2, QUARTERS * part, 2 * F), jnp.float32),
            pltpu.VMEM((row_steps, part, 2 * F), jnp.bfloat16),
            pltpu.VMEM((row_steps, chan_count, slots, 2 * F), jnp.bfloat16),
            pltpu.VMEM((chan_count * 2 * CAP, 2 * ch_dev), jnp.bfloat16),
            pltpu.SemaphoreType.DMA((row_steps + 1, QUARTERS)),
            pltpu.SemaphoreType.DMA((row_steps, 2 + 2 * (part // ch_dev))),
        ],
        compiler_params=pltpu.CompilerParams(vmem_limit_bytes=SPECTRA_VMEM_LIMIT),
        cost_estimate=pl.CostEstimate(
            flops=2 * rows * length * 2 * F, bytes_accessed=2 * rows * length, transcendentals=rows * F
        ),
        name="spectra",
    )(chan, traces, jnp.asarray(forward_table(length)), quality, owners, places)


def cross_kernel(last, with_sum, own_windows, skipped, win_ref, first_ref, second_ref, *refs):
    refs = list(refs)
    sum_ref = refs.pop(0) if with_sum else None
    if last:
        table_ref, out_ref, zero_ref, wide, spread, total, lags, sems = refs
    else:
        total, zero_ref, wide, spread = refs
    zero_ref[0] = 0
    windows, own_count = spread.shape[:2]
    ch_dev = wide.shape[1] // 2
    base = pl.multiple_of(win_ref[0] * own_count, 8)

    def widen(w, carry):
        if own_windows:
            wide[w, :ch_dev, :] = first_ref[w].astype(jnp.float32)
            wide[w, ch_dev:, :] = second_ref[w].astype(jnp.float32)
        else:
            shared = ch_dev - own_count
            wide[w, shared:ch_dev, :] = first_ref[skipped + w].astype(jnp.float32)
            rows = second_ref[w].astype(jnp.float32)
            for tile in range(ch_dev // 8):
                at = base + 8 * tile
                at = pl.multiple_of(jnp.where(at < shared, at, at + own_count), 8)
                wide[w, pl.ds(at, 8), :] = rows[8 * tile : 8 * tile + 8]
        return carry

    lax.fori_loop(0, windows, widen, 0)

    def repeat(w, carry):
        for tile in range(own_count // 8):
            rows = wide[w, pl.ds(pl.multiple_of(base + 8 * tile, 8), 8), :]
            for i in range(8):
                for q in range(4):
                    spread[w, 8 * tile + i, q] = jnp.broadcast_to(rows[i : i + 1, q * H : (q + 1) * H], (8, H))
        return carry

    lax.fori_loop(0, windows, repeat, 0)

    group, tiles = 4, 3
    rounds = SPAN // (8 * tiles)

    def block(index, carry):
        g = index // rounds
        j = index % rounds
        start = pl.multiple_of(base + 8 * (g // 2) + 8 * tiles * j, 8)

        def add_window(w, sums):
            sums = list(sums)
            right = [
                [wide[w, pl.ds(pl.multiple_of(start + 8 * t, 8), 8), q * H : (q + 1) * H] for q in range(4)]
                for t in range(tiles)
            ]
            for i in range(group):
                left = [spread[w, group * g + i, q] for q in range(4)]
                for t in range(tiles):
                    at = 3 * (i * tiles + t)
                    r = right[t]
                    sums[at] = sums[at] + (left[0] * r[0] + left[1] * r[1])
                    sums[at + 1] = sums[at + 1] + (left[2] * r[2] + left[3] * r[3])
                    sums[at + 2] = sums[at + 2] + ((left[1] * r[0] - left[0] * r[1]) + (left[2] * r[3] - left[3] * r[2]))
            return tuple(sums)

        zero = jnp.zeros((8, H), jnp.float32)
        sums = lax.fori_loop(0, windows, add_window, (zero,) * (3 * group * tiles), unroll=2)
        for i in range(group):
            for t in range(tiles):
                at = 3 * (i * tiles + t)
                real, imag = fold_columns(sums[at], sums[at + 1], sums[at + 2])
                where = pl.ds(pl.multiple_of(8 * tiles * j + 8 * t, 8), 8)
                if with_sum:
                    real = real + sum_ref[group * g + i, where, :H]
                    imag = imag + sum_ref[group * g + i, where, H:]
                total[group * g + i, where, :H] = real
                total[group * g + i, where, H:] = imag
        return carry

    lax.fori_loop(0, own_count // group * rounds, block, 0)

    if last:
        copies = []
        for eight in range(own_count // 8):
            first = 8 * eight
            stacks = total[first : first + 8].reshape(8 * SPAN, F).astype(jnp.bfloat16)
            lagged = jnp.dot(stacks, table_ref[...], preferred_element_type=jnp.float32).reshape(8, SPAN, NLAG)
            for i in range(8):
                lags[first + i] = lagged[i, i + 1 : i + 1 + REACH, :]
            some = pl.ds(first, 8)
            copies.append(pltpu.make_async_copy(lags.at[some], out_ref.at[some], sems.at[eight]))
            copies[-1].start()
        for copy in copies:
            copy.wait()


def cross_call(win, first, second, windows, ch_dev, own_count, sums, table, own_windows, skipped=0):
    columns = 2 * F
    last = table is not None
    with_sum = sums is not None
    operands = [win, first, second]
    if with_sum:
        operands.append(sums)
    scratch = [
        pltpu.VMEM((windows, 2 * ch_dev, columns), jnp.float32),
        pltpu.VMEM((windows, own_count, 4, 8, H), jnp.float32),
    ]
    if last:
        operands.append(table)
        scratch += [
            pltpu.VMEM((own_count, SPAN, F), jnp.float32),
            pltpu.VMEM((own_count, REACH, NLAG), jnp.float32),
            pltpu.SemaphoreType.DMA((own_count // 8,)),
        ]
    shape = (own_count, REACH, NLAG) if last else (own_count, SPAN, F)
    out_shape = [jax.ShapeDtypeStruct(shape, jnp.float32), jax.ShapeDtypeStruct((1,), jnp.int32)]
    out_specs = [pl.BlockSpec(memory_space=pl.ANY) if last else vmem_spec(), smem_spec()]
    return pl.pallas_call(
        functools.partial(cross_kernel, last, with_sum, own_windows, skipped),
        in_specs=[smem_spec()] + [vmem_spec()] * (len(operands) - 1),
        out_specs=out_specs,
        out_shape=out_shape,
        scratch_shapes=scratch,
        compiler_params=pltpu.CompilerParams(vmem_limit_bytes=VMEM_LIMIT),
        cost_estimate=pl.CostEstimate(
            flops=15_000_000_000, bytes_accessed=4 * windows * ch_dev * columns + 4 * own_count * SPAN * F, transcendentals=0
        ),
        name="cross",
    )(*operands)


def offer_kernel(win_count, shift, win_ref, after_ref, lower_ref, upper_ref, out_ref, same_ref):
    same_ref[0] = win_ref[0]
    shared, ch_dev = lower_ref.shape[1], upper_ref.shape[1]
    own_count = ch_dev - shared
    target = lax.rem(win_ref[0] + shift, win_count)
    for number in range(win_count):
        below = shared - number * own_count

        @pl.when(target == number)
        def _():
            if below:
                out_ref[:, :below, :] = lower_ref[:, shared - below :, :]
            out_ref[:, below:, :] = upper_ref[:, : ch_dev - below, :]


def offer_call(win, after, lower, upper, win_count, shift):
    if (upper.shape[1] // win_count) % 16:
        rows = jnp.concatenate([lower, upper], axis=1)
        target = (win[0] + shift) % win_count * (upper.shape[1] - lower.shape[1])
        return lax.dynamic_slice_in_dim(rows, target, upper.shape[1], 1), win
    return pl.pallas_call(
        functools.partial(offer_kernel, win_count, shift),
        in_specs=[smem_spec(), smem_spec(), vmem_spec(), vmem_spec()],
        out_specs=[vmem_spec(), smem_spec()],
        out_shape=[jax.ShapeDtypeStruct(upper.shape, upper.dtype), jax.ShapeDtypeStruct((1,), jnp.int32)],
        compiler_params=pltpu.CompilerParams(vmem_limit_bytes=FOLD_VMEM_LIMIT),
        cost_estimate=pl.CostEstimate(flops=0, bytes_accessed=4 * upper.size, transcendentals=0),
        name="offer",
    )(win, after, lower, upper)


def fold_kernel(
    chan_ref, incoming_ref, early_ref, late_ref, owners_ref, high_ref, low_ref, earlier_ref, out_ref, own, sems
):
    ch_dev = out_ref.shape[0]
    copies = [
        pltpu.make_async_copy(source, own.at[n], sems.at[n]) for n, source in enumerate((early_ref, late_ref))
    ]
    for copy in copies:
        copy.start()
    rows = 2 * ch_dev
    pairs = 2 * early_ref.shape[0] // rows
    count, slots, columns = incoming_ref.shape
    owners = owners_ref[...].astype(jnp.float32)
    per_row = owners.shape[1] // ch_dev
    device = chan_ref[0]
    line = jnp.sum(jnp.where(rows_of(owners.shape) == device // per_row, owners, 0.0), axis=0, keepdims=True)
    shape = (rows, owners.shape[1])
    line = jnp.broadcast_to(line, shape)
    first = device % per_row * ch_dev
    place = first + rows_of(shape) % ch_dev
    lane = lanes_of(shape)
    owner = jnp.sum(jnp.where(lane == place, line, 0.0), axis=1, keepdims=True)
    earlier = (lane >= first) & (lane < place) & (line == owner)
    rank = jnp.sum(earlier.astype(jnp.float32), axis=1, keepdims=True)
    source = (2 * CAP * owner + rank).astype(jnp.int32)
    shape = (rows, count * 2 * CAP)
    target = source + CAP * (rows_of(shape) // ch_dev)
    picker = (lanes_of(shape) == target).astype(jnp.float32).astype(jnp.bfloat16)
    rights = [
        jnp.dot(
            picker,
            incoming_ref[:, 2 * CAP * n : 2 * CAP * (n + 1), :].reshape(count * 2 * CAP, columns),
            preferred_element_type=jnp.float32,
        )
        for n in range(pairs)
    ]
    for copy in copies:
        copy.wait()
    sums = None
    for n, right in enumerate(rights):
        late, place = divmod(n, pairs // 2)
        left = own[late, rows * place : rows * (place + 1), :].astype(jnp.float32)
        l = [left[:, q * H : (q + 1) * H] for q in range(4)]
        r = [right[:, q * H : (q + 1) * H] for q in range(4)]
        terms = [
            l[0] * r[0] + l[1] * r[1],
            l[2] * r[2] + l[3] * r[3],
            (l[1] * r[0] - l[0] * r[1]) + (l[2] * r[3] - l[3] * r[2]),
        ]
        sums = terms if sums is None else [total + term for total, term in zip(sums, terms)]
    stacks = jnp.concatenate(fold_columns(*[total[:ch_dev] + total[ch_dev:] for total in sums]), axis=1)
    out_ref[...] = lag_transform(stacks, high_ref[...], low_ref[...])


def fold_call(chan, incoming, early, late, owners, ch_dev, tables, earlier):
    return pl.pallas_call(
        fold_kernel,
        in_specs=[smem_spec(), vmem_spec()]
        + [pl.BlockSpec(memory_space=pl.ANY)] * 2
        + [vmem_spec()] * 3
        + [smem_spec()],
        out_specs=vmem_spec(),
        out_shape=jax.ShapeDtypeStruct((ch_dev, NLAG), jnp.float32),
        scratch_shapes=[pltpu.VMEM((2,) + early.shape, jnp.bfloat16), pltpu.SemaphoreType.DMA((2,))],
        compiler_params=pltpu.CompilerParams(vmem_limit_bytes=FOLD_VMEM_LIMIT),
        cost_estimate=pl.CostEstimate(
            flops=4 * ch_dev * incoming.size, bytes_accessed=2 * (incoming.size + 2 * early.size), transcendentals=0
        ),
        name="fold",
    )(chan, incoming, early, late, owners, *tables, earlier)


def from_above(block):
    count = lax.axis_size("chan")
    return lax.ppermute(block, "chan", [(i, i - 1) for i in range(1, count)])


def round_win(block, shift):
    count = lax.axis_size("win")
    return lax.ppermute(block, "win", [(i, (i + shift) % count) for i in range(count)])


def local(traces, quality, fold_block, fold_offset):
    win_dev, ch_dev, length = traces.shape
    chan_count = lax.axis_size("chan")
    win_count = lax.axis_size("win")
    window_part = lax.axis_index("win")
    own_count = ch_dev // win_count
    shared = ch_dev - own_count
    chan = lax.axis_index("chan").astype(jnp.int32).reshape(1)
    win = window_part.astype(jnp.int32).reshape(1)
    tables = [jnp.asarray(t) for t in inverse_tables(1.0 / math.sqrt(F * win_dev * win_count))]
    owners = fold_block.reshape(-1, 2 * ch_dev)
    places = fold_offset.reshape(-1, 2 * ch_dev)
    early, late, outgoing, *row_parts = spectra_call(
        chan, traces.reshape(win_dev * ch_dev, length), quality.reshape(1, ch_dev), owners, places, chan_count, own_count
    )
    half = win_dev // 2
    halves = [rows.reshape(half, ch_dev, 2 * F) for rows in (early, late)]
    if not row_parts:
        row_parts = [jnp.concatenate([block[:, shared:] for block in halves], axis=0)]
        row_parts += [block[:, :shared] for block in halves]
    ready, *lower = row_parts
    upper = [from_above(block) for block in halves]
    common = [round_win(ready, shift) for shift in range(1, win_count)]
    incoming = lax.all_to_all(outgoing, "chan", split_axis=0, concat_axis=0, tiled=True)

    sums, done = None, win
    relayed = []
    for part in range(2):
        relayed.append([])
        for shift in range(1, win_count):
            block, win = offer_call(win, done, lower[part], upper[part], win_count, shift)
            relayed[part].append(round_win(block, shift))
        sums, done = cross_call(win, halves[part], upper[part], half, ch_dev, own_count, sums, None, True)
    arrived = [(rows, block, n * half) for rows, *pair in zip(common, *relayed) for n, block in enumerate(pair)]
    for n, (rows, block, skipped) in enumerate(arrived):
        ends = tables[0] if n == len(arrived) - 1 else None
        sums, done = cross_call(win, rows, block, half, ch_dev, own_count, sums, ends, False, skipped)
    share = fold_call(chan, incoming, early, late, owners, ch_dev, tables, done)
    fold = lax.dynamic_slice_in_dim(share, window_part * own_count, own_count, 0)
    for shift in range(1, win_count):
        target = (window_part + shift) % win_count * own_count
        fold = fold + round_win(lax.dynamic_slice_in_dim(share, target, own_count, 0), shift)
    return (sums, fold)


def solution(mesh):
    in_specs = (P("win", "chan", None), P("chan"), P(), P())
    out_specs = (P(("chan", "win"), None, None), P(("chan", "win"), None))
    return jax.shard_map(local, mesh=mesh, in_specs=in_specs, out_specs=out_specs, check_vma=False)
```

```python
import functools
import math

import jax
import jax.numpy as jnp
import numpy as np
from jax import lax
from jax.experimental import pallas as pl
from jax.experimental.pallas import tpu as pltpu
from jax.sharding import PartitionSpec as P

F = 256
H = F // 2
BAND_LO = 32
NLAG = 256
REACH = 64
CAP = 8
SPAN = REACH + 8
smooth_reach = 4
QUARTERS = 4
VMEM_LIMIT = 24 * 1024 * 1024
FOLD_VMEM_LIMIT = 16 * 1024 * 1024
SPECTRA_VMEM_LIMIT = 59 * 1024 * 1024


def bin_order():
    residues = np.arange(H)
    first = (residues - BAND_LO) % F
    second = (-residues - BAND_LO) % F
    second[0] = (H - BAND_LO) % F
    return first, second


def forward_table(length):
    samples = np.arange(length // 4, dtype=np.int64)[:, None]
    parts = []
    for bins in bin_order():
        angles = (samples * (bins + BAND_LO)[None, :] % length) * (2.0 * math.pi / length)
        parts += [np.cos(angles), -np.sin(angles)]
    return np.concatenate(parts, axis=1).astype(np.float32).astype(jnp.bfloat16)


def inverse_tables(factor):
    shifts = (np.arange(NLAG) + NLAG // 2)[None, :]
    residues = np.arange(H)[:, None]
    angles = (residues * shifts % NLAG) * (2.0 * math.pi / NLAG)
    sign = np.where(shifts[0] % 2 == 0, 1.0, -1.0)
    real, imag = np.cos(angles), -np.sin(angles)
    real[0] = (1.0 + sign) / 2.0
    imag[0] = (1.0 - sign) / 2.0
    table = np.concatenate([real, imag], axis=0) * factor
    high = table.astype(np.float32).astype(jnp.bfloat16)
    low = (table - high.astype(np.float64)).astype(np.float32).astype(jnp.bfloat16)
    return high, low


def lag_transform(stacks, high, low):
    top = stacks.astype(jnp.bfloat16)
    rest = (stacks - top.astype(jnp.float32)).astype(jnp.bfloat16)
    dot = functools.partial(jnp.dot, preferred_element_type=jnp.float32)
    return dot(top, high) + (dot(rest, high) + dot(top, low))


def fold_columns(first, second, imag):
    lane = lax.broadcasted_iota(jnp.int32, first.shape, first.ndim - 1)
    return first + second, jnp.where(lane == 0, first - second, imag)


def lanes_of(shape):
    return lax.broadcasted_iota(jnp.int32, shape, len(shape) - 1)


def rows_of(shape):
    return lax.broadcasted_iota(jnp.int32, shape, len(shape) - 2)


def band_matrix():
    def bins(index):
        lane = index & (H - 1)
        residue = jnp.where(index < H, lane, jnp.where(lane == 0, H, F - lane))
        return (residue - BAND_LO + F) & (F - 1)

    apart = bins(rows_of((F, F))) - bins(lanes_of((F, F)))
    return (jnp.abs(apart) <= smooth_reach).astype(jnp.float32).astype(jnp.bfloat16)


def exact_dot(left, right):
    return jnp.dot(left.astype(jnp.bfloat16), right.astype(jnp.bfloat16), preferred_element_type=jnp.float32)


def over(value, power):
    return value >> (power.bit_length() - 1)


def within(value, power):
    return value & (power - 1)


def slot_selector(owners, places, device, ch_dev):
    height, width = owners.shape
    per_row = width // ch_dev
    wanted = (owners == device).astype(jnp.float32)
    before = rows_of((width, width))
    after = lanes_of((width, width))
    earlier = ((before < after) & (over(before, ch_dev) == over(after, ch_dev))).astype(jnp.float32)
    ranks = exact_dot(wanted, earlier)
    slots = jnp.where(wanted > 0, ranks, float(CAP))
    count = height * per_row * 2 * CAP
    to_row = (over(rows_of((count, height)), 2 * CAP * per_row) == lanes_of((count, height))).astype(jnp.float32)
    row_slots = exact_dot(to_row, slots)
    row_places = exact_dot(to_row, places.astype(jnp.float32))
    shape = (count, width)
    row = rows_of(shape)
    mine = (row_slots == within(row, CAP).astype(jnp.float32)) & (
        over(lanes_of(shape), ch_dev) == within(over(row, 2 * CAP), per_row)
    )
    place = jnp.sum(jnp.where(mine, row_places + 1.0, 0.0), axis=1, keepdims=True).astype(jnp.int32) - 1
    shape = (count, 2 * ch_dev)
    half = within(over(rows_of(shape), CAP), 2)
    lane = lanes_of(shape)
    return ((lane == place + ch_dev * half) & (place >= 0)).astype(jnp.float32).astype(jnp.bfloat16)


def turned_sum(quarters, real, imag, negative):
    rows = quarters[0].shape[0]
    lane = lanes_of((rows, H))
    residue = ((F - lane) if negative else lane) & 3
    sign = jnp.where((residue & 1) == 0, 1.0, -1.0)
    straight = jnp.where(residue == 0, 1.0, jnp.where(residue == 2, -1.0, 0.0))
    turned = jnp.where(residue == 1, 1.0, jnp.where(residue == 3, -1.0, 0.0))
    re = [quarter[:, real * H : (real + 1) * H] for quarter in quarters]
    im = [quarter[:, imag * H : (imag + 1) * H] for quarter in quarters]
    odd_re, odd_im = re[1] + sign * re[3], im[1] + sign * im[3]
    return (
        re[0] + sign * re[2] + (straight * odd_re + turned * odd_im),
        im[0] + sign * im[2] + (straight * odd_im - turned * odd_re),
    )


def spectra_kernel(chan_ref, traces_ref, table_ref, quality_ref, owners_ref, places_ref, *refs):
    early_ref, late_ref, whitened_ref, outgoing_ref, *row_refs = refs[:-14]
    traces, table, quality, owners, places, band, keep_rows, products, white, white_windows, sent, selector, sems, out_sems = refs[-14:]
    row_parts, chunks, rows, depth = traces.shape
    ch_dev = quality.shape[1]
    pair = 2 * ch_dev
    count = outgoing_ref.shape[0]
    slots = sent.shape[2]

    def traces_copy(part, k):
        source = traces_ref.at[pl.ds(part * rows, rows), pl.ds(k * depth, depth)]
        return pltpu.make_async_copy(source, traces.at[part, k], sems.at[part, k])

    small = [
        pltpu.make_async_copy(source, target, sems.at[row_parts, k])
        for k, (source, target) in enumerate(
            ((table_ref, table), (quality_ref, quality), (owners_ref, owners), (places_ref, places))
        )
    ]
    for copy in small:
        copy.start()
    for part in range(row_parts):
        for k in range(chunks):
            traces_copy(part, k).start()

    small[0].wait()
    leaving = []

    def prepare():
        band[...] = band_matrix()
        for copy in small[1:]:
            copy.wait()
        shape = (rows, ch_dev)
        keep = jnp.sum(
            jnp.where(within(rows_of(shape), ch_dev) == lanes_of(shape), quality[...].astype(jnp.float32), 0.0),
            axis=1, keepdims=True,
        )
        selector[...] = slot_selector(owners[...], places[...], chan_ref[0], ch_dev)
        keep_rows[...] = jnp.broadcast_to(keep, keep_rows.shape)

    def transform(part):
        for k in range(chunks):
            traces_copy(part, k).wait()
        stacked = traces[part].reshape(chunks * rows, depth)
        products[part % 2] = jnp.dot(stacked, table[...], preferred_element_type=jnp.float32)

    def whiten(part):
        quarters = [products[part % 2, k * rows : (k + 1) * rows, :] for k in range(chunks)]
        parts = turned_sum(quarters, 0, 1, False) + turned_sum(quarters, 2, 3, True)
        energy = jnp.concatenate(
            [parts[0] * parts[0] + parts[1] * parts[1], parts[2] * parts[2] + parts[3] * parts[3]], axis=1
        )
        top = energy.astype(jnp.bfloat16)
        rest = (energy - top.astype(jnp.float32)).astype(jnp.bfloat16)
        smooth = jnp.dot(top, band[...], preferred_element_type=jnp.float32) + jnp.dot(
            rest, band[...], preferred_element_type=jnp.float32
        )
        water = jnp.sum(energy, axis=1, keepdims=True) * (1.0 / F)
        scaling = lax.rsqrt(smooth * (1.0 / (2.0 * smooth_reach + 1.0)) + (0.1 * water + 1e-06))
        near, far = scaling[:, :H] * keep_rows[...], scaling[:, H:] * keep_rows[...]
        values = jnp.concatenate(
            [parts[0] * near, parts[1] * near, parts[2] * far, parts[3] * far], axis=1
        ).astype(jnp.bfloat16)
        white[part] = values
        if row_refs:
            white_windows[part] = values.reshape(rows // ch_dev, ch_dev, values.shape[-1])
        for n in range(rows // pair):
            chosen = jnp.dot(
                selector[...], values[pair * n : pair * (n + 1), :], preferred_element_type=jnp.float32
            ).astype(jnp.bfloat16)
            sent[part, :, 2 * CAP * n : 2 * CAP * (n + 1), :] = chosen.reshape(count, 2 * CAP, chosen.shape[-1])

    def leave(part):
        late, place = divmod(part, row_parts // 2)
        copies = [
            (white.at[part], (early_ref, late_ref)[late].at[pl.ds(place * rows, rows), :]),
            (sent.at[part], outgoing_ref.at[:, pl.ds(part * slots, slots), :]),
            (white.at[part], whitened_ref.at[pl.ds(part * rows, rows), :]),
        ]
        if row_refs:
            shared_ref, *lower_refs = row_refs
            height = shared_ref.shape[1]
            split = ch_dev - height
            count_here = rows // ch_dev
            copies += [
                (
                    white_windows.at[part, :, pl.ds(split, height), :],
                    shared_ref.at[pl.ds(part * count_here, count_here)],
                ),
                (
                    white_windows.at[part, :, pl.ds(0, split), :],
                    lower_refs[late].at[pl.ds(place * count_here, count_here)],
                ),
            ]
        for n, (source, target) in enumerate(copies):
            leaving.append(pltpu.make_async_copy(source, target, out_sems.at[part, n]))
            leaving[-1].start()

    for part in range(row_parts + 1):
        if part < row_parts:
            transform(part)
        if part == 0:
            prepare()
        else:
            whiten(part - 1)
            leave(part - 1)
    for copy in leaving:
        copy.wait()


def vmem_spec():
    return pl.BlockSpec(memory_space=pltpu.VMEM)


def smem_spec():
    return pl.BlockSpec(memory_space=pltpu.SMEM)


def whole(array):
    return pl.BlockSpec(array.shape, lambda s: (0,) * array.ndim)


def spectra_call(chan, traces, quality, owners, places, chan_count, own_count):
    rows, length = traces.shape
    ch_dev = quality.shape[1]
    row_steps = rows // (2 * ch_dev)
    part, depth = rows // row_steps, length // QUARTERS
    slots = part // (2 * ch_dev) * 2 * CAP
    anywhere = pl.BlockSpec(memory_space=pl.ANY)
    out_shape = [
        jax.ShapeDtypeStruct((rows // 2, 2 * F), jnp.bfloat16),
        jax.ShapeDtypeStruct((rows // 2, 2 * F), jnp.bfloat16),
        jax.ShapeDtypeStruct((rows, 2 * F), jnp.bfloat16),
        jax.ShapeDtypeStruct((chan_count, row_steps * slots, 2 * F), jnp.bfloat16),
    ]
    if own_count % 16 == 0:
        windows, lower = rows // ch_dev, ch_dev - own_count
        out_shape += [
            jax.ShapeDtypeStruct((windows, own_count, 2 * F), jnp.bfloat16),
            jax.ShapeDtypeStruct((windows // 2, lower, 2 * F), jnp.bfloat16),
            jax.ShapeDtypeStruct((windows // 2, lower, 2 * F), jnp.bfloat16),
        ]
    return pl.pallas_call(
        spectra_kernel,
        in_specs=[smem_spec()] + [anywhere] * 5,
        out_specs=[anywhere] * len(out_shape),
        out_shape=out_shape,
        scratch_shapes=[
            pltpu.VMEM((row_steps, QUARTERS, part, depth), jnp.bfloat16),
            pltpu.VMEM((depth, 2 * F), jnp.bfloat16),
            pltpu.VMEM(quality.shape, jnp.int32),
            pltpu.VMEM(owners.shape, jnp.int32),
            pltpu.VMEM(places.shape, jnp.int32),
            pltpu.VMEM((F, F), jnp.bfloat16),
            pltpu.VMEM((part, H), jnp.float32),
            pltpu.VMEM((2, QUARTERS * part, 2 * F), jnp.float32),
            pltpu.VMEM((row_steps, part, 2 * F), jnp.bfloat16),
            pltpu.VMEM((row_steps, part // ch_dev, ch_dev, 2 * F), jnp.bfloat16),
            pltpu.VMEM((row_steps, chan_count, slots, 2 * F), jnp.bfloat16),
            pltpu.VMEM((chan_count * 2 * CAP, 2 * ch_dev), jnp.bfloat16),
            pltpu.SemaphoreType.DMA((row_steps + 1, QUARTERS)),
            pltpu.SemaphoreType.DMA((row_steps, 5)),
        ],
        compiler_params=pltpu.CompilerParams(vmem_limit_bytes=SPECTRA_VMEM_LIMIT),
        cost_estimate=pl.CostEstimate(
            flops=2 * rows * length * 2 * F, bytes_accessed=2 * rows * length, transcendentals=rows * F
        ),
        name="spectra",
    )(chan, traces, jnp.asarray(forward_table(length)), quality, owners, places)


def cross_kernel(last, with_sum, skipped, through, win_ref, *refs):
    refs = list(refs)
    blocks = [refs.pop(0) for _ in range(2 if with_sum else 3)]
    refs = refs[through:]
    sum_ref = refs.pop(0) if with_sum else None
    if last:
        table_ref, out_ref, zero_ref, wide, spread, total, lags, sems = refs
    else:
        total, zero_ref, *refs = refs
        wide, spread = refs[through:]
    zero_ref[0] = 0
    windows, own_count = spread.shape[:2]
    ch_dev = wide.shape[1] // 2
    base = pl.multiple_of(win_ref[0] * own_count, 8)

    def widen(w, carry):
        if with_sum:
            shared = ch_dev - own_count
            wide[w, shared:ch_dev, :] = blocks[0][skipped + w].astype(jnp.float32)
            rows = blocks[1][w].astype(jnp.float32)
            for tile in range(ch_dev // 8):
                at = base + 8 * tile
                at = pl.multiple_of(jnp.where(at < shared, at, at + own_count), 8)
                wide[w, pl.ds(at, 8), :] = rows[8 * tile : 8 * tile + 8]
        else:
            for half in range(2):
                place = half * (windows // 2) + w
                wide[place, :ch_dev, :] = blocks[0][place].astype(jnp.float32)
                wide[place, ch_dev:, :] = blocks[1 + half][w].astype(jnp.float32)
        return carry

    lax.fori_loop(0, windows if with_sum else windows // 2, widen, 0)

    def repeat(w, carry):
        for tile in range(own_count // 8):
            rows = wide[w, pl.ds(pl.multiple_of(base + 8 * tile, 8), 8), :]
            for i in range(8):
                for q in range(4):
                    spread[w, 8 * tile + i, q] = jnp.broadcast_to(rows[i : i + 1, q * H : (q + 1) * H], (8, H))
        return carry

    lax.fori_loop(0, windows, repeat, 0)

    group, tiles = 4, 3
    rounds = SPAN // (8 * tiles)

    def block(index, carry):
        g = index // rounds
        j = index % rounds
        start = pl.multiple_of(base + 8 * (g // 2) + 8 * tiles * j, 8)

        def add_window(w, sums):
            sums = list(sums)
            right = [
                [wide[w, pl.ds(pl.multiple_of(start + 8 * t, 8), 8), q * H : (q + 1) * H] for q in range(4)]
                for t in range(tiles)
            ]
            for i in range(group):
                left = [spread[w, group * g + i, q] for q in range(4)]
                for t in range(tiles):
                    at = 3 * (i * tiles + t)
                    r = right[t]
                    sums[at] = sums[at] + (left[0] * r[0] + left[1] * r[1])
                    sums[at + 1] = sums[at + 1] + (left[2] * r[2] + left[3] * r[3])
                    sums[at + 2] = sums[at + 2] + ((left[1] * r[0] - left[0] * r[1]) + (left[2] * r[3] - left[3] * r[2]))
            return tuple(sums)

        zero = jnp.zeros((8, H), jnp.float32)
        sums = lax.fori_loop(0, windows, add_window, (zero,) * (3 * group * tiles), unroll=2)
        for i in range(group):
            for t in range(tiles):
                at = 3 * (i * tiles + t)
                real, imag = fold_columns(sums[at], sums[at + 1], sums[at + 2])
                where = pl.ds(pl.multiple_of(8 * tiles * j + 8 * t, 8), 8)
                if with_sum:
                    real = real + sum_ref[group * g + i, where, :H]
                    imag = imag + sum_ref[group * g + i, where, H:]
                total[group * g + i, where, :H] = real
                total[group * g + i, where, H:] = imag
        return carry

    lax.fori_loop(0, own_count // group * rounds, block, 0)

    if last:
        copies = []
        for eight in range(own_count // 8):
            first = 8 * eight
            stacks = total[first : first + 8].reshape(8 * SPAN, F).astype(jnp.bfloat16)
            lagged = jnp.dot(stacks, table_ref[...], preferred_element_type=jnp.float32).reshape(8, SPAN, NLAG)
            for i in range(8):
                lags[first + i] = lagged[i, i + 1 : i + 1 + REACH, :]
            some = pl.ds(first, 8)
            copies.append(pltpu.make_async_copy(lags.at[some], out_ref.at[some], sems.at[eight]))
            copies[-1].start()
        for copy in copies:
            copy.wait()


def cross_call(win, blocks, windows, ch_dev, own_count, sums, table, skipped, share, through=()):
    columns = 2 * F
    last = table is not None
    with_sum = sums is not None
    operands = [win, *blocks, *through]
    anywhere = [pl.BlockSpec(memory_space=pl.ANY)] * len(through)
    in_specs = [smem_spec()] + [vmem_spec()] * len(blocks) + anywhere
    if with_sum:
        operands.append(sums)
    scratch = [
        pltpu.VMEM((windows, 2 * ch_dev, columns), jnp.float32),
        pltpu.VMEM((windows, own_count, 4, 8, H), jnp.float32),
    ]
    if last:
        operands.append(table)
        scratch += [
            pltpu.VMEM((own_count, SPAN, F), jnp.float32),
            pltpu.VMEM((own_count, REACH, NLAG), jnp.float32),
            pltpu.SemaphoreType.DMA((own_count // 8,)),
        ]
    shape = (own_count, REACH, NLAG) if last else (own_count, SPAN, F)
    out_shape = [jax.ShapeDtypeStruct(shape, jnp.float32), jax.ShapeDtypeStruct((1,), jnp.int32)]
    out_specs = [pl.BlockSpec(memory_space=pl.ANY) if last else vmem_spec(), smem_spec()] + anywhere
    out_shape += [jax.ShapeDtypeStruct(array.shape, array.dtype) for array in through]
    return pl.pallas_call(
        functools.partial(cross_kernel, last, with_sum, skipped, len(through)),
        in_specs=in_specs + [vmem_spec()] * (len(operands) - len(in_specs)),
        input_output_aliases={1 + len(blocks) + n: 2 + n for n in range(len(through))},
        out_specs=out_specs,
        out_shape=out_shape,
        scratch_shapes=scratch,
        compiler_params=pltpu.CompilerParams(vmem_limit_bytes=VMEM_LIMIT),
        cost_estimate=pl.CostEstimate(
            flops=int(30_000_000_000 * share), bytes_accessed=4 * windows * ch_dev * columns + 4 * own_count * SPAN * F, transcendentals=0
        ),
        name="cross",
    )(*operands)


def fold_kernel(chan_ref, incoming_ref, own_ref, owners_ref, high_ref, low_ref, earlier_ref, out_ref):
    ch_dev = out_ref.shape[0]
    rows = 2 * ch_dev
    pairs = own_ref.shape[0] // rows
    count, slots, columns = incoming_ref.shape
    owners = owners_ref[...].astype(jnp.float32)
    per_row = owners.shape[1] // ch_dev
    device = chan_ref[0]
    line = jnp.sum(jnp.where(rows_of(owners.shape) == device // per_row, owners, 0.0), axis=0, keepdims=True)
    shape = (rows, owners.shape[1])
    line = jnp.broadcast_to(line, shape)
    first = device % per_row * ch_dev
    place = first + rows_of(shape) % ch_dev
    lane = lanes_of(shape)
    owner = jnp.sum(jnp.where(lane == place, line, 0.0), axis=1, keepdims=True)
    earlier = (lane >= first) & (lane < place) & (line == owner)
    rank = jnp.sum(earlier.astype(jnp.float32), axis=1, keepdims=True)
    source = (2 * CAP * owner + rank).astype(jnp.int32)
    shape = (rows, count * 2 * CAP)
    target = source + CAP * (rows_of(shape) // ch_dev)
    picker = (lanes_of(shape) == target).astype(jnp.float32).astype(jnp.bfloat16)
    sums = None
    for n in range(pairs):
        arrived = incoming_ref[:, 2 * CAP * n : 2 * CAP * (n + 1), :].reshape(count * 2 * CAP, columns)
        right = jnp.dot(picker, arrived, preferred_element_type=jnp.float32)
        left = own_ref[rows * n : rows * (n + 1), :].astype(jnp.float32)
        l = [left[:, q * H : (q + 1) * H] for q in range(4)]
        r = [right[:, q * H : (q + 1) * H] for q in range(4)]
        terms = [
            l[0] * r[0] + l[1] * r[1],
            l[2] * r[2] + l[3] * r[3],
            (l[1] * r[0] - l[0] * r[1]) + (l[2] * r[3] - l[3] * r[2]),
        ]
        sums = terms if sums is None else [total + term for total, term in zip(sums, terms)]
    stacks = jnp.concatenate(fold_columns(*[total[:ch_dev] + total[ch_dev:] for total in sums]), axis=1)
    out_ref[...] = lag_transform(stacks, high_ref[...], low_ref[...])


def fold_call(chan, incoming, own, owners, ch_dev, tables, earlier):
    return pl.pallas_call(
        fold_kernel,
        in_specs=[smem_spec()] + [vmem_spec()] * 5 + [smem_spec()],
        out_specs=vmem_spec(),
        out_shape=jax.ShapeDtypeStruct((ch_dev, NLAG), jnp.float32),
        compiler_params=pltpu.CompilerParams(vmem_limit_bytes=FOLD_VMEM_LIMIT),
        cost_estimate=pl.CostEstimate(
            flops=4 * ch_dev * incoming.size, bytes_accessed=2 * (incoming.size + own.size), transcendentals=0
        ),
        name="fold",
    )(chan, incoming, own, owners, *tables, earlier)


def from_above(block):
    count = lax.axis_size("chan")
    return lax.ppermute(block, "chan", [(i, i - 1) for i in range(1, count)])


def round_win(block, shift):
    count = lax.axis_size("win")
    return lax.ppermute(block, "win", [(i, (i + shift) % count) for i in range(count)])


def local(traces, quality, fold_block, fold_offset):
    win_dev, ch_dev, length = traces.shape
    chan_count = lax.axis_size("chan")
    win_count = lax.axis_size("win")
    window_part = lax.axis_index("win")
    own_count = ch_dev // win_count
    shared = ch_dev - own_count
    chan = lax.axis_index("chan").astype(jnp.int32).reshape(1)
    win = window_part.astype(jnp.int32).reshape(1)
    tables = [jnp.asarray(t) for t in inverse_tables(1.0 / math.sqrt(F * win_dev * win_count))]
    owners = fold_block.reshape(-1, 2 * ch_dev)
    places = fold_offset.reshape(-1, 2 * ch_dev)
    early, late, flat, outgoing, *row_parts = spectra_call(
        chan, traces.reshape(win_dev * ch_dev, length), quality.reshape(1, ch_dev), owners, places, chan_count, own_count
    )
    half = win_dev // 2
    halves = [rows.reshape(half, ch_dev, 2 * F) for rows in (early, late)]
    if not row_parts:
        row_parts = [jnp.concatenate([block[:, shared:] for block in halves], axis=0)]
        row_parts += [block[:, :shared] for block in halves]
    ready, *lower = row_parts
    upper = [from_above(block) for block in halves]
    common = [round_win(ready, shift) for shift in range(1, win_count)]
    incoming = lax.all_to_all(outgoing, "chan", split_axis=0, concat_axis=0, tiled=True)

    def offers(part):
        rows = jnp.concatenate([lower[part], upper[part]], axis=1)
        return [
            lax.dynamic_slice_in_dim(rows, (window_part + shift) % win_count * own_count, ch_dev, 1)
            for shift in range(1, win_count)
        ]

    sooner = [round_win(block, shift) for shift, block in enumerate(offers(0), 1)]
    sums, _, *waiting = cross_call(
        win, [flat.reshape(win_dev, ch_dev, 2 * F)] + upper, win_dev, ch_dev, own_count, None, None, 0, 1.0, through=offers(1)
    )
    later = [round_win(block, shift) for shift, block in enumerate(waiting, 1)]
    arrived = []
    for rows, *others in zip(common, sooner, later):
        arrived += [([rows, block], n * half) for n, block in enumerate(others)]
    for n, (blocks, skipped) in enumerate(arrived):
        ends = tables[0] if n == len(arrived) - 1 else None
        sums, done = cross_call(win, blocks, half, ch_dev, own_count, sums, ends, skipped, 0.5)
    share = fold_call(chan, incoming, flat, owners, ch_dev, tables, done)
    fold = lax.dynamic_slice_in_dim(share, window_part * own_count, own_count, 0)
    for shift in range(1, win_count):
        target = (window_part + shift) % win_count * own_count
        fold = fold + round_win(lax.dynamic_slice_in_dim(share, target, own_count, 0), shift)
    return (sums, fold)


def solution(mesh):
    in_specs = (P("win", "chan", None), P("chan"), P(), P())
    out_specs = (P(("chan", "win"), None, None), P(("chan", "win"), None))
    return jax.shard_map(local, mesh=mesh, in_specs=in_specs, out_specs=out_specs, check_vma=False)
```

```python
import functools
import math

import jax
import jax.numpy as jnp
import numpy as np
from jax import lax
from jax.experimental import pallas as pl
from jax.experimental.pallas import tpu as pltpu
from jax.sharding import PartitionSpec as P

F = 256
H = F // 2
BAND_LO = 32
NLAG = 256
REACH = 64
CAP = 8
SPAN = REACH + 8
smooth_reach = 4
QUARTERS = 4
VMEM_LIMIT = 24 * 1024 * 1024
FOLD_VMEM_LIMIT = 16 * 1024 * 1024
SPECTRA_VMEM_LIMIT = 59 * 1024 * 1024


def bin_order():
    residues = np.arange(H)
    first = (residues - BAND_LO) % F
    second = (-residues - BAND_LO) % F
    second[0] = (H - BAND_LO) % F
    return first, second


def forward_table(length):
    samples = np.arange(length // 4, dtype=np.int64)[:, None]
    parts = []
    for bins in bin_order():
        angles = (samples * (bins + BAND_LO)[None, :] % length) * (2.0 * math.pi / length)
        parts += [np.cos(angles), -np.sin(angles)]
    return np.concatenate(parts, axis=1).astype(np.float32).astype(jnp.bfloat16)


def inverse_tables(factor):
    shifts = (np.arange(NLAG) + NLAG // 2)[None, :]
    residues = np.arange(H)[:, None]
    angles = (residues * shifts % NLAG) * (2.0 * math.pi / NLAG)
    sign = np.where(shifts[0] % 2 == 0, 1.0, -1.0)
    real, imag = np.cos(angles), -np.sin(angles)
    real[0] = (1.0 + sign) / 2.0
    imag[0] = (1.0 - sign) / 2.0
    table = np.concatenate([real, imag], axis=0) * factor
    high = table.astype(np.float32).astype(jnp.bfloat16)
    low = (table - high.astype(np.float64)).astype(np.float32).astype(jnp.bfloat16)
    return high, low


def lag_transform(stacks, high, low):
    top = stacks.astype(jnp.bfloat16)
    rest = (stacks - top.astype(jnp.float32)).astype(jnp.bfloat16)
    dot = functools.partial(jnp.dot, preferred_element_type=jnp.float32)
    return dot(top, high) + (dot(rest, high) + dot(top, low))


def fold_columns(first, second, imag):
    lane = lax.broadcasted_iota(jnp.int32, first.shape, first.ndim - 1)
    return first + second, jnp.where(lane == 0, first - second, imag)


def lanes_of(shape):
    return lax.broadcasted_iota(jnp.int32, shape, len(shape) - 1)


def rows_of(shape):
    return lax.broadcasted_iota(jnp.int32, shape, len(shape) - 2)


def band_matrix():
    def bins(index):
        lane = index & (H - 1)
        residue = jnp.where(index < H, lane, jnp.where(lane == 0, H, F - lane))
        return (residue - BAND_LO + F) & (F - 1)

    apart = bins(rows_of((F, F))) - bins(lanes_of((F, F)))
    return (jnp.abs(apart) <= smooth_reach).astype(jnp.float32).astype(jnp.bfloat16)


def exact_dot(left, right):
    return jnp.dot(left.astype(jnp.bfloat16), right.astype(jnp.bfloat16), preferred_element_type=jnp.float32)


def over(value, power):
    return value >> (power.bit_length() - 1)


def within(value, power):
    return value & (power - 1)


def slot_selector(owners, places, device, ch_dev):
    height, width = owners.shape
    per_row = width // ch_dev
    wanted = (owners == device).astype(jnp.float32)
    before = rows_of((width, width))
    after = lanes_of((width, width))
    earlier = ((before < after) & (over(before, ch_dev) == over(after, ch_dev))).astype(jnp.float32)
    ranks = exact_dot(wanted, earlier)
    slots = jnp.where(wanted > 0, ranks, float(CAP))
    count = height * per_row * 2 * CAP
    to_row = (over(rows_of((count, height)), 2 * CAP * per_row) == lanes_of((count, height))).astype(jnp.float32)
    row_slots = exact_dot(to_row, slots)
    row_places = exact_dot(to_row, places.astype(jnp.float32))
    shape = (count, width)
    row = rows_of(shape)
    mine = (row_slots == within(row, CAP).astype(jnp.float32)) & (
        over(lanes_of(shape), ch_dev) == within(over(row, 2 * CAP), per_row)
    )
    place = jnp.sum(jnp.where(mine, row_places + 1.0, 0.0), axis=1, keepdims=True).astype(jnp.int32) - 1
    shape = (count, 2 * ch_dev)
    half = within(over(rows_of(shape), CAP), 2)
    lane = lanes_of(shape)
    return ((lane == place + ch_dev * half) & (place >= 0)).astype(jnp.float32).astype(jnp.bfloat16)


def turned_sum(quarters, real, imag, negative):
    rows = quarters[0].shape[0]
    lane = lanes_of((rows, H))
    residue = ((F - lane) if negative else lane) & 3
    sign = jnp.where((residue & 1) == 0, 1.0, -1.0)
    straight = jnp.where(residue == 0, 1.0, jnp.where(residue == 2, -1.0, 0.0))
    turned = jnp.where(residue == 1, 1.0, jnp.where(residue == 3, -1.0, 0.0))
    re = [quarter[:, real * H : (real + 1) * H] for quarter in quarters]
    im = [quarter[:, imag * H : (imag + 1) * H] for quarter in quarters]
    odd_re, odd_im = re[1] + sign * re[3], im[1] + sign * im[3]
    return (
        re[0] + sign * re[2] + (straight * odd_re + turned * odd_im),
        im[0] + sign * im[2] + (straight * odd_im - turned * odd_re),
    )


def spectra_kernel(chan_ref, traces_ref, table_ref, quality_ref, owners_ref, places_ref, *refs):
    early_ref, late_ref, whitened_ref, outgoing_ref, *row_refs = refs[:-14]
    traces, table, quality, owners, places, band, keep_rows, products, white, white_windows, sent, selector, sems, out_sems = refs[-14:]
    row_parts, chunks, rows, depth = traces.shape
    ch_dev = quality.shape[1]
    pair = 2 * ch_dev
    count = outgoing_ref.shape[0]
    slots = sent.shape[2]

    def traces_copy(part, k):
        source = traces_ref.at[pl.ds(part * rows, rows), pl.ds(k * depth, depth)]
        return pltpu.make_async_copy(source, traces.at[part, k], sems.at[part, k])

    small = [
        pltpu.make_async_copy(source, target, sems.at[row_parts, k])
        for k, (source, target) in enumerate(
            ((table_ref, table), (quality_ref, quality), (owners_ref, owners), (places_ref, places))
        )
    ]
    for copy in small:
        copy.start()
    for part in range(row_parts):
        for k in range(chunks):
            traces_copy(part, k).start()

    small[0].wait()
    leaving = []

    def prepare():
        band[...] = band_matrix()
        for copy in small[1:]:
            copy.wait()
        shape = (rows, ch_dev)
        keep = jnp.sum(
            jnp.where(within(rows_of(shape), ch_dev) == lanes_of(shape), quality[...].astype(jnp.float32), 0.0),
            axis=1, keepdims=True,
        )
        selector[...] = slot_selector(owners[...], places[...], chan_ref[0], ch_dev)
        keep_rows[...] = jnp.broadcast_to(keep, keep_rows.shape)

    def transform(part):
        for k in range(chunks):
            traces_copy(part, k).wait()
        stacked = traces[part].reshape(chunks * rows, depth)
        products[part % 2] = jnp.dot(stacked, table[...], preferred_element_type=jnp.float32)

    def whiten(part):
        quarters = [products[part % 2, k * rows : (k + 1) * rows, :] for k in range(chunks)]
        parts = turned_sum(quarters, 0, 1, False) + turned_sum(quarters, 2, 3, True)
        energy = jnp.concatenate(
            [parts[0] * parts[0] + parts[1] * parts[1], parts[2] * parts[2] + parts[3] * parts[3]], axis=1
        )
        top = energy.astype(jnp.bfloat16)
        rest = (energy - top.astype(jnp.float32)).astype(jnp.bfloat16)
        smooth = jnp.dot(top, band[...], preferred_element_type=jnp.float32) + jnp.dot(
            rest, band[...], preferred_element_type=jnp.float32
        )
        water = jnp.sum(energy, axis=1, keepdims=True) * (1.0 / F)
        scaling = lax.rsqrt(smooth * (1.0 / (2.0 * smooth_reach + 1.0)) + (0.1 * water + 1e-06))
        near, far = scaling[:, :H] * keep_rows[...], scaling[:, H:] * keep_rows[...]
        values = jnp.concatenate(
            [parts[0] * near, parts[1] * near, parts[2] * far, parts[3] * far], axis=1
        ).astype(jnp.bfloat16)
        white[part] = values
        if row_refs:
            white_windows[part] = values.reshape(rows // ch_dev, ch_dev, values.shape[-1])
        for n in range(rows // pair):
            chosen = jnp.dot(
                selector[...], values[pair * n : pair * (n + 1), :], preferred_element_type=jnp.float32
            ).astype(jnp.bfloat16)
            sent[part, :, 2 * CAP * n : 2 * CAP * (n + 1), :] = chosen.reshape(count, 2 * CAP, chosen.shape[-1])

    def leave(part):
        late, place = divmod(part, row_parts // 2)
        copies = [
            (white.at[part], (early_ref, late_ref)[late].at[pl.ds(place * rows, rows), :]),
            (sent.at[part], outgoing_ref.at[:, pl.ds(part * slots, slots), :]),
            (white.at[part], whitened_ref.at[pl.ds(part * rows, rows), :]),
        ]
        if row_refs:
            shared_ref, *lower_refs = row_refs
            height = shared_ref.shape[1]
            split = ch_dev - height
            count_here = rows // ch_dev
            copies += [
                (
                    white_windows.at[part, :, pl.ds(split, height), :],
                    shared_ref.at[pl.ds(part * count_here, count_here)],
                ),
                (
                    white_windows.at[part, :, pl.ds(0, split), :],
                    lower_refs[late].at[pl.ds(place * count_here, count_here)],
                ),
            ]
        for n, (source, target) in enumerate(copies):
            leaving.append(pltpu.make_async_copy(source, target, out_sems.at[part, n]))
            leaving[-1].start()

    for part in range(row_parts + 1):
        if part < row_parts:
            transform(part)
        if part == 0:
            prepare()
        else:
            whiten(part - 1)
            leave(part - 1)
    for copy in leaving:
        copy.wait()


def vmem_spec():
    return pl.BlockSpec(memory_space=pltpu.VMEM)


def smem_spec():
    return pl.BlockSpec(memory_space=pltpu.SMEM)


def whole(array):
    return pl.BlockSpec(array.shape, lambda s: (0,) * array.ndim)


def spectra_call(chan, traces, quality, owners, places, chan_count, own_count):
    rows, length = traces.shape
    ch_dev = quality.shape[1]
    row_steps = rows // (2 * ch_dev)
    part, depth = rows // row_steps, length // QUARTERS
    slots = part // (2 * ch_dev) * 2 * CAP
    anywhere = pl.BlockSpec(memory_space=pl.ANY)
    out_shape = [
        jax.ShapeDtypeStruct((rows // 2, 2 * F), jnp.bfloat16),
        jax.ShapeDtypeStruct((rows // 2, 2 * F), jnp.bfloat16),
        jax.ShapeDtypeStruct((rows, 2 * F), jnp.bfloat16),
        jax.ShapeDtypeStruct((chan_count, row_steps * slots, 2 * F), jnp.bfloat16),
    ]
    if own_count % 16 == 0:
        windows, lower = rows // ch_dev, ch_dev - own_count
        out_shape += [
            jax.ShapeDtypeStruct((windows, own_count, 2 * F), jnp.bfloat16),
            jax.ShapeDtypeStruct((windows // 2, lower, 2 * F), jnp.bfloat16),
            jax.ShapeDtypeStruct((windows // 2, lower, 2 * F), jnp.bfloat16),
        ]
    return pl.pallas_call(
        spectra_kernel,
        in_specs=[smem_spec()] + [anywhere] * 5,
        out_specs=[anywhere] * len(out_shape),
        out_shape=out_shape,
        scratch_shapes=[
            pltpu.VMEM((row_steps, QUARTERS, part, depth), jnp.bfloat16),
            pltpu.VMEM((depth, 2 * F), jnp.bfloat16),
            pltpu.VMEM(quality.shape, jnp.int32),
            pltpu.VMEM(owners.shape, jnp.int32),
            pltpu.VMEM(places.shape, jnp.int32),
            pltpu.VMEM((F, F), jnp.bfloat16),
            pltpu.VMEM((part, H), jnp.float32),
            pltpu.VMEM((2, QUARTERS * part, 2 * F), jnp.float32),
            pltpu.VMEM((row_steps, part, 2 * F), jnp.bfloat16),
            pltpu.VMEM((row_steps, part // ch_dev, ch_dev, 2 * F), jnp.bfloat16),
            pltpu.VMEM((row_steps, chan_count, slots, 2 * F), jnp.bfloat16),
            pltpu.VMEM((chan_count * 2 * CAP, 2 * ch_dev), jnp.bfloat16),
            pltpu.SemaphoreType.DMA((row_steps + 1, QUARTERS)),
            pltpu.SemaphoreType.DMA((row_steps, 5)),
        ],
        compiler_params=pltpu.CompilerParams(vmem_limit_bytes=SPECTRA_VMEM_LIMIT),
        cost_estimate=pl.CostEstimate(
            flops=2 * rows * length * 2 * F, bytes_accessed=2 * rows * length, transcendentals=rows * F
        ),
        name="spectra",
    )(chan, traces, jnp.asarray(forward_table(length)), quality, owners, places)


def cross_kernel(last, with_sum, skipped, through, kept, win_ref, *refs):
    refs = list(refs)
    blocks = [refs.pop(0) for _ in range(2 if with_sum else 3)]
    refs = refs[through:]
    kept_ref = refs.pop(0) if kept else None
    sum_ref = refs.pop(0) if with_sum else None
    if last:
        table_ref, out_ref, zero_ref, wide, spread, total, lags, sems = refs
    else:
        total, zero_ref, *refs = refs
        if kept:
            refs[through][...] = kept_ref[...]
        wide, spread = refs[through + kept :]
    zero_ref[0] = 0
    windows, own_count = spread.shape[:2]
    ch_dev = wide.shape[1] // 2
    base = pl.multiple_of(win_ref[0] * own_count, 8)

    def spread_out(rows):
        kinds = []
        for half in range(2):
            re, im = rows[:, 2 * half * H : (2 * half + 1) * H], rows[:, (2 * half + 1) * H : (2 * half + 2) * H]
            first = lanes_of(re.shape) == 0
            kinds += [re, jnp.where(first, re - im, re + im), im - re]
        return kinds

    def put(w, at, rows):
        for k, values in enumerate(spread_out(rows)):
            wide[w, at, k * H : (k + 1) * H] = values

    def widen(w, carry):
        if with_sum:
            shared = ch_dev - own_count
            put(w, pl.ds(shared, own_count), blocks[0][skipped + w].astype(jnp.float32))
            rows = blocks[1][w].astype(jnp.float32)
            for tile in range(ch_dev // 8):
                at = base + 8 * tile
                at = pl.multiple_of(jnp.where(at < shared, at, at + own_count), 8)
                put(w, pl.ds(at, 8), rows[8 * tile : 8 * tile + 8])
        else:
            for half in range(2):
                place = half * (windows // 2) + w
                put(place, pl.ds(0, ch_dev), blocks[0][place].astype(jnp.float32))
                put(place, pl.ds(ch_dev, ch_dev), blocks[1 + half][w].astype(jnp.float32))
        return carry

    lax.fori_loop(0, windows if with_sum else windows // 2, widen, 0)

    def repeat(w, carry):
        for tile in range(own_count // 8):
            rows = wide[w, pl.ds(pl.multiple_of(base + 8 * tile, 8), 8), :]
            kinds = []
            for half in range(2):
                re, less = rows[:, 3 * half * H : (3 * half + 1) * H], rows[:, (3 * half + 2) * H : (3 * half + 3) * H]
                im = re + less
                second = jnp.where(lanes_of(re.shape) == 0, im, re)
                kinds += [re + im, -second if half else second, im]
            for i in range(8):
                for k, values in enumerate(kinds):
                    spread[w, 8 * tile + i, k] = jnp.broadcast_to(values[i : i + 1, :], (8, H))
        return carry

    lax.fori_loop(0, windows, repeat, 0)

    group, tiles = 2, 3
    rounds = SPAN // (8 * tiles)

    def block(index, carry):
        g = index // rounds
        j = index % rounds
        start = pl.multiple_of(base + 8 * (g // (8 // group)) + 8 * tiles * j, 8)

        def add_window(w, sums):
            sums = list(sums)
            right = [
                [wide[w, pl.ds(pl.multiple_of(start + 8 * t, 8), 8), k * H : (k + 1) * H] for k in range(6)]
                for t in range(tiles)
            ]
            for i in range(group):
                left = [spread[w, group * g + i, k] for k in range(6)]
                for t in range(tiles):
                    at = 4 * (i * tiles + t)
                    r = right[t]
                    sums[at] = sums[at] + left[0] * r[0]
                    sums[at + 1] = sums[at + 1] + left[3] * r[3]
                    sums[at + 2] = sums[at + 2] + (left[1] * r[1] + left[4] * r[4])
                    sums[at + 3] = sums[at + 3] + (left[2] * r[2] + left[5] * r[5])
            return tuple(sums)

        zero = jnp.zeros((8, H), jnp.float32)
        sums = lax.fori_loop(0, windows, add_window, (zero,) * (4 * group * tiles), unroll=2)
        for i in range(group):
            for t in range(tiles):
                near, far, turned, straight = sums[4 * (i * tiles + t) : 4 * (i * tiles + t) + 4]
                real = (near + far) + straight
                imag = (near - far) - turned
                where = pl.ds(pl.multiple_of(8 * tiles * j + 8 * t, 8), 8)
                if with_sum:
                    real = real + sum_ref[group * g + i, where, :H]
                    imag = imag + sum_ref[group * g + i, where, H:]
                total[group * g + i, where, :H] = real
                total[group * g + i, where, H:] = imag
        return carry

    lax.fori_loop(0, own_count // group * rounds, block, 0)

    if last:
        copies = []
        for eight in range(own_count // 8):
            first = 8 * eight
            stacks = total[first : first + 8].reshape(8 * SPAN, F).astype(jnp.bfloat16)
            lagged = jnp.dot(stacks, table_ref[...], preferred_element_type=jnp.float32).reshape(8, SPAN, NLAG)
            for i in range(8):
                lags[first + i] = lagged[i, i + 1 : i + 1 + REACH, :]
            some = pl.ds(first, 8)
            copies.append(pltpu.make_async_copy(lags.at[some], out_ref.at[some], sems.at[eight]))
            copies[-1].start()
        for copy in copies:
            copy.wait()


def cross_call(win, blocks, windows, ch_dev, own_count, sums, table, skipped, share, through=(), kept=()):
    columns = 6 * H
    last = table is not None
    with_sum = sums is not None
    operands = [win, *blocks, *through, *kept]
    anywhere = [pl.BlockSpec(memory_space=pl.ANY)] * len(through)
    in_specs = [smem_spec()] + [vmem_spec()] * len(blocks) + anywhere
    if with_sum:
        operands.append(sums)
    scratch = [
        pltpu.VMEM((windows, 2 * ch_dev, columns), jnp.float32),
        pltpu.VMEM((windows, own_count, 6, 8, H), jnp.float32),
    ]
    if last:
        operands.append(table)
        scratch += [
            pltpu.VMEM((own_count, SPAN, F), jnp.float32),
            pltpu.VMEM((own_count, REACH, NLAG), jnp.float32),
            pltpu.SemaphoreType.DMA((own_count // 8,)),
        ]
    shape = (own_count, REACH, NLAG) if last else (own_count, SPAN, F)
    out_shape = [jax.ShapeDtypeStruct(shape, jnp.float32), jax.ShapeDtypeStruct((1,), jnp.int32)]
    out_specs = [pl.BlockSpec(memory_space=pl.ANY) if last else vmem_spec(), smem_spec()] + anywhere
    out_specs += [vmem_spec()] * len(kept)
    out_shape += [jax.ShapeDtypeStruct(array.shape, array.dtype) for array in (*through, *kept)]
    return pl.pallas_call(
        functools.partial(cross_kernel, last, with_sum, skipped, len(through), len(kept)),
        in_specs=in_specs + [vmem_spec()] * (len(operands) - len(in_specs)),
        input_output_aliases={1 + len(blocks) + n: 2 + n for n in range(len(through))},
        out_specs=out_specs,
        out_shape=out_shape,
        scratch_shapes=scratch,
        compiler_params=pltpu.CompilerParams(vmem_limit_bytes=VMEM_LIMIT),
        cost_estimate=pl.CostEstimate(
            flops=int(30_000_000_000 * share), bytes_accessed=4 * windows * ch_dev * columns + 4 * own_count * SPAN * F, transcendentals=0
        ),
        name="cross",
    )(*operands)


def fold_kernel(chan_ref, incoming_ref, own_ref, owners_ref, high_ref, low_ref, earlier_ref, out_ref):
    ch_dev = out_ref.shape[0]
    rows = 2 * ch_dev
    pairs = own_ref.shape[0] // rows
    count, slots, columns = incoming_ref.shape
    owners = owners_ref[...].astype(jnp.float32)
    per_row = owners.shape[1] // ch_dev
    device = chan_ref[0]
    line = jnp.sum(jnp.where(rows_of(owners.shape) == device // per_row, owners, 0.0), axis=0, keepdims=True)
    shape = (rows, owners.shape[1])
    line = jnp.broadcast_to(line, shape)
    first = device % per_row * ch_dev
    place = first + rows_of(shape) % ch_dev
    lane = lanes_of(shape)
    owner = jnp.sum(jnp.where(lane == place, line, 0.0), axis=1, keepdims=True)
    earlier = (lane >= first) & (lane < place) & (line == owner)
    rank = jnp.sum(earlier.astype(jnp.float32), axis=1, keepdims=True)
    source = (2 * CAP * owner + rank).astype(jnp.int32)
    shape = (rows, count * 2 * CAP)
    target = source + CAP * (rows_of(shape) // ch_dev)
    picker = (lanes_of(shape) == target).astype(jnp.float32).astype(jnp.bfloat16)
    sums = None
    for n in range(pairs):
        arrived = incoming_ref[:, 2 * CAP * n : 2 * CAP * (n + 1), :].reshape(count * 2 * CAP, columns)
        right = jnp.dot(picker, arrived, preferred_element_type=jnp.float32)
        left = own_ref[rows * n : rows * (n + 1), :].astype(jnp.float32)
        l = [left[:, q * H : (q + 1) * H] for q in range(4)]
        r = [right[:, q * H : (q + 1) * H] for q in range(4)]
        terms = [
            l[0] * r[0] + l[1] * r[1],
            l[2] * r[2] + l[3] * r[3],
            (l[1] * r[0] - l[0] * r[1]) + (l[2] * r[3] - l[3] * r[2]),
        ]
        sums = terms if sums is None else [total + term for total, term in zip(sums, terms)]
    stacks = jnp.concatenate(fold_columns(*[total[:ch_dev] + total[ch_dev:] for total in sums]), axis=1)
    out_ref[...] = lag_transform(stacks, high_ref[...], low_ref[...])


def fold_call(chan, incoming, own, owners, ch_dev, tables, earlier):
    return pl.pallas_call(
        fold_kernel,
        in_specs=[smem_spec()] + [vmem_spec()] * 5 + [smem_spec()],
        out_specs=vmem_spec(),
        out_shape=jax.ShapeDtypeStruct((ch_dev, NLAG), jnp.float32),
        compiler_params=pltpu.CompilerParams(vmem_limit_bytes=FOLD_VMEM_LIMIT),
        cost_estimate=pl.CostEstimate(
            flops=4 * ch_dev * incoming.size, bytes_accessed=2 * (incoming.size + own.size), transcendentals=0
        ),
        name="fold",
    )(chan, incoming, own, owners, *tables, earlier)


def from_above(block):
    count = lax.axis_size("chan")
    return lax.ppermute(block, "chan", [(i, i - 1) for i in range(1, count)])


def round_win(block, shift):
    count = lax.axis_size("win")
    return lax.ppermute(block, "win", [(i, (i + shift) % count) for i in range(count)])


def local(traces, quality, fold_block, fold_offset):
    win_dev, ch_dev, length = traces.shape
    chan_count = lax.axis_size("chan")
    win_count = lax.axis_size("win")
    window_part = lax.axis_index("win")
    own_count = ch_dev // win_count
    shared = ch_dev - own_count
    chan = lax.axis_index("chan").astype(jnp.int32).reshape(1)
    win = window_part.astype(jnp.int32).reshape(1)
    tables = [jnp.asarray(t) for t in inverse_tables(1.0 / math.sqrt(F * win_dev * win_count))]
    owners = fold_block.reshape(-1, 2 * ch_dev)
    places = fold_offset.reshape(-1, 2 * ch_dev)
    early, late, flat, outgoing, *row_parts = spectra_call(
        chan, traces.reshape(win_dev * ch_dev, length), quality.reshape(1, ch_dev), owners, places, chan_count, own_count
    )
    half = win_dev // 2
    halves = [rows.reshape(half, ch_dev, 2 * F) for rows in (early, late)]
    if not row_parts:
        row_parts = [jnp.concatenate([block[:, shared:] for block in halves], axis=0)]
        row_parts += [block[:, :shared] for block in halves]
    ready, *lower = row_parts
    upper = [from_above(block) for block in halves]
    common = [round_win(ready, shift) for shift in range(1, win_count)]
    incoming = lax.all_to_all(outgoing, "chan", split_axis=0, concat_axis=0, tiled=True)

    def offers(part):
        rows = jnp.concatenate([lower[part], upper[part]], axis=1)
        return [
            lax.dynamic_slice_in_dim(rows, (window_part + shift) % win_count * own_count, ch_dev, 1)
            for shift in range(1, win_count)
        ]

    sooner = [round_win(block, shift) for shift, block in enumerate(offers(0), 1)]
    sums, _, *waiting = cross_call(
        win, [flat.reshape(win_dev, ch_dev, 2 * F)] + upper, win_dev, ch_dev, own_count, None, None, 0, 1.0, through=offers(1)
    )
    later = [round_win(block, shift) for shift, block in enumerate(waiting, 1)]
    arrived = []
    for rows, *others in zip(common, sooner, later):
        arrived += [([rows, block], n * half) for n, block in enumerate(others)]
    for n, (blocks, skipped) in enumerate(arrived):
        ends = tables[0] if n == len(arrived) - 1 else None
        kept = [flat] if n == len(arrived) - 2 else []
        sums, done, *copies = cross_call(
            win, blocks, half, ch_dev, own_count, sums, ends, skipped, 0.5, kept=kept
        )
        flat = copies[0] if copies else flat
    share = fold_call(chan, incoming, flat, owners, ch_dev, tables, done)
    fold = lax.dynamic_slice_in_dim(share, window_part * own_count, own_count, 0)
    for shift in range(1, win_count):
        target = (window_part + shift) % win_count * own_count
        fold = fold + round_win(lax.dynamic_slice_in_dim(share, target, own_count, 0), shift)
    return (sums, fold)


def solution(mesh):
    in_specs = (P("win", "chan", None), P("chan"), P(), P())
    out_specs = (P(("chan", "win"), None, None), P(("chan", "win"), None))
    return jax.shard_map(local, mesh=mesh, in_specs=in_specs, out_specs=out_specs, check_vma=False)
```

```python
import functools
import math

import jax
import jax.numpy as jnp
import numpy as np
from jax import lax
from jax.experimental import pallas as pl
from jax.experimental.pallas import tpu as pltpu
from jax.sharding import PartitionSpec as P

F = 256
H = F // 2
BAND_LO = 32
NLAG = 256
REACH = 64
CAP = 8
SPAN = REACH + 8
smooth_reach = 4
QUARTERS = 4
VMEM_LIMIT = 24 * 1024 * 1024
FOLD_VMEM_LIMIT = 16 * 1024 * 1024
SPECTRA_VMEM_LIMIT = 59 * 1024 * 1024


def bin_order():
    residues = np.arange(H)
    first = (residues - BAND_LO) % F
    second = (-residues - BAND_LO) % F
    second[0] = (H - BAND_LO) % F
    return first, second


def forward_table(length):
    samples = np.arange(length // 4, dtype=np.int64)[:, None]
    parts = []
    for bins in bin_order():
        angles = (samples * (bins + BAND_LO)[None, :] % length) * (2.0 * math.pi / length)
        parts += [np.cos(angles), -np.sin(angles)]
    return np.concatenate(parts, axis=1).astype(np.float32).astype(jnp.bfloat16)


def inverse_tables(factor):
    shifts = (np.arange(NLAG) + NLAG // 2)[None, :]
    residues = np.arange(H)[:, None]
    angles = (residues * shifts % NLAG) * (2.0 * math.pi / NLAG)
    sign = np.where(shifts[0] % 2 == 0, 1.0, -1.0)
    real, imag = np.cos(angles), -np.sin(angles)
    real[0] = (1.0 + sign) / 2.0
    imag[0] = (1.0 - sign) / 2.0
    table = np.concatenate([real, imag], axis=0) * factor
    high = table.astype(np.float32).astype(jnp.bfloat16)
    low = (table - high.astype(np.float64)).astype(np.float32).astype(jnp.bfloat16)
    return high, low


def lag_transform(stacks, high, low):
    top = stacks.astype(jnp.bfloat16)
    rest = (stacks - top.astype(jnp.float32)).astype(jnp.bfloat16)
    dot = functools.partial(jnp.dot, preferred_element_type=jnp.float32)
    return dot(top, high) + (dot(rest, high) + dot(top, low))


def fold_columns(first, second, imag):
    lane = lax.broadcasted_iota(jnp.int32, first.shape, first.ndim - 1)
    return first + second, jnp.where(lane == 0, first - second, imag)


def lanes_of(shape):
    return lax.broadcasted_iota(jnp.int32, shape, len(shape) - 1)


def rows_of(shape):
    return lax.broadcasted_iota(jnp.int32, shape, len(shape) - 2)


def band_matrix():
    def bins(index):
        lane = index & (H - 1)
        residue = jnp.where(index < H, lane, jnp.where(lane == 0, H, F - lane))
        return (residue - BAND_LO + F) & (F - 1)

    apart = bins(rows_of((F, F))) - bins(lanes_of((F, F)))
    return (jnp.abs(apart) <= smooth_reach).astype(jnp.float32).astype(jnp.bfloat16)


def exact_dot(left, right):
    return jnp.dot(left.astype(jnp.bfloat16), right.astype(jnp.bfloat16), preferred_element_type=jnp.float32)


def over(value, power):
    return value >> (power.bit_length() - 1)


def within(value, power):
    return value & (power - 1)


def slot_selector(owners, places, device, ch_dev):
    height, width = owners.shape
    per_row = width // ch_dev
    wanted = (owners == device).astype(jnp.float32)
    before = rows_of((width, width))
    after = lanes_of((width, width))
    earlier = ((before < after) & (over(before, ch_dev) == over(after, ch_dev))).astype(jnp.float32)
    ranks = exact_dot(wanted, earlier)
    slots = jnp.where(wanted > 0, ranks, float(CAP))
    count = height * per_row * 2 * CAP
    to_row = (over(rows_of((count, height)), 2 * CAP * per_row) == lanes_of((count, height))).astype(jnp.float32)
    row_slots = exact_dot(to_row, slots)
    row_places = exact_dot(to_row, places.astype(jnp.float32))
    shape = (count, width)
    row = rows_of(shape)
    mine = (row_slots == within(row, CAP).astype(jnp.float32)) & (
        over(lanes_of(shape), ch_dev) == within(over(row, 2 * CAP), per_row)
    )
    place = jnp.sum(jnp.where(mine, row_places + 1.0, 0.0), axis=1, keepdims=True).astype(jnp.int32) - 1
    shape = (count, 2 * ch_dev)
    half = within(over(rows_of(shape), CAP), 2)
    lane = lanes_of(shape)
    return ((lane == place + ch_dev * half) & (place >= 0)).astype(jnp.float32).astype(jnp.bfloat16)


def turned_sum(quarters, real, imag, negative):
    rows = quarters[0].shape[0]
    lane = lanes_of((rows, H))
    residue = ((F - lane) if negative else lane) & 3
    sign = jnp.where((residue & 1) == 0, 1.0, -1.0)
    straight = jnp.where(residue == 0, 1.0, jnp.where(residue == 2, -1.0, 0.0))
    turned = jnp.where(residue == 1, 1.0, jnp.where(residue == 3, -1.0, 0.0))
    re = [quarter[:, real * H : (real + 1) * H] for quarter in quarters]
    im = [quarter[:, imag * H : (imag + 1) * H] for quarter in quarters]
    odd_re, odd_im = re[1] + sign * re[3], im[1] + sign * im[3]
    return (
        re[0] + sign * re[2] + (straight * odd_re + turned * odd_im),
        im[0] + sign * im[2] + (straight * odd_im - turned * odd_re),
    )


def spectra_kernel(traces_ref, table_ref, quality_ref, owners_ref, places_ref, *refs):
    early_ref, late_ref, whitened_ref, outgoing_ref, *row_refs = refs[:-14]
    traces, table, quality, owners, places, band, keep_rows, products, white, white_windows, sent, selector, sems, out_sems = refs[-14:]
    row_parts, chunks, rows, depth = traces.shape
    ch_dev = quality.shape[1]
    pair = 2 * ch_dev
    count = outgoing_ref.shape[0]
    slots = sent.shape[2]

    def traces_copy(part, k):
        source = traces_ref.at[pl.ds(part * rows, rows), pl.ds(k * depth, depth)]
        return pltpu.make_async_copy(source, traces.at[part, k], sems.at[part, k])

    small = [
        pltpu.make_async_copy(source, target, sems.at[row_parts, k])
        for k, (source, target) in enumerate(
            ((table_ref, table), (quality_ref, quality), (owners_ref, owners), (places_ref, places))
        )
    ]
    for copy in small:
        copy.start()
    for part in range(row_parts):
        for k in range(chunks):
            traces_copy(part, k).start()

    small[0].wait()
    leaving = []

    def prepare():
        band[...] = band_matrix()
        for copy in small[1:]:
            copy.wait()
        shape = (rows, ch_dev)
        keep = jnp.sum(
            jnp.where(within(rows_of(shape), ch_dev) == lanes_of(shape), quality[...].astype(jnp.float32), 0.0),
            axis=1, keepdims=True,
        )
        selector[...] = slot_selector(owners[...], places[...], lax.axis_index("chan"), ch_dev)
        keep_rows[...] = jnp.broadcast_to(keep, keep_rows.shape)

    def transform(part):
        for k in range(chunks):
            traces_copy(part, k).wait()
        stacked = traces[part].reshape(chunks * rows, depth)
        products[part % 2] = jnp.dot(stacked, table[...], preferred_element_type=jnp.float32)

    def whiten(part):
        quarters = [products[part % 2, k * rows : (k + 1) * rows, :] for k in range(chunks)]
        parts = turned_sum(quarters, 0, 1, False) + turned_sum(quarters, 2, 3, True)
        energy = jnp.concatenate(
            [parts[0] * parts[0] + parts[1] * parts[1], parts[2] * parts[2] + parts[3] * parts[3]], axis=1
        )
        top = energy.astype(jnp.bfloat16)
        rest = (energy - top.astype(jnp.float32)).astype(jnp.bfloat16)
        smooth = jnp.dot(top, band[...], preferred_element_type=jnp.float32) + jnp.dot(
            rest, band[...], preferred_element_type=jnp.float32
        )
        water = jnp.sum(energy, axis=1, keepdims=True) * (1.0 / F)
        scaling = lax.rsqrt(smooth * (1.0 / (2.0 * smooth_reach + 1.0)) + (0.1 * water + 1e-06))
        near, far = scaling[:, :H] * keep_rows[...], scaling[:, H:] * keep_rows[...]
        values = jnp.concatenate(
            [parts[0] * near, parts[1] * near, parts[2] * far, parts[3] * far], axis=1
        ).astype(jnp.bfloat16)
        white[part] = values
        if row_refs:
            white_windows[part] = values.reshape(rows // ch_dev, ch_dev, values.shape[-1])
        for n in range(rows // pair):
            chosen = jnp.dot(
                selector[...], values[pair * n : pair * (n + 1), :], preferred_element_type=jnp.float32
            ).astype(jnp.bfloat16)
            sent[part, :, 2 * CAP * n : 2 * CAP * (n + 1), :] = chosen.reshape(count, 2 * CAP, chosen.shape[-1])

    def leave(part):
        late, place = divmod(part, row_parts // 2)
        copies = [
            (white.at[part], (early_ref, late_ref)[late].at[pl.ds(place * rows, rows), :]),
            (sent.at[part], outgoing_ref.at[:, pl.ds(part * slots, slots), :]),
            (white.at[part], whitened_ref.at[pl.ds(part * rows, rows), :]),
        ]
        if row_refs:
            shared_ref, *lower_refs = row_refs
            height = shared_ref.shape[1]
            split = ch_dev - height
            count_here = rows // ch_dev
            copies += [
                (
                    white_windows.at[part, :, pl.ds(split, height), :],
                    shared_ref.at[pl.ds(part * count_here, count_here)],
                ),
                (
                    white_windows.at[part, :, pl.ds(0, split), :],
                    lower_refs[late].at[pl.ds(place * count_here, count_here)],
                ),
            ]
        for n, (source, target) in enumerate(copies):
            leaving.append(pltpu.make_async_copy(source, target, out_sems.at[part, n]))
            leaving[-1].start()

    for part in range(row_parts + 1):
        if part < row_parts:
            transform(part)
        if part == 0:
            prepare()
        else:
            whiten(part - 1)
            leave(part - 1)
    for copy in leaving:
        copy.wait()


def vmem_spec():
    return pl.BlockSpec(memory_space=pltpu.VMEM)


def smem_spec():
    return pl.BlockSpec(memory_space=pltpu.SMEM)


def whole(array):
    return pl.BlockSpec(array.shape, lambda s: (0,) * array.ndim)


def spectra_call(traces, quality, owners, places, chan_count, own_count):
    rows, length = traces.shape
    ch_dev = quality.shape[1]
    row_steps = rows // (2 * ch_dev)
    part, depth = rows // row_steps, length // QUARTERS
    slots = part // (2 * ch_dev) * 2 * CAP
    anywhere = pl.BlockSpec(memory_space=pl.ANY)
    out_shape = [
        jax.ShapeDtypeStruct((rows // 2, 2 * F), jnp.bfloat16),
        jax.ShapeDtypeStruct((rows // 2, 2 * F), jnp.bfloat16),
        jax.ShapeDtypeStruct((rows, 2 * F), jnp.bfloat16),
        jax.ShapeDtypeStruct((chan_count, row_steps * slots, 2 * F), jnp.bfloat16),
    ]
    if own_count % 16 == 0:
        windows, lower = rows // ch_dev, ch_dev - own_count
        out_shape += [
            jax.ShapeDtypeStruct((windows, own_count, 2 * F), jnp.bfloat16),
            jax.ShapeDtypeStruct((windows // 2, lower, 2 * F), jnp.bfloat16),
            jax.ShapeDtypeStruct((windows // 2, lower, 2 * F), jnp.bfloat16),
        ]
    return pl.pallas_call(
        spectra_kernel,
        in_specs=[anywhere] * 5,
        out_specs=[anywhere] * len(out_shape),
        out_shape=out_shape,
        scratch_shapes=[
            pltpu.VMEM((row_steps, QUARTERS, part, depth), jnp.bfloat16),
            pltpu.VMEM((depth, 2 * F), jnp.bfloat16),
            pltpu.VMEM(quality.shape, jnp.int32),
            pltpu.VMEM(owners.shape, jnp.int32),
            pltpu.VMEM(places.shape, jnp.int32),
            pltpu.VMEM((F, F), jnp.bfloat16),
            pltpu.VMEM((part, H), jnp.float32),
            pltpu.VMEM((2, QUARTERS * part, 2 * F), jnp.float32),
            pltpu.VMEM((row_steps, part, 2 * F), jnp.bfloat16),
            pltpu.VMEM((row_steps, part // ch_dev, ch_dev, 2 * F), jnp.bfloat16),
            pltpu.VMEM((row_steps, chan_count, slots, 2 * F), jnp.bfloat16),
            pltpu.VMEM((chan_count * 2 * CAP, 2 * ch_dev), jnp.bfloat16),
            pltpu.SemaphoreType.DMA((row_steps + 1, QUARTERS)),
            pltpu.SemaphoreType.DMA((row_steps, 5)),
        ],
        compiler_params=pltpu.CompilerParams(vmem_limit_bytes=SPECTRA_VMEM_LIMIT),
        cost_estimate=pl.CostEstimate(
            flops=2 * rows * length * 2 * F, bytes_accessed=2 * rows * length, transcendentals=rows * F
        ),
        name="spectra",
    )(traces, jnp.asarray(forward_table(length)), quality, owners, places)


def cross_kernel(last, with_sum, skipped, through, *refs):
    refs = list(refs)
    blocks = [refs.pop(0) for _ in range(2 if with_sum else 3)]
    refs = refs[through:]
    sum_ref = refs.pop(0) if with_sum else None
    if last:
        table_ref, out_ref, done_ref, wide, spread, total, lags, sems = refs
        done_ref[...] = jnp.zeros_like(done_ref)
    else:
        total, *refs = refs
        wide, spread = refs[through:]
    windows, own_count = spread.shape[:2]
    ch_dev = wide.shape[1] // 2
    base = pl.multiple_of(lax.axis_index("win") * own_count, 8)

    def widen(w, carry):
        if with_sum:
            shared = ch_dev - own_count
            wide[w, shared:ch_dev, :] = blocks[0][skipped + w].astype(jnp.float32)
            rows = blocks[1][w].astype(jnp.float32)
            for tile in range(ch_dev // 8):
                at = base + 8 * tile
                at = pl.multiple_of(jnp.where(at < shared, at, at + own_count), 8)
                wide[w, pl.ds(at, 8), :] = rows[8 * tile : 8 * tile + 8]
        else:
            for half in range(2):
                place = half * (windows // 2) + w
                wide[place, :ch_dev, :] = blocks[0][place].astype(jnp.float32)
                wide[place, ch_dev:, :] = blocks[1 + half][w].astype(jnp.float32)
        return carry

    lax.fori_loop(0, windows if with_sum else windows // 2, widen, 0)

    def repeat(w, carry):
        for tile in range(own_count // 8):
            rows = wide[w, pl.ds(pl.multiple_of(base + 8 * tile, 8), 8), :]
            for i in range(8):
                for q in range(4):
                    spread[w, 8 * tile + i, q] = jnp.broadcast_to(rows[i : i + 1, q * H : (q + 1) * H], (8, H))
        return carry

    lax.fori_loop(0, windows, repeat, 0)

    group, tiles = 4, 3
    rounds = SPAN // (8 * tiles)

    def block(index, carry):
        g = index // rounds
        j = index % rounds
        start = pl.multiple_of(base + 8 * (g // 2) + 8 * tiles * j, 8)

        def add_window(w, sums):
            sums = list(sums)
            right = [
                [wide[w, pl.ds(pl.multiple_of(start + 8 * t, 8), 8), q * H : (q + 1) * H] for q in range(4)]
                for t in range(tiles)
            ]
            for i in range(group):
                left = [spread[w, group * g + i, q] for q in range(4)]
                for t in range(tiles):
                    at = 3 * (i * tiles + t)
                    r = right[t]
                    sums[at] = sums[at] + (left[0] * r[0] + left[1] * r[1])
                    sums[at + 1] = sums[at + 1] + (left[2] * r[2] + left[3] * r[3])
                    sums[at + 2] = sums[at + 2] + ((left[1] * r[0] - left[0] * r[1]) + (left[2] * r[3] - left[3] * r[2]))
            return tuple(sums)

        zero = jnp.zeros((8, H), jnp.float32)
        sums = lax.fori_loop(0, windows, add_window, (zero,) * (3 * group * tiles), unroll=2)
        for i in range(group):
            for t in range(tiles):
                at = 3 * (i * tiles + t)
                real, imag = fold_columns(sums[at], sums[at + 1], sums[at + 2])
                where = pl.ds(pl.multiple_of(8 * tiles * j + 8 * t, 8), 8)
                if with_sum:
                    real = real + sum_ref[group * g + i, where, :H]
                    imag = imag + sum_ref[group * g + i, where, H:]
                total[group * g + i, where, :H] = real
                total[group * g + i, where, H:] = imag
        return carry

    lax.fori_loop(0, own_count // group * rounds, block, 0)

    if last:
        copies = []
        for eight in range(own_count // 8):
            first = 8 * eight
            stacks = total[first : first + 8].reshape(8 * SPAN, F).astype(jnp.bfloat16)
            lagged = jnp.dot(stacks, table_ref[...], preferred_element_type=jnp.float32).reshape(8, SPAN, NLAG)
            for i in range(8):
                lags[first + i] = lagged[i, i + 1 : i + 1 + REACH, :]
            some = pl.ds(first, 8)
            copies.append(pltpu.make_async_copy(lags.at[some], out_ref.at[some], sems.at[eight]))
            copies[-1].start()
        for copy in copies:
            copy.wait()


def cross_call(blocks, windows, ch_dev, own_count, sums, table, skipped, share, through=()):
    columns = 2 * F
    last = table is not None
    with_sum = sums is not None
    operands = [*blocks, *through]
    anywhere = [pl.BlockSpec(memory_space=pl.ANY)] * len(through)
    in_specs = [vmem_spec()] * len(blocks) + anywhere
    if with_sum:
        operands.append(sums)
    scratch = [
        pltpu.VMEM((windows, 2 * ch_dev, columns), jnp.float32),
        pltpu.VMEM((windows, own_count, 4, 8, H), jnp.float32),
    ]
    if last:
        operands.append(table)
        scratch += [
            pltpu.VMEM((own_count, SPAN, F), jnp.float32),
            pltpu.VMEM((own_count, REACH, NLAG), jnp.float32),
            pltpu.SemaphoreType.DMA((own_count // 8,)),
        ]
    shape = (own_count, REACH, NLAG) if last else (own_count, SPAN, F)
    out_shape = [jax.ShapeDtypeStruct(shape, jnp.float32)]
    out_specs = [pl.BlockSpec(memory_space=pl.ANY) if last else vmem_spec()] + anywhere
    if last:
        out_shape.append(jax.ShapeDtypeStruct((8, H), jnp.float32))
        out_specs.append(vmem_spec())
    out_shape += [jax.ShapeDtypeStruct(array.shape, array.dtype) for array in through]
    return pl.pallas_call(
        functools.partial(cross_kernel, last, with_sum, skipped, len(through)),
        in_specs=in_specs + [vmem_spec()] * (len(operands) - len(in_specs)),
        input_output_aliases={len(blocks) + n: 1 + n for n in range(len(through))},
        out_specs=out_specs,
        out_shape=out_shape,
        scratch_shapes=scratch,
        compiler_params=pltpu.CompilerParams(vmem_limit_bytes=VMEM_LIMIT),
        cost_estimate=pl.CostEstimate(
            flops=int(30_000_000_000 * share), bytes_accessed=4 * windows * ch_dev * columns + 4 * own_count * SPAN * F, transcendentals=0
        ),
        name="cross",
    )(*operands)


def fold_kernel(incoming_ref, own_ref, owners_ref, high_ref, low_ref, earlier_ref, out_ref):
    ch_dev = out_ref.shape[0]
    rows = 2 * ch_dev
    pairs = own_ref.shape[0] // rows
    count, slots, columns = incoming_ref.shape
    owners = owners_ref[...].astype(jnp.float32)
    per_row = owners.shape[1] // ch_dev
    device = lax.axis_index("chan")
    line = jnp.sum(jnp.where(rows_of(owners.shape) == device // per_row, owners, 0.0), axis=0, keepdims=True)
    shape = (rows, owners.shape[1])
    line = jnp.broadcast_to(line, shape)
    first = device % per_row * ch_dev
    place = first + rows_of(shape) % ch_dev
    lane = lanes_of(shape)
    owner = jnp.sum(jnp.where(lane == place, line, 0.0), axis=1, keepdims=True)
    earlier = (lane >= first) & (lane < place) & (line == owner)
    rank = jnp.sum(earlier.astype(jnp.float32), axis=1, keepdims=True)
    source = (2 * CAP * owner + rank).astype(jnp.int32)
    shape = (rows, count * 2 * CAP)
    target = source + CAP * (rows_of(shape) // ch_dev)
    picker = (lanes_of(shape) == target).astype(jnp.float32).astype(jnp.bfloat16)
    sums = None
    for n in range(pairs):
        arrived = incoming_ref[:, 2 * CAP * n : 2 * CAP * (n + 1), :].reshape(count * 2 * CAP, columns)
        right = jnp.dot(picker, arrived, preferred_element_type=jnp.float32)
        left = own_ref[rows * n : rows * (n + 1), :].astype(jnp.float32)
        l = [left[:, q * H : (q + 1) * H] for q in range(4)]
        r = [right[:, q * H : (q + 1) * H] for q in range(4)]
        terms = [
            l[0] * r[0] + l[1] * r[1],
            l[2] * r[2] + l[3] * r[3],
            (l[1] * r[0] - l[0] * r[1]) + (l[2] * r[3] - l[3] * r[2]),
        ]
        sums = terms if sums is None else [total + term for total, term in zip(sums, terms)]
    stacks = jnp.concatenate(fold_columns(*[total[:ch_dev] + total[ch_dev:] for total in sums]), axis=1)
    out_ref[...] = lag_transform(stacks, high_ref[...], low_ref[...])


def fold_call(incoming, own, owners, ch_dev, tables, earlier):
    return pl.pallas_call(
        fold_kernel,
        in_specs=[vmem_spec()] * 5 + [pl.BlockSpec(memory_space=pl.ANY)],
        out_specs=vmem_spec(),
        out_shape=jax.ShapeDtypeStruct((ch_dev, NLAG), jnp.float32),
        compiler_params=pltpu.CompilerParams(vmem_limit_bytes=FOLD_VMEM_LIMIT),
        cost_estimate=pl.CostEstimate(
            flops=4 * ch_dev * incoming.size, bytes_accessed=2 * (incoming.size + own.size), transcendentals=0
        ),
        name="fold",
    )(incoming, own, owners, *tables, earlier)


def from_above(block):
    count = lax.axis_size("chan")
    return lax.ppermute(block, "chan", [(i, i - 1) for i in range(1, count)])


def round_win(block, shift):
    count = lax.axis_size("win")
    return lax.ppermute(block, "win", [(i, (i + shift) % count) for i in range(count)])


def local(traces, quality, fold_block, fold_offset):
    win_dev, ch_dev, length = traces.shape
    chan_count = lax.axis_size("chan")
    win_count = lax.axis_size("win")
    window_part = lax.axis_index("win")
    own_count = ch_dev // win_count
    shared = ch_dev - own_count
    tables = [jnp.asarray(t) for t in inverse_tables(1.0 / math.sqrt(F * win_dev * win_count))]
    owners = fold_block.reshape(-1, 2 * ch_dev)
    places = fold_offset.reshape(-1, 2 * ch_dev)
    early, late, flat, outgoing, *row_parts = spectra_call(
        traces.reshape(win_dev * ch_dev, length), quality.reshape(1, ch_dev), owners, places, chan_count, own_count
    )
    half = win_dev // 2
    halves = [rows.reshape(half, ch_dev, 2 * F) for rows in (early, late)]
    if not row_parts:
        row_parts = [jnp.concatenate([block[:, shared:] for block in halves], axis=0)]
        row_parts += [block[:, :shared] for block in halves]
    ready, *lower = row_parts
    upper = [from_above(block) for block in halves]
    common = [round_win(ready, shift) for shift in range(1, win_count)]
    incoming = lax.all_to_all(outgoing, "chan", split_axis=0, concat_axis=0, tiled=True)

    def offers(part):
        rows = jnp.concatenate([lower[part], upper[part]], axis=1)
        return [
            lax.dynamic_slice_in_dim(rows, (window_part + shift) % win_count * own_count, ch_dev, 1)
            for shift in range(1, win_count)
        ]

    sooner = [round_win(block, shift) for shift, block in enumerate(offers(0), 1)]
    sums, *waiting = cross_call(
        [flat.reshape(win_dev, ch_dev, 2 * F)] + upper, win_dev, ch_dev, own_count, None, None, 0, 1.0, through=offers(1)
    )
    later = [round_win(block, shift) for shift, block in enumerate(waiting, 1)]
    arrived = []
    for rows, *others in zip(common, sooner, later):
        arrived += [([rows, block], n * half) for n, block in enumerate(others)]
    for n, (blocks, skipped) in enumerate(arrived):
        ends = tables[0] if n == len(arrived) - 1 else None
        sums, *done = cross_call(blocks, half, ch_dev, own_count, sums, ends, skipped, 0.5)
    share = fold_call(incoming, flat, owners, ch_dev, tables, done[0])
    fold = lax.dynamic_slice_in_dim(share, window_part * own_count, own_count, 0)
    for shift in range(1, win_count):
        target = (window_part + shift) % win_count * own_count
        fold = fold + round_win(lax.dynamic_slice_in_dim(share, target, own_count, 0), shift)
    return (sums, fold)


def solution(mesh):
    in_specs = (P("win", "chan", None), P("chan"), P(), P())
    out_specs = (P(("chan", "win"), None, None), P(("chan", "win"), None))
    return jax.shard_map(local, mesh=mesh, in_specs=in_specs, out_specs=out_specs, check_vma=False)
```

```python
import functools
import math

import jax
import jax.numpy as jnp
import numpy as np
from jax import lax
from jax.experimental import pallas as pl
from jax.experimental.pallas import tpu as pltpu
from jax.sharding import PartitionSpec as P

F = 256
H = F // 2
BAND_LO = 32
NLAG = 256
REACH = 64
CAP = 8
SPAN = REACH + 8
smooth_reach = 4
QUARTERS = 4
VMEM_LIMIT = 24 * 1024 * 1024
FOLD_VMEM_LIMIT = 16 * 1024 * 1024
SPECTRA_VMEM_LIMIT = 59 * 1024 * 1024


def bin_order():
    residues = np.arange(H)
    first = (residues - BAND_LO) % F
    second = (-residues - BAND_LO) % F
    second[0] = (H - BAND_LO) % F
    return first, second


def forward_table(length):
    samples = np.arange(length // 4, dtype=np.int64)[:, None]
    parts = []
    for bins in bin_order():
        angles = (samples * (bins + BAND_LO)[None, :] % length) * (2.0 * math.pi / length)
        parts += [np.cos(angles), -np.sin(angles)]
    return np.concatenate(parts, axis=1).astype(np.float32).astype(jnp.bfloat16)


def inverse_tables(factor):
    shifts = (np.arange(NLAG) + NLAG // 2)[None, :]
    residues = np.arange(H)[:, None]
    angles = (residues * shifts % NLAG) * (2.0 * math.pi / NLAG)
    sign = np.where(shifts[0] % 2 == 0, 1.0, -1.0)
    real, imag = np.cos(angles), -np.sin(angles)
    real[0] = (1.0 + sign) / 2.0
    imag[0] = (1.0 - sign) / 2.0
    table = np.concatenate([real, imag], axis=0) * factor
    high = table.astype(np.float32).astype(jnp.bfloat16)
    low = (table - high.astype(np.float64)).astype(np.float32).astype(jnp.bfloat16)
    return high, low


def lag_transform(stacks, high, low):
    top = stacks.astype(jnp.bfloat16)
    rest = (stacks - top.astype(jnp.float32)).astype(jnp.bfloat16)
    dot = functools.partial(jnp.dot, preferred_element_type=jnp.float32)
    return dot(top, high) + (dot(rest, high) + dot(top, low))


def fold_columns(first, second, imag):
    lane = lax.broadcasted_iota(jnp.int32, first.shape, first.ndim - 1)
    return first + second, jnp.where(lane == 0, first - second, imag)


def lanes_of(shape):
    return lax.broadcasted_iota(jnp.int32, shape, len(shape) - 1)


def rows_of(shape):
    return lax.broadcasted_iota(jnp.int32, shape, len(shape) - 2)


def band_matrix():
    def bins(index):
        lane = index & (H - 1)
        residue = jnp.where(index < H, lane, jnp.where(lane == 0, H, F - lane))
        return (residue - BAND_LO + F) & (F - 1)

    apart = bins(rows_of((F, F))) - bins(lanes_of((F, F)))
    return (jnp.abs(apart) <= smooth_reach).astype(jnp.float32).astype(jnp.bfloat16)


def exact_dot(left, right):
    return jnp.dot(left.astype(jnp.bfloat16), right.astype(jnp.bfloat16), preferred_element_type=jnp.float32)


def over(value, power):
    return value >> (power.bit_length() - 1)


def within(value, power):
    return value & (power - 1)


def slot_selector(owners, places, device, ch_dev):
    height, width = owners.shape
    per_row = width // ch_dev
    wanted = (owners == device).astype(jnp.float32)
    before = rows_of((width, width))
    after = lanes_of((width, width))
    earlier = ((before < after) & (over(before, ch_dev) == over(after, ch_dev))).astype(jnp.float32)
    ranks = exact_dot(wanted, earlier)
    slots = jnp.where(wanted > 0, ranks, float(CAP))
    count = height * per_row * 2 * CAP
    to_row = (over(rows_of((count, height)), 2 * CAP * per_row) == lanes_of((count, height))).astype(jnp.float32)
    row_slots = exact_dot(to_row, slots)
    row_places = exact_dot(to_row, places.astype(jnp.float32))
    shape = (count, width)
    row = rows_of(shape)
    mine = (row_slots == within(row, CAP).astype(jnp.float32)) & (
        over(lanes_of(shape), ch_dev) == within(over(row, 2 * CAP), per_row)
    )
    place = jnp.sum(jnp.where(mine, row_places + 1.0, 0.0), axis=1, keepdims=True).astype(jnp.int32) - 1
    shape = (count, 2 * ch_dev)
    half = within(over(rows_of(shape), CAP), 2)
    lane = lanes_of(shape)
    return ((lane == place + ch_dev * half) & (place >= 0)).astype(jnp.float32).astype(jnp.bfloat16)


def turned_sum(quarters, real, imag, negative):
    rows = quarters[0].shape[0]
    lane = lanes_of((rows, H))
    residue = ((F - lane) if negative else lane) & 3
    sign = jnp.where((residue & 1) == 0, 1.0, -1.0)
    straight = jnp.where(residue == 0, 1.0, jnp.where(residue == 2, -1.0, 0.0))
    turned = jnp.where(residue == 1, 1.0, jnp.where(residue == 3, -1.0, 0.0))
    re = [quarter[:, real * H : (real + 1) * H] for quarter in quarters]
    im = [quarter[:, imag * H : (imag + 1) * H] for quarter in quarters]
    odd_re, odd_im = re[1] + sign * re[3], im[1] + sign * im[3]
    return (
        re[0] + sign * re[2] + (straight * odd_re + turned * odd_im),
        im[0] + sign * im[2] + (straight * odd_im - turned * odd_re),
    )


def spectra_kernel(traces_ref, table_ref, quality_ref, owners_ref, places_ref, *refs):
    early_ref, late_ref, whitened_ref, outgoing_ref, *row_refs = refs[:-14]
    traces, table, quality, owners, places, band, keep_rows, products, white, white_windows, sent, selector, sems, out_sems = refs[-14:]
    row_parts, chunks, rows, depth = traces.shape
    ch_dev = quality.shape[1]
    pair = 2 * ch_dev
    count = outgoing_ref.shape[0]
    slots = sent.shape[2]

    def traces_copy(part, k):
        source = traces_ref.at[pl.ds(part * rows, rows), pl.ds(k * depth, depth)]
        return pltpu.make_async_copy(source, traces.at[part, k], sems.at[part, k])

    small = [
        pltpu.make_async_copy(source, target, sems.at[row_parts, k])
        for k, (source, target) in enumerate(
            ((table_ref, table), (quality_ref, quality), (owners_ref, owners), (places_ref, places))
        )
    ]
    for copy in small:
        copy.start()
    for part in range(row_parts):
        for k in range(chunks):
            traces_copy(part, k).start()

    small[0].wait()
    leaving = []

    def prepare():
        band[...] = band_matrix()
        for copy in small[1:]:
            copy.wait()
        shape = (rows, ch_dev)
        keep = jnp.sum(
            jnp.where(within(rows_of(shape), ch_dev) == lanes_of(shape), quality[...].astype(jnp.float32), 0.0),
            axis=1, keepdims=True,
        )
        selector[...] = slot_selector(owners[...], places[...], lax.axis_index("chan"), ch_dev)
        keep_rows[...] = jnp.broadcast_to(keep, keep_rows.shape)

    def transform(part):
        for k in range(chunks):
            traces_copy(part, k).wait()
        stacked = traces[part].reshape(chunks * rows, depth)
        products[part % 2] = jnp.dot(stacked, table[...], preferred_element_type=jnp.float32)

    def whiten(part):
        quarters = [products[part % 2, k * rows : (k + 1) * rows, :] for k in range(chunks)]
        parts = turned_sum(quarters, 0, 1, False) + turned_sum(quarters, 2, 3, True)
        energy = jnp.concatenate(
            [parts[0] * parts[0] + parts[1] * parts[1], parts[2] * parts[2] + parts[3] * parts[3]], axis=1
        )
        top = energy.astype(jnp.bfloat16)
        rest = (energy - top.astype(jnp.float32)).astype(jnp.bfloat16)
        smooth = jnp.dot(top, band[...], preferred_element_type=jnp.float32) + jnp.dot(
            rest, band[...], preferred_element_type=jnp.float32
        )
        water = jnp.sum(energy, axis=1, keepdims=True) * (1.0 / F)
        scaling = lax.rsqrt(smooth * (1.0 / (2.0 * smooth_reach + 1.0)) + (0.1 * water + 1e-06))
        near, far = scaling[:, :H] * keep_rows[...], scaling[:, H:] * keep_rows[...]
        values = jnp.concatenate(
            [parts[0] * near, parts[1] * near, parts[2] * far, parts[3] * far], axis=1
        ).astype(jnp.bfloat16)
        white[part] = values
        if row_refs:
            white_windows[part] = values.reshape(rows // ch_dev, ch_dev, values.shape[-1])
        for n in range(rows // pair):
            chosen = jnp.dot(
                selector[...], values[pair * n : pair * (n + 1), :], preferred_element_type=jnp.float32
            ).astype(jnp.bfloat16)
            sent[part, :, 2 * CAP * n : 2 * CAP * (n + 1), :] = chosen.reshape(count, 2 * CAP, chosen.shape[-1])

    def leave(part):
        pairs = rows // pair
        copies = [
            (sent.at[part], outgoing_ref.at[:, pl.ds(part * slots, slots), :]),
            (white.at[part], whitened_ref.at[pl.ds(part * rows, rows), :]),
        ]
        if row_refs:
            shared_ref, *lower_refs = row_refs
            height = shared_ref.shape[1]
            split = ch_dev - height
            copies.append(
                (white_windows.at[part, :, pl.ds(split, height), :], shared_ref.at[pl.ds(2 * pairs * part, 2 * pairs)])
            )
        for n in range(pairs):
            late, place = divmod(part * pairs + n, row_parts * pairs // 2)
            copies.append(
                (white.at[part, pl.ds(n * pair, pair), :], (early_ref, late_ref)[late].at[pl.ds(place * pair, pair), :])
            )
            if row_refs:
                copies.append(
                    (
                        white_windows.at[part, pl.ds(2 * n, 2), pl.ds(0, split), :],
                        lower_refs[late].at[pl.ds(2 * place, 2)],
                    )
                )
        for n, (source, target) in enumerate(copies):
            leaving.append(pltpu.make_async_copy(source, target, out_sems.at[part, n]))
            leaving[-1].start()

    for part in range(row_parts + 1):
        if part < row_parts:
            transform(part)
        if part == 0:
            prepare()
        else:
            whiten(part - 1)
            leave(part - 1)
    for copy in leaving:
        copy.wait()


def vmem_spec():
    return pl.BlockSpec(memory_space=pltpu.VMEM)


def smem_spec():
    return pl.BlockSpec(memory_space=pltpu.SMEM)


def whole(array):
    return pl.BlockSpec(array.shape, lambda s: (0,) * array.ndim)


def spectra_call(traces, quality, owners, places, chan_count, own_count):
    rows, length = traces.shape
    ch_dev = quality.shape[1]
    row_steps = rows // (4 * ch_dev) if rows % (4 * ch_dev) == 0 else rows // (2 * ch_dev)
    part, depth = rows // row_steps, length // QUARTERS
    slots = part // (2 * ch_dev) * 2 * CAP
    anywhere = pl.BlockSpec(memory_space=pl.ANY)
    out_shape = [
        jax.ShapeDtypeStruct((rows // 2, 2 * F), jnp.bfloat16),
        jax.ShapeDtypeStruct((rows // 2, 2 * F), jnp.bfloat16),
        jax.ShapeDtypeStruct((rows, 2 * F), jnp.bfloat16),
        jax.ShapeDtypeStruct((chan_count, row_steps * slots, 2 * F), jnp.bfloat16),
    ]
    if own_count % 16 == 0:
        windows, lower = rows // ch_dev, ch_dev - own_count
        out_shape += [
            jax.ShapeDtypeStruct((windows, own_count, 2 * F), jnp.bfloat16),
            jax.ShapeDtypeStruct((windows // 2, lower, 2 * F), jnp.bfloat16),
            jax.ShapeDtypeStruct((windows // 2, lower, 2 * F), jnp.bfloat16),
        ]
    return pl.pallas_call(
        spectra_kernel,
        in_specs=[anywhere] * 5,
        out_specs=[anywhere] * len(out_shape),
        out_shape=out_shape,
        scratch_shapes=[
            pltpu.VMEM((row_steps, QUARTERS, part, depth), jnp.bfloat16),
            pltpu.VMEM((depth, 2 * F), jnp.bfloat16),
            pltpu.VMEM(quality.shape, jnp.int32),
            pltpu.VMEM(owners.shape, jnp.int32),
            pltpu.VMEM(places.shape, jnp.int32),
            pltpu.VMEM((F, F), jnp.bfloat16),
            pltpu.VMEM((part, H), jnp.float32),
            pltpu.VMEM((2, QUARTERS * part, 2 * F), jnp.float32),
            pltpu.VMEM((row_steps, part, 2 * F), jnp.bfloat16),
            pltpu.VMEM((row_steps, part // ch_dev, ch_dev, 2 * F), jnp.bfloat16),
            pltpu.VMEM((row_steps, chan_count, slots, 2 * F), jnp.bfloat16),
            pltpu.VMEM((chan_count * 2 * CAP, 2 * ch_dev), jnp.bfloat16),
            pltpu.SemaphoreType.DMA((row_steps + 1, QUARTERS)),
            pltpu.SemaphoreType.DMA((row_steps, 3 + 2 * (part // (2 * ch_dev)))),
        ],
        compiler_params=pltpu.CompilerParams(vmem_limit_bytes=SPECTRA_VMEM_LIMIT),
        cost_estimate=pl.CostEstimate(
            flops=2 * rows * length * 2 * F, bytes_accessed=2 * rows * length, transcendentals=rows * F
        ),
        name="spectra",
    )(traces, jnp.asarray(forward_table(length)), quality, owners, places)


def cross_kernel(last, with_sum, skipped, through, *refs):
    refs = list(refs)
    blocks = [refs.pop(0) for _ in range(2 if with_sum else 3)]
    refs = refs[through:]
    sum_ref = refs.pop(0) if with_sum else None
    if last:
        table_ref, out_ref, done_ref, wide, spread, total, lags, sems = refs
        done_ref[...] = jnp.zeros_like(done_ref)
    else:
        total, *refs = refs
        wide, spread = refs[through:]
    windows, own_count = spread.shape[:2]
    ch_dev = wide.shape[1] // 2
    base = pl.multiple_of(lax.axis_index("win") * own_count, 8)

    def widen(w, carry):
        if with_sum:
            shared = ch_dev - own_count
            wide[w, shared:ch_dev, :] = blocks[0][skipped + w].astype(jnp.float32)
            rows = blocks[1][w].astype(jnp.float32)
            for tile in range(ch_dev // 8):
                at = base + 8 * tile
                at = pl.multiple_of(jnp.where(at < shared, at, at + own_count), 8)
                wide[w, pl.ds(at, 8), :] = rows[8 * tile : 8 * tile + 8]
        else:
            for half in range(2):
                place = half * (windows // 2) + w
                wide[place, :ch_dev, :] = blocks[0][place].astype(jnp.float32)
                wide[place, ch_dev:, :] = blocks[1 + half][w].astype(jnp.float32)
        return carry

    lax.fori_loop(0, windows if with_sum else windows // 2, widen, 0)

    def repeat(w, carry):
        for tile in range(own_count // 8):
            rows = wide[w, pl.ds(pl.multiple_of(base + 8 * tile, 8), 8), :]
            for i in range(8):
                for q in range(4):
                    spread[w, 8 * tile + i, q] = jnp.broadcast_to(rows[i : i + 1, q * H : (q + 1) * H], (8, H))
        return carry

    lax.fori_loop(0, windows, repeat, 0)

    group, tiles = 4, 3
    rounds = SPAN // (8 * tiles)

    def block(index, carry):
        g = index // rounds
        j = index % rounds
        start = pl.multiple_of(base + 8 * (g // 2) + 8 * tiles * j, 8)

        def add_window(w, sums):
            sums = list(sums)
            right = [
                [wide[w, pl.ds(pl.multiple_of(start + 8 * t, 8), 8), q * H : (q + 1) * H] for q in range(4)]
                for t in range(tiles)
            ]
            for i in range(group):
                left = [spread[w, group * g + i, q] for q in range(4)]
                for t in range(tiles):
                    at = 3 * (i * tiles + t)
                    r = right[t]
                    sums[at] = sums[at] + (left[0] * r[0] + left[1] * r[1])
                    sums[at + 1] = sums[at + 1] + (left[2] * r[2] + left[3] * r[3])
                    sums[at + 2] = sums[at + 2] + ((left[1] * r[0] - left[0] * r[1]) + (left[2] * r[3] - left[3] * r[2]))
            return tuple(sums)

        zero = jnp.zeros((8, H), jnp.float32)
        sums = lax.fori_loop(0, windows, add_window, (zero,) * (3 * group * tiles), unroll=2)
        for i in range(group):
            for t in range(tiles):
                at = 3 * (i * tiles + t)
                real, imag = fold_columns(sums[at], sums[at + 1], sums[at + 2])
                where = pl.ds(pl.multiple_of(8 * tiles * j + 8 * t, 8), 8)
                if with_sum:
                    real = real + sum_ref[group * g + i, where, :H]
                    imag = imag + sum_ref[group * g + i, where, H:]
                total[group * g + i, where, :H] = real
                total[group * g + i, where, H:] = imag
        return carry

    lax.fori_loop(0, own_count // group * rounds, block, 0)

    if last:
        copies = []
        for eight in range(own_count // 8):
            first = 8 * eight
            stacks = total[first : first + 8].reshape(8 * SPAN, F).astype(jnp.bfloat16)
            lagged = jnp.dot(stacks, table_ref[...], preferred_element_type=jnp.float32).reshape(8, SPAN, NLAG)
            for i in range(8):
                lags[first + i] = lagged[i, i + 1 : i + 1 + REACH, :]
            some = pl.ds(first, 8)
            copies.append(pltpu.make_async_copy(lags.at[some], out_ref.at[some], sems.at[eight]))
            copies[-1].start()
        for copy in copies:
            copy.wait()


def cross_call(blocks, windows, ch_dev, own_count, sums, table, skipped, share, through=()):
    columns = 2 * F
    last = table is not None
    with_sum = sums is not None
    operands = [*blocks, *through]
    anywhere = [pl.BlockSpec(memory_space=pl.ANY)] * len(through)
    in_specs = [vmem_spec()] * len(blocks) + anywhere
    if with_sum:
        operands.append(sums)
    scratch = [
        pltpu.VMEM((windows, 2 * ch_dev, columns), jnp.float32),
        pltpu.VMEM((windows, own_count, 4, 8, H), jnp.float32),
    ]
    if last:
        operands.append(table)
        scratch += [
            pltpu.VMEM((own_count, SPAN, F), jnp.float32),
            pltpu.VMEM((own_count, REACH, NLAG), jnp.float32),
            pltpu.SemaphoreType.DMA((own_count // 8,)),
        ]
    shape = (own_count, REACH, NLAG) if last else (own_count, SPAN, F)
    out_shape = [jax.ShapeDtypeStruct(shape, jnp.float32)]
    out_specs = [pl.BlockSpec(memory_space=pl.ANY) if last else vmem_spec()] + anywhere
    if last:
        out_shape.append(jax.ShapeDtypeStruct((8, H), jnp.float32))
        out_specs.append(vmem_spec())
    out_shape += [jax.ShapeDtypeStruct(array.shape, array.dtype) for array in through]
    return pl.pallas_call(
        functools.partial(cross_kernel, last, with_sum, skipped, len(through)),
        in_specs=in_specs + [vmem_spec()] * (len(operands) - len(in_specs)),
        input_output_aliases={len(blocks) + n: 1 + n for n in range(len(through))},
        out_specs=out_specs,
        out_shape=out_shape,
        scratch_shapes=scratch,
        compiler_params=pltpu.CompilerParams(vmem_limit_bytes=VMEM_LIMIT),
        cost_estimate=pl.CostEstimate(
            flops=int(30_000_000_000 * share), bytes_accessed=4 * windows * ch_dev * columns + 4 * own_count * SPAN * F, transcendentals=0
        ),
        name="cross",
    )(*operands)


def fold_kernel(incoming_ref, own_ref, owners_ref, high_ref, low_ref, earlier_ref, out_ref):
    ch_dev = out_ref.shape[0]
    rows = 2 * ch_dev
    pairs = own_ref.shape[0] // rows
    count, slots, columns = incoming_ref.shape
    owners = owners_ref[...].astype(jnp.float32)
    per_row = owners.shape[1] // ch_dev
    device = lax.axis_index("chan")
    line = jnp.sum(jnp.where(rows_of(owners.shape) == device // per_row, owners, 0.0), axis=0, keepdims=True)
    shape = (rows, owners.shape[1])
    line = jnp.broadcast_to(line, shape)
    first = device % per_row * ch_dev
    place = first + rows_of(shape) % ch_dev
    lane = lanes_of(shape)
    owner = jnp.sum(jnp.where(lane == place, line, 0.0), axis=1, keepdims=True)
    earlier = (lane >= first) & (lane < place) & (line == owner)
    rank = jnp.sum(earlier.astype(jnp.float32), axis=1, keepdims=True)
    source = (2 * CAP * owner + rank).astype(jnp.int32)
    shape = (rows, count * 2 * CAP)
    target = source + CAP * (rows_of(shape) // ch_dev)
    picker = (lanes_of(shape) == target).astype(jnp.float32).astype(jnp.bfloat16)
    sums = None
    for n in range(pairs):
        arrived = incoming_ref[:, 2 * CAP * n : 2 * CAP * (n + 1), :].reshape(count * 2 * CAP, columns)
        right = jnp.dot(picker, arrived, preferred_element_type=jnp.float32)
        left = own_ref[rows * n : rows * (n + 1), :].astype(jnp.float32)
        l = [left[:, q * H : (q + 1) * H] for q in range(4)]
        r = [right[:, q * H : (q + 1) * H] for q in range(4)]
        terms = [
            l[0] * r[0] + l[1] * r[1],
            l[2] * r[2] + l[3] * r[3],
            (l[1] * r[0] - l[0] * r[1]) + (l[2] * r[3] - l[3] * r[2]),
        ]
        sums = terms if sums is None else [total + term for total, term in zip(sums, terms)]
    stacks = jnp.concatenate(fold_columns(*[total[:ch_dev] + total[ch_dev:] for total in sums]), axis=1)
    out_ref[...] = lag_transform(stacks, high_ref[...], low_ref[...])


def fold_call(incoming, own, owners, ch_dev, tables, earlier):
    return pl.pallas_call(
        fold_kernel,
        in_specs=[vmem_spec()] * 5 + [pl.BlockSpec(memory_space=pl.ANY)],
        out_specs=vmem_spec(),
        out_shape=jax.ShapeDtypeStruct((ch_dev, NLAG), jnp.float32),
        compiler_params=pltpu.CompilerParams(vmem_limit_bytes=FOLD_VMEM_LIMIT),
        cost_estimate=pl.CostEstimate(
            flops=4 * ch_dev * incoming.size, bytes_accessed=2 * (incoming.size + own.size), transcendentals=0
        ),
        name="fold",
    )(incoming, own, owners, *tables, earlier)


def from_above(block):
    count = lax.axis_size("chan")
    return lax.ppermute(block, "chan", [(i, i - 1) for i in range(1, count)])


def round_win(block, shift):
    count = lax.axis_size("win")
    return lax.ppermute(block, "win", [(i, (i + shift) % count) for i in range(count)])


def local(traces, quality, fold_block, fold_offset):
    win_dev, ch_dev, length = traces.shape
    chan_count = lax.axis_size("chan")
    win_count = lax.axis_size("win")
    window_part = lax.axis_index("win")
    own_count = ch_dev // win_count
    shared = ch_dev - own_count
    tables = [jnp.asarray(t) for t in inverse_tables(1.0 / math.sqrt(F * win_dev * win_count))]
    owners = fold_block.reshape(-1, 2 * ch_dev)
    places = fold_offset.reshape(-1, 2 * ch_dev)
    early, late, flat, outgoing, *row_parts = spectra_call(
        traces.reshape(win_dev * ch_dev, length), quality.reshape(1, ch_dev), owners, places, chan_count, own_count
    )
    half = win_dev // 2
    halves = [rows.reshape(half, ch_dev, 2 * F) for rows in (early, late)]
    if not row_parts:
        row_parts = [jnp.concatenate([block[:, shared:] for block in halves], axis=0)]
        row_parts += [block[:, :shared] for block in halves]
    ready, *lower = row_parts
    upper = [from_above(block) for block in halves]
    common = [round_win(ready, shift) for shift in range(1, win_count)]
    incoming = lax.all_to_all(outgoing, "chan", split_axis=0, concat_axis=0, tiled=True)

    def offers(part):
        rows = jnp.concatenate([lower[part], upper[part]], axis=1)
        return [
            lax.dynamic_slice_in_dim(rows, (window_part + shift) % win_count * own_count, ch_dev, 1)
            for shift in range(1, win_count)
        ]

    sooner = [round_win(block, shift) for shift, block in enumerate(offers(0), 1)]
    sums, *waiting = cross_call(
        [flat.reshape(win_dev, ch_dev, 2 * F)] + upper, win_dev, ch_dev, own_count, None, None, 0, 1.0, through=offers(1)
    )
    later = [round_win(block, shift) for shift, block in enumerate(waiting, 1)]
    arrived = []
    for rows, *others in zip(common, sooner, later):
        arrived += [([rows, block], n * half) for n, block in enumerate(others)]
    for n, (blocks, skipped) in enumerate(arrived):
        ends = tables[0] if n == len(arrived) - 1 else None
        sums, *done = cross_call(blocks, half, ch_dev, own_count, sums, ends, skipped, 0.5)
    share = fold_call(incoming, flat, owners, ch_dev, tables, done[0])
    fold = lax.dynamic_slice_in_dim(share, window_part * own_count, own_count, 0)
    for shift in range(1, win_count):
        target = (window_part + shift) % win_count * own_count
        fold = fold + round_win(lax.dynamic_slice_in_dim(share, target, own_count, 0), shift)
    return (sums, fold)


def solution(mesh):
    in_specs = (P("win", "chan", None), P("chan"), P(), P())
    out_specs = (P(("chan", "win"), None, None), P(("chan", "win"), None))
    return jax.shard_map(local, mesh=mesh, in_specs=in_specs, out_specs=out_specs, check_vma=False)
```

```python
import functools
import math

import jax
import jax.numpy as jnp
import numpy as np
from jax import lax
from jax.experimental import pallas as pl
from jax.experimental.pallas import tpu as pltpu
from jax.sharding import PartitionSpec as P

F = 256
H = F // 2
BAND_LO = 32
NLAG = 256
REACH = 64
CAP = 8
SPAN = REACH + 8
smooth_reach = 4
QUARTERS = 4
VMEM_LIMIT = 24 * 1024 * 1024
FOLD_VMEM_LIMIT = 16 * 1024 * 1024
SPECTRA_VMEM_LIMIT = 59 * 1024 * 1024


def bin_order():
    residues = np.arange(H)
    first = (residues - BAND_LO) % F
    second = (-residues - BAND_LO) % F
    second[0] = (H - BAND_LO) % F
    return first, second


def forward_table(length):
    samples = np.arange(length // 4, dtype=np.int64)[:, None]
    parts = []
    for bins in bin_order():
        angles = (samples * (bins + BAND_LO)[None, :] % length) * (2.0 * math.pi / length)
        parts += [np.cos(angles), -np.sin(angles)]
    return np.concatenate(parts, axis=1).astype(np.float32).astype(jnp.bfloat16)


def inverse_tables(factor):
    shifts = (np.arange(NLAG) + NLAG // 2)[None, :]
    residues = np.arange(H)[:, None]
    angles = (residues * shifts % NLAG) * (2.0 * math.pi / NLAG)
    sign = np.where(shifts[0] % 2 == 0, 1.0, -1.0)
    real, imag = np.cos(angles), -np.sin(angles)
    real[0] = (1.0 + sign) / 2.0
    imag[0] = (1.0 - sign) / 2.0
    table = np.concatenate([real, imag], axis=0) * factor
    high = table.astype(np.float32).astype(jnp.bfloat16)
    low = (table - high.astype(np.float64)).astype(np.float32).astype(jnp.bfloat16)
    return high, low


def lag_transform(stacks, high, low):
    top = stacks.astype(jnp.bfloat16)
    rest = (stacks - top.astype(jnp.float32)).astype(jnp.bfloat16)
    dot = functools.partial(jnp.dot, preferred_element_type=jnp.float32)
    return dot(top, high) + (dot(rest, high) + dot(top, low))


def fold_columns(first, second, imag):
    lane = lax.broadcasted_iota(jnp.int32, first.shape, first.ndim - 1)
    return first + second, jnp.where(lane == 0, first - second, imag)


def lanes_of(shape):
    return lax.broadcasted_iota(jnp.int32, shape, len(shape) - 1)


def rows_of(shape):
    return lax.broadcasted_iota(jnp.int32, shape, len(shape) - 2)


def band_matrix():
    def bins(index):
        lane = index & (H - 1)
        residue = jnp.where(index < H, lane, jnp.where(lane == 0, H, F - lane))
        return (residue - BAND_LO + F) & (F - 1)

    apart = bins(rows_of((F, F))) - bins(lanes_of((F, F)))
    return (jnp.abs(apart) <= smooth_reach).astype(jnp.float32).astype(jnp.bfloat16)


def exact_dot(left, right):
    return jnp.dot(left.astype(jnp.bfloat16), right.astype(jnp.bfloat16), preferred_element_type=jnp.float32)


def over(value, power):
    return value >> (power.bit_length() - 1)


def within(value, power):
    return value & (power - 1)


def slot_selector(owners, places, device, ch_dev):
    height, width = owners.shape
    per_row = width // ch_dev
    wanted = (owners == device).astype(jnp.float32)
    before = rows_of((width, width))
    after = lanes_of((width, width))
    earlier = ((before < after) & (over(before, ch_dev) == over(after, ch_dev))).astype(jnp.float32)
    ranks = exact_dot(wanted, earlier)
    slots = jnp.where(wanted > 0, ranks, float(CAP))
    count = height * per_row * 2 * CAP
    to_row = (over(rows_of((count, height)), 2 * CAP * per_row) == lanes_of((count, height))).astype(jnp.float32)
    row_slots = exact_dot(to_row, slots)
    row_places = exact_dot(to_row, places.astype(jnp.float32))
    shape = (count, width)
    row = rows_of(shape)
    mine = (row_slots == within(row, CAP).astype(jnp.float32)) & (
        over(lanes_of(shape), ch_dev) == within(over(row, 2 * CAP), per_row)
    )
    place = jnp.sum(jnp.where(mine, row_places + 1.0, 0.0), axis=1, keepdims=True).astype(jnp.int32) - 1
    shape = (count, 2 * ch_dev)
    half = within(over(rows_of(shape), CAP), 2)
    lane = lanes_of(shape)
    return ((lane == place + ch_dev * half) & (place >= 0)).astype(jnp.float32).astype(jnp.bfloat16)


def turned_sum(quarters, real, imag, negative):
    rows = quarters[0].shape[0]
    lane = lanes_of((rows, H))
    residue = ((F - lane) if negative else lane) & 3
    sign = jnp.where((residue & 1) == 0, 1.0, -1.0)
    straight = jnp.where(residue == 0, 1.0, jnp.where(residue == 2, -1.0, 0.0))
    turned = jnp.where(residue == 1, 1.0, jnp.where(residue == 3, -1.0, 0.0))
    re = [quarter[:, real * H : (real + 1) * H] for quarter in quarters]
    im = [quarter[:, imag * H : (imag + 1) * H] for quarter in quarters]
    odd_re, odd_im = re[1] + sign * re[3], im[1] + sign * im[3]
    return (
        re[0] + sign * re[2] + (straight * odd_re + turned * odd_im),
        im[0] + sign * im[2] + (straight * odd_im - turned * odd_re),
    )


def spectra_kernel(traces_ref, table_ref, quality_ref, owners_ref, places_ref, *refs):
    early_ref, late_ref, whitened_ref, outgoing_ref, *row_refs = refs[:-14]
    traces, table, quality, owners, places, band, keep_rows, products, white, white_windows, sent, selector, sems, out_sems = refs[-14:]
    row_parts, chunks, rows, depth = traces.shape
    ch_dev = quality.shape[1]
    pair = 2 * ch_dev
    count = outgoing_ref.shape[0]
    slots = sent.shape[2]

    def traces_copy(part, k):
        source = traces_ref.at[pl.ds(part * rows, rows), pl.ds(k * depth, depth)]
        return pltpu.make_async_copy(source, traces.at[part, k], sems.at[part, k])

    small = [
        pltpu.make_async_copy(source, target, sems.at[row_parts, k])
        for k, (source, target) in enumerate(
            ((table_ref, table), (quality_ref, quality), (owners_ref, owners), (places_ref, places))
        )
    ]
    for copy in small:
        copy.start()
    for part in range(row_parts):
        for k in range(chunks):
            traces_copy(part, k).start()

    small[0].wait()
    leaving = []

    def prepare():
        band[...] = band_matrix()
        for copy in small[1:]:
            copy.wait()
        shape = (rows, ch_dev)
        keep = jnp.sum(
            jnp.where(within(rows_of(shape), ch_dev) == lanes_of(shape), quality[...].astype(jnp.float32), 0.0),
            axis=1, keepdims=True,
        )
        selector[...] = slot_selector(owners[...], places[...], lax.axis_index("chan"), ch_dev)
        keep_rows[...] = jnp.broadcast_to(keep, keep_rows.shape)

    def transform(part):
        for k in range(chunks):
            traces_copy(part, k).wait()
        stacked = traces[part].reshape(chunks * rows, depth)
        products[part % 2] = jnp.dot(stacked, table[...], preferred_element_type=jnp.float32)

    def whiten(part):
        quarters = [products[part % 2, k * rows : (k + 1) * rows, :] for k in range(chunks)]
        parts = turned_sum(quarters, 0, 1, False) + turned_sum(quarters, 2, 3, True)
        energy = jnp.concatenate(
            [parts[0] * parts[0] + parts[1] * parts[1], parts[2] * parts[2] + parts[3] * parts[3]], axis=1
        )
        top = energy.astype(jnp.bfloat16)
        rest = (energy - top.astype(jnp.float32)).astype(jnp.bfloat16)
        smooth = jnp.dot(top, band[...], preferred_element_type=jnp.float32) + jnp.dot(
            rest, band[...], preferred_element_type=jnp.float32
        )
        water = jnp.sum(energy, axis=1, keepdims=True) * (1.0 / F)
        scaling = lax.rsqrt(smooth * (1.0 / (2.0 * smooth_reach + 1.0)) + (0.1 * water + 1e-06))
        near, far = scaling[:, :H] * keep_rows[...], scaling[:, H:] * keep_rows[...]
        values = jnp.concatenate(
            [parts[0] * near, parts[1] * near, parts[2] * far, parts[3] * far], axis=1
        ).astype(jnp.bfloat16)
        white[part] = values
        if row_refs:
            white_windows[part] = values.reshape(rows // ch_dev, ch_dev, values.shape[-1])
        for n in range(rows // pair):
            chosen = jnp.dot(
                selector[...], values[pair * n : pair * (n + 1), :], preferred_element_type=jnp.float32
            ).astype(jnp.bfloat16)
            sent[part, :, 2 * CAP * n : 2 * CAP * (n + 1), :] = chosen.reshape(count, 2 * CAP, chosen.shape[-1])

    def leave(part):
        pairs = rows // pair
        copies = [
            (sent.at[part], outgoing_ref.at[:, pl.ds(part * slots, slots), :]),
            (white.at[part], whitened_ref.at[pl.ds(part * rows, rows), :]),
        ]
        if row_refs:
            shared_ref, *lower_refs = row_refs
            height = shared_ref.shape[1]
            split = ch_dev - height
            copies.append(
                (white_windows.at[part, :, pl.ds(split, height), :], shared_ref.at[pl.ds(2 * pairs * part, 2 * pairs)])
            )
        for n in range(pairs):
            late, place = divmod(part * pairs + n, row_parts * pairs // 2)
            copies.append(
                (white.at[part, pl.ds(n * pair, pair), :], (early_ref, late_ref)[late].at[pl.ds(place * pair, pair), :])
            )
            if row_refs:
                copies.append(
                    (
                        white_windows.at[part, pl.ds(2 * n, 2), pl.ds(0, split), :],
                        lower_refs[late].at[pl.ds(2 * place, 2)],
                    )
                )
        for n, (source, target) in enumerate(copies):
            leaving.append(pltpu.make_async_copy(source, target, out_sems.at[part, n]))
            leaving[-1].start()

    for part in range(row_parts + 1):
        if part < row_parts:
            transform(part)
        if part == 0:
            prepare()
        else:
            whiten(part - 1)
            leave(part - 1)
    for copy in leaving:
        copy.wait()


def vmem_spec():
    return pl.BlockSpec(memory_space=pltpu.VMEM)


def smem_spec():
    return pl.BlockSpec(memory_space=pltpu.SMEM)


def whole(array):
    return pl.BlockSpec(array.shape, lambda s: (0,) * array.ndim)


def spectra_call(traces, quality, owners, places, chan_count, own_count):
    rows, length = traces.shape
    ch_dev = quality.shape[1]
    row_steps = rows // (6 * ch_dev) if rows % (6 * ch_dev) == 0 else rows // (2 * ch_dev)
    part, depth = rows // row_steps, length // QUARTERS
    slots = part // (2 * ch_dev) * 2 * CAP
    anywhere = pl.BlockSpec(memory_space=pl.ANY)
    out_shape = [
        jax.ShapeDtypeStruct((rows // 2, 2 * F), jnp.bfloat16),
        jax.ShapeDtypeStruct((rows // 2, 2 * F), jnp.bfloat16),
        jax.ShapeDtypeStruct((rows, 2 * F), jnp.bfloat16),
        jax.ShapeDtypeStruct((chan_count, row_steps * slots, 2 * F), jnp.bfloat16),
    ]
    if own_count % 16 == 0:
        windows, lower = rows // ch_dev, ch_dev - own_count
        out_shape += [
            jax.ShapeDtypeStruct((windows, own_count, 2 * F), jnp.bfloat16),
            jax.ShapeDtypeStruct((windows // 2, lower, 2 * F), jnp.bfloat16),
            jax.ShapeDtypeStruct((windows // 2, lower, 2 * F), jnp.bfloat16),
        ]
    return pl.pallas_call(
        spectra_kernel,
        in_specs=[anywhere] * 5,
        out_specs=[anywhere] * len(out_shape),
        out_shape=out_shape,
        scratch_shapes=[
            pltpu.VMEM((row_steps, QUARTERS, part, depth), jnp.bfloat16),
            pltpu.VMEM((depth, 2 * F), jnp.bfloat16),
            pltpu.VMEM(quality.shape, jnp.int32),
            pltpu.VMEM(owners.shape, jnp.int32),
            pltpu.VMEM(places.shape, jnp.int32),
            pltpu.VMEM((F, F), jnp.bfloat16),
            pltpu.VMEM((part, H), jnp.float32),
            pltpu.VMEM((2, QUARTERS * part, 2 * F), jnp.float32),
            pltpu.VMEM((row_steps, part, 2 * F), jnp.bfloat16),
            pltpu.VMEM((row_steps, part // ch_dev, ch_dev, 2 * F), jnp.bfloat16),
            pltpu.VMEM((row_steps, chan_count, slots, 2 * F), jnp.bfloat16),
            pltpu.VMEM((chan_count * 2 * CAP, 2 * ch_dev), jnp.bfloat16),
            pltpu.SemaphoreType.DMA((row_steps + 1, QUARTERS)),
            pltpu.SemaphoreType.DMA((row_steps, 3 + 2 * (part // (2 * ch_dev)))),
        ],
        compiler_params=pltpu.CompilerParams(vmem_limit_bytes=SPECTRA_VMEM_LIMIT),
        cost_estimate=pl.CostEstimate(
            flops=2 * rows * length * 2 * F, bytes_accessed=2 * rows * length, transcendentals=rows * F
        ),
        name="spectra",
    )(traces, jnp.asarray(forward_table(length)), quality, owners, places)


def cross_kernel(last, with_sum, skipped, through, *refs):
    refs = list(refs)
    blocks = [refs.pop(0) for _ in range(2 if with_sum else 3)]
    refs = refs[through:]
    sum_ref = refs.pop(0) if with_sum else None
    if last:
        table_ref, out_ref, done_ref, wide, spread, total, lags, sems = refs
        done_ref[...] = jnp.zeros_like(done_ref)
    else:
        total, *refs = refs
        wide, spread = refs[through:]
    windows, own_count = spread.shape[:2]
    ch_dev = wide.shape[1] // 2
    base = pl.multiple_of(lax.axis_index("win") * own_count, 8)

    def widen(w, carry):
        if with_sum:
            shared = ch_dev - own_count
            wide[w, shared:ch_dev, :] = blocks[0][skipped + w].astype(jnp.float32)
            rows = blocks[1][w].astype(jnp.float32)
            for tile in range(ch_dev // 8):
                at = base + 8 * tile
                at = pl.multiple_of(jnp.where(at < shared, at, at + own_count), 8)
                wide[w, pl.ds(at, 8), :] = rows[8 * tile : 8 * tile + 8]
        else:
            for half in range(2):
                place = half * (windows // 2) + w
                wide[place, :ch_dev, :] = blocks[0][place].astype(jnp.float32)
                wide[place, ch_dev:, :] = blocks[1 + half][w].astype(jnp.float32)
        return carry

    lax.fori_loop(0, windows if with_sum else windows // 2, widen, 0)

    def repeat(w, carry):
        for tile in range(own_count // 8):
            rows = wide[w, pl.ds(pl.multiple_of(base + 8 * tile, 8), 8), :]
            for i in range(8):
                for q in range(4):
                    spread[w, 8 * tile + i, q] = jnp.broadcast_to(rows[i : i + 1, q * H : (q + 1) * H], (8, H))
        return carry

    lax.fori_loop(0, windows, repeat, 0)

    group, tiles = 4, 3
    rounds = SPAN // (8 * tiles)

    def block(index, carry):
        g = index // rounds
        j = index % rounds
        start = pl.multiple_of(base + 8 * (g // 2) + 8 * tiles * j, 8)

        def add_window(w, sums):
            sums = list(sums)
            right = [
                [wide[w, pl.ds(pl.multiple_of(start + 8 * t, 8), 8), q * H : (q + 1) * H] for q in range(4)]
                for t in range(tiles)
            ]
            for i in range(group):
                left = [spread[w, group * g + i, q] for q in range(4)]
                for t in range(tiles):
                    at = 3 * (i * tiles + t)
                    r = right[t]
                    sums[at] = sums[at] + (left[0] * r[0] + left[1] * r[1])
                    sums[at + 1] = sums[at + 1] + (left[2] * r[2] + left[3] * r[3])
                    sums[at + 2] = sums[at + 2] + ((left[1] * r[0] - left[0] * r[1]) + (left[2] * r[3] - left[3] * r[2]))
            return tuple(sums)

        zero = jnp.zeros((8, H), jnp.float32)
        sums = lax.fori_loop(0, windows, add_window, (zero,) * (3 * group * tiles), unroll=3)
        for i in range(group):
            for t in range(tiles):
                at = 3 * (i * tiles + t)
                real, imag = fold_columns(sums[at], sums[at + 1], sums[at + 2])
                where = pl.ds(pl.multiple_of(8 * tiles * j + 8 * t, 8), 8)
                if with_sum:
                    real = real + sum_ref[group * g + i, where, :H]
                    imag = imag + sum_ref[group * g + i, where, H:]
                total[group * g + i, where, :H] = real
                total[group * g + i, where, H:] = imag
        return carry

    lax.fori_loop(0, own_count // group * rounds, block, 0)

    if last:
        copies = []
        for eight in range(own_count // 8):
            first = 8 * eight
            stacks = total[first : first + 8].reshape(8 * SPAN, F).astype(jnp.bfloat16)
            lagged = jnp.dot(stacks, table_ref[...], preferred_element_type=jnp.float32).reshape(8, SPAN, NLAG)
            for i in range(8):
                lags[first + i] = lagged[i, i + 1 : i + 1 + REACH, :]
            some = pl.ds(first, 8)
            copies.append(pltpu.make_async_copy(lags.at[some], out_ref.at[some], sems.at[eight]))
            copies[-1].start()
        for copy in copies:
            copy.wait()


def cross_call(blocks, windows, ch_dev, own_count, sums, table, skipped, share, through=()):
    columns = 2 * F
    last = table is not None
    with_sum = sums is not None
    operands = [*blocks, *through]
    anywhere = [pl.BlockSpec(memory_space=pl.ANY)] * len(through)
    in_specs = [vmem_spec()] * len(blocks) + anywhere
    if with_sum:
        operands.append(sums)
    scratch = [
        pltpu.VMEM((windows, 2 * ch_dev, columns), jnp.float32),
        pltpu.VMEM((windows, own_count, 4, 8, H), jnp.float32),
    ]
    if last:
        operands.append(table)
        scratch += [
            pltpu.VMEM((own_count, SPAN, F), jnp.float32),
            pltpu.VMEM((own_count, REACH, NLAG), jnp.float32),
            pltpu.SemaphoreType.DMA((own_count // 8,)),
        ]
    shape = (own_count, REACH, NLAG) if last else (own_count, SPAN, F)
    out_shape = [jax.ShapeDtypeStruct(shape, jnp.float32)]
    out_specs = [pl.BlockSpec(memory_space=pl.ANY) if last else vmem_spec()] + anywhere
    if last:
        out_shape.append(jax.ShapeDtypeStruct((8, H), jnp.float32))
        out_specs.append(vmem_spec())
    out_shape += [jax.ShapeDtypeStruct(array.shape, array.dtype) for array in through]
    return pl.pallas_call(
        functools.partial(cross_kernel, last, with_sum, skipped, len(through)),
        in_specs=in_specs + [vmem_spec()] * (len(operands) - len(in_specs)),
        input_output_aliases={len(blocks) + n: 1 + n for n in range(len(through))},
        out_specs=out_specs,
        out_shape=out_shape,
        scratch_shapes=scratch,
        compiler_params=pltpu.CompilerParams(vmem_limit_bytes=VMEM_LIMIT),
        cost_estimate=pl.CostEstimate(
            flops=int(30_000_000_000 * share), bytes_accessed=4 * windows * ch_dev * columns + 4 * own_count * SPAN * F, transcendentals=0
        ),
        name="cross",
    )(*operands)


def fold_kernel(incoming_ref, own_ref, owners_ref, high_ref, low_ref, earlier_ref, out_ref):
    ch_dev = out_ref.shape[0]
    rows = 2 * ch_dev
    pairs = own_ref.shape[0] // rows
    count, slots, columns = incoming_ref.shape
    owners = owners_ref[...].astype(jnp.float32)
    per_row = owners.shape[1] // ch_dev
    device = lax.axis_index("chan")
    line = jnp.sum(jnp.where(rows_of(owners.shape) == device // per_row, owners, 0.0), axis=0, keepdims=True)
    shape = (rows, owners.shape[1])
    line = jnp.broadcast_to(line, shape)
    first = device % per_row * ch_dev
    place = first + rows_of(shape) % ch_dev
    lane = lanes_of(shape)
    owner = jnp.sum(jnp.where(lane == place, line, 0.0), axis=1, keepdims=True)
    earlier = (lane >= first) & (lane < place) & (line == owner)
    rank = jnp.sum(earlier.astype(jnp.float32), axis=1, keepdims=True)
    source = (2 * CAP * owner + rank).astype(jnp.int32)
    shape = (rows, count * 2 * CAP)
    target = source + CAP * (rows_of(shape) // ch_dev)
    picker = (lanes_of(shape) == target).astype(jnp.float32).astype(jnp.bfloat16)
    sums = None
    for n in range(pairs):
        arrived = incoming_ref[:, 2 * CAP * n : 2 * CAP * (n + 1), :].reshape(count * 2 * CAP, columns)
        right = jnp.dot(picker, arrived, preferred_element_type=jnp.float32)
        left = own_ref[rows * n : rows * (n + 1), :].astype(jnp.float32)
        l = [left[:, q * H : (q + 1) * H] for q in range(4)]
        r = [right[:, q * H : (q + 1) * H] for q in range(4)]
        terms = [
            l[0] * r[0] + l[1] * r[1],
            l[2] * r[2] + l[3] * r[3],
            (l[1] * r[0] - l[0] * r[1]) + (l[2] * r[3] - l[3] * r[2]),
        ]
        sums = terms if sums is None else [total + term for total, term in zip(sums, terms)]
    stacks = jnp.concatenate(fold_columns(*[total[:ch_dev] + total[ch_dev:] for total in sums]), axis=1)
    out_ref[...] = lag_transform(stacks, high_ref[...], low_ref[...])


def fold_call(incoming, own, owners, ch_dev, tables, earlier):
    return pl.pallas_call(
        fold_kernel,
        in_specs=[vmem_spec()] * 5 + [pl.BlockSpec(memory_space=pl.ANY)],
        out_specs=vmem_spec(),
        out_shape=jax.ShapeDtypeStruct((ch_dev, NLAG), jnp.float32),
        compiler_params=pltpu.CompilerParams(vmem_limit_bytes=FOLD_VMEM_LIMIT),
        cost_estimate=pl.CostEstimate(
            flops=4 * ch_dev * incoming.size, bytes_accessed=2 * (incoming.size + own.size), transcendentals=0
        ),
        name="fold",
    )(incoming, own, owners, *tables, earlier)


def from_above(block):
    count = lax.axis_size("chan")
    return lax.ppermute(block, "chan", [(i, i - 1) for i in range(1, count)])


def round_win(block, shift):
    count = lax.axis_size("win")
    return lax.ppermute(block, "win", [(i, (i + shift) % count) for i in range(count)])


def local(traces, quality, fold_block, fold_offset):
    win_dev, ch_dev, length = traces.shape
    chan_count = lax.axis_size("chan")
    win_count = lax.axis_size("win")
    window_part = lax.axis_index("win")
    own_count = ch_dev // win_count
    shared = ch_dev - own_count
    tables = [jnp.asarray(t) for t in inverse_tables(1.0 / math.sqrt(F * win_dev * win_count))]
    owners = fold_block.reshape(-1, 2 * ch_dev)
    places = fold_offset.reshape(-1, 2 * ch_dev)
    early, late, flat, outgoing, *row_parts = spectra_call(
        traces.reshape(win_dev * ch_dev, length), quality.reshape(1, ch_dev), owners, places, chan_count, own_count
    )
    half = win_dev // 2
    halves = [rows.reshape(half, ch_dev, 2 * F) for rows in (early, late)]
    if not row_parts:
        row_parts = [jnp.concatenate([block[:, shared:] for block in halves], axis=0)]
        row_parts += [block[:, :shared] for block in halves]
    ready, *lower = row_parts
    upper = [from_above(block) for block in halves]
    common = [round_win(ready, shift) for shift in range(1, win_count)]
    incoming = lax.all_to_all(outgoing, "chan", split_axis=0, concat_axis=0, tiled=True)

    def offers(part):
        rows = jnp.concatenate([lower[part], upper[part]], axis=1)
        return [
            lax.dynamic_slice_in_dim(rows, (window_part + shift) % win_count * own_count, ch_dev, 1)
            for shift in range(1, win_count)
        ]

    sooner = [round_win(block, shift) for shift, block in enumerate(offers(0), 1)]
    sums, *waiting = cross_call(
        [flat.reshape(win_dev, ch_dev, 2 * F)] + upper, win_dev, ch_dev, own_count, None, None, 0, 1.0, through=offers(1)
    )
    later = [round_win(block, shift) for shift, block in enumerate(waiting, 1)]
    arrived = []
    for rows, *others in zip(common, sooner, later):
        arrived += [([rows, block], n * half) for n, block in enumerate(others)]
    for n, (blocks, skipped) in enumerate(arrived):
        ends = tables[0] if n == len(arrived) - 1 else None
        sums, *done = cross_call(blocks, half, ch_dev, own_count, sums, ends, skipped, 0.5)
    share = fold_call(incoming, flat, owners, ch_dev, tables, done[0])
    fold = lax.dynamic_slice_in_dim(share, window_part * own_count, own_count, 0)
    for shift in range(1, win_count):
        target = (window_part + shift) % win_count * own_count
        fold = fold + round_win(lax.dynamic_slice_in_dim(share, target, own_count, 0), shift)
    return (sums, fold)


def solution(mesh):
    in_specs = (P("win", "chan", None), P("chan"), P(), P())
    out_specs = (P(("chan", "win"), None, None), P(("chan", "win"), None))
    return jax.shard_map(local, mesh=mesh, in_specs=in_specs, out_specs=out_specs, check_vma=False)
```

```python
import functools
import math

import jax
import jax.numpy as jnp
import numpy as np
from jax import lax
from jax.experimental import pallas as pl
from jax.experimental.pallas import tpu as pltpu
from jax.sharding import PartitionSpec as P

F = 256
H = F // 2
BAND_LO = 32
NLAG = 256
REACH = 64
CAP = 8
SPAN = REACH + 8
smooth_reach = 4
QUARTERS = 4
VMEM_LIMIT = 24 * 1024 * 1024
FOLD_VMEM_LIMIT = 16 * 1024 * 1024
SPECTRA_VMEM_LIMIT = 59 * 1024 * 1024


def bin_order():
    residues = np.arange(H)
    first = (residues - BAND_LO) % F
    second = (-residues - BAND_LO) % F
    second[0] = (H - BAND_LO) % F
    return first, second


def forward_table(length):
    samples = np.arange(length // 4, dtype=np.int64)[:, None]
    parts = []
    for bins in bin_order():
        angles = (samples * (bins + BAND_LO)[None, :] % length) * (2.0 * math.pi / length)
        parts += [np.cos(angles), -np.sin(angles)]
    return np.concatenate(parts, axis=1).astype(np.float32).astype(jnp.bfloat16)


def inverse_tables(factor):
    shifts = (np.arange(NLAG) + NLAG // 2)[None, :]
    residues = np.arange(H)[:, None]
    angles = (residues * shifts % NLAG) * (2.0 * math.pi / NLAG)
    sign = np.where(shifts[0] % 2 == 0, 1.0, -1.0)
    real, imag = np.cos(angles), -np.sin(angles)
    real[0] = (1.0 + sign) / 2.0
    imag[0] = (1.0 - sign) / 2.0
    table = np.concatenate([real, imag], axis=0) * factor
    high = table.astype(np.float32).astype(jnp.bfloat16)
    low = (table - high.astype(np.float64)).astype(np.float32).astype(jnp.bfloat16)
    return high, low


def lag_transform(stacks, high, low):
    top = stacks.astype(jnp.bfloat16)
    rest = (stacks - top.astype(jnp.float32)).astype(jnp.bfloat16)
    dot = functools.partial(jnp.dot, preferred_element_type=jnp.float32)
    return dot(top, high) + (dot(rest, high) + dot(top, low))


def fold_columns(first, second, imag):
    lane = lax.broadcasted_iota(jnp.int32, first.shape, first.ndim - 1)
    return first + second, jnp.where(lane == 0, first - second, imag)


def lanes_of(shape):
    return lax.broadcasted_iota(jnp.int32, shape, len(shape) - 1)


def rows_of(shape):
    return lax.broadcasted_iota(jnp.int32, shape, len(shape) - 2)


def band_matrix():
    def bins(index):
        lane = index & (H - 1)
        residue = jnp.where(index < H, lane, jnp.where(lane == 0, H, F - lane))
        return (residue - BAND_LO + F) & (F - 1)

    apart = bins(rows_of((F, F))) - bins(lanes_of((F, F)))
    return (jnp.abs(apart) <= smooth_reach).astype(jnp.float32).astype(jnp.bfloat16)


def exact_dot(left, right):
    return jnp.dot(left.astype(jnp.bfloat16), right.astype(jnp.bfloat16), preferred_element_type=jnp.float32)


def over(value, power):
    return value >> (power.bit_length() - 1)


def within(value, power):
    return value & (power - 1)


def slot_selector(owners, places, device, ch_dev):
    height, width = owners.shape
    per_row = width // ch_dev
    wanted = (owners == device).astype(jnp.float32)
    before = rows_of((width, width))
    after = lanes_of((width, width))
    earlier = ((before < after) & (over(before, ch_dev) == over(after, ch_dev))).astype(jnp.float32)
    ranks = exact_dot(wanted, earlier)
    slots = jnp.where(wanted > 0, ranks, float(CAP))
    count = height * per_row * 2 * CAP
    to_row = (over(rows_of((count, height)), 2 * CAP * per_row) == lanes_of((count, height))).astype(jnp.float32)
    row_slots = exact_dot(to_row, slots)
    row_places = exact_dot(to_row, places.astype(jnp.float32))
    shape = (count, width)
    row = rows_of(shape)
    mine = (row_slots == within(row, CAP).astype(jnp.float32)) & (
        over(lanes_of(shape), ch_dev) == within(over(row, 2 * CAP), per_row)
    )
    place = jnp.sum(jnp.where(mine, row_places + 1.0, 0.0), axis=1, keepdims=True).astype(jnp.int32) - 1
    shape = (count, 2 * ch_dev)
    half = within(over(rows_of(shape), CAP), 2)
    lane = lanes_of(shape)
    return ((lane == place + ch_dev * half) & (place >= 0)).astype(jnp.float32).astype(jnp.bfloat16)


def turned_sum(quarters, real, imag, negative):
    rows = quarters[0].shape[0]
    lane = lanes_of((rows, H))
    residue = ((F - lane) if negative else lane) & 3
    sign = jnp.where((residue & 1) == 0, 1.0, -1.0)
    straight = jnp.where(residue == 0, 1.0, jnp.where(residue == 2, -1.0, 0.0))
    turned = jnp.where(residue == 1, 1.0, jnp.where(residue == 3, -1.0, 0.0))
    re = [quarter[:, real * H : (real + 1) * H] for quarter in quarters]
    im = [quarter[:, imag * H : (imag + 1) * H] for quarter in quarters]
    odd_re, odd_im = re[1] + sign * re[3], im[1] + sign * im[3]
    return (
        re[0] + sign * re[2] + (straight * odd_re + turned * odd_im),
        im[0] + sign * im[2] + (straight * odd_im - turned * odd_re),
    )


def spectra_kernel(traces_ref, table_ref, quality_ref, owners_ref, places_ref, *refs):
    early_ref, late_ref, whitened_ref, outgoing_ref, *row_refs = refs[:-14]
    traces, table, quality, owners, places, band, keep_rows, products, white, white_windows, sent, selector, sems, out_sems = refs[-14:]
    row_parts, chunks, rows, depth = traces.shape
    ch_dev = quality.shape[1]
    pair = 2 * ch_dev
    count = outgoing_ref.shape[0]
    slots = sent.shape[2]

    def traces_copy(part, k):
        source = traces_ref.at[pl.ds(part * rows, rows), pl.ds(k * depth, depth)]
        return pltpu.make_async_copy(source, traces.at[part, k], sems.at[part, k])

    small = [
        pltpu.make_async_copy(source, target, sems.at[row_parts, k])
        for k, (source, target) in enumerate(
            ((table_ref, table), (quality_ref, quality), (owners_ref, owners), (places_ref, places))
        )
    ]
    for copy in small:
        copy.start()
    for part in range(row_parts):
        for k in range(chunks):
            traces_copy(part, k).start()

    small[0].wait()
    leaving = []

    def prepare():
        band[...] = band_matrix()
        for copy in small[1:]:
            copy.wait()
        shape = (rows, ch_dev)
        keep = jnp.sum(
            jnp.where(within(rows_of(shape), ch_dev) == lanes_of(shape), quality[...].astype(jnp.float32), 0.0),
            axis=1, keepdims=True,
        )
        selector[...] = slot_selector(owners[...], places[...], lax.axis_index("chan"), ch_dev)
        keep_rows[...] = jnp.broadcast_to(keep, keep_rows.shape)

    def transform(part):
        for k in range(chunks):
            traces_copy(part, k).wait()
        stacked = traces[part].reshape(chunks * rows, depth)
        products[part % 2] = jnp.dot(stacked, table[...], preferred_element_type=jnp.float32)

    def whiten(part):
        quarters = [products[part % 2, k * rows : (k + 1) * rows, :] for k in range(chunks)]
        parts = turned_sum(quarters, 0, 1, False) + turned_sum(quarters, 2, 3, True)
        energy = jnp.concatenate(
            [parts[0] * parts[0] + parts[1] * parts[1], parts[2] * parts[2] + parts[3] * parts[3]], axis=1
        )
        top = energy.astype(jnp.bfloat16)
        rest = (energy - top.astype(jnp.float32)).astype(jnp.bfloat16)
        smooth = jnp.dot(top, band[...], preferred_element_type=jnp.float32) + jnp.dot(
            rest, band[...], preferred_element_type=jnp.float32
        )
        water = jnp.sum(energy, axis=1, keepdims=True) * (1.0 / F)
        scaling = lax.rsqrt(smooth * (1.0 / (2.0 * smooth_reach + 1.0)) + (0.1 * water + 1e-06))
        near, far = scaling[:, :H] * keep_rows[...], scaling[:, H:] * keep_rows[...]
        values = jnp.concatenate(
            [parts[0] * near, parts[1] * near, parts[2] * far, parts[3] * far], axis=1
        ).astype(jnp.bfloat16)
        white[part] = values
        if row_refs:
            white_windows[part] = values.reshape(rows // ch_dev, ch_dev, values.shape[-1])
        for n in range(rows // pair):
            chosen = jnp.dot(
                selector[...], values[pair * n : pair * (n + 1), :], preferred_element_type=jnp.float32
            ).astype(jnp.bfloat16)
            sent[part, :, 2 * CAP * n : 2 * CAP * (n + 1), :] = chosen.reshape(count, 2 * CAP, chosen.shape[-1])

    def leave(part):
        pairs = rows // pair
        copies = [
            (sent.at[part], outgoing_ref.at[:, pl.ds(part * slots, slots), :]),
            (white.at[part], whitened_ref.at[pl.ds(part * rows, rows), :]),
        ]
        if row_refs:
            shared_ref, *lower_refs = row_refs
            height = shared_ref.shape[1]
            split = ch_dev - height
            copies.append(
                (white_windows.at[part, :, pl.ds(split, height), :], shared_ref.at[pl.ds(2 * pairs * part, 2 * pairs)])
            )
        for n in range(pairs):
            late, place = divmod(part * pairs + n, row_parts * pairs // 2)
            copies.append(
                (white.at[part, pl.ds(n * pair, pair), :], (early_ref, late_ref)[late].at[pl.ds(place * pair, pair), :])
            )
            if row_refs:
                copies.append(
                    (
                        white_windows.at[part, pl.ds(2 * n, 2), pl.ds(0, split), :],
                        lower_refs[late].at[pl.ds(2 * place, 2)],
                    )
                )
        for n, (source, target) in enumerate(copies):
            leaving.append(pltpu.make_async_copy(source, target, out_sems.at[part, n]))
            leaving[-1].start()

    for part in range(row_parts + 1):
        if part < row_parts:
            transform(part)
        if part == 0:
            prepare()
        else:
            whiten(part - 1)
            leave(part - 1)
    for copy in leaving:
        copy.wait()


def vmem_spec():
    return pl.BlockSpec(memory_space=pltpu.VMEM)


def smem_spec():
    return pl.BlockSpec(memory_space=pltpu.SMEM)


def whole(array):
    return pl.BlockSpec(array.shape, lambda s: (0,) * array.ndim)


def spectra_call(traces, quality, owners, places, chan_count, own_count):
    rows, length = traces.shape
    ch_dev = quality.shape[1]
    row_steps = rows // (4 * ch_dev) if rows % (4 * ch_dev) == 0 else rows // (2 * ch_dev)
    part, depth = rows // row_steps, length // QUARTERS
    slots = part // (2 * ch_dev) * 2 * CAP
    anywhere = pl.BlockSpec(memory_space=pl.ANY)
    out_shape = [
        jax.ShapeDtypeStruct((rows // 2, 2 * F), jnp.bfloat16),
        jax.ShapeDtypeStruct((rows // 2, 2 * F), jnp.bfloat16),
        jax.ShapeDtypeStruct((rows, 2 * F), jnp.bfloat16),
        jax.ShapeDtypeStruct((chan_count, row_steps * slots, 2 * F), jnp.bfloat16),
    ]
    if own_count % 16 == 0:
        windows, lower = rows // ch_dev, ch_dev - own_count
        out_shape += [
            jax.ShapeDtypeStruct((windows, own_count, 2 * F), jnp.bfloat16),
            jax.ShapeDtypeStruct((windows // 2, lower, 2 * F), jnp.bfloat16),
            jax.ShapeDtypeStruct((windows // 2, lower, 2 * F), jnp.bfloat16),
        ]
    return pl.pallas_call(
        spectra_kernel,
        in_specs=[anywhere] * 5,
        out_specs=[anywhere] * len(out_shape),
        out_shape=out_shape,
        scratch_shapes=[
            pltpu.VMEM((row_steps, QUARTERS, part, depth), jnp.bfloat16),
            pltpu.VMEM((depth, 2 * F), jnp.bfloat16),
            pltpu.VMEM(quality.shape, jnp.int32),
            pltpu.VMEM(owners.shape, jnp.int32),
            pltpu.VMEM(places.shape, jnp.int32),
            pltpu.VMEM((F, F), jnp.bfloat16),
            pltpu.VMEM((part, H), jnp.float32),
            pltpu.VMEM((2, QUARTERS * part, 2 * F), jnp.float32),
            pltpu.VMEM((row_steps, part, 2 * F), jnp.bfloat16),
            pltpu.VMEM((row_steps, part // ch_dev, ch_dev, 2 * F), jnp.bfloat16),
            pltpu.VMEM((row_steps, chan_count, slots, 2 * F), jnp.bfloat16),
            pltpu.VMEM((chan_count * 2 * CAP, 2 * ch_dev), jnp.bfloat16),
            pltpu.SemaphoreType.DMA((row_steps + 1, QUARTERS)),
            pltpu.SemaphoreType.DMA((row_steps, 3 + 2 * (part // (2 * ch_dev)))),
        ],
        compiler_params=pltpu.CompilerParams(vmem_limit_bytes=SPECTRA_VMEM_LIMIT),
        cost_estimate=pl.CostEstimate(
            flops=2 * rows * length * 2 * F, bytes_accessed=2 * rows * length, transcendentals=rows * F
        ),
        name="spectra",
    )(traces, jnp.asarray(forward_table(length)), quality, owners, places)


def cross_kernel(last, with_sum, skipped, through, *refs):
    refs = list(refs)
    blocks = [refs.pop(0) for _ in range(2 if with_sum else 3)]
    refs = refs[through:]
    sum_ref = refs.pop(0) if with_sum else None
    if last:
        table_ref, out_ref, done_ref, wide, spread, total, lags, sems = refs
        done_ref[...] = jnp.zeros_like(done_ref)
    else:
        total, *refs = refs
        wide, spread = refs[through:]
    windows, own_count = spread.shape[:2]
    ch_dev = wide.shape[1] // 2
    base = pl.multiple_of(lax.axis_index("win") * own_count, 8)

    def widen(w, carry):
        if with_sum:
            shared = ch_dev - own_count
            wide[w, shared:ch_dev, :] = blocks[0][skipped + w].astype(jnp.float32)
            rows = blocks[1][w].astype(jnp.float32)
            for tile in range(ch_dev // 8):
                at = base + 8 * tile
                at = pl.multiple_of(jnp.where(at < shared, at, at + own_count), 8)
                wide[w, pl.ds(at, 8), :] = rows[8 * tile : 8 * tile + 8]
        else:
            for half in range(2):
                place = half * (windows // 2) + w
                wide[place, :ch_dev, :] = blocks[0][place].astype(jnp.float32)
                wide[place, ch_dev:, :] = blocks[1 + half][w].astype(jnp.float32)
        return carry

    lax.fori_loop(0, windows if with_sum else windows // 2, widen, 0)

    def repeat(w, carry):
        for tile in range(own_count // 8):
            rows = wide[w, pl.ds(pl.multiple_of(base + 8 * tile, 8), 8), :]
            for i in range(8):
                for q in range(4):
                    spread[w, 8 * tile + i, q] = jnp.broadcast_to(rows[i : i + 1, q * H : (q + 1) * H], (8, H))
        return carry

    lax.fori_loop(0, windows, repeat, 0)

    group, tiles = 4, 3
    rounds = SPAN // (8 * tiles)

    def block(index, carry):
        g = index // rounds
        j = index % rounds
        start = pl.multiple_of(base + 8 * (g // 2) + 8 * tiles * j, 8)

        def add_window(w, sums):
            sums = list(sums)
            right = [
                [wide[w, pl.ds(pl.multiple_of(start + 8 * t, 8), 8), q * H : (q + 1) * H] for q in range(4)]
                for t in range(tiles)
            ]
            for i in range(group):
                left = [spread[w, group * g + i, q] for q in range(4)]
                for t in range(tiles):
                    at = 3 * (i * tiles + t)
                    r = right[t]
                    sums[at] = sums[at] + (left[0] * r[0] + left[1] * r[1])
                    sums[at + 1] = sums[at + 1] + (left[2] * r[2] + left[3] * r[3])
                    sums[at + 2] = sums[at + 2] + ((left[1] * r[0] - left[0] * r[1]) + (left[2] * r[3] - left[3] * r[2]))
            return tuple(sums)

        zero = jnp.zeros((8, H), jnp.float32)
        sums = lax.fori_loop(0, windows, add_window, (zero,) * (3 * group * tiles), unroll=3)
        for i in range(group):
            for t in range(tiles):
                at = 3 * (i * tiles + t)
                real, imag = fold_columns(sums[at], sums[at + 1], sums[at + 2])
                where = pl.ds(pl.multiple_of(8 * tiles * j + 8 * t, 8), 8)
                if with_sum:
                    real = real + sum_ref[group * g + i, where, :H]
                    imag = imag + sum_ref[group * g + i, where, H:]
                total[group * g + i, where, :H] = real
                total[group * g + i, where, H:] = imag
        return carry

    lax.fori_loop(0, own_count // group * rounds, block, 0)

    if last:
        copies = []
        for eight in range(own_count // 8):
            first = 8 * eight
            stacks = total[first : first + 8].reshape(8 * SPAN, F).astype(jnp.bfloat16)
            lagged = jnp.dot(stacks, table_ref[...], preferred_element_type=jnp.float32).reshape(8, SPAN, NLAG)
            for i in range(8):
                lags[first + i] = lagged[i, i + 1 : i + 1 + REACH, :]
            some = pl.ds(first, 8)
            copies.append(pltpu.make_async_copy(lags.at[some], out_ref.at[some], sems.at[eight]))
            copies[-1].start()
        for copy in copies:
            copy.wait()


def cross_call(blocks, windows, ch_dev, own_count, sums, table, skipped, share, through=()):
    columns = 2 * F
    last = table is not None
    with_sum = sums is not None
    operands = [*blocks, *through]
    anywhere = [pl.BlockSpec(memory_space=pl.ANY)] * len(through)
    in_specs = [vmem_spec()] * len(blocks) + anywhere
    if with_sum:
        operands.append(sums)
    scratch = [
        pltpu.VMEM((windows, 2 * ch_dev, columns), jnp.float32),
        pltpu.VMEM((windows, own_count, 4, 8, H), jnp.float32),
    ]
    if last:
        operands.append(table)
        scratch += [
            pltpu.VMEM((own_count, SPAN, F), jnp.float32),
            pltpu.VMEM((own_count, REACH, NLAG), jnp.float32),
            pltpu.SemaphoreType.DMA((own_count // 8,)),
        ]
    shape = (own_count, REACH, NLAG) if last else (own_count, SPAN, F)
    out_shape = [jax.ShapeDtypeStruct(shape, jnp.float32)]
    out_specs = [pl.BlockSpec(memory_space=pl.ANY) if last else vmem_spec()] + anywhere
    if last:
        out_shape.append(jax.ShapeDtypeStruct((8, H), jnp.float32))
        out_specs.append(vmem_spec())
    out_shape += [jax.ShapeDtypeStruct(array.shape, array.dtype) for array in through]
    return pl.pallas_call(
        functools.partial(cross_kernel, last, with_sum, skipped, len(through)),
        in_specs=in_specs + [vmem_spec()] * (len(operands) - len(in_specs)),
        input_output_aliases={len(blocks) + n: 1 + n for n in range(len(through))},
        out_specs=out_specs,
        out_shape=out_shape,
        scratch_shapes=scratch,
        compiler_params=pltpu.CompilerParams(vmem_limit_bytes=VMEM_LIMIT),
        cost_estimate=pl.CostEstimate(
            flops=int(30_000_000_000 * share), bytes_accessed=4 * windows * ch_dev * columns + 4 * own_count * SPAN * F, transcendentals=0
        ),
        name="cross",
    )(*operands)


def fold_kernel(incoming_ref, own_ref, owners_ref, high_ref, low_ref, earlier_ref, out_ref):
    ch_dev = out_ref.shape[0]
    rows = 2 * ch_dev
    pairs = own_ref.shape[0] // rows
    count, slots, columns = incoming_ref.shape
    owners = owners_ref[...].astype(jnp.float32)
    per_row = owners.shape[1] // ch_dev
    device = lax.axis_index("chan")
    line = jnp.sum(jnp.where(rows_of(owners.shape) == device // per_row, owners, 0.0), axis=0, keepdims=True)
    shape = (rows, owners.shape[1])
    line = jnp.broadcast_to(line, shape)
    first = device % per_row * ch_dev
    place = first + rows_of(shape) % ch_dev
    lane = lanes_of(shape)
    owner = jnp.sum(jnp.where(lane == place, line, 0.0), axis=1, keepdims=True)
    earlier = (lane >= first) & (lane < place) & (line == owner)
    rank = jnp.sum(earlier.astype(jnp.float32), axis=1, keepdims=True)
    source = (2 * CAP * owner + rank).astype(jnp.int32)
    shape = (rows, count * 2 * CAP)
    target = source + CAP * (rows_of(shape) // ch_dev)
    picker = (lanes_of(shape) == target).astype(jnp.float32).astype(jnp.bfloat16)
    sums = None
    for n in range(pairs):
        arrived = incoming_ref[:, 2 * CAP * n : 2 * CAP * (n + 1), :].reshape(count * 2 * CAP, columns)
        right = jnp.dot(picker, arrived, preferred_element_type=jnp.float32)
        left = own_ref[rows * n : rows * (n + 1), :].astype(jnp.float32)
        l = [left[:, q * H : (q + 1) * H] for q in range(4)]
        r = [right[:, q * H : (q + 1) * H] for q in range(4)]
        terms = [
            l[0] * r[0] + l[1] * r[1],
            l[2] * r[2] + l[3] * r[3],
            (l[1] * r[0] - l[0] * r[1]) + (l[2] * r[3] - l[3] * r[2]),
        ]
        sums = terms if sums is None else [total + term for total, term in zip(sums, terms)]
    stacks = jnp.concatenate(fold_columns(*[total[:ch_dev] + total[ch_dev:] for total in sums]), axis=1)
    out_ref[...] = lag_transform(stacks, high_ref[...], low_ref[...])


def fold_call(incoming, own, owners, ch_dev, tables, earlier):
    return pl.pallas_call(
        fold_kernel,
        in_specs=[vmem_spec()] * 5 + [pl.BlockSpec(memory_space=pl.ANY)],
        out_specs=vmem_spec(),
        out_shape=jax.ShapeDtypeStruct((ch_dev, NLAG), jnp.float32),
        compiler_params=pltpu.CompilerParams(vmem_limit_bytes=FOLD_VMEM_LIMIT),
        cost_estimate=pl.CostEstimate(
            flops=4 * ch_dev * incoming.size, bytes_accessed=2 * (incoming.size + own.size), transcendentals=0
        ),
        name="fold",
    )(incoming, own, owners, *tables, earlier)


def from_above(block):
    count = lax.axis_size("chan")
    return lax.ppermute(block, "chan", [(i, i - 1) for i in range(1, count)])


def round_win(block, shift):
    count = lax.axis_size("win")
    return lax.ppermute(block, "win", [(i, (i + shift) % count) for i in range(count)])


def local(traces, quality, fold_block, fold_offset):
    win_dev, ch_dev, length = traces.shape
    chan_count = lax.axis_size("chan")
    win_count = lax.axis_size("win")
    window_part = lax.axis_index("win")
    own_count = ch_dev // win_count
    shared = ch_dev - own_count
    tables = [jnp.asarray(t) for t in inverse_tables(1.0 / math.sqrt(F * win_dev * win_count))]
    owners = fold_block.reshape(-1, 2 * ch_dev)
    places = fold_offset.reshape(-1, 2 * ch_dev)
    early, late, flat, outgoing, *row_parts = spectra_call(
        traces.reshape(win_dev * ch_dev, length), quality.reshape(1, ch_dev), owners, places, chan_count, own_count
    )
    half = win_dev // 2
    halves = [rows.reshape(half, ch_dev, 2 * F) for rows in (early, late)]
    if not row_parts:
        row_parts = [jnp.concatenate([block[:, shared:] for block in halves], axis=0)]
        row_parts += [block[:, :shared] for block in halves]
    ready, *lower = row_parts
    upper = [from_above(block) for block in halves]
    common = [round_win(ready, shift) for shift in range(1, win_count)]
    incoming = lax.all_to_all(outgoing, "chan", split_axis=0, concat_axis=0, tiled=True)

    def offers(part):
        rows = jnp.concatenate([lower[part], upper[part]], axis=1)
        return [
            lax.dynamic_slice_in_dim(rows, (window_part + shift) % win_count * own_count, ch_dev, 1)
            for shift in range(1, win_count)
        ]

    sooner = [round_win(block, shift) for shift, block in enumerate(offers(0), 1)]
    sums, *waiting = cross_call(
        [flat.reshape(win_dev, ch_dev, 2 * F)] + upper, win_dev, ch_dev, own_count, None, None, 0, 1.0, through=offers(1)
    )
    later = [round_win(block, shift) for shift, block in enumerate(waiting, 1)]
    arrived = []
    for rows, *others in zip(common, sooner, later):
        arrived += [([rows, block], n * half) for n, block in enumerate(others)]
    for n, (blocks, skipped) in enumerate(arrived):
        ends = tables[0] if n == len(arrived) - 1 else None
        sums, *done = cross_call(blocks, half, ch_dev, own_count, sums, ends, skipped, 0.5)
    share = fold_call(incoming, flat, owners, ch_dev, tables, done[0])
    fold = lax.dynamic_slice_in_dim(share, window_part * own_count, own_count, 0)
    for shift in range(1, win_count):
        target = (window_part + shift) % win_count * own_count
        fold = fold + round_win(lax.dynamic_slice_in_dim(share, target, own_count, 0), shift)
    return (sums, fold)


def solution(mesh):
    in_specs = (P("win", "chan", None), P("chan"), P(), P())
    out_specs = (P(("chan", "win"), None, None), P(("chan", "win"), None))
    return jax.shard_map(local, mesh=mesh, in_specs=in_specs, out_specs=out_specs, check_vma=False)
```
